32 devices in a mesh: seq: 8 (over y, x, core), mp: 4 (over z).
Axes of the slice: x: 2, y: 2, z: 4, core: 2. Of those that a mesh axis runs over, the one named last changes fastest.
Arguments:
- tokens: bfloat16 [8192, 2048], P(('seq', 'mp'))
- gain_mix: float32 [2048], replicated, may hold values from 0.25 to 1.75
- w_query: bfloat16 [2048, 2048], P(None, 'mp')
- w_key: bfloat16 [2048, 2048], P(None, 'mp')
- w_value: bfloat16 [2048, 4096], P(None, 'mp')
- w_gate: bfloat16 [2048, 4096], P(None, 'mp')
- w_out: bfloat16 [4096, 2048], P('mp')
- gain_ffn: float32 [2048], replicated, may hold values from 0.25 to 1.75
- w_up: bfloat16 [2048, 4096], P(None, 'mp')
- w_down: bfloat16 [4096, 2048], P('mp')
- cotangent: bfloat16 [8192, 2048], P(('seq', 'mp'))
Outputs:
- output: bfloat16 [8192, 2048], P(('seq', 'mp'))
- grad_tokens: bfloat16 [8192, 2048], P(('seq', 'mp'))
- grad_gain_mix: float32 [2048], replicated
- grad_w_query: float32 [2048, 2048], P('seq', 'mp')
- grad_w_key: float32 [2048, 2048], P('seq', 'mp')
- grad_w_value: float32 [2048, 4096], P('seq', 'mp')
- grad_w_gate: float32 [2048, 4096], P('seq', 'mp')
- grad_w_out: float32 [4096, 2048], P(('mp', 'seq'))
- grad_gain_ffn: float32 [2048], replicated
- grad_w_up: float32 [2048, 4096], P('seq', 'mp')
- grad_w_down: float32 [4096, 2048], P(('mp', 'seq'))
The draws below stay inside these ranges and needn't reach their ends.
All inputs are finite; a program needn't handle non-finite values.
Results may differ from the reference program's by a relative error of at most 0.02.
Values may be sent and summed in bfloat16 or wider, within the bound.
A program may use at most 320 MiB of HBM per device.

```python
import jax
import jax.numpy as jnp
from jax import lax

D = 2048
HEADS = 8
DK = 256
DV = 512
FFH = 4096
STRETCH = 256
SPAN = 1024
LENGTH = 4096
TOKENS = 8192


def drawn_law(key, shape, scale):
    return jnp.clip(jax.random.normal(key, shape, jnp.float32), -6.0, 6.0) * scale


def draw_tokens(key, part):
    key = jax.random.fold_in(key, 3)
    value_key = jax.random.fold_in(key, 0)
    pair_key = jax.random.fold_in(key, 2)
    values = drawn_law(value_key, (TOKENS, D), 1.0)
    groups = TOKENS // SPAN
    pairing = jax.random.permutation(pair_key, groups)
    row_group = jnp.arange(TOKENS, dtype=jnp.int32) // SPAN
    column_group = jnp.arange(D, dtype=jnp.int32) // (D // groups)
    chosen = pairing[row_group][:, None] == column_group[None, :]
    values = jnp.where(chosen, 3.0 * values, values)
    return values.astype(jnp.bfloat16)


def draw_w_query(key, part):
    key = jax.random.fold_in(key, 11)
    values = drawn_law(key, (D, HEADS * DK), D ** (-0.5))
    return values.astype(jnp.bfloat16)


def draw_w_key(key, part):
    key = jax.random.fold_in(key, 13)
    values = drawn_law(key, (D, HEADS * DK), D ** (-0.5))
    return values.astype(jnp.bfloat16)


def draw_w_value(key, part):
    key = jax.random.fold_in(key, 17)
    values = drawn_law(key, (D, HEADS * DV), D ** (-0.5))
    return values.astype(jnp.bfloat16)


def draw_w_gate(key, part):
    key = jax.random.fold_in(key, 19)
    values = drawn_law(key, (D, HEADS * DV), D ** (-0.5))
    return values.astype(jnp.bfloat16)


def draw_w_out(key, part):
    key = jax.random.fold_in(key, 23)
    scale = (HEADS * DV // 2) ** (-0.5)
    values = drawn_law(key, (HEADS * DV, D), scale)
    return values.astype(jnp.bfloat16)


def draw_w_up(key, part):
    key = jax.random.fold_in(key, 29)
    values = drawn_law(key, (D, FFH), D ** (-0.5))
    return values.astype(jnp.bfloat16)


def draw_w_down(key, part):
    key = jax.random.fold_in(key, 31)
    scale = (FFH // 2) ** (-0.5)
    values = drawn_law(key, (FFH, D), scale)
    return values.astype(jnp.bfloat16)


def draw_cotangent(key, part):
    key = jax.random.fold_in(key, 37)
    value_key = jax.random.fold_in(key, 0)
    values = drawn_law(value_key, (TOKENS, D), 1.0)
    return values.astype(jnp.bfloat16)


def setup_inputs(seed: int = 0) -> dict:
    key_of = jax.random.split(jax.random.key(seed), 12)
    tokens = draw_tokens(jax.random.fold_in(key_of[11], 71), 0)
    gain_mix = jnp.clip(1.0 + 0.15 * jax.random.normal(key_of[1], (D,), jnp.float32), 0.25, 1.75)
    w_query = draw_w_query(jax.random.fold_in(key_of[11], 71), 0)
    w_key = draw_w_key(jax.random.fold_in(key_of[11], 71), 0)
    w_value = draw_w_value(jax.random.fold_in(key_of[11], 71), 0)
    w_gate = draw_w_gate(jax.random.fold_in(key_of[11], 71), 0)
    w_out = draw_w_out(jax.random.fold_in(key_of[11], 71), 0)
    gain_ffn = jnp.clip(1.0 + 0.15 * jax.random.normal(key_of[7], (D,), jnp.float32), 0.25, 1.75)
    w_up = draw_w_up(jax.random.fold_in(key_of[11], 71), 0)
    w_down = draw_w_down(jax.random.fold_in(key_of[11], 71), 0)
    cotangent = draw_cotangent(jax.random.fold_in(key_of[11], 71), 0)
    return {"tokens": tokens, "gain_mix": gain_mix, "w_query": w_query, "w_key": w_key, "w_value": w_value, "w_gate": w_gate, "w_out": w_out, "gain_ffn": gain_ffn, "w_up": w_up, "w_down": w_down, "cotangent": cotangent}


@jax.custom_vjp
def lower_part(v):
    return lax.optimization_barrier(v.astype(jnp.bfloat16)).astype(jnp.float32)

@jax.custom_vjp
def lower_part_backward(v):
    return v

def low_keep(v):
    return (lower_part(v), None)

def low_pass(kept, grad):
    return (grad,)

def back_keep(v):
    return (v, None)

def back_low(kept, grad):
    return (lower_part(grad),)
lower_part.defvjp(low_keep, low_pass)
lower_part_backward.defvjp(back_keep, back_low)
eps = 1e-05
upper_part = lax.Precision.HIGHEST

def matmul(left, right):
    return jnp.dot(left, right, precision=upper_part)

def normalize(rows):
    centre = rows - lax.optimization_barrier(jnp.mean(rows, axis=-1, keepdims=True))
    return centre * lax.rsqrt(lax.optimization_barrier(jnp.mean(centre * centre, axis=-1, keepdims=True)) + eps)

def rotate(values, positions):
    half = DK // 2
    freq = jnp.exp(-jnp.log(10000.0) * jnp.arange(half, dtype=jnp.float32) / (half - 1))
    phase = positions.astype(jnp.float32)[:, None] * freq[None, :]
    cosine = jnp.cos(phase)[:, None, :]
    sine = jnp.sin(phase)[:, None, :]
    first = values[..., :half]
    second = values[..., half:]
    return jnp.concatenate([first * cosine - second * sine, second * cosine + first * sine], axis=-1)

def retention(query, keys, values):
    blocks = LENGTH // STRETCH
    logs = jnp.log1p(-jnp.exp2(-5.0 - jnp.arange(HEADS, dtype=jnp.float32)))
    steps = jnp.arange(STRETCH, dtype=jnp.float32)
    gaps = steps[:, None] - steps[None, :]
    mask = jnp.where(gaps >= 0, jnp.exp(logs[:, None, None] * jnp.maximum(gaps, 0.0)), 0.0)
    q_scale = jnp.exp(logs[:, None] * (steps + 1.0))
    k_scale = jnp.exp(logs[:, None] * (STRETCH - 1.0 - steps))
    stretch_decay = jnp.exp(logs * STRETCH)
    q_blk = query.reshape(blocks, STRETCH, HEADS, DK).transpose(0, 2, 1, 3)
    k_blk = keys.reshape(blocks, STRETCH, HEADS, DK).transpose(0, 2, 1, 3)
    v_blk = values.reshape(blocks, STRETCH, HEADS, DV).transpose(0, 2, 1, 3)

    def block_step(carried_state, inputs):
        q_one, single_key, v_one = inputs
        scores = jnp.einsum('hik,hjk->hij', q_one, single_key, precision=upper_part)
        weights = lower_part(lower_part_backward(scores) * mask)
        layer_result = jnp.einsum('hij,hjv->hiv', weights, v_one, precision=upper_part)
        query_decayed = lower_part(q_one * q_scale[:, :, None])
        value_decayed = lower_part(v_one * k_scale[:, :, None])
        layer_result = layer_result + jnp.einsum('uoj,ujn->uon', query_decayed, lower_part(carried_state), precision=upper_part)
        growth_factor = lower_part_backward(jnp.einsum('amw,amd->awd', single_key, value_decayed, precision=upper_part))
        carried_state = stretch_decay[:, None, None] * carried_state + growth_factor
        return (carried_state, layer_result)
    start = jnp.zeros((HEADS, DK, DV), jnp.float32)
    last, mixed = lax.scan(jax.checkpoint(block_step), start, (q_blk, k_blk, v_blk))
    return mixed.transpose(0, 2, 1, 3).reshape(LENGTH, HEADS, DV)

def block(x, gain_mix, w_query, w_key, w_value, w_gate, w_out, gain_ffn, w_up, w_down):
    positions = jnp.arange(LENGTH, dtype=jnp.int32)
    normed_mix = lower_part(normalize(x) * gain_mix)
    query_pre = lower_part_backward(matmul(normed_mix, w_query)).reshape(LENGTH, HEADS, DK)
    key_pre = lower_part_backward(matmul(normed_mix, w_key)).reshape(LENGTH, HEADS, DK)
    value_pre = lower_part_backward(matmul(normed_mix, w_value))
    gate_pre = lower_part_backward(matmul(normed_mix, w_gate))
    query = lower_part(rotate(query_pre, positions))
    keys = lower_part(rotate(key_pre, positions))
    values = lower_part(value_pre).reshape(LENGTH, HEADS, DV)
    mixed = lower_part_backward(retention(query, keys, values))
    grouped = normalize(mixed).reshape(LENGTH, HEADS * DV)
    gated = lower_part(jax.nn.silu(gate_pre) * grouped)
    hidden = x + lower_part_backward(matmul(gated, w_out))
    normed_ffn = lower_part(normalize(hidden) * gain_ffn)
    up = lower_part_backward(matmul(normed_ffn, w_up))
    act = lower_part(jax.nn.gelu(up, approximate=False))
    return hidden + matmul(act, w_down)

def reference(tokens, gain_mix, w_query, w_key, w_value, w_gate, w_out, gain_ffn, w_up, w_down, cotangent):
    params = tuple((p.astype(jnp.float32) for p in (gain_mix, w_query, w_key, w_value, w_gate, w_out, gain_ffn, w_up, w_down)))
    count = TOKENS // LENGTH
    rows = tokens.astype(jnp.float32).reshape(count, LENGTH, D)
    cots = cotangent.astype(jnp.float32).reshape(count, LENGTH, D)

    def one(total, inputs):
        x_seq, dy_seq = inputs
        layer_result, back = jax.vjp(block, x_seq, *params)
        grads = back(dy_seq)
        total = tuple((a + b for a, b in zip(total, grads[1:])))
        return (total, (layer_result.astype(jnp.bfloat16), grads[0].astype(jnp.bfloat16)))
    zeros = tuple((jnp.zeros_like(p) for p in params))
    total, outputs = lax.scan(one, zeros, (rows, cots))
    output = outputs[0].reshape(TOKENS, D)
    grad_tokens = outputs[1].reshape(TOKENS, D)
    return (output, grad_tokens, total[0], total[1], total[2], total[3], total[4], total[5], total[6], total[7], total[8])
```

```python
import math

import jax
import jax.numpy as jnp
from jax import lax
from jax.sharding import PartitionSpec as P

DK = 256
DV = 512
STRETCH = 256
SEQ_DEVS = 4


eps = 1e-05


def carried_in(state, decay, place, backward):
    count = lax.axis_size("seq")
    groups = [list(range(i, i + SEQ_DEVS)) for i in range(0, count, SEQ_DEVS)]
    gathered = lax.all_gather(state.astype(jnp.bfloat16), "seq", axis_index_groups=groups)
    total = jnp.zeros_like(state)
    for other in range(SEQ_DEVS):
        hops = other - place - 1 if backward else place - other - 1
        weight = jnp.where(hops >= 0, decay ** jnp.maximum(hops, 0).astype(jnp.float32), 0.0)
        total = total + weight[:, None, None] * gathered[other].astype(jnp.float32)
    return total


def core_swap(value):
    count = lax.axis_size("seq")
    return lax.ppermute(value, "seq", [(i, i ^ 1) for i in range(count)])


def mp_swap(value, bit):
    count = lax.axis_size("mp")
    return lax.ppermute(value, "mp", [(i, i ^ bit) for i in range(count)])


def same_core():
    count = lax.axis_size("seq")
    return [list(range(core, count, 2)) for core in range(2)]


def group_rows(own):
    chip = jnp.concatenate([own, mp_swap(own, 1)], axis=0)
    return jnp.concatenate([chip, core_swap(chip)], axis=0)


def group_sum(part):
    f32, bf16 = jnp.float32, jnp.bfloat16
    rows = part.shape[0] // 4
    keep = part[: 2 * rows] + core_swap(part[2 * rows :].astype(bf16)).astype(f32)
    return keep[:rows] + mp_swap(keep[rows:].astype(bf16), 1).astype(f32)


def far_shard(weight):
    rows = weight.shape[0] // lax.axis_size("seq")
    piece = lax.dynamic_slice_in_dim(weight, lax.axis_index("seq") * rows, rows, 0)
    return lax.all_gather(mp_swap(piece, 2), "seq", axis=0, tiled=True)


def scatter_pair(grad):
    f32, bf16 = jnp.float32, jnp.bfloat16
    count = lax.axis_size("seq")
    core = lax.axis_index("seq") % 2
    parts = grad.astype(bf16).reshape(count // 2, 2, grad.shape[0] // count, grad.shape[1])
    away = lax.dynamic_index_in_dim(parts, 1 - core, 1, False)
    kept = lax.dynamic_index_in_dim(parts, core, 1, False)
    total = (kept.astype(f32) + core_swap(away).astype(f32)).astype(bf16)
    total = total.reshape(grad.shape[0] // 2, grad.shape[1])
    return lax.psum_scatter(
        total, "seq", scatter_dimension=0, tiled=True, axis_index_groups=same_core()
    ).astype(f32)


def scatter_far(grad):
    f32, bf16 = jnp.float32, jnp.bfloat16
    count, depth = lax.axis_size("seq"), lax.axis_size("mp")
    core = lax.axis_index("seq") % 2
    part = lax.psum_scatter(
        grad.astype(bf16), "seq", scatter_dimension=0, tiled=True, axis_index_groups=same_core()
    )
    half = part.shape[0] // 2
    first, second = part[:half], part[half:]
    crossed, straight = [], []
    for s in range(count):
        for z in range(depth):
            here = s * depth + z
            if s % 2 == 0:
                crossed.append((here, (s + 1) * depth + z))
            else:
                crossed.append((here, (s - 1) * depth + (z ^ 2)))
                straight.append((here, s * depth + (z ^ 2)))
    one = lax.ppermute(jnp.where(core == 0, second, first), ("seq", "mp"), crossed)
    two = lax.ppermute(second, ("seq", "mp"), straight)
    return one.astype(f32) + jnp.where(core == 0, first, two).astype(f32)


def normalize(rows):
    centre = rows - jnp.mean(rows, axis=-1, keepdims=True)
    inverse = lax.rsqrt(jnp.mean(centre * centre, axis=-1, keepdims=True) + eps)
    return (centre * inverse, inverse)


def norm_back(grad_hat, unit, inverse):
    first = jnp.mean(grad_hat, axis=-1, keepdims=True)
    second = jnp.mean(grad_hat * unit, axis=-1, keepdims=True)
    return inverse * (grad_hat - first - unit * second)


def angles(positions):
    half = DK // 2
    freq = jnp.exp(-math.log(10000.0) * jnp.arange(half, dtype=jnp.float32) / (half - 1))
    phase = positions.astype(jnp.float32)[:, None] * freq[None, :]
    return (jnp.cos(phase)[:, None, :], jnp.sin(phase)[:, None, :])


def rotate(values, cosine, sine):
    half = DK // 2
    first = values[..., :half]
    second = values[..., half:]
    return jnp.concatenate(
        [first * cosine - second * sine, second * cosine + first * sine], axis=-1
    )


def to_blocks(rows, heads, width):
    count = rows.shape[0] // STRETCH
    return rows.reshape(count, STRETCH, heads, width).transpose(2, 0, 1, 3)


def from_blocks(blocks):
    heads, count, size, width = blocks.shape
    return blocks.transpose(1, 2, 0, 3).reshape(count * size, heads * width)


def product_t(left, right):
    return lax.dot_general(
        left, right, (((0,), (0,)), ((), ())), preferred_element_type=jnp.float32
    )


def product_rt(left, right):
    return lax.dot_general(
        left, right, (((1,), (1,)), ((), ())), preferred_element_type=jnp.float32
    )


def shards(
    tokens, gain_mix, w_query, w_key, w_value, w_gate, w_out, gain_ffn, w_up, w_down, cotangent
):
    bf16 = jnp.bfloat16
    f32 = jnp.float32
    span_rows = lax.axis_size("mp") * tokens.shape[0]
    local_heads = w_query.shape[1] // DK
    blocks = span_rows // STRETCH
    place = lax.axis_index("seq") % SEQ_DEVS
    core = lax.axis_index("seq") % 2
    resid = tokens.astype(f32)
    unit_mix, inv_mix = normalize(resid)
    normed_mix = (unit_mix * gain_mix).astype(bf16)
    gathered_mix = lax.all_gather(normed_mix, "mp", axis=0, tiled=True)
    w_up = jnp.where(core == 0, w_up, far_shard(w_up))
    w_down = jnp.where(core == 0, w_down, far_shard(w_down))
    cot_rows = group_rows(cotangent)
    query_pre = jnp.dot(gathered_mix, w_query, preferred_element_type=f32)
    key_pre = jnp.dot(gathered_mix, w_key, preferred_element_type=f32)
    value_pre = jnp.dot(gathered_mix, w_value, preferred_element_type=f32)
    gate_pre = jnp.dot(gathered_mix, w_gate, preferred_element_type=f32)
    positions = place * span_rows + jnp.arange(span_rows, dtype=jnp.int32)
    cosine, sine = angles(positions)
    query = rotate(query_pre.reshape(span_rows, local_heads, DK), cosine, sine).astype(bf16)
    keys = rotate(key_pre.reshape(span_rows, local_heads, DK), cosine, sine).astype(bf16)
    q_blk = to_blocks(query.reshape(span_rows, local_heads * DK), local_heads, DK)
    k_blk = to_blocks(keys.reshape(span_rows, local_heads * DK), local_heads, DK)
    v_blk = to_blocks(value_pre.astype(bf16), local_heads, DV)
    heads = (lax.axis_index("mp") * local_heads).astype(f32) + jnp.arange(local_heads, dtype=f32)
    logs = jnp.log1p(-jnp.exp2(-5.0 - heads))
    steps = jnp.arange(STRETCH, dtype=f32)
    gaps = steps[:, None] - steps[None, :]
    mask = jnp.where(gaps >= 0, jnp.exp(logs[:, None, None] * jnp.maximum(gaps, 0.0)), 0.0)
    q_scale = jnp.exp(logs[:, None] * (steps + 1.0))[:, None, :, None]
    k_scale = jnp.exp(logs[:, None] * (STRETCH - 1.0 - steps))[:, None, :, None]
    stretch_decay = jnp.exp(logs * STRETCH)[:, None, None]
    span_decay = jnp.exp(logs * span_rows)
    scores = jnp.einsum("hcik,hcjk->hcij", q_blk, k_blk, preferred_element_type=f32)
    weights = (scores * mask[:, None]).astype(bf16)
    intra = jnp.einsum("hcij,hcjv->hciv", weights, v_blk, preferred_element_type=f32)
    value_dec = (v_blk.astype(f32) * k_scale).astype(bf16)
    query_dec = (q_blk.astype(f32) * q_scale).astype(bf16)
    local_states = jnp.einsum("hcjk,hcjv->hckv", k_blk, value_dec, preferred_element_type=f32)
    span_state = jnp.zeros_like(local_states[:, 0])
    for index in range(blocks):
        span_state = stretch_decay * span_state + local_states[:, index]
    incoming = carried_in(span_state, span_decay, place, False)
    carried_state = incoming
    entering = []
    for index in range(blocks):
        entering.append(carried_state)
        carried_state = stretch_decay * carried_state + local_states[:, index]
    entering = jnp.stack(entering, axis=1).astype(bf16)
    cross = jnp.einsum("hcik,hckv->hciv", query_dec, entering, preferred_element_type=f32)
    mixed = intra + cross
    unit_grp, inv_grp = normalize(mixed)
    unit_rows = from_blocks(unit_grp)
    swish = jax.nn.silu(gate_pre)
    gated = (swish * unit_rows).astype(bf16)
    mixer = lax.psum_scatter(
        jnp.dot(gated, w_out, preferred_element_type=f32).astype(jnp.bfloat16),
        "mp",
        scatter_dimension=0,
        tiled=True,
    ).astype(jnp.float32)
    hidden = resid + mixer
    unit_ffn, inv_ffn = normalize(hidden)
    normed_ffn = (unit_ffn * gain_ffn).astype(bf16)
    gathered_ffn = group_rows(normed_ffn)
    up = jnp.dot(gathered_ffn, w_up, preferred_element_type=f32)
    act = jax.nn.gelu(up, approximate=False).astype(bf16)
    output = (hidden + group_sum(jnp.dot(act, w_down, preferred_element_type=f32))).astype(bf16)
    grad_down = product_t(act, cot_rows)
    grad_act = product_rt(cot_rows, w_down)
    gelu_value, gelu_back = jax.vjp(lambda v: jax.nn.gelu(v, approximate=False), up)
    grad_up = gelu_back(grad_act)[0].astype(bf16)
    grad_up_w = product_t(gathered_ffn, grad_up)
    grad_normed_ffn = group_sum(product_rt(grad_up, w_up))
    gain_ffn_part = jnp.sum(grad_normed_ffn * unit_ffn, axis=0)
    grad_hidden = cotangent.astype(f32) + norm_back(grad_normed_ffn * gain_ffn, unit_ffn, inv_ffn)
    hidden_rows = lax.all_gather(grad_hidden.astype(bf16), "mp", axis=0, tiled=True)
    grad_out_w = product_t(gated, hidden_rows)
    grad_gated = product_rt(hidden_rows, w_out)
    silu_value, silu_back = jax.vjp(jax.nn.silu, gate_pre)
    grad_gate = silu_back(grad_gated * unit_rows)[0].astype(bf16)
    grad_unit = to_blocks(grad_gated * swish, local_heads, DV)
    grad_mixed = norm_back(grad_unit, unit_grp, inv_grp).astype(bf16)
    grad_raw = jnp.einsum("hciv,hcjv->hcij", grad_mixed, v_blk, preferred_element_type=f32)
    grad_scores = (grad_raw * mask[:, None]).astype(bf16)
    grad_q = jnp.einsum("hcij,hcjk->hcik", grad_scores, k_blk, preferred_element_type=f32)
    grad_k = jnp.einsum("hcij,hcik->hcjk", grad_scores, q_blk, preferred_element_type=f32)
    grad_v = jnp.einsum("hcij,hciv->hcjv", weights, grad_mixed, preferred_element_type=f32)
    grad_q = grad_q + q_scale * jnp.einsum(
        "hciv,hckv->hcik", grad_mixed, entering, preferred_element_type=f32
    )
    grad_enter = jnp.einsum("hcik,hciv->hckv", query_dec, grad_mixed, preferred_element_type=f32)
    local_grad = jnp.zeros_like(span_state)
    for index in reversed(range(blocks)):
        local_grad = stretch_decay * local_grad + grad_enter[:, index]
    leaving = carried_in(local_grad, span_decay, place, True)
    carried = leaving
    grad_local = [None] * blocks
    for index in reversed(range(blocks)):
        grad_local[index] = carried
        carried = grad_enter[:, index] + stretch_decay * carried
    grad_local = jnp.stack(grad_local, axis=1).astype(bf16)
    grad_k = grad_k + jnp.einsum(
        "hcjv,hckv->hcjk", value_dec, grad_local, preferred_element_type=f32
    )
    grad_v = grad_v + k_scale * jnp.einsum(
        "hcjk,hckv->hcjv", k_blk, grad_local, preferred_element_type=f32
    )
    back_sine = -sine
    grad_query = rotate(from_blocks(grad_q).reshape(span_rows, local_heads, DK), cosine, back_sine)
    grad_query = grad_query.reshape(span_rows, local_heads * DK).astype(bf16)
    grad_key = rotate(from_blocks(grad_k).reshape(span_rows, local_heads, DK), cosine, back_sine)
    grad_key = grad_key.reshape(span_rows, local_heads * DK).astype(bf16)
    grad_value = from_blocks(grad_v).astype(bf16)
    grad_in = jnp.concatenate([grad_query, grad_key, grad_value, grad_gate], axis=1)
    grad_in_w = scatter_pair(product_t(gathered_mix, grad_in))
    part_mix = product_rt(grad_query, w_query) + product_rt(grad_key, w_key)
    part_mix = part_mix + product_rt(grad_value, w_value) + product_rt(grad_gate, w_gate)
    grad_normed_mix = lax.psum_scatter(
        part_mix.astype(jnp.bfloat16), "mp", scatter_dimension=0, tiled=True
    ).astype(jnp.float32)
    gain_mix_part = jnp.sum(grad_normed_mix * unit_mix, axis=0)
    grad_tokens = (grad_hidden + norm_back(grad_normed_mix * gain_mix, unit_mix, inv_mix)).astype(
        bf16
    )
    gain_mix_sum, gain_ffn_sum = lax.psum((gain_mix_part, gain_ffn_part), ("seq", "mp"))
    wide = w_query.shape[1]
    tall = w_value.shape[1]
    final_query, final_key, final_value, final_gate = jnp.split(
        grad_in_w, [wide, 2 * wide, 2 * wide + tall], axis=1
    )
    final_out = scatter_pair(grad_out_w)
    final_up = scatter_far(grad_up_w)
    final_down = scatter_far(grad_down)
    return (
        output,
        grad_tokens,
        gain_mix_sum,
        final_query,
        final_key,
        final_value,
        final_gate,
        final_out,
        gain_ffn_sum,
        final_up,
        final_down,
    )


def solution(mesh):
    return jax.shard_map(
        shards,
        mesh=mesh,
        in_specs=(
            P(("seq", "mp"), None),
            P(),
            P(None, "mp"),
            P(None, "mp"),
            P(None, "mp"),
            P(None, "mp"),
            P("mp", None),
            P(),
            P(None, "mp"),
            P("mp", None),
            P(("seq", "mp"), None),
        ),
        out_specs=(
            P(("seq", "mp"), None),
            P(("seq", "mp"), None),
            P(),
            P("seq", "mp"),
            P("seq", "mp"),
            P("seq", "mp"),
            P("seq", "mp"),
            P(("mp", "seq"), None),
            P(),
            P("seq", "mp"),
            P(("mp", "seq"), None),
        ),
        check_vma=False,
    )
```

```python
import math

import jax
import jax.numpy as jnp
from jax import lax
from jax.experimental import pallas as pl
from jax.experimental.pallas import tpu as pltpu
from jax.sharding import PartitionSpec as P

DK = 256
DV = 512
STRETCH = 256
SEQ_DEVS = 4


eps = 1e-05


def carried_in(state, decay, place, backward):
    count = lax.axis_size("seq")
    groups = [list(range(i, i + SEQ_DEVS)) for i in range(0, count, SEQ_DEVS)]
    gathered = lax.all_gather(state.astype(jnp.bfloat16), "seq", axis_index_groups=groups)
    total = jnp.zeros_like(state)
    for other in range(SEQ_DEVS):
        hops = other - place - 1 if backward else place - other - 1
        weight = jnp.where(hops >= 0, decay ** jnp.maximum(hops, 0).astype(jnp.float32), 0.0)
        total = total + weight[:, None, None] * gathered[other].astype(jnp.float32)
    return total


def core_swap(value):
    count = lax.axis_size("seq")
    return lax.ppermute(value, "seq", [(i, i ^ 1) for i in range(count)])


def mp_swap(value, bit):
    count = lax.axis_size("mp")
    return lax.ppermute(value, "mp", [(i, i ^ bit) for i in range(count)])


def same_core():
    count = lax.axis_size("seq")
    return [list(range(core, count, 2)) for core in range(2)]


def group_rows(own):
    chip = jnp.concatenate([own, mp_swap(own, 1)], axis=0)
    return jnp.concatenate([chip, core_swap(chip)], axis=0)


def group_sum(part):
    f32, bf16 = jnp.float32, jnp.bfloat16
    rows = part.shape[0] // 4
    keep = part[: 2 * rows] + core_swap(part[2 * rows :].astype(bf16)).astype(f32)
    return keep[:rows] + mp_swap(keep[rows:].astype(bf16), 1).astype(f32)


def far_shard(weight):
    rows = weight.shape[0] // lax.axis_size("seq")
    piece = lax.dynamic_slice_in_dim(weight, lax.axis_index("seq") * rows, rows, 0)
    return lax.all_gather(mp_swap(piece, 2), "seq", axis=0, tiled=True)


def scatter_pair(grad):
    f32, bf16 = jnp.float32, jnp.bfloat16
    count = lax.axis_size("seq")
    core = lax.axis_index("seq") % 2
    parts = grad.astype(bf16).reshape(count // 2, 2, grad.shape[0] // count, grad.shape[1])
    away = lax.dynamic_index_in_dim(parts, 1 - core, 1, False)
    kept = lax.dynamic_index_in_dim(parts, core, 1, False)
    total = (kept.astype(f32) + core_swap(away).astype(f32)).astype(bf16)
    total = total.reshape(grad.shape[0] // 2, grad.shape[1])
    return lax.psum_scatter(
        total, "seq", scatter_dimension=0, tiled=True, axis_index_groups=same_core()
    ).astype(f32)


def scatter_far(grad):
    f32, bf16 = jnp.float32, jnp.bfloat16
    count, depth = lax.axis_size("seq"), lax.axis_size("mp")
    core = lax.axis_index("seq") % 2
    part = lax.psum_scatter(
        grad.astype(bf16), "seq", scatter_dimension=0, tiled=True, axis_index_groups=same_core()
    )
    half = part.shape[0] // 2
    first, second = part[:half], part[half:]
    crossed, straight = [], []
    for s in range(count):
        for z in range(depth):
            here = s * depth + z
            if s % 2 == 0:
                crossed.append((here, (s + 1) * depth + z))
            else:
                crossed.append((here, (s - 1) * depth + (z ^ 2)))
                straight.append((here, s * depth + (z ^ 2)))
    one = lax.ppermute(jnp.where(core == 0, second, first), ("seq", "mp"), crossed)
    two = lax.ppermute(second, ("seq", "mp"), straight)
    return one.astype(f32) + jnp.where(core == 0, first, two).astype(f32)


def normalize(rows):
    centre = rows - jnp.mean(rows, axis=-1, keepdims=True)
    inverse = lax.rsqrt(jnp.mean(centre * centre, axis=-1, keepdims=True) + eps)
    return (centre * inverse, inverse)


def norm_back(grad_hat, unit, inverse):
    first = jnp.mean(grad_hat, axis=-1, keepdims=True)
    second = jnp.mean(grad_hat * unit, axis=-1, keepdims=True)
    return inverse * (grad_hat - first - unit * second)


def angles(positions):
    half = DK // 2
    freq = jnp.exp(-math.log(10000.0) * jnp.arange(half, dtype=jnp.float32) / (half - 1))
    phase = positions.astype(jnp.float32)[:, None] * freq[None, :]
    return (jnp.cos(phase)[:, None, :], jnp.sin(phase)[:, None, :])


def rotate(values, cosine, sine):
    half = DK // 2
    first = values[..., :half]
    second = values[..., half:]
    return jnp.concatenate(
        [first * cosine - second * sine, second * cosine + first * sine], axis=-1
    )


def to_blocks(rows, heads, width):
    count = rows.shape[0] // STRETCH
    return rows.reshape(count, STRETCH, heads, width).transpose(2, 0, 1, 3)


def from_blocks(blocks):
    heads, count, size, width = blocks.shape
    return blocks.transpose(1, 2, 0, 3).reshape(count * size, heads * width)


def product_t(left, right):
    return lax.dot_general(
        left, right, (((0,), (0,)), ((), ())), preferred_element_type=jnp.float32
    )


def product_rt(left, right):
    return lax.dot_general(
        left, right, (((1,), (1,)), ((), ())), preferred_element_type=jnp.float32
    )


MESH = pl.DeviceIdType.MESH
LIMIT = 62 * 1024 * 1024


def remote(src, dst, send, recv, s, z):
    return pltpu.make_async_remote_copy(
        src_ref=src,
        dst_ref=dst,
        send_sem=send,
        recv_sem=recv,
        device_id=(s, z),
        device_id_type=MESH,
    )


def greet(partners):
    barrier = pltpu.get_barrier_semaphore()
    count = 0
    for present, s, z in partners:

        @pl.when(present)
        def _():
            pl.semaphore_signal(barrier, inc=1, device_id=(s, z), device_id_type=MESH)

        count = count + jnp.where(present, 1, 0)
    pl.semaphore_wait(barrier, count)


def dot(left, right):
    return jnp.dot(left, right, preferred_element_type=jnp.float32)


def line_push(x, send, recv, s, z, slot, way):
    return remote(x.at[slot], x.at[slot], send.at[way, slot], recv.at[slot], s, z + 1 - 2 * way)


def line_gather(x, send, recv, s, z, depth, use):
    @pl.when(z < depth - 1)
    def _():
        line_push(x, send, recv, s, z, z, 0).start()

    @pl.when(z > 0)
    def _():
        line_push(x, send, recv, s, z, z, 1).start()

    def one(turn, _):
        away = (turn + 1) // 2
        left, right = z - away, z + away

        @pl.when((turn % 2 == 1) & (left >= 0))
        def _():
            remote(x.at[left], x.at[left], send.at[0, left], recv.at[left], s, z - 1).wait_recv()

            @pl.when(z < depth - 1)
            def _():
                line_push(x, send, recv, s, z, left, 0).start()

        @pl.when((turn % 2 == 1) & (right < depth))
        def _():
            remote(x.at[right], x.at[right], send.at[1, right], recv.at[right], s, z + 1).wait_recv()

            @pl.when(z > 0)
            def _():
                line_push(x, send, recv, s, z, right, 1).start()

        slot = jnp.where(turn % 2 == 1, left, right)

        @pl.when((slot >= 0) & (slot < depth))
        def _():
            use(slot)

        return 0

    lax.fori_loop(0, 2 * depth - 1, one, 0)


def line_gather_end(x, send, recv, s, z, depth):
    def one(slot, _):
        @pl.when((slot <= z) & (z < depth - 1))
        def _():
            line_push(x, send, recv, s, z, slot, 0).wait_send()

        @pl.when((slot >= z) & (z > 0))
        def _():
            line_push(x, send, recv, s, z, slot, 1).wait_send()

        return 0

    lax.fori_loop(0, depth, one, 0)


def add_rows(into, other):
    step = 32

    def one(i, _):
        rows = pl.ds(pl.multiple_of(i * step, step), step)
        into[rows, :] = (
            into[rows, :].astype(jnp.float32) + other[rows, :].astype(jnp.float32)
        ).astype(into.dtype)
        return 0

    lax.fori_loop(0, into.shape[0] // step, one, 0)


def line_scatter(sbuf, rbuf, total, send, recv, s, z, depth, partial, own):
    def right(j):
        return remote(sbuf.at[j], rbuf.at[j], send.at[j], recv.at[j], s, z + 1)

    def left(j):
        slot = jnp.where(j == z - 1, depth, j)
        return remote(sbuf.at[j], rbuf.at[slot], send.at[j], recv.at[slot], s, z - 1)

    def arrived(slot, sender):
        remote(sbuf.at[0], rbuf.at[slot], send.at[0], recv.at[slot], s, sender).wait_recv()

    def first(turn, _):
        up = depth - 1 + z - turn // 2
        down = turn // 2 - (depth - 1) + z
        j = jnp.where(turn % 2 == 0, up, down)
        valid = jnp.where(turn % 2 == 0, (up > z) & (up < depth), (down >= 0) & (down < z))

        @pl.when(valid)
        def _():
            partial(j)

            @pl.when((z == 0) & (j > z))
            def _():
                right(j).start()

            @pl.when((z == depth - 1) & (j < z))
            def _():
                left(j).start()

        return 0

    lax.fori_loop(0, 2 * (depth - 1), first, 0)
    own()

    def event(turn, _):
        up = depth - 1 + z - turn
        down = turn - (depth - 1) + z

        @pl.when((z > 0) & (up >= z) & (up < depth))
        def _():
            arrived(up, z - 1)

            @pl.when(up > z)
            def _():
                add_rows(sbuf.at[up], rbuf.at[up])
                right(up).start()

            @pl.when(up == z)
            def _():
                add_rows(total, rbuf.at[up])

        @pl.when((z < depth - 1) & (down >= 0) & (down <= z))
        def _():
            slot = jnp.where(down == z, depth, down)
            arrived(slot, z + 1)

            @pl.when(down < z)
            def _():
                add_rows(sbuf.at[down], rbuf.at[down])
                left(down).start()

            @pl.when(down == z)
            def _():
                add_rows(total, rbuf.at[depth])

        return 0

    lax.fori_loop(0, depth, event, 0)

    def end(j, _):
        @pl.when(j > z)
        def _():
            right(j).wait_send()

        @pl.when(j < z)
        def _():
            left(j).wait_send()

        return 0

    lax.fori_loop(0, depth, end, 0)


def centred(rows):
    centre = rows - jnp.mean(rows, axis=-1, keepdims=True)
    inverse = lax.rsqrt(jnp.mean(centre * centre, axis=-1, keepdims=True) + eps)
    return centre * inverse, inverse


def block(rows, index):
    return pl.ds(pl.multiple_of(index * rows, rows), rows)


def attend_kernel(
    tok,
    gain,
    cot,
    w_query,
    w_key,
    w_value,
    w_gate,
    w_out,
    cosine,
    sine,
    mask,
    q_scale,
    k_scale,
    decay,
    x_out,
    q_out,
    k_out,
    v_out,
    gp_out,
    gn_out,
    gated_out,
    inv_out,
    p_out,
    r_out,
    hidden_out,
    cot_rows,
    xg,
    q,
    k,
    v,
    gp,
    gn,
    gated,
    inv,
    weights,
    grown,
    entering,
    tile,
    state,
    state_in,
    state_to,
    rbuf,
    total,
    wq,
    wk,
    wv,
    wg,
    wo,
    load,
    save,
    g_send,
    g_recv,
    s_send,
    s_recv,
    c_send,
    c_recv,
    x_send,
    x_recv,
):
    f32, bf16 = jnp.float32, jnp.bfloat16
    depth = xg.shape[0]
    rows = xg.shape[1]
    heads = mask.shape[0]
    s, z = lax.axis_index("seq"), lax.axis_index("mp")
    place = lax.rem(s, SEQ_DEVS)
    pair = z + 1 - 2 * lax.rem(z, 2)
    twin = s + 1 - 2 * lax.rem(s, 2)
    loads = [
        pltpu.make_async_copy(a, b, load.at[i])
        for i, (a, b) in enumerate(
            [(w_query, wq), (w_key, wk), (w_value, wv), (w_gate, wg), (w_out, wo)]
        )
    ]
    for copy in loads:
        copy.start()

    def norm(i, _):
        part = pl.ds(pl.multiple_of(i * 32, 32), 32)
        unit, _ = centred(tok[part, :].astype(f32))
        xg[z, part, :] = (unit * gain[...]).astype(bf16)
        return 0

    lax.fori_loop(0, rows // 32, norm, 0)
    greet(
        [
            (z > 0, s, z - 1),
            (z < depth - 1, s, z + 1),
            (place > 0, s - 1, z),
            (place < SEQ_DEVS - 1, s + 1, z),
        ]
    )

    @pl.when(place == 0)
    def _():
        state_in[...] = jnp.zeros_like(state_in)

    def use(j):
        at = block(rows, j)
        @pl.when(j == z)
        def _():
            for copy in loads:
                copy.wait()

        c, sn = cosine[at, :], sine[at, :]
        for h in range(heads):
            cols = slice(h * DK, (h + 1) * DK)
            for w, out in ((wq, q), (wk, k)):
                p = dot(xg[j], w[:, cols])
                a, b = p[:, : DK // 2], p[:, DK // 2 :]
                out[at, h * DK : h * DK + DK // 2] = (a * c - b * sn).astype(bf16)
                out[at, h * DK + DK // 2 : (h + 1) * DK] = (b * c + a * sn).astype(bf16)
        for h in range(heads):
            wide = slice(h * DV, (h + 1) * DV)
            v[at, wide] = dot(xg[j], wv[:, wide]).astype(bf16)
            gp[at, wide] = dot(xg[j], wg[:, wide]).astype(bf16)
        for h in range(heads):
            cols = slice(h * DK, (h + 1) * DK)
            wide = slice(h * DV, (h + 1) * DV)
            kb, vb = k[at, cols], v[at, wide]
            vd = (vb.astype(f32) * k_scale[h]).astype(bf16)
            grown[h, j] = product_t(kb, vd)
            weights[h, j] = (product_rt(q[at, cols], kb) * mask[h]).astype(bf16)

    line_gather(xg, g_send, g_recv, s, z, depth, use)
    mine = pltpu.make_async_copy(cot, cot_rows.at[0], x_send.at[3])
    mine.start()
    swap = remote(cot, cot_rows.at[1], x_send.at[0], x_recv.at[0], s, pair)
    swap.start()
    near = remote(cot, cot_rows.at[2], x_send.at[1], x_recv.at[1], twin, z)
    near.start()
    for h in range(heads):
        state[h] = grown[h, 0]
        for b in range(1, depth):
            state[h] = decay[h, 0] * state[h] + grown[h, b]
    chain = remote(state_to, state_in, c_send, c_recv, s + 1, z)

    @pl.when(place > 0)
    def _():
        remote(state_to, state_in, c_send, c_recv, s - 1, z).wait_recv()

    @pl.when(place < SEQ_DEVS - 1)
    def _():
        for h in range(heads):
            state_to[h] = (decay[h, 1] * state_in[h].astype(f32) + state[h]).astype(bf16)
        chain.start()

    saves = [
        pltpu.make_async_copy(a, b, save.at[i])
        for i, (a, b) in enumerate(
            [
                (xg, x_out),
                (q, q_out),
                (k, k_out),
                (v, v_out),
                (gp, gp_out),
                (weights, p_out),
                (entering, r_out),
                (gn, gn_out),
                (gated, gated_out),
                (inv, inv_out),
            ]
        )
    ]
    for copy in saves[:6]:
        copy.start()
    for h in range(heads):
        cols = slice(h * DK, (h + 1) * DK)
        wide = slice(h * DV, (h + 1) * DV)
        state[h] = state_in[h].astype(f32)

        def cross(b, _):
            at = block(rows, b)
            entering[h, b] = state[h].astype(bf16)
            state[h] = decay[h, 0] * state[h] + grown[h, b]
            qd = (q[at, cols].astype(f32) * q_scale[h]).astype(bf16)
            tile[...] = dot(weights[h, b], v[at, wide]) + dot(qd, entering[h, b])

            def norm(i, _):
                here = block(32, i)
                there = pl.ds(pl.multiple_of(b * rows + i * 32, 32), 32)
                unit, inverse = centred(tile[here, :])
                gate = gp[there, wide].astype(f32)
                gn[there, wide] = unit.astype(bf16)
                gated[there, wide] = (unit * gate / (1.0 + jnp.exp(-gate))).astype(bf16)
                inv[h, there, :] = jnp.broadcast_to(inverse, (32, inv.shape[2]))
                return 0

            lax.fori_loop(0, rows // 32, norm, 0)
            return 0

        lax.fori_loop(0, depth, cross, 0)
    for copy in saves[6:]:
        copy.start()
    line_gather_end(xg, g_send, g_recv, s, z, depth)
    saves[0].wait()
    swap.wait_recv()
    far = remote(cot_rows.at[1], cot_rows.at[3], x_send.at[2], x_recv.at[2], twin, z)
    far.start()
    wide = 512

    def partial(j):
        for n in range(0, total.shape[1], wide):
            xg[j, :, n : n + wide] = dot(gated[block(rows, j), :], wo[:, n : n + wide]).astype(bf16)

    def own():
        for n in range(0, total.shape[1], wide):
            total[:, n : n + wide] = tok[:, n : n + wide].astype(f32) + dot(
                gated[block(rows, z), :], wo[:, n : n + wide]
            )

    line_scatter(xg, rbuf, total, s_send, s_recv, s, z, depth, partial, own)
    done = pltpu.make_async_copy(total, hidden_out, save.at[0])
    done.start()

    @pl.when(place < SEQ_DEVS - 1)
    def _():
        chain.wait_send()

    swap.wait_send()
    near.wait()
    far.wait()
    mine.wait()
    for copy in saves[1:]:
        copy.wait()
    done.wait()


def attend(
    tok, gain, cot, w_query, w_key, w_value, w_gate, w_out, cosine, sine, mask, q_scale, k_scale, decay
):
    f32, bf16 = jnp.float32, jnp.bfloat16
    depth = lax.axis_size("mp")
    rows, width = tok.shape
    span = depth * rows
    heads = mask.shape[0]
    hk, hv = w_query.shape[1], w_value.shape[1]
    any_ = pl.BlockSpec(memory_space=pl.ANY)
    vmem = pl.BlockSpec(memory_space=pltpu.VMEM)
    shapes = [
        ((depth, rows, width), bf16),
        ((span, hk), bf16),
        ((span, hk), bf16),
        ((span, hv), bf16),
        ((span, hv), bf16),
        ((span, hv), bf16),
        ((span, hv), bf16),
        ((heads, span, 128), f32),
        ((heads, depth, rows, rows), bf16),
        ((heads, depth, DK, DV), bf16),
        ((rows, width), f32),
        ((4, rows, width), bf16),
    ]
    dma = pltpu.SemaphoreType.DMA
    return pl.pallas_call(
        attend_kernel,
        out_shape=[jax.ShapeDtypeStruct(*one) for one in shapes],
        in_specs=[vmem, vmem, any_] + [any_] * 5 + [vmem] * 6,
        out_specs=[any_] * len(shapes),
        scratch_shapes=[
            pltpu.VMEM((depth, rows, width), bf16),
            pltpu.VMEM((span, hk), bf16),
            pltpu.VMEM((span, hk), bf16),
            pltpu.VMEM((span, hv), bf16),
            pltpu.VMEM((span, hv), bf16),
            pltpu.VMEM((span, hv), bf16),
            pltpu.VMEM((span, hv), bf16),
            pltpu.VMEM((heads, span, 128), f32),
            pltpu.VMEM((heads, depth, rows, rows), bf16),
            pltpu.VMEM((heads, depth, DK, DV), f32),
            pltpu.VMEM((heads, depth, DK, DV), bf16),
            pltpu.VMEM((rows, DV), f32),
            pltpu.VMEM((heads, DK, DV), f32),
            pltpu.VMEM((heads, DK, DV), bf16),
            pltpu.VMEM((heads, DK, DV), bf16),
            pltpu.VMEM((depth + 1, rows, width), bf16),
            pltpu.VMEM((rows, width), f32),
            pltpu.VMEM(w_query.shape, bf16),
            pltpu.VMEM(w_key.shape, bf16),
            pltpu.VMEM(w_value.shape, bf16),
            pltpu.VMEM(w_gate.shape, bf16),
            pltpu.VMEM(w_out.shape, bf16),
            dma((5,)),
            dma((10,)),
            dma((2, depth)),
            dma((depth,)),
            dma((depth,)),
            dma((depth + 1,)),
            dma,
            dma,
            dma((4,)),
            dma((3,)),
        ],
        compiler_params=pltpu.CompilerParams(
            collective_id=0, has_side_effects=True, vmem_limit_bytes=LIMIT
        ),
        cost_estimate=pl.CostEstimate(
            flops=30 * 10**9, bytes_accessed=60 * 10**6, transcendentals=2 * 10**6
        ),
        name="attend",
    )(tok, gain, cot, w_query, w_key, w_value, w_gate, w_out, cosine, sine, mask, q_scale, k_scale, decay)


def shards(
    tokens, gain_mix, w_query, w_key, w_value, w_gate, w_out, gain_ffn, w_up, w_down, cotangent
):
    bf16 = jnp.bfloat16
    f32 = jnp.float32
    span_rows = lax.axis_size("mp") * tokens.shape[0]
    local_heads = w_query.shape[1] // DK
    blocks = span_rows // STRETCH
    place = lax.axis_index("seq") % SEQ_DEVS
    core = lax.axis_index("seq") % 2
    resid = tokens.astype(f32)
    unit_mix, inv_mix = normalize(resid)
    w_up = jnp.where(core == 0, w_up, far_shard(w_up))
    w_down = jnp.where(core == 0, w_down, far_shard(w_down))
    positions = place * span_rows + jnp.arange(span_rows, dtype=jnp.int32)
    cosine, sine = angles(positions)
    heads = (lax.axis_index("mp") * local_heads).astype(f32) + jnp.arange(local_heads, dtype=f32)
    logs = jnp.log1p(-jnp.exp2(-5.0 - heads))
    steps = jnp.arange(STRETCH, dtype=f32)
    gaps = steps[:, None] - steps[None, :]
    mask = jnp.where(gaps >= 0, jnp.exp(logs[:, None, None] * jnp.maximum(gaps, 0.0)), 0.0)
    q_scale = jnp.exp(logs[:, None] * (steps + 1.0))[:, :, None]
    k_scale = jnp.exp(logs[:, None] * (STRETCH - 1.0 - steps))[:, :, None]
    stretch_decay = jnp.exp(logs * STRETCH)[:, None, None]
    span_decay = jnp.exp(logs * span_rows)
    decay = jnp.broadcast_to(
        jnp.stack([jnp.exp(logs * STRETCH), span_decay], axis=1)[:, :, None, None],
        (local_heads, 2, 1, DV),
    )
    gathered_mix, q_all, k_all, v_all, gate_pre, unit_rows, gated, inv_wide, weights, entering, hidden, cot_rows = attend(
        tokens, gain_mix[None, :], cotangent, w_query, w_key, w_value, w_gate, w_out,
        cosine[:, 0], sine[:, 0], mask, q_scale, k_scale, decay,
    )
    gathered_mix = gathered_mix.reshape(span_rows, -1)
    q_blk = to_blocks(q_all, local_heads, DK)
    k_blk = to_blocks(k_all, local_heads, DK)
    v_blk = to_blocks(v_all, local_heads, DV)
    gate_pre = gate_pre.astype(f32)
    unit_rows = unit_rows.astype(f32)
    unit_grp = to_blocks(unit_rows, local_heads, DV)
    inv_grp = inv_wide[:, :, :1].reshape(local_heads, blocks, STRETCH, 1)
    swish = jax.nn.silu(gate_pre)
    q_scale = q_scale[:, None]
    k_scale = k_scale[:, None]
    value_dec = (v_blk.astype(f32) * k_scale).astype(bf16)
    query_dec = (q_blk.astype(f32) * q_scale).astype(bf16)
    cot_rows = cot_rows.reshape(span_rows, -1)
    unit_ffn, inv_ffn = normalize(hidden)
    normed_ffn = (unit_ffn * gain_ffn).astype(bf16)
    gathered_ffn = group_rows(normed_ffn)
    up = jnp.dot(gathered_ffn, w_up, preferred_element_type=f32)
    act = jax.nn.gelu(up, approximate=False).astype(bf16)
    output = (hidden + group_sum(jnp.dot(act, w_down, preferred_element_type=f32))).astype(bf16)
    grad_down = product_t(act, cot_rows)
    grad_act = product_rt(cot_rows, w_down)
    gelu_value, gelu_back = jax.vjp(lambda v: jax.nn.gelu(v, approximate=False), up)
    grad_up = gelu_back(grad_act)[0].astype(bf16)
    grad_up_w = product_t(gathered_ffn, grad_up)
    grad_normed_ffn = group_sum(product_rt(grad_up, w_up))
    gain_ffn_part = jnp.sum(grad_normed_ffn * unit_ffn, axis=0)
    grad_hidden = cotangent.astype(f32) + norm_back(grad_normed_ffn * gain_ffn, unit_ffn, inv_ffn)
    hidden_rows = lax.all_gather(grad_hidden.astype(bf16), "mp", axis=0, tiled=True)
    grad_out_w = product_t(gated, hidden_rows)
    grad_gated = product_rt(hidden_rows, w_out)
    silu_value, silu_back = jax.vjp(jax.nn.silu, gate_pre)
    grad_gate = silu_back(grad_gated * unit_rows)[0].astype(bf16)
    grad_unit = to_blocks(grad_gated * swish, local_heads, DV)
    grad_mixed = norm_back(grad_unit, unit_grp, inv_grp).astype(bf16)
    grad_raw = jnp.einsum("hciv,hcjv->hcij", grad_mixed, v_blk, preferred_element_type=f32)
    grad_scores = (grad_raw * mask[:, None]).astype(bf16)
    grad_q = jnp.einsum("hcij,hcjk->hcik", grad_scores, k_blk, preferred_element_type=f32)
    grad_k = jnp.einsum("hcij,hcik->hcjk", grad_scores, q_blk, preferred_element_type=f32)
    grad_v = jnp.einsum("hcij,hciv->hcjv", weights, grad_mixed, preferred_element_type=f32)
    grad_q = grad_q + q_scale * jnp.einsum(
        "hciv,hckv->hcik", grad_mixed, entering, preferred_element_type=f32
    )
    grad_enter = jnp.einsum("hcik,hciv->hckv", query_dec, grad_mixed, preferred_element_type=f32)
    local_grad = jnp.zeros((local_heads, DK, DV), f32)
    for index in reversed(range(blocks)):
        local_grad = stretch_decay * local_grad + grad_enter[:, index]
    leaving = carried_in(local_grad, span_decay, place, True)
    carried = leaving
    grad_local = [None] * blocks
    for index in reversed(range(blocks)):
        grad_local[index] = carried
        carried = grad_enter[:, index] + stretch_decay * carried
    grad_local = jnp.stack(grad_local, axis=1).astype(bf16)
    grad_k = grad_k + jnp.einsum(
        "hcjv,hckv->hcjk", value_dec, grad_local, preferred_element_type=f32
    )
    grad_v = grad_v + k_scale * jnp.einsum(
        "hcjk,hckv->hcjv", k_blk, grad_local, preferred_element_type=f32
    )
    back_sine = -sine
    grad_query = rotate(from_blocks(grad_q).reshape(span_rows, local_heads, DK), cosine, back_sine)
    grad_query = grad_query.reshape(span_rows, local_heads * DK).astype(bf16)
    grad_key = rotate(from_blocks(grad_k).reshape(span_rows, local_heads, DK), cosine, back_sine)
    grad_key = grad_key.reshape(span_rows, local_heads * DK).astype(bf16)
    grad_value = from_blocks(grad_v).astype(bf16)
    grad_in = jnp.concatenate([grad_query, grad_key, grad_value, grad_gate], axis=1)
    grad_in_w = scatter_pair(product_t(gathered_mix, grad_in))
    part_mix = product_rt(grad_query, w_query) + product_rt(grad_key, w_key)
    part_mix = part_mix + product_rt(grad_value, w_value) + product_rt(grad_gate, w_gate)
    grad_normed_mix = lax.psum_scatter(
        part_mix.astype(jnp.bfloat16), "mp", scatter_dimension=0, tiled=True
    ).astype(jnp.float32)
    gain_mix_part = jnp.sum(grad_normed_mix * unit_mix, axis=0)
    grad_tokens = (grad_hidden + norm_back(grad_normed_mix * gain_mix, unit_mix, inv_mix)).astype(
        bf16
    )
    gain_mix_sum, gain_ffn_sum = lax.psum((gain_mix_part, gain_ffn_part), ("seq", "mp"))
    wide = w_query.shape[1]
    tall = w_value.shape[1]
    final_query, final_key, final_value, final_gate = jnp.split(
        grad_in_w, [wide, 2 * wide, 2 * wide + tall], axis=1
    )
    final_out = scatter_pair(grad_out_w)
    final_up = scatter_far(grad_up_w)
    final_down = scatter_far(grad_down)
    return (
        output,
        grad_tokens,
        gain_mix_sum,
        final_query,
        final_key,
        final_value,
        final_gate,
        final_out,
        gain_ffn_sum,
        final_up,
        final_down,
    )


def solution(mesh):
    return jax.shard_map(
        shards,
        mesh=mesh,
        in_specs=(
            P(("seq", "mp"), None),
            P(),
            P(None, "mp"),
            P(None, "mp"),
            P(None, "mp"),
            P(None, "mp"),
            P("mp", None),
            P(),
            P(None, "mp"),
            P("mp", None),
            P(("seq", "mp"), None),
        ),
        out_specs=(
            P(("seq", "mp"), None),
            P(("seq", "mp"), None),
            P(),
            P("seq", "mp"),
            P("seq", "mp"),
            P("seq", "mp"),
            P("seq", "mp"),
            P(("mp", "seq"), None),
            P(),
            P("seq", "mp"),
            P(("mp", "seq"), None),
        ),
        check_vma=False,
    )
```

```python
import math

import jax
import jax.numpy as jnp
from jax import lax
from jax.experimental import pallas as pl
from jax.experimental.pallas import tpu as pltpu
from jax.sharding import PartitionSpec as P

DK = 256
DV = 512
STRETCH = 256
SEQ_DEVS = 4


eps = 1e-05


def same_core():
    count = lax.axis_size("seq")
    return [list(range(core, count, 2)) for core in range(2)]


def angles(positions):
    half = DK // 2
    freq = jnp.exp(-math.log(10000.0) * jnp.arange(half, dtype=jnp.float32) / (half - 1))
    phase = positions.astype(jnp.float32)[:, None] * freq[None, :]
    return (jnp.cos(phase)[:, None, :], jnp.sin(phase)[:, None, :])


def product_t(left, right):
    return lax.dot_general(
        left, right, (((0,), (0,)), ((), ())), preferred_element_type=jnp.float32
    )


def product_rt(left, right):
    return lax.dot_general(
        left, right, (((1,), (1,)), ((), ())), preferred_element_type=jnp.float32
    )


MESH = pl.DeviceIdType.MESH
LIMIT = 62 * 1024 * 1024


def remote(src, dst, send, recv, s, z):
    return pltpu.make_async_remote_copy(
        src_ref=src,
        dst_ref=dst,
        send_sem=send,
        recv_sem=recv,
        device_id=(s, z),
        device_id_type=MESH,
    )


def greet(partners):
    barrier = pltpu.get_barrier_semaphore()
    count = 0
    for present, s, z in partners:

        @pl.when(present)
        def _():
            pl.semaphore_signal(barrier, inc=1, device_id=(s, z), device_id_type=MESH)

        count = count + jnp.where(present, 1, 0)
    pl.semaphore_wait(barrier, count)


def dot(left, right):
    return jnp.dot(left, right, preferred_element_type=jnp.float32)


def line_push(x, send, recv, s, z, slot, way):
    return remote(x.at[slot], x.at[slot], send.at[way, slot], recv.at[slot], s, z + 1 - 2 * way)


def line_gather(x, send, recv, s, z, depth, use, after=None):
    @pl.when(z < depth - 1)
    def _():
        line_push(x, send, recv, s, z, z, 0).start()

    @pl.when(z > 0)
    def _():
        line_push(x, send, recv, s, z, z, 1).start()

    def one(turn, _):
        away = (turn + 1) // 2
        left, right = z - away, z + away

        @pl.when((turn % 2 == 1) & (left >= 0))
        def _():
            remote(x.at[left], x.at[left], send.at[0, left], recv.at[left], s, z - 1).wait_recv()

            @pl.when(z < depth - 1)
            def _():
                line_push(x, send, recv, s, z, left, 0).start()

        @pl.when((turn % 2 == 1) & (right < depth))
        def _():
            remote(x.at[right], x.at[right], send.at[1, right], recv.at[right], s, z + 1).wait_recv()

            @pl.when(z > 0)
            def _():
                line_push(x, send, recv, s, z, right, 1).start()

        if after is not None:
            after(turn)
        slot = jnp.where(turn % 2 == 1, left, right)

        @pl.when((slot >= 0) & (slot < depth))
        def _():
            use(slot)

        return 0

    lax.fori_loop(0, 2 * depth - 1, one, 0)


def line_gather_end(x, send, recv, s, z, depth):
    def one(slot, _):
        @pl.when((slot <= z) & (z < depth - 1))
        def _():
            line_push(x, send, recv, s, z, slot, 0).wait_send()

        @pl.when((slot >= z) & (z > 0))
        def _():
            line_push(x, send, recv, s, z, slot, 1).wait_send()

        return 0

    lax.fori_loop(0, depth, one, 0)


def add_rows(into, other):
    step = 32

    def one(i, _):
        rows = pl.ds(pl.multiple_of(i * step, step), step)
        into[rows, :] = (
            into[rows, :].astype(jnp.float32) + other[rows, :].astype(jnp.float32)
        ).astype(into.dtype)
        return 0

    lax.fori_loop(0, into.shape[0] // step, one, 0)


def line_scatter(sbuf, rbuf, total, send, recv, s, z, depth, partial, own, hook=None):
    def right(j):
        return remote(sbuf.at[j], rbuf.at[j], send.at[j], recv.at[j], s, z + 1)

    def left(j):
        slot = jnp.where(j == z - 1, depth, j)
        return remote(sbuf.at[j], rbuf.at[slot], send.at[j], recv.at[slot], s, z - 1)

    def arrived(slot, sender):
        remote(sbuf.at[0], rbuf.at[slot], send.at[0], recv.at[slot], s, sender).wait_recv()

    def first(turn, _):
        up = depth - 1 + z - turn // 2
        down = turn // 2 - (depth - 1) + z
        j = jnp.where(turn % 2 == 0, up, down)
        valid = jnp.where(turn % 2 == 0, (up > z) & (up < depth), (down >= 0) & (down < z))

        @pl.when(valid)
        def _():
            partial(j)

            @pl.when((z == 0) & (j > z))
            def _():
                right(j).start()

            @pl.when((z == depth - 1) & (j < z))
            def _():
                left(j).start()

        return 0

    lax.fori_loop(0, 2 * (depth - 1), first, 0)
    own()

    def event(turn, _):
        up = depth - 1 + z - turn
        down = turn - (depth - 1) + z

        @pl.when((z > 0) & (up >= z) & (up < depth))
        def _():
            arrived(up, z - 1)

            @pl.when(up > z)
            def _():
                add_rows(sbuf.at[up], rbuf.at[up])
                right(up).start()

            @pl.when(up == z)
            def _():
                add_rows(total, rbuf.at[up])

        @pl.when((z < depth - 1) & (down >= 0) & (down <= z))
        def _():
            slot = jnp.where(down == z, depth, down)
            arrived(slot, z + 1)

            @pl.when(down < z)
            def _():
                add_rows(sbuf.at[down], rbuf.at[down])
                left(down).start()

            @pl.when(down == z)
            def _():
                add_rows(total, rbuf.at[depth])

        if hook is not None:
            hook(turn)
        return 0

    lax.fori_loop(0, depth, event, 0)

    def end(j, _):
        @pl.when(j > z)
        def _():
            right(j).wait_send()

        @pl.when(j < z)
        def _():
            left(j).wait_send()

        return 0

    lax.fori_loop(0, depth, end, 0)


def centred(rows):
    centre = rows - jnp.mean(rows, axis=-1, keepdims=True)
    inverse = lax.rsqrt(jnp.mean(centre * centre, axis=-1, keepdims=True) + eps)
    return centre * inverse, inverse


def block(rows, index):
    return pl.ds(pl.multiple_of(index * rows, rows), rows)


def attend_kernel(
    tok,
    gain,
    cot,
    w_query,
    w_key,
    w_value,
    w_gate,
    w_out,
    w_up,
    w_down,
    cosine,
    sine,
    mask,
    q_scale,
    k_scale,
    decay,
    x_out,
    q_out,
    k_out,
    v_out,
    gp_out,
    gn_out,
    gated_out,
    inv_out,
    p_out,
    r_out,
    hidden_out,
    cot_rows,
    far_up,
    far_down,
    xg,
    q,
    k,
    v,
    gp,
    gn,
    gated,
    inv,
    weights,
    grown,
    entering,
    tile,
    state,
    state_in,
    state_to,
    rbuf,
    total,
    wq,
    wk,
    wv,
    wg,
    wo,
    load,
    save,
    g_send,
    g_recv,
    s_send,
    s_recv,
    c_send,
    c_recv,
    x_send,
    x_recv,
    f_send,
    f_recv,
    p_send,
    p_recv,
):
    f32, bf16 = jnp.float32, jnp.bfloat16
    depth = xg.shape[0]
    rows = xg.shape[1]
    heads = mask.shape[0]
    s, z = lax.axis_index("seq"), lax.axis_index("mp")
    place = lax.rem(s, SEQ_DEVS)
    pair = z + 1 - 2 * lax.rem(z, 2)
    twin = s + 1 - 2 * lax.rem(s, 2)
    loads = [
        pltpu.make_async_copy(a, b, load.at[i])
        for i, (a, b) in enumerate(
            [(w_query, wq), (w_key, wk), (w_value, wv), (w_gate, wg), (w_out, wo)]
        )
    ]
    for copy in loads:
        copy.start()

    def norm(i, _):
        part = pl.ds(pl.multiple_of(i * 32, 32), 32)
        unit, _ = centred(tok[part, :].astype(f32))
        xg[z, part, :] = (unit * gain[...]).astype(bf16)
        return 0

    lax.fori_loop(0, rows // 32, norm, 0)
    count = lax.axis_size("seq")
    across = flip(z, 2)
    greet(
        [(z > 0, s, z - 1), (z < depth - 1, s, z + 1), (z >= 0, s, across)]
        + [(s != other, other, z) for other in range(count)]
    )
    tall, few = w_up.shape[0] // count, w_down.shape[0] // count
    mine = pltpu.make_async_copy(cot, cot_rows.at[0], x_send.at[3])
    near = remote(cot, cot_rows.at[2], x_send.at[1], x_recv.at[1], twin, z)
    swap = remote(cot, cot_rows.at[1], x_send.at[0], x_recv.at[0], s, pair)
    far = remote(cot_rows.at[1], cot_rows.at[3], x_send.at[2], x_recv.at[2], twin, z)

    def piece(source):
        return block(tall, source), block(few, source)

    up_at, down_at = piece(s)
    moves = [
        remote(w_up.at[up_at], far_up.at[up_at], f_send.at[0], f_recv.at[0], s, across),
        remote(w_down.at[down_at], far_down.at[down_at], f_send.at[1], f_recv.at[1], s, across),
    ]
    edge = (z == 0) | (z == depth - 1)

    def spread(source, chip):
        up_, down_ = piece(source)
        to = 2 * chip + 1
        return [
            remote(far_up.at[up_], far_up.at[up_], p_send.at[0, chip], p_recv.at[0, source], to, z),
            remote(
                far_down.at[down_], far_down.at[down_], p_send.at[1, chip], p_recv.at[1, source], to, z
            ),
        ]

    mine.start()
    near.start()

    @pl.when(place == 0)
    def _():
        state_in[...] = jnp.zeros_like(state_in)

    def after(turn):
        @pl.when(edge & (turn == 1))
        def _():
            swap.start()

        @pl.when(edge & (turn == 3))
        def _():
            for copy in moves:
                copy.start()

    def use(j):
        at = block(rows, j)

        @pl.when(j == z)
        def _():
            for copy in loads:
                copy.wait()

        c, sn = cosine[at, :], sine[at, :]
        for h in range(heads):
            cols = slice(h * DK, (h + 1) * DK)
            for w, out in ((wq, q), (wk, k)):
                p = dot(xg[j], w[:, cols])
                a, b = p[:, : DK // 2], p[:, DK // 2 :]
                out[at, h * DK : h * DK + DK // 2] = (a * c - b * sn).astype(bf16)
                out[at, h * DK + DK // 2 : (h + 1) * DK] = (b * c + a * sn).astype(bf16)
        for h in range(heads):
            wide = slice(h * DV, (h + 1) * DV)
            v[at, wide] = dot(xg[j], wv[:, wide]).astype(bf16)
            gp[at, wide] = dot(xg[j], wg[:, wide])
        for h in range(heads):
            cols = slice(h * DK, (h + 1) * DK)
            wide = slice(h * DV, (h + 1) * DV)
            kb, vb = k[at, cols], v[at, wide]
            vd = (vb.astype(f32) * k_scale[h]).astype(bf16)
            grown[h, j] = product_t(kb, vd)
            weights[h, j] = (product_rt(q[at, cols], kb) * mask[h]).astype(bf16)

    line_gather(xg, g_send, g_recv, s, z, depth, use, after)
    @pl.when(jnp.logical_not(edge))
    def _():
        for copy in moves:
            copy.start()

    for h in range(heads):
        state[h] = grown[h, 0]
        for b in range(1, depth):
            state[h] = decay[h, 0] * state[h] + grown[h, b]
    chain = remote(state_to, state_in, c_send, c_recv, s + 1, z)

    @pl.when(place > 0)
    def _():
        remote(state_to, state_in, c_send, c_recv, s - 1, z).wait_recv()

    @pl.when(place < SEQ_DEVS - 1)
    def _():
        for h in range(heads):
            state_to[h] = (decay[h, 1] * state_in[h].astype(f32) + state[h]).astype(bf16)
        chain.start()

    saves = [
        pltpu.make_async_copy(a, b, save.at[i])
        for i, (a, b) in enumerate(
            [
                (xg, x_out),
                (q, q_out),
                (k, k_out),
                (v, v_out),
                (gp, gp_out),
                (weights, p_out),
                (entering, r_out),
                (gn, gn_out),
                (gated, gated_out),
                (inv, inv_out),
            ]
        )
    ]
    for copy in saves[:6]:
        copy.start()

    def hand_out():
        for copy in moves:
            copy.wait_recv()

        def to_chip(chip, _):
            @pl.when(2 * chip + 1 != s)
            def _():
                for copy in spread(s, chip):
                    copy.start()

            return 0

        lax.fori_loop(0, count // 2, to_chip, 0)

    @pl.when(jnp.logical_not(edge))
    def _():
        hand_out()

    for h in range(heads):
        cols = slice(h * DK, (h + 1) * DK)
        wide = slice(h * DV, (h + 1) * DV)
        state[h] = state_in[h].astype(f32)

        def cross(b, _):
            at = block(rows, b)
            entering[h, b] = state[h].astype(bf16)
            state[h] = decay[h, 0] * state[h] + grown[h, b]
            qd = (q[at, cols].astype(f32) * q_scale[h]).astype(bf16)
            tile[...] = dot(weights[h, b], v[at, wide]) + dot(qd, entering[h, b])

            def norm(i, _):
                here = block(32, i)
                there = pl.ds(pl.multiple_of(b * rows + i * 32, 32), 32)
                unit, inverse = centred(tile[here, :])
                gate = gp[there, wide]
                gn[there, wide] = unit
                gated[there, wide] = (unit * gate / (1.0 + jnp.exp(-gate))).astype(bf16)
                inv[h, there, :] = jnp.broadcast_to(inverse, (32, inv.shape[2]))
                return 0

            lax.fori_loop(0, rows // 32, norm, 0)
            return 0

        lax.fori_loop(0, depth, cross, 0)
    for copy in saves[6:]:
        copy.start()
    line_gather_end(xg, g_send, g_recv, s, z, depth)
    saves[0].wait()
    wide = 512

    def hook(turn):
        @pl.when((turn == 0) & jnp.logical_not(edge))
        def _():
            swap.start()

        @pl.when((turn == 0) & edge)
        def _():
            hand_out()

        @pl.when(turn == 2)
        def _():
            swap.wait_recv()
            far.start()

    def partial(j):
        for n in range(0, total.shape[1], wide):
            xg[j, :, n : n + wide] = dot(gated[block(rows, j), :], wo[:, n : n + wide]).astype(bf16)

    def own():
        for n in range(0, total.shape[1], wide):
            total[:, n : n + wide] = tok[:, n : n + wide].astype(f32) + dot(
                gated[block(rows, z), :], wo[:, n : n + wide]
            )

    line_scatter(xg, rbuf, total, s_send, s_recv, s, z, depth, partial, own, hook)
    done = pltpu.make_async_copy(total, hidden_out, save.at[0])
    done.start()

    @pl.when(place < SEQ_DEVS - 1)
    def _():
        chain.wait_send()

    def sent(chip, _):
        @pl.when(2 * chip + 1 != s)
        def _():
            for copy in spread(s, chip):
                copy.wait_send()

        return 0

    lax.fori_loop(0, count // 2, sent, 0)

    def came(source, _):
        @pl.when((source != s) & (lax.rem(s, 2) == 1))
        def _():
            for copy in spread(source, 0):
                copy.wait_recv()

        return 0

    lax.fori_loop(0, count, came, 0)
    for copy in moves:
        copy.wait_send()
    swap.wait_send()
    near.wait()
    far.wait()
    mine.wait()
    for copy in saves[1:]:
        copy.wait()
    done.wait()


def attend(
    tok, gain, cot, w_query, w_key, w_value, w_gate, w_out, w_up, w_down, cosine, sine, mask, q_scale, k_scale, decay
):
    f32, bf16 = jnp.float32, jnp.bfloat16
    depth = lax.axis_size("mp")
    rows, width = tok.shape
    span = depth * rows
    heads = mask.shape[0]
    hk, hv = w_query.shape[1], w_value.shape[1]
    any_ = pl.BlockSpec(memory_space=pl.ANY)
    vmem = pl.BlockSpec(memory_space=pltpu.VMEM)
    shapes = [
        ((depth, rows, width), bf16),
        ((span, hk), bf16),
        ((span, hk), bf16),
        ((span, hv), bf16),
        ((span, hv), f32),
        ((span, hv), f32),
        ((span, hv), bf16),
        ((heads, span, 128), f32),
        ((heads, depth, rows, rows), bf16),
        ((heads, depth, DK, DV), bf16),
        ((rows, width), f32),
        ((4, rows, width), bf16),
        (w_up.shape, bf16),
        (w_down.shape, bf16),
    ]
    count = lax.axis_size("seq")
    dma = pltpu.SemaphoreType.DMA
    return pl.pallas_call(
        attend_kernel,
        out_shape=[jax.ShapeDtypeStruct(*one) for one in shapes],
        in_specs=[vmem, vmem, any_] + [any_] * 7 + [vmem] * 6,
        out_specs=[any_] * len(shapes),
        scratch_shapes=[
            pltpu.VMEM((depth, rows, width), bf16),
            pltpu.VMEM((span, hk), bf16),
            pltpu.VMEM((span, hk), bf16),
            pltpu.VMEM((span, hv), bf16),
            pltpu.VMEM((span, hv), f32),
            pltpu.VMEM((span, hv), f32),
            pltpu.VMEM((span, hv), bf16),
            pltpu.VMEM((heads, span, 128), f32),
            pltpu.VMEM((heads, depth, rows, rows), bf16),
            pltpu.VMEM((heads, depth, DK, DV), f32),
            pltpu.VMEM((heads, depth, DK, DV), bf16),
            pltpu.VMEM((rows, DV), f32),
            pltpu.VMEM((heads, DK, DV), f32),
            pltpu.VMEM((heads, DK, DV), bf16),
            pltpu.VMEM((heads, DK, DV), bf16),
            pltpu.VMEM((depth + 1, rows, width), bf16),
            pltpu.VMEM((rows, width), f32),
            pltpu.VMEM(w_query.shape, bf16),
            pltpu.VMEM(w_key.shape, bf16),
            pltpu.VMEM(w_value.shape, bf16),
            pltpu.VMEM(w_gate.shape, bf16),
            pltpu.VMEM(w_out.shape, bf16),
            dma((5,)),
            dma((10,)),
            dma((2, depth)),
            dma((depth,)),
            dma((depth,)),
            dma((depth + 1,)),
            dma,
            dma,
            dma((4,)),
            dma((3,)),
            dma((2,)),
            dma((2,)),
            dma((2, count // 2)),
            dma((2, count)),
        ],
        compiler_params=pltpu.CompilerParams(
            collective_id=0, has_side_effects=True, vmem_limit_bytes=LIMIT
        ),
        cost_estimate=pl.CostEstimate(
            flops=190 * 10**9, bytes_accessed=60 * 10**6, transcendentals=2 * 10**6
        ),
        name="attend",
    )(tok, gain, cot, w_query, w_key, w_value, w_gate, w_out, w_up, w_down, cosine, sine, mask, q_scale, k_scale, decay)


def row_loop(rows, step, body):
    def one(i, _):
        body(pl.ds(pl.multiple_of(i * step, step), step), i)
        return 0

    lax.fori_loop(0, rows // step, one, 0)


def norm_rows_back(grad_hat, unit, inverse):
    first = jnp.mean(grad_hat, axis=-1, keepdims=True)
    second = jnp.mean(grad_hat * unit, axis=-1, keepdims=True)
    return inverse * (grad_hat - first - unit * second)


def feed_kernel(
    hidden,
    gain,
    cot,
    cot_rows,
    w_up,
    w_down,
    far_up,
    far_down,
    y_keep,
    y_send,
    grad_hidden,
    gain_part,
    g_all_out,
    x,
    dy,
    act,
    du,
    part_y,
    part_x,
    got_x,
    got_y,
    u_tile,
    d_tile,
    g_all,
    up,
    down,
    load,
    save,
    send,
    recv,
):
    f32, bf16 = jnp.float32, jnp.bfloat16
    rows, width = hidden.shape
    units = up.shape[1]
    s, z = lax.axis_index("seq"), lax.axis_index("mp")
    pair = z + 1 - 2 * lax.rem(z, 2)
    twin = s + 1 - 2 * lax.rem(s, 2)
    own_loads = [
        pltpu.make_async_copy(w_up, up, load.at[0]),
        pltpu.make_async_copy(w_down, down, load.at[1]),
    ]
    far_loads = [
        pltpu.make_async_copy(far_up, up, load.at[0]),
        pltpu.make_async_copy(far_down, down, load.at[1]),
    ]

    @pl.when(lax.rem(s, 2) == 0)
    def _():
        for copy in own_loads:
            copy.start()

    @pl.when(lax.rem(s, 2) == 1)
    def _():
        for copy in far_loads:
            copy.start()

    rest = [
        pltpu.make_async_copy(cot_rows.at[r], dy.at[pl.ds(r * rows, rows)], load.at[2 + r])
        for r in range(4)
    ]
    loads = own_loads + rest
    for copy in rest:
        copy.start()

    def norm(here, i):
        unit, _ = centred(hidden[here, :])
        x[here, :] = (unit * gain[...]).astype(bf16)

    row_loop(rows, 32, norm)
    greet([(z >= 0, s, pair), (z >= 0, twin, z)])
    slot = [pl.ds(r * rows, rows) for r in range(4)]
    over = remote(x.at[slot[0]], x.at[slot[1]], send.at[0], recv.at[0], s, pair)
    near = remote(x.at[slot[0]], x.at[slot[2]], send.at[1], recv.at[1], twin, z)
    far = remote(x.at[slot[1]], x.at[slot[3]], send.at[2], recv.at[2], twin, z)
    near.start()
    over.start()
    back_near = remote(part_x.at[slot[2]], got_x.at[0], send.at[3], recv.at[3], twin, z)
    back_far = remote(part_x.at[slot[3]], got_x.at[1], send.at[4], recv.at[4], twin, z)
    back_over = remote(part_x.at[slot[1]], got_x.at[2], send.at[5], recv.at[5], s, pair)
    y_back = remote(
        part_y.at[pl.ds(2 * rows, 2 * rows)], got_y, send.at[6], recv.at[6], twin, z
    )
    for copy in loads:
        copy.wait()
    step = 512

    def one(turn, _):
        r = lax.rem(turn, 2) * 2 + turn // 2
        at = block(rows, r)

        @pl.when(turn == 1)
        def _():
            near.wait_recv()

        @pl.when(turn == 2)
        def _():
            over.wait_recv()
            far.start()

        @pl.when(turn == 3)
        def _():
            far.wait_recv()

        for n in range(0, units, step):
            cols = slice(n, n + step)
            u_tile[...] = dot(x[at, :], up[:, cols])
            d_tile[...] = product_rt(dy[at, :], down[cols, :])

            def gelu(here, i):
                there = pl.ds(pl.multiple_of(r * rows + i * 32, 32), 32)
                u = u_tile[here, :]
                normal = 0.5 * (1.0 + lax.erf(u * (2.0**-0.5)))
                slope = normal + u * (jnp.exp(-0.5 * u * u) * ((2.0 * math.pi) ** -0.5))
                act[there, cols] = (u * normal).astype(bf16)
                du[there, cols] = (d_tile[here, :] * slope).astype(bf16)

            row_loop(rows, 32, gelu)
        for n in range(0, width, step):
            part_x[at, n : n + step] = product_rt(du[at, :], up[n : n + step, :]).astype(bf16)

        @pl.when(turn == 1)
        def _():
            back_near.start()

        @pl.when(turn == 3)
        def _():
            back_far.start()

        return 0

    lax.fori_loop(0, 4, one, 0)
    back_far.wait_recv()
    add_rows(part_x.at[slot[1]], got_x.at[1])
    back_over.start()

    def y_terms(r, _):
        at = block(rows, r)
        for n in range(0, width, step):
            part_y[at, n : n + step] = dot(act[at, :], down[:, n : n + step]).astype(bf16)
        return 0

    lax.fori_loop(0, 4, y_terms, 0)
    y_back.start()

    chips, _, high, _ = g_all.shape
    few = units // (2 * chips)
    tall = width // (2 * chips)

    def up_terms(m, _):
        cols = pl.ds(pl.multiple_of(m * 256, 256), 256)
        for n in range(0, units, step):
            value = product_t(x[:, cols], du[:, n : n + step]).astype(bf16)
            for part in range(256 // tall):
                to = m * (256 // tall) + part
                g_all[to // 2, lax.rem(to, 2), 0:tall, n : n + step] = value[
                    part * tall : (part + 1) * tall
                ]
        return 0

    lax.fori_loop(0, width // 256, up_terms, 0)

    def down_terms(m, _):
        cols = pl.ds(pl.multiple_of(m * 256, 256), 256)
        for n in range(0, width, step):
            value = product_t(act[:, cols], dy[:, n : n + step]).astype(bf16)
            first = tall + n // units * few
            for part in range(256 // few):
                to = m * (256 // few) + part
                g_all[to // 2, lax.rem(to, 2), first : first + few, n % units : n % units + step] = (
                    value[part * few : (part + 1) * few]
                )
        return 0

    lax.fori_loop(0, units // 256, down_terms, 0)
    saves = [pltpu.make_async_copy(g_all, g_all_out, save.at[0])]
    saves[0].start()
    y_back.wait_recv()

    def y_sum(here, i):
        there = pl.ds(pl.multiple_of(rows + i * 32, 32), 32)
        y_keep[here, :] = (
            hidden[here, :] + part_y[here, :].astype(f32) + got_y[here, :].astype(f32)
        )
        y_send[here, :] = (part_y[there, :].astype(f32) + got_y[there, :].astype(f32)).astype(bf16)

    row_loop(rows, 32, y_sum)
    back_near.wait_recv()
    back_over.wait_recv()
    gain_part[...] = jnp.zeros_like(gain_part)

    def finish(here, i):
        unit, inverse = centred(hidden[here, :])
        grad = (
            part_x[here, :].astype(f32) + got_x[0, here, :].astype(f32)
        ) + got_x[2, here, :].astype(f32)
        gain_part[...] += jnp.sum(grad * unit, axis=0, keepdims=True)
        grad_hidden[here, :] = cot[here, :].astype(f32) + norm_rows_back(
            grad * gain[...], unit, inverse
        )

    row_loop(rows, 32, finish)
    for copy in (near, over, far, back_near, back_far, back_over, y_back):
        copy.wait_send()
    for copy in saves:
        copy.wait()


def feed(hidden, gain, cot, cot_rows, w_up, w_down, far_up, far_down):
    f32, bf16 = jnp.float32, jnp.bfloat16
    rows, width = hidden.shape
    units = w_up.shape[1]
    count = lax.axis_size("seq")
    gathered = (count // 2, 2, width // count + width // count, units)
    any_ = pl.BlockSpec(memory_space=pl.ANY)
    vmem = pl.BlockSpec(memory_space=pltpu.VMEM)
    dma = pltpu.SemaphoreType.DMA
    return pl.pallas_call(
        feed_kernel,
        out_shape=[
            jax.ShapeDtypeStruct((rows, width), f32),
            jax.ShapeDtypeStruct((rows, width), bf16),
            jax.ShapeDtypeStruct((rows, width), f32),
            jax.ShapeDtypeStruct((1, width), f32),
            jax.ShapeDtypeStruct(gathered, bf16),
        ],
        in_specs=[vmem, vmem, vmem] + [any_] * 5,
        out_specs=[vmem] * 4 + [any_],
        scratch_shapes=[
            pltpu.VMEM((4 * rows, width), bf16),
            pltpu.VMEM((4 * rows, width), bf16),
            pltpu.VMEM((4 * rows, units), bf16),
            pltpu.VMEM((4 * rows, units), bf16),
            pltpu.VMEM((4 * rows, width), bf16),
            pltpu.VMEM((4 * rows, width), bf16),
            pltpu.VMEM((3, rows, width), bf16),
            pltpu.VMEM((2 * rows, width), bf16),
            pltpu.VMEM((rows, 512), f32),
            pltpu.VMEM((rows, 512), f32),
            pltpu.VMEM(gathered, bf16),
            pltpu.VMEM(w_up.shape, bf16),
            pltpu.VMEM(w_down.shape, bf16),
            dma((6,)),
            dma((1,)),
            dma((7,)),
            dma((7,)),
        ],
        compiler_params=pltpu.CompilerParams(
            collective_id=1, has_side_effects=True, vmem_limit_bytes=LIMIT
        ),
        cost_estimate=pl.CostEstimate(
            flops=75 * 10**9, bytes_accessed=30 * 10**6, transcendentals=2 * 10**6
        ),
        name="feed",
    )(hidden, gain, cot, cot_rows, w_up, w_down, far_up, far_down)


def retract_kernel(
    grad_hidden,
    y_send,
    w_out,
    q_in,
    k_in,
    v_in,
    gp_in,
    gn_in,
    gated_in,
    inv_in,
    p_in,
    r_in,
    cosine,
    sine,
    mask,
    q_scale,
    k_scale,
    decay,
    d_out,
    g_out,
    y_got,
    dx,
    q,
    k,
    v,
    gp,
    gn,
    gated,
    inv,
    weights,
    entering,
    wo,
    dall,
    do,
    tile,
    grown,
    dk,
    dv,
    state,
    state_in,
    state_to,
    g_wo,
    load,
    save,
    g_send,
    g_recv,
    c_send,
    c_recv,
    y_sems,
):
    f32, bf16 = jnp.float32, jnp.bfloat16
    depth, rows, width = dx.shape
    heads = mask.shape[0]
    hk, hv = q.shape[1], v.shape[1]
    s, z = lax.axis_index("seq"), lax.axis_index("mp")
    place = lax.rem(s, SEQ_DEVS)
    pair = z + 1 - 2 * lax.rem(z, 2)
    loads = [
        pltpu.make_async_copy(a, b, load.at[i])
        for i, (a, b) in enumerate(
            [
                (w_out, wo),
                (q_in, q),
                (k_in, k),
                (v_in, v),
                (gp_in, gp),
                (gn_in, gn),
                (gated_in, gated),
                (inv_in, inv),
                (p_in, weights),
                (r_in, entering),
            ]
        )
    ]
    for copy in loads:
        copy.start()

    def low(here, i):
        dx[z, here, :] = grad_hidden[here, :].astype(bf16)

    row_loop(rows, 32, low)
    greet(
        [
            (z > 0, s, z - 1),
            (z < depth - 1, s, z + 1),
            (place > 0, s - 1, z),
            (place < SEQ_DEVS - 1, s + 1, z),
        ]
    )

    @pl.when(place == SEQ_DEVS - 1)
    def _():
        state_in[...] = jnp.zeros_like(state_in)

    def turn_back(value, at, start):
        c, sn = cosine[at, :], sine[at, :]
        half = DK // 2
        a, b = value[:, :half], value[:, half:]
        dall[at, start : start + half] = (a * c + b * sn).astype(bf16)
        dall[at, start + half : start + DK] = (b * c - a * sn).astype(bf16)

    def use(j):
        at = block(rows, j)

        @pl.when(j == z)
        def _():
            for copy in loads:
                copy.wait()

        for h in range(heads):
            wide = slice(h * DV, (h + 1) * DV)
            tile[...] = product_rt(dx[j], wo[wide, :])

            def gate_back(here, i):
                there = pl.ds(pl.multiple_of(j * rows + i * 32, 32), 32)
                grad = tile[here, :]
                gate = gp[there, wide]
                unit = gn[there, wide]
                open_ = 1.0 / (1.0 + jnp.exp(-gate))
                slope = open_ * (1.0 + gate * (1.0 - open_))
                first = 2 * hk + hv + h * DV
                dall[there, first : first + DV] = (grad * unit * slope).astype(bf16)
                inverse = inv[h, there, :][:, :1]
                do[there, wide] = norm_rows_back(grad * gate * open_, unit, inverse).astype(bf16)

            row_loop(rows, 32, gate_back)
        for h in range(heads):
            cols = slice(h * DK, (h + 1) * DK)
            wide = slice(h * DV, (h + 1) * DV)
            qb, kb, vb, db = q[at, cols], k[at, cols], v[at, wide], do[at, wide]
            ds = (product_rt(db, vb) * mask[h]).astype(bf16)
            dv[at, wide] = product_t(weights[h, j], db)
            dk[at, cols] = product_t(ds, qb)
            turn_back(dot(ds, kb) + q_scale[h] * product_rt(db, entering[h, j]), at, h * DK)
            qd = (qb.astype(f32) * q_scale[h]).astype(bf16)
            grown[h, j] = product_t(qd, db)

    line_gather(dx, g_send, g_recv, s, z, depth, use)
    swap = remote(y_send, y_got, y_sems.at[0], y_sems.at[1], s, pair)
    swap.start()
    for h in range(heads):
        state[h] = grown[h, depth - 1]
        for b in reversed(range(depth - 1)):
            state[h] = decay[h, 0] * state[h] + grown[h, b]

    def out_terms(m, _):
        cols = pl.ds(pl.multiple_of(m * 256, 256), 256)
        for n in range(0, width, 512):
            right = dx[:, :, n : n + 512].reshape(depth * rows, 512)
            g_wo[cols, n : n + 512] = product_t(gated[:, cols], right).astype(bf16)
        return 0

    def out_grad():
        lax.fori_loop(0, hv // 256, out_terms, 0)

    @pl.when(place <= 1)
    def _():
        out_grad()

    @pl.when(place < SEQ_DEVS - 1)
    def _():
        remote(state_to, state_in, c_send, c_recv, s + 1, z).wait_recv()

    chain = remote(state_to, state_in, c_send, c_recv, s - 1, z)

    @pl.when(place > 0)
    def _():
        for h in range(heads):
            state_to[h] = (decay[h, 1] * state_in[h].astype(f32) + state[h]).astype(bf16)
        chain.start()

    for h in range(heads):
        cols = slice(h * DK, (h + 1) * DK)
        wide = slice(h * DV, (h + 1) * DV)
        state[h] = state_in[h].astype(f32)

        def cross(turn, _):
            b = depth - 1 - turn
            at = block(rows, b)
            leaving = state[h].astype(bf16)
            state[h] = grown[h, b] + decay[h, 0] * state[h]
            kb = k[at, cols]
            vd = (v[at, wide].astype(f32) * k_scale[h]).astype(bf16)
            turn_back(dk[at, cols] + product_rt(vd, leaving), at, hk + h * DK)
            dall[at, 2 * hk + h * DV : 2 * hk + (h + 1) * DV] = (
                dv[at, wide] + k_scale[h] * dot(kb, leaving)
            ).astype(bf16)
            return 0

        lax.fori_loop(0, depth, cross, 0)
    saves = [
        pltpu.make_async_copy(dall, d_out, save.at[0]),
        pltpu.make_async_copy(g_wo, g_out, save.at[1]),
    ]
    saves[0].start()

    @pl.when(place > 1)
    def _():
        out_grad()

    saves[1].start()
    line_gather_end(dx, g_send, g_recv, s, z, depth)

    @pl.when(place > 0)
    def _():
        chain.wait_send()

    swap.wait()
    for copy in saves:
        copy.wait()


def retract(
    grad_hidden, y_send, w_out, q, k, v, gp, gn, gated, inv, p, r, cosine, sine, mask, q_scale, k_scale, decay
):
    f32, bf16 = jnp.float32, jnp.bfloat16
    depth = lax.axis_size("mp")
    rows, width = grad_hidden.shape
    span = depth * rows
    heads = mask.shape[0]
    hk, hv = q.shape[1], v.shape[1]
    any_ = pl.BlockSpec(memory_space=pl.ANY)
    vmem = pl.BlockSpec(memory_space=pltpu.VMEM)
    dma = pltpu.SemaphoreType.DMA
    return pl.pallas_call(
        retract_kernel,
        out_shape=[
            jax.ShapeDtypeStruct((span, 2 * hk + 2 * hv), bf16),
            jax.ShapeDtypeStruct((hv, width), bf16),
            jax.ShapeDtypeStruct((rows, width), bf16),
        ],
        in_specs=[vmem] + [any_] * 11 + [vmem] * 6,
        out_specs=[any_] * 3,
        scratch_shapes=[
            pltpu.VMEM((depth, rows, width), bf16),
            pltpu.VMEM((span, hk), bf16),
            pltpu.VMEM((span, hk), bf16),
            pltpu.VMEM((span, hv), bf16),
            pltpu.VMEM((span, hv), f32),
            pltpu.VMEM((span, hv), f32),
            pltpu.VMEM((span, hv), bf16),
            pltpu.VMEM((heads, span, 128), f32),
            pltpu.VMEM((heads, depth, rows, rows), bf16),
            pltpu.VMEM((heads, depth, DK, DV), bf16),
            pltpu.VMEM(w_out.shape, bf16),
            pltpu.VMEM((span, 2 * hk + 2 * hv), bf16),
            pltpu.VMEM((span, hv), bf16),
            pltpu.VMEM((rows, DV), f32),
            pltpu.VMEM((heads, depth, DK, DV), f32),
            pltpu.VMEM((span, hk), f32),
            pltpu.VMEM((span, hv), f32),
            pltpu.VMEM((heads, DK, DV), f32),
            pltpu.VMEM((heads, DK, DV), bf16),
            pltpu.VMEM((heads, DK, DV), bf16),
            pltpu.VMEM((hv, width), bf16),
            dma((10,)),
            dma((2,)),
            dma((2, depth)),
            dma((depth,)),
            dma,
            dma,
            dma((2,)),
        ],
        compiler_params=pltpu.CompilerParams(
            collective_id=2, has_side_effects=True, vmem_limit_bytes=LIMIT
        ),
        cost_estimate=pl.CostEstimate(
            flops=120 * 10**9, bytes_accessed=40 * 10**6, transcendentals=2 * 10**6
        ),
        name="retract",
    )(grad_hidden, y_send, w_out, q, k, v, gp, gn, gated, inv, p, r, cosine, sine, mask, q_scale, k_scale, decay)


def flip(index, bit):
    return index + bit - 2 * bit * lax.rem(index // bit, 2)


def pair_kernel(
    x, d, wo_parts, far, out, far_got, stage, got, wo_mine, wo_got, result, save, send, recv, w_sems, f_sems
):
    f32, bf16 = jnp.float32, jnp.bfloat16
    _, chips, rows, _ = stage.shape
    few = wo_mine.shape[1]
    third = result.shape[2]
    s, z = lax.axis_index("seq"), lax.axis_index("mp")
    core = lax.rem(s, 2)
    twin = flip(s, 1)
    across = flip(z, 2)
    edge = (z == 0) | (z == lax.axis_size("mp") - 1)
    greet([(z >= 0, twin, z), (z >= 0, s, across), (z >= 0, twin, across)])
    crossed = remote(far.at[0], far_got, f_sems.at[0], f_sems.at[1], twin, across)
    straight = remote(far.at[1], far_got, f_sems.at[2], f_sems.at[3], s, across)

    @pl.when(edge & (core == 1))
    def _():
        crossed.start()
        straight.start()

    wo_load = pltpu.make_async_copy(wo_parts.at[:, core], wo_mine, w_sems.at[0])
    wo_load.start()
    wo_send = remote(wo_parts.at[:, 1 - core], wo_got, w_sems.at[1], w_sems.at[2], twin, z)
    wo_send.start()
    span = max(256, 2 * rows)
    each = span // (2 * rows)

    def give(i):
        return remote(stage.at[1 - core, i], got.at[i], send.at[i], recv.at[i], twin, z)

    def keep(i):
        return pltpu.make_async_copy(result.at[i], out.at[i], save.at[i])

    def take(i):
        give(i).wait_recv()
        for t in range(d.shape[1] // third):

            def add(here, r):
                there = pl.ds(pl.multiple_of(t * rows + r * 32, 32), 32)
                cols = slice(t * third, (t + 1) * third)
                result[i, there, :] = (
                    stage[core, i, here, cols].astype(f32) + got[i, here, cols].astype(f32)
                ).astype(bf16)

            row_loop(rows, 32, add)

    def one(g, _):
        for c in range(span // 256):
            chunk = g * (span // 256) + c
            cols = pl.ds(pl.multiple_of(chunk * 256, 256), 256)
            for n in range(0, d.shape[1], 512):
                value = product_t(x[:, cols], d[:, n : n + 512]).astype(bf16)
                for part in range(max(1, 256 // rows)):
                    to = (c if each == 1 and rows >= 256 else part) % 2
                    i = g * each + (0 if rows >= 256 else part // 2)
                    stage[to, i, :, n : n + 512] = value[part * rows : (part + 1) * rows]
        for e in range(each):
            give(g * each + e).start()

        @pl.when(g > 0)
        def _():
            for e in range(each):
                take((g - 1) * each + e)

        return 0

    groups = chips // each
    lax.fori_loop(0, groups, one, 0)
    wo_load.wait()
    wo_send.wait()
    base = rows * (d.shape[1] // third)

    def wo_add(i, _):
        for t in range(wo_mine.shape[2] // third):
            cols = slice(t * third, (t + 1) * third)
            result[i, base + t * few : base + (t + 1) * few, :] = (
                wo_mine[i, :, cols].astype(f32) + wo_got[i, :, cols].astype(f32)
            ).astype(bf16)
        return 0

    lax.fori_loop(0, chips, wo_add, 0)
    for e in range(each):
        take((groups - 1) * each + e)

    def begin(i, _):
        keep(i).start()
        return 0

    def end(i, _):
        keep(i).wait()
        give(i).wait_send()
        return 0

    lax.fori_loop(0, chips, begin, 0)
    lax.fori_loop(0, chips, end, 0)

    @pl.when(edge & (core == 1))
    def _():
        crossed.wait_send()
        straight.wait_send()

    @pl.when(jnp.logical_not(edge) & (core == 0))
    def _():
        crossed.wait_recv()

    @pl.when(jnp.logical_not(edge) & (core == 1))
    def _():
        straight.wait_recv()


def pair_sum(x, d, g_out, far):
    bf16 = jnp.bfloat16
    count = lax.axis_size("seq")
    chips = count // 2
    rows, few = x.shape[1] // count, g_out.shape[0] // count
    wide, third = d.shape[1], d.shape[1] // 3
    high = 3 * rows + few * g_out.shape[1] // third
    any_ = pl.BlockSpec(memory_space=pl.ANY)
    vmem = pl.BlockSpec(memory_space=pltpu.VMEM)
    dma = pltpu.SemaphoreType.DMA
    return pl.pallas_call(
        pair_kernel,
        out_shape=[
            jax.ShapeDtypeStruct((chips, high, third), bf16),
            jax.ShapeDtypeStruct(far.shape[1:], bf16),
        ],
        in_specs=[vmem, vmem, any_, any_],
        out_specs=[any_, any_],
        scratch_shapes=[
            pltpu.VMEM((2, chips, rows, wide), bf16),
            pltpu.VMEM((chips, rows, wide), bf16),
            pltpu.VMEM((chips, few, g_out.shape[1]), bf16),
            pltpu.VMEM((chips, few, g_out.shape[1]), bf16),
            pltpu.VMEM((chips, high, third), bf16),
            dma((chips,)),
            dma((chips,)),
            dma((chips,)),
            dma((3,)),
            dma((4,)),
        ],
        compiler_params=pltpu.CompilerParams(
            collective_id=3, has_side_effects=True, vmem_limit_bytes=LIMIT
        ),
        cost_estimate=pl.CostEstimate(
            flops=25 * 10**9, bytes_accessed=30 * 10**6, transcendentals=0
        ),
        name="pair_sum",
    )(x, d, g_out.reshape(chips, 2, few, g_out.shape[1]), far)


def finish_kernel(
    d,
    x,
    tok,
    gain,
    gain_part,
    grad_hidden,
    w_query,
    w_key,
    w_value,
    w_gate,
    far,
    far_got,
    grad_tok,
    gains,
    g_up,
    g_down,
    sbuf,
    rbuf,
    total,
    wq,
    wk,
    wv,
    wg,
    mine,
    other,
    gain_all,
    gain_line,
    load,
    s_send,
    s_recv,
    f_sems,
    h_send,
    h_recv,
    l_send,
    l_recv,
):
    f32, bf16 = jnp.float32, jnp.bfloat16
    depth, rows, width = x.shape
    s, z = lax.axis_index("seq"), lax.axis_index("mp")
    core = lax.rem(s, 2)
    twin, across = flip(s, 1), flip(z, 2)
    count = lax.axis_size("seq")
    loads = [
        pltpu.make_async_copy(a, b, load.at[i])
        for i, (a, b) in enumerate([(w_query, wq), (w_key, wk), (w_value, wv), (w_gate, wg)])
    ]
    for copy in loads:
        copy.start()
    gains[...] = jnp.zeros_like(gains)
    gains[1:2, :] = gain_part[...]
    greet(
        [(z >= 0, twin, across)]
        + [(z != other, s, other) for other in range(depth)]
        + [(s != other, other, z) for other in range(count)]
    )
    near = remote(far.at[1], other, f_sems.at[0], f_sems.at[1], twin, z)
    crossed = remote(far.at[0], other, f_sems.at[0], f_sems.at[1], twin, across)
    straight = remote(far.at[1], mine, f_sems.at[2], f_sems.at[3], s, across)
    edge = (z == 0) | (z == depth - 1)
    inner = jnp.logical_not(edge)
    local = pltpu.make_async_copy(far.at[0], mine, f_sems.at[4])
    to_other = pltpu.make_async_copy(far_got, other, f_sems.at[5])
    to_mine = pltpu.make_async_copy(far_got, mine, f_sems.at[5])

    @pl.when(core == 0)
    def _():
        near.start()
        local.start()

    @pl.when(inner & (core == 0))
    def _():
        to_other.start()

    @pl.when(inner & (core == 1))
    def _():
        to_mine.start()
        crossed.start()
        straight.start()

    for copy in loads:
        copy.wait()
    step = 512
    starts, at_col = [], 0
    for w in (wq, wk, wv, wg):
        starts.append((w, at_col, at_col + w.shape[1]))
        at_col += w.shape[1]

    def term(j, n):
        at = block(rows, j)
        value = None
        for w, a, b in starts:
            one = product_rt(d[at, a:b], w[n : n + step, :])
            value = one if value is None else value + one
        gains[0:1, n : n + step] += jnp.sum(
            value * x[j, :, n : n + step].astype(f32), axis=0, keepdims=True
        )
        return value

    def partial(j):
        for n in range(0, width, step):
            sbuf[j, :, n : n + step] = term(j, n).astype(bf16)

    def plane(to):
        return remote(gain_all.at[s], gain_all.at[s], h_send.at[to], h_recv.at[s], to, z)

    def line(to):
        return remote(gain_line.at[z], gain_line.at[z], l_send.at[to], l_recv.at[z], s, to)

    def others(count, me, act):
        def one(i, _):
            @pl.when(i != me)
            def _():
                act(i)

            return 0

        lax.fori_loop(0, count, one, 0)

    def own():
        for n in range(0, width, step):
            total[:, n : n + step] = term(z, n)
        gains[0:1, :] = gains[0:1, :] / gain[...]
        gain_all[s] = gains[...]
        others(count, s, lambda to: plane(to).start())

    line_scatter(sbuf, rbuf, total, s_send, s_recv, s, z, depth, partial, own)

    def plane_came(i):
        remote(gain_all.at[i], gain_all.at[i], h_send.at[i], h_recv.at[i], twin, z).wait_recv()

    def line_came(i):
        remote(gain_line.at[i], gain_line.at[i], l_send.at[i], l_recv.at[i], s, across).wait_recv()

    others(count, s, plane_came)
    gains[...] = gain_all[0]
    for i in range(1, count):
        gains[...] += gain_all[i]
    gain_line[z] = gains[...]
    others(depth, z, lambda to: line(to).start())

    def last(here, i):
        unit, inverse = centred(tok[here, :].astype(f32))
        grad_tok[here, :] = (
            grad_hidden[here, :] + norm_rows_back(total[here, :] * gain[...], unit, inverse)
        ).astype(bf16)

    row_loop(rows, 32, last)
    others(depth, z, line_came)
    gains[...] = gain_line[0]
    for i in range(1, depth):
        gains[...] += gain_line[i]
    others(count, s, lambda to: plane(to).wait_send())
    others(depth, z, lambda to: line(to).wait_send())

    @pl.when(core == 0)
    def _():
        near.wait_send()
        local.wait()

    @pl.when(core == 1)
    def _():
        near.wait_recv()

    @pl.when(inner & (core == 0))
    def _():
        to_other.wait()

    @pl.when(edge & (core == 0))
    def _():
        crossed.wait_recv()

    @pl.when(inner & (core == 1))
    def _():
        to_mine.wait()
        crossed.wait_send()
        straight.wait_send()

    @pl.when(edge & (core == 1))
    def _():
        straight.wait_recv()

    high, few = g_up.shape[0], g_down.shape[0]
    third = g_up.shape[1]

    g_up[...] = mine[0:high, :].astype(f32) + other[0:high, :].astype(f32)
    for t in range(g_down.shape[1] // third):
        at = slice(high + t * few, high + (t + 1) * few)
        g_down[:, t * third : (t + 1) * third] = mine[at, :].astype(f32) + other[at, :].astype(f32)


def finish(d, x, tok, gain, gain_part, grad_hidden, w_query, w_key, w_value, w_gate, far, far_got):
    f32, bf16 = jnp.float32, jnp.bfloat16
    depth, rows, width = x.shape
    count = lax.axis_size("seq")
    units = far.shape[2]
    any_ = pl.BlockSpec(memory_space=pl.ANY)
    vmem = pl.BlockSpec(memory_space=pltpu.VMEM)
    dma = pltpu.SemaphoreType.DMA
    return pl.pallas_call(
        finish_kernel,
        out_shape=[
            jax.ShapeDtypeStruct((rows, width), bf16),
            jax.ShapeDtypeStruct((8, width), f32),
            jax.ShapeDtypeStruct((width // count, units), f32),
            jax.ShapeDtypeStruct((units // count, width), f32),
        ],
        in_specs=[vmem] * 6 + [any_] * 6,
        out_specs=[vmem] * 4,
        scratch_shapes=[
            pltpu.VMEM((depth, rows, width), bf16),
            pltpu.VMEM((depth + 1, rows, width), bf16),
            pltpu.VMEM((rows, width), f32),
            pltpu.VMEM(w_query.shape, bf16),
            pltpu.VMEM(w_key.shape, bf16),
            pltpu.VMEM(w_value.shape, bf16),
            pltpu.VMEM(w_gate.shape, bf16),
            pltpu.VMEM(far.shape[1:], bf16),
            pltpu.VMEM(far.shape[1:], bf16),
            pltpu.VMEM((count, 8, width), f32),
            pltpu.VMEM((depth, 8, width), f32),
            dma((4,)),
            dma((depth,)),
            dma((depth + 1,)),
            dma((6,)),
            dma((count,)),
            dma((count,)),
            dma((depth,)),
            dma((depth,)),
        ],
        compiler_params=pltpu.CompilerParams(
            collective_id=4, has_side_effects=True, vmem_limit_bytes=LIMIT
        ),
        cost_estimate=pl.CostEstimate(
            flops=110 * 10**9, bytes_accessed=30 * 10**6, transcendentals=0
        ),
        name="finish",
    )(d, x, tok, gain, gain_part, grad_hidden, w_query, w_key, w_value, w_gate, far, far_got)


def shards(
    tokens, gain_mix, w_query, w_key, w_value, w_gate, w_out, gain_ffn, w_up, w_down, cotangent
):
    bf16 = jnp.bfloat16
    f32 = jnp.float32
    span_rows = lax.axis_size("mp") * tokens.shape[0]
    local_heads = w_query.shape[1] // DK
    place = lax.axis_index("seq") % SEQ_DEVS
    positions = place * span_rows + jnp.arange(span_rows, dtype=jnp.int32)
    cosine, sine = angles(positions)
    heads = (lax.axis_index("mp") * local_heads).astype(f32) + jnp.arange(local_heads, dtype=f32)
    logs = jnp.log1p(-jnp.exp2(-5.0 - heads))
    steps = jnp.arange(STRETCH, dtype=f32)
    gaps = steps[:, None] - steps[None, :]
    mask = jnp.where(gaps >= 0, jnp.exp(logs[:, None, None] * jnp.maximum(gaps, 0.0)), 0.0)
    q_scale = jnp.exp(logs[:, None] * (steps + 1.0))[:, :, None]
    k_scale = jnp.exp(logs[:, None] * (STRETCH - 1.0 - steps))[:, :, None]
    span_decay = jnp.exp(logs * span_rows)
    decay = jnp.broadcast_to(
        jnp.stack([jnp.exp(logs * STRETCH), span_decay], axis=1)[:, :, None, None],
        (local_heads, 2, 1, DV),
    )
    trig = (cosine[:, 0], sine[:, 0], mask, q_scale, k_scale, decay)
    (
        x_rows,
        q_all,
        k_all,
        v_all,
        gate,
        unit,
        gated,
        inverse,
        weights,
        entering,
        hidden,
        cot_rows,
        far_up,
        far_down,
    ) = attend(
        tokens, gain_mix[None, :], cotangent, w_query, w_key, w_value, w_gate, w_out, w_up, w_down, *trig
    )
    y_keep, y_send, grad_hidden, gain_ffn_part, grad_ffn = feed(
        hidden, gain_ffn[None, :], cotangent, cot_rows, w_up, w_down, far_up, far_down
    )
    far = lax.psum_scatter(
        grad_ffn, "seq", scatter_dimension=0, tiled=False, axis_index_groups=same_core()
    )
    grad_in, grad_out_w, y_got = retract(
        grad_hidden, y_send, w_out, q_all, k_all, v_all, gate, unit, gated, inverse, weights, entering, *trig
    )
    output = (y_keep + y_got.astype(f32)).astype(bf16)
    pairs, far_got = pair_sum(x_rows.reshape(span_rows, -1), grad_in, grad_out_w, far)
    summed = lax.psum_scatter(
        pairs, "seq", scatter_dimension=0, tiled=False, axis_index_groups=same_core()
    )
    grad_in, pairs = lax.optimization_barrier((grad_in, pairs))
    grad_tokens, gains, final_up, final_down = finish(
        grad_in, x_rows, tokens, gain_mix[None, :], gain_ffn_part, grad_hidden, w_query, w_key, w_value, w_gate, far, far_got
    )
    summed, gains = lax.optimization_barrier((summed, gains))
    summed = summed.astype(f32)
    gain_mix_sum, gain_ffn_sum = gains[0], gains[1]
    count = lax.axis_size("seq")
    rows, few = w_query.shape[0] // count, w_out.shape[0] // count
    wide, tall = w_query.shape[1], w_value.shape[1]
    final_query = summed[:rows, :wide]
    final_key = summed[:rows, wide:]
    final_value = summed[rows : 2 * rows]
    final_gate = summed[2 * rows : 3 * rows]
    final_out = jnp.concatenate(
        [summed[3 * rows : 3 * rows + few], summed[3 * rows + few :]], axis=1
    )
    return (
        output,
        grad_tokens,
        gain_mix_sum,
        final_query,
        final_key,
        final_value,
        final_gate,
        final_out,
        gain_ffn_sum,
        final_up,
        final_down,
    )


def solution(mesh):
    return jax.shard_map(
        shards,
        mesh=mesh,
        in_specs=(
            P(("seq", "mp"), None),
            P(),
            P(None, "mp"),
            P(None, "mp"),
            P(None, "mp"),
            P(None, "mp"),
            P("mp", None),
            P(),
            P(None, "mp"),
            P("mp", None),
            P(("seq", "mp"), None),
        ),
        out_specs=(
            P(("seq", "mp"), None),
            P(("seq", "mp"), None),
            P(),
            P("seq", "mp"),
            P("seq", "mp"),
            P("seq", "mp"),
            P("seq", "mp"),
            P(("mp", "seq"), None),
            P(),
            P("seq", "mp"),
            P(("mp", "seq"), None),
        ),
        check_vma=False,
    )
```

```python
import math

import jax
import jax.numpy as jnp
from jax import lax
from jax.experimental import pallas as pl
from jax.experimental.pallas import tpu as pltpu
from jax.sharding import PartitionSpec as P

DK = 256
DV = 512
STRETCH = 256
SEQ_DEVS = 4


eps = 1e-05


def same_core():
    count = lax.axis_size("seq")
    return [list(range(core, count, 2)) for core in range(2)]


def angles(positions):
    half = DK // 2
    freq = jnp.exp(-math.log(10000.0) * jnp.arange(half, dtype=jnp.float32) / (half - 1))
    phase = positions.astype(jnp.float32)[:, None] * freq[None, :]
    return (jnp.cos(phase)[:, None, :], jnp.sin(phase)[:, None, :])


def product_t(left, right):
    return lax.dot_general(
        left, right, (((0,), (0,)), ((), ())), preferred_element_type=jnp.float32
    )


def product_rt(left, right):
    return lax.dot_general(
        left, right, (((1,), (1,)), ((), ())), preferred_element_type=jnp.float32
    )


MESH = pl.DeviceIdType.MESH
LIMIT = 62 * 1024 * 1024


def remote(src, dst, send, recv, s, z):
    return pltpu.make_async_remote_copy(
        src_ref=src,
        dst_ref=dst,
        send_sem=send,
        recv_sem=recv,
        device_id=(s, z),
        device_id_type=MESH,
    )


def greet(partners):
    barrier = pltpu.get_barrier_semaphore()
    count = 0
    for present, s, z in partners:

        @pl.when(present)
        def _():
            pl.semaphore_signal(barrier, inc=1, device_id=(s, z), device_id_type=MESH)

        count = count + jnp.where(present, 1, 0)
    pl.semaphore_wait(barrier, count)


def dot(left, right):
    return jnp.dot(left, right, preferred_element_type=jnp.float32)


def line_push(x, send, recv, s, z, slot, way):
    return remote(x.at[slot], x.at[slot], send.at[way, slot], recv.at[slot], s, z + 1 - 2 * way)


def line_gather(x, send, recv, s, z, depth, use, after=None):
    @pl.when(z < depth - 1)
    def _():
        line_push(x, send, recv, s, z, z, 0).start()

    @pl.when(z > 0)
    def _():
        line_push(x, send, recv, s, z, z, 1).start()

    def one(turn, _):
        away = (turn + 1) // 2
        left, right = z - away, z + away

        @pl.when((turn % 2 == 1) & (left >= 0))
        def _():
            remote(x.at[left], x.at[left], send.at[0, left], recv.at[left], s, z - 1).wait_recv()

            @pl.when(z < depth - 1)
            def _():
                line_push(x, send, recv, s, z, left, 0).start()

        @pl.when((turn % 2 == 1) & (right < depth))
        def _():
            remote(x.at[right], x.at[right], send.at[1, right], recv.at[right], s, z + 1).wait_recv()

            @pl.when(z > 0)
            def _():
                line_push(x, send, recv, s, z, right, 1).start()

        if after is not None:
            after(turn)
        slot = jnp.where(turn % 2 == 1, left, right)

        @pl.when((slot >= 0) & (slot < depth))
        def _():
            use(slot)

        return 0

    lax.fori_loop(0, 2 * depth - 1, one, 0)


def line_gather_end(x, send, recv, s, z, depth):
    def one(slot, _):
        @pl.when((slot <= z) & (z < depth - 1))
        def _():
            line_push(x, send, recv, s, z, slot, 0).wait_send()

        @pl.when((slot >= z) & (z > 0))
        def _():
            line_push(x, send, recv, s, z, slot, 1).wait_send()

        return 0

    lax.fori_loop(0, depth, one, 0)


def add_rows(into, other):
    step = 32

    def one(i, _):
        rows = pl.ds(pl.multiple_of(i * step, step), step)
        into[rows, :] = (
            into[rows, :].astype(jnp.float32) + other[rows, :].astype(jnp.float32)
        ).astype(into.dtype)
        return 0

    lax.fori_loop(0, into.shape[0] // step, one, 0)


def line_scatter(sbuf, rbuf, total, send, recv, s, z, depth, partial, own, hook=None):
    def right(j):
        return remote(sbuf.at[j], rbuf.at[j], send.at[j], recv.at[j], s, z + 1)

    def left(j):
        slot = jnp.where(j == z - 1, depth, j)
        return remote(sbuf.at[j], rbuf.at[slot], send.at[j], recv.at[slot], s, z - 1)

    def arrived(slot, sender):
        remote(sbuf.at[0], rbuf.at[slot], send.at[0], recv.at[slot], s, sender).wait_recv()

    def first(turn, _):
        up = depth - 1 + z - turn // 2
        down = turn // 2 - (depth - 1) + z
        j = jnp.where(turn % 2 == 0, up, down)
        valid = jnp.where(turn % 2 == 0, (up > z) & (up < depth), (down >= 0) & (down < z))

        @pl.when(valid)
        def _():
            partial(j)

            @pl.when((z == 0) & (j > z))
            def _():
                right(j).start()

            @pl.when((z == depth - 1) & (j < z))
            def _():
                left(j).start()

        return 0

    lax.fori_loop(0, 2 * (depth - 1), first, 0)
    own()

    def event(turn, _):
        up = depth - 1 + z - turn
        down = turn - (depth - 1) + z

        @pl.when((z > 0) & (up >= z) & (up < depth))
        def _():
            arrived(up, z - 1)

            @pl.when(up > z)
            def _():
                add_rows(sbuf.at[up], rbuf.at[up])
                right(up).start()

            @pl.when(up == z)
            def _():
                add_rows(total, rbuf.at[up])

        @pl.when((z < depth - 1) & (down >= 0) & (down <= z))
        def _():
            slot = jnp.where(down == z, depth, down)
            arrived(slot, z + 1)

            @pl.when(down < z)
            def _():
                add_rows(sbuf.at[down], rbuf.at[down])
                left(down).start()

            @pl.when(down == z)
            def _():
                add_rows(total, rbuf.at[depth])

        if hook is not None:
            hook(turn)
        return 0

    lax.fori_loop(0, depth, event, 0)

    def end(j, _):
        @pl.when(j > z)
        def _():
            right(j).wait_send()

        @pl.when(j < z)
        def _():
            left(j).wait_send()

        return 0

    lax.fori_loop(0, depth, end, 0)


def centred(rows):
    centre = rows - jnp.mean(rows, axis=-1, keepdims=True)
    inverse = lax.rsqrt(jnp.mean(centre * centre, axis=-1, keepdims=True) + eps)
    return centre * inverse, inverse


def block(rows, index):
    return pl.ds(pl.multiple_of(index * rows, rows), rows)


def attend_kernel(
    tok,
    gain,
    cot,
    w_query,
    w_key,
    w_value,
    w_gate,
    w_out,
    w_up,
    w_down,
    cosine,
    sine,
    mask,
    q_scale,
    k_scale,
    decay,
    x_out,
    q_out,
    k_out,
    v_out,
    gp_out,
    gn_out,
    gated_out,
    inv_out,
    p_out,
    r_out,
    hidden_out,
    cot_rows,
    far_up,
    far_down,
    xg,
    q,
    k,
    v,
    gp,
    gn,
    gated,
    inv,
    weights,
    grown,
    entering,
    tile,
    state,
    state_in,
    state_to,
    rbuf,
    total,
    wq,
    wk,
    wv,
    wg,
    wo,
    load,
    save,
    g_send,
    g_recv,
    s_send,
    s_recv,
    c_send,
    c_recv,
    x_send,
    x_recv,
    f_send,
    f_recv,
    p_send,
    p_recv,
):
    f32, bf16 = jnp.float32, jnp.bfloat16
    depth = xg.shape[0]
    rows = xg.shape[1]
    heads = mask.shape[0]
    s, z = lax.axis_index("seq"), lax.axis_index("mp")
    place = lax.rem(s, SEQ_DEVS)
    pair = z + 1 - 2 * lax.rem(z, 2)
    twin = s + 1 - 2 * lax.rem(s, 2)
    loads = [
        pltpu.make_async_copy(a, b, load.at[i])
        for i, (a, b) in enumerate(
            [(w_query, wq), (w_key, wk), (w_value, wv), (w_gate, wg), (w_out, wo)]
        )
    ]
    for copy in loads:
        copy.start()

    def norm(i, _):
        part = pl.ds(pl.multiple_of(i * 32, 32), 32)
        unit, _ = centred(tok[part, :].astype(f32))
        xg[z, part, :] = (unit * gain[...]).astype(bf16)
        return 0

    lax.fori_loop(0, rows // 32, norm, 0)
    count = lax.axis_size("seq")
    across = flip(z, 2)
    greet(
        [(z > 0, s, z - 1), (z < depth - 1, s, z + 1), (z >= 0, s, across)]
        + [(s != other, other, z) for other in range(count)]
    )
    tall, few = w_up.shape[0] // count, w_down.shape[0] // count
    mine = pltpu.make_async_copy(cot, cot_rows.at[0], x_send.at[3])
    near = remote(cot, cot_rows.at[2], x_send.at[1], x_recv.at[1], twin, z)
    swap = remote(cot, cot_rows.at[1], x_send.at[0], x_recv.at[0], s, pair)
    far = remote(cot_rows.at[1], cot_rows.at[3], x_send.at[2], x_recv.at[2], twin, z)

    def piece(source):
        return block(tall, source), block(few, source)

    up_at, down_at = piece(s)
    moves = [
        remote(w_up.at[up_at], far_up.at[up_at], f_send.at[0], f_recv.at[0], s, across),
        remote(w_down.at[down_at], far_down.at[down_at], f_send.at[1], f_recv.at[1], s, across),
    ]
    edge = (z == 0) | (z == depth - 1)

    def spread(source, chip):
        up_, down_ = piece(source)
        to = 2 * chip + 1
        return [
            remote(far_up.at[up_], far_up.at[up_], p_send.at[0, chip], p_recv.at[0, source], to, z),
            remote(
                far_down.at[down_], far_down.at[down_], p_send.at[1, chip], p_recv.at[1, source], to, z
            ),
        ]

    mine.start()
    near.start()

    @pl.when(place == 0)
    def _():
        state_in[...] = jnp.zeros_like(state_in)

    def after(turn):
        @pl.when(edge & (turn == 1))
        def _():
            swap.start()

        @pl.when(edge & (turn == 3))
        def _():
            for copy in moves:
                copy.start()

    def use(j):
        at = block(rows, j)

        @pl.when(j == z)
        def _():
            for copy in loads:
                copy.wait()

        c, sn = cosine[at, :], sine[at, :]
        for h in range(heads):
            cols = slice(h * DK, (h + 1) * DK)
            for w, out in ((wq, q), (wk, k)):
                p = dot(xg[j], w[:, cols])
                a, b = p[:, : DK // 2], p[:, DK // 2 :]
                out[at, h * DK : h * DK + DK // 2] = (a * c - b * sn).astype(bf16)
                out[at, h * DK + DK // 2 : (h + 1) * DK] = (b * c + a * sn).astype(bf16)
        for h in range(heads):
            wide = slice(h * DV, (h + 1) * DV)
            v[at, wide] = dot(xg[j], wv[:, wide]).astype(bf16)
            gp[at, wide] = dot(xg[j], wg[:, wide])
        for h in range(heads):
            cols = slice(h * DK, (h + 1) * DK)
            wide = slice(h * DV, (h + 1) * DV)
            kb, vb = k[at, cols], v[at, wide]
            vd = (vb.astype(f32) * k_scale[h]).astype(bf16)
            grown[h, j] = product_t(kb, vd)
            weights[h, j] = (product_rt(q[at, cols], kb) * mask[h]).astype(bf16)

    line_gather(xg, g_send, g_recv, s, z, depth, use, after)
    def chain(h, to):
        return remote(state_to.at[h], state_in.at[h], c_send.at[h], c_recv.at[h], to, z)

    for h in range(heads):
        state[h] = grown[h, 0]
        for b in range(1, depth):
            state[h] = decay[h, 0] * state[h] + grown[h, b]

        @pl.when(place > 0)
        def _():
            chain(h, s - 1).wait_recv()

        @pl.when(place < SEQ_DEVS - 1)
        def _():
            state_to[h] = (decay[h, 1] * state_in[h].astype(f32) + state[h]).astype(bf16)
            chain(h, s + 1).start()

    saves = [
        pltpu.make_async_copy(a, b, save.at[i])
        for i, (a, b) in enumerate(
            [
                (xg, x_out),
                (q, q_out),
                (k, k_out),
                (v, v_out),
                (gp, gp_out),
                (weights, p_out),
                (entering, r_out),
                (gn, gn_out),
                (gated, gated_out),
                (inv, inv_out),
            ]
        )
    ]
    for copy in saves[:6]:
        copy.start()

    def hand_out():
        for copy in moves:
            copy.wait_recv()

        def to_chip(chip, _):
            @pl.when(2 * chip + 1 != s)
            def _():
                for copy in spread(s, chip):
                    copy.start()

            return 0

        lax.fori_loop(0, count // 2, to_chip, 0)

    for h in range(heads):
        cols = slice(h * DK, (h + 1) * DK)
        wide = slice(h * DV, (h + 1) * DV)
        state[h] = state_in[h].astype(f32)

        def cross(b, _):
            at = block(rows, b)
            entering[h, b] = state[h].astype(bf16)
            state[h] = decay[h, 0] * state[h] + grown[h, b]
            qd = (q[at, cols].astype(f32) * q_scale[h]).astype(bf16)
            tile[...] = dot(weights[h, b], v[at, wide]) + dot(qd, entering[h, b])

            def norm(i, _):
                here = block(32, i)
                there = pl.ds(pl.multiple_of(b * rows + i * 32, 32), 32)
                unit, inverse = centred(tile[here, :])
                gate = gp[there, wide]
                gn[there, wide] = unit
                gated[there, wide] = (unit * gate / (1.0 + jnp.exp(-gate))).astype(bf16)
                inv[h, there, :] = jnp.broadcast_to(inverse, (32, inv.shape[2]))
                return 0

            lax.fori_loop(0, rows // 32, norm, 0)
            return 0

        lax.fori_loop(0, depth, cross, 0)
    for copy in saves[6:]:
        copy.start()
    line_gather_end(xg, g_send, g_recv, s, z, depth)

    @pl.when(jnp.logical_not(edge))
    def _():
        hand_out()

    saves[0].wait()
    wide = 512

    def hook(turn):
        @pl.when((turn == 0) & jnp.logical_not(edge))
        def _():
            for copy in moves:
                copy.start()
            swap.start()

        @pl.when((turn == 0) & edge)
        def _():
            hand_out()

        @pl.when(turn == 2)
        def _():
            swap.wait_recv()
            far.start()

    def partial(j):
        for n in range(0, total.shape[1], wide):
            xg[j, :, n : n + wide] = dot(gated[block(rows, j), :], wo[:, n : n + wide]).astype(bf16)

    def own():
        for n in range(0, total.shape[1], wide):
            total[:, n : n + wide] = tok[:, n : n + wide].astype(f32) + dot(
                gated[block(rows, z), :], wo[:, n : n + wide]
            )

    line_scatter(xg, rbuf, total, s_send, s_recv, s, z, depth, partial, own, hook)
    done = pltpu.make_async_copy(total, hidden_out, save.at[0])
    done.start()

    @pl.when(place < SEQ_DEVS - 1)
    def _():
        for h in range(heads):
            chain(h, s + 1).wait_send()

    def sent(chip, _):
        @pl.when(2 * chip + 1 != s)
        def _():
            for copy in spread(s, chip):
                copy.wait_send()

        return 0

    lax.fori_loop(0, count // 2, sent, 0)

    def came(source, _):
        @pl.when((source != s) & (lax.rem(s, 2) == 1))
        def _():
            for copy in spread(source, 0):
                copy.wait_recv()

        return 0

    lax.fori_loop(0, count, came, 0)
    for copy in moves:
        copy.wait_send()
    swap.wait_send()
    near.wait()
    far.wait()
    mine.wait()
    for copy in saves[1:]:
        copy.wait()
    done.wait()


def attend(
    tok, gain, cot, w_query, w_key, w_value, w_gate, w_out, w_up, w_down, cosine, sine, mask, q_scale, k_scale, decay
):
    f32, bf16 = jnp.float32, jnp.bfloat16
    depth = lax.axis_size("mp")
    rows, width = tok.shape
    span = depth * rows
    heads = mask.shape[0]
    hk, hv = w_query.shape[1], w_value.shape[1]
    any_ = pl.BlockSpec(memory_space=pl.ANY)
    vmem = pl.BlockSpec(memory_space=pltpu.VMEM)
    shapes = [
        ((depth, rows, width), bf16),
        ((span, hk), bf16),
        ((span, hk), bf16),
        ((span, hv), bf16),
        ((span, hv), f32),
        ((span, hv), f32),
        ((span, hv), bf16),
        ((heads, span, 128), f32),
        ((heads, depth, rows, rows), bf16),
        ((heads, depth, DK, DV), bf16),
        ((rows, width), f32),
        ((4, rows, width), bf16),
        (w_up.shape, bf16),
        (w_down.shape, bf16),
    ]
    count = lax.axis_size("seq")
    dma = pltpu.SemaphoreType.DMA
    return pl.pallas_call(
        attend_kernel,
        out_shape=[jax.ShapeDtypeStruct(*one) for one in shapes],
        in_specs=[vmem, vmem, any_] + [any_] * 7 + [vmem] * 6,
        out_specs=[any_] * len(shapes),
        scratch_shapes=[
            pltpu.VMEM((depth, rows, width), bf16),
            pltpu.VMEM((span, hk), bf16),
            pltpu.VMEM((span, hk), bf16),
            pltpu.VMEM((span, hv), bf16),
            pltpu.VMEM((span, hv), f32),
            pltpu.VMEM((span, hv), f32),
            pltpu.VMEM((span, hv), bf16),
            pltpu.VMEM((heads, span, 128), f32),
            pltpu.VMEM((heads, depth, rows, rows), bf16),
            pltpu.VMEM((heads, depth, DK, DV), f32),
            pltpu.VMEM((heads, depth, DK, DV), bf16),
            pltpu.VMEM((rows, DV), f32),
            pltpu.VMEM((heads, DK, DV), f32),
            pltpu.VMEM((heads, DK, DV), bf16),
            pltpu.VMEM((heads, DK, DV), bf16),
            pltpu.VMEM((depth + 1, rows, width), bf16),
            pltpu.VMEM((rows, width), f32),
            pltpu.VMEM(w_query.shape, bf16),
            pltpu.VMEM(w_key.shape, bf16),
            pltpu.VMEM(w_value.shape, bf16),
            pltpu.VMEM(w_gate.shape, bf16),
            pltpu.VMEM(w_out.shape, bf16),
            dma((5,)),
            dma((10,)),
            dma((2, depth)),
            dma((depth,)),
            dma((depth,)),
            dma((depth + 1,)),
            dma((heads,)),
            dma((heads,)),
            dma((4,)),
            dma((3,)),
            dma((2,)),
            dma((2,)),
            dma((2, count // 2)),
            dma((2, count)),
        ],
        compiler_params=pltpu.CompilerParams(
            collective_id=0, has_side_effects=True, vmem_limit_bytes=LIMIT
        ),
        cost_estimate=pl.CostEstimate(
            flops=190 * 10**9, bytes_accessed=60 * 10**6, transcendentals=2 * 10**6
        ),
        name="attend",
    )(tok, gain, cot, w_query, w_key, w_value, w_gate, w_out, w_up, w_down, cosine, sine, mask, q_scale, k_scale, decay)


def row_loop(rows, step, body):
    def one(i, _):
        body(pl.ds(pl.multiple_of(i * step, step), step), i)
        return 0

    lax.fori_loop(0, rows // step, one, 0)


def norm_rows_back(grad_hat, unit, inverse):
    first = jnp.mean(grad_hat, axis=-1, keepdims=True)
    second = jnp.mean(grad_hat * unit, axis=-1, keepdims=True)
    return inverse * (grad_hat - first - unit * second)


def feed_kernel(
    hidden,
    gain,
    cot,
    cot_rows,
    w_up,
    w_down,
    far_up,
    far_down,
    y_keep,
    y_send,
    grad_hidden,
    gain_part,
    g_all_out,
    x,
    dy,
    act,
    du,
    part_y,
    part_x,
    got_x,
    got_y,
    u_tile,
    d_tile,
    g_all,
    up,
    down,
    load,
    save,
    send,
    recv,
):
    f32, bf16 = jnp.float32, jnp.bfloat16
    rows, width = hidden.shape
    units = up.shape[1]
    s, z = lax.axis_index("seq"), lax.axis_index("mp")
    pair = z + 1 - 2 * lax.rem(z, 2)
    twin = s + 1 - 2 * lax.rem(s, 2)
    own_loads = [
        pltpu.make_async_copy(w_up, up, load.at[0]),
        pltpu.make_async_copy(w_down, down, load.at[1]),
    ]
    far_loads = [
        pltpu.make_async_copy(far_up, up, load.at[0]),
        pltpu.make_async_copy(far_down, down, load.at[1]),
    ]

    @pl.when(lax.rem(s, 2) == 0)
    def _():
        for copy in own_loads:
            copy.start()

    @pl.when(lax.rem(s, 2) == 1)
    def _():
        for copy in far_loads:
            copy.start()

    rest = [
        pltpu.make_async_copy(cot_rows.at[r], dy.at[pl.ds(r * rows, rows)], load.at[2 + r])
        for r in range(4)
    ]
    loads = own_loads + rest
    for copy in rest:
        copy.start()

    def norm(here, i):
        unit, _ = centred(hidden[here, :])
        x[here, :] = (unit * gain[...]).astype(bf16)

    row_loop(rows, 32, norm)
    greet([(z >= 0, s, pair), (z >= 0, twin, z)])
    slot = [pl.ds(r * rows, rows) for r in range(4)]
    over = remote(x.at[slot[0]], x.at[slot[1]], send.at[0], recv.at[0], s, pair)
    near = remote(x.at[slot[0]], x.at[slot[2]], send.at[1], recv.at[1], twin, z)
    far = remote(x.at[slot[1]], x.at[slot[3]], send.at[2], recv.at[2], twin, z)
    near.start()
    over.start()
    back_near = remote(part_x.at[slot[2]], got_x.at[0], send.at[3], recv.at[3], twin, z)
    back_far = remote(part_x.at[slot[3]], got_x.at[1], send.at[4], recv.at[4], twin, z)
    back_over = remote(part_x.at[slot[1]], got_x.at[2], send.at[5], recv.at[5], s, pair)
    y_back = remote(
        part_y.at[pl.ds(2 * rows, 2 * rows)], got_y, send.at[6], recv.at[6], twin, z
    )
    for copy in loads:
        copy.wait()
    step = 512

    def one(turn, _):
        r = lax.rem(turn, 2) * 2 + turn // 2
        at = block(rows, r)

        @pl.when(turn == 1)
        def _():
            near.wait_recv()

        @pl.when(turn == 2)
        def _():
            over.wait_recv()
            far.start()

        @pl.when(turn == 3)
        def _():
            far.wait_recv()

        for n in range(0, units, step):
            cols = slice(n, n + step)
            u_tile[...] = dot(x[at, :], up[:, cols])
            d_tile[...] = product_rt(dy[at, :], down[cols, :])

            def gelu(here, i):
                there = pl.ds(pl.multiple_of(r * rows + i * 32, 32), 32)
                u = u_tile[here, :]
                normal = 0.5 * (1.0 + lax.erf(u * (2.0**-0.5)))
                slope = normal + u * (jnp.exp(-0.5 * u * u) * ((2.0 * math.pi) ** -0.5))
                act[there, cols] = (u * normal).astype(bf16)
                du[there, cols] = (d_tile[here, :] * slope).astype(bf16)

            row_loop(rows, 32, gelu)
        for n in range(0, width, step):
            part_x[at, n : n + step] = product_rt(du[at, :], up[n : n + step, :]).astype(bf16)

        @pl.when(turn == 1)
        def _():
            back_near.start()

        @pl.when(turn == 3)
        def _():
            back_far.start()

        return 0

    lax.fori_loop(0, 4, one, 0)
    back_far.wait_recv()
    add_rows(part_x.at[slot[1]], got_x.at[1])
    back_over.start()

    def y_terms(r, _):
        at = block(rows, r)
        for n in range(0, width, step):
            part_y[at, n : n + step] = dot(act[at, :], down[:, n : n + step]).astype(bf16)
        return 0

    lax.fori_loop(0, 4, y_terms, 0)
    y_back.start()

    chips, _, high, _ = g_all.shape
    few = units // (2 * chips)
    tall = width // (2 * chips)

    def up_terms(m, _):
        cols = pl.ds(pl.multiple_of(m * 256, 256), 256)
        for n in range(0, units, step):
            value = product_t(x[:, cols], du[:, n : n + step]).astype(bf16)
            for part in range(256 // tall):
                to = m * (256 // tall) + part
                g_all[to // 2, lax.rem(to, 2), 0:tall, n : n + step] = value[
                    part * tall : (part + 1) * tall
                ]
        return 0

    lax.fori_loop(0, width // 256, up_terms, 0)

    def down_terms(m, _):
        cols = pl.ds(pl.multiple_of(m * 256, 256), 256)
        for n in range(0, width, step):
            value = product_t(act[:, cols], dy[:, n : n + step]).astype(bf16)
            first = tall + n // units * few
            for part in range(256 // few):
                to = m * (256 // few) + part
                g_all[to // 2, lax.rem(to, 2), first : first + few, n % units : n % units + step] = (
                    value[part * few : (part + 1) * few]
                )
        return 0

    lax.fori_loop(0, units // 256, down_terms, 0)
    saves = [pltpu.make_async_copy(g_all, g_all_out, save.at[0])]
    saves[0].start()
    y_back.wait_recv()

    def y_sum(here, i):
        there = pl.ds(pl.multiple_of(rows + i * 32, 32), 32)
        y_keep[here, :] = (
            hidden[here, :] + part_y[here, :].astype(f32) + got_y[here, :].astype(f32)
        )
        y_send[here, :] = (part_y[there, :].astype(f32) + got_y[there, :].astype(f32)).astype(bf16)

    row_loop(rows, 32, y_sum)
    back_near.wait_recv()
    back_over.wait_recv()
    gain_part[...] = jnp.zeros_like(gain_part)

    def finish(here, i):
        unit, inverse = centred(hidden[here, :])
        grad = (
            part_x[here, :].astype(f32) + got_x[0, here, :].astype(f32)
        ) + got_x[2, here, :].astype(f32)
        gain_part[...] += jnp.sum(grad * unit, axis=0, keepdims=True)
        grad_hidden[here, :] = cot[here, :].astype(f32) + norm_rows_back(
            grad * gain[...], unit, inverse
        )

    row_loop(rows, 32, finish)
    for copy in (near, over, far, back_near, back_far, back_over, y_back):
        copy.wait_send()
    for copy in saves:
        copy.wait()


def feed(hidden, gain, cot, cot_rows, w_up, w_down, far_up, far_down):
    f32, bf16 = jnp.float32, jnp.bfloat16
    rows, width = hidden.shape
    units = w_up.shape[1]
    count = lax.axis_size("seq")
    gathered = (count // 2, 2, width // count + width // count, units)
    any_ = pl.BlockSpec(memory_space=pl.ANY)
    vmem = pl.BlockSpec(memory_space=pltpu.VMEM)
    dma = pltpu.SemaphoreType.DMA
    return pl.pallas_call(
        feed_kernel,
        out_shape=[
            jax.ShapeDtypeStruct((rows, width), f32),
            jax.ShapeDtypeStruct((rows, width), bf16),
            jax.ShapeDtypeStruct((rows, width), f32),
            jax.ShapeDtypeStruct((1, width), f32),
            jax.ShapeDtypeStruct(gathered, bf16),
        ],
        in_specs=[vmem, vmem, vmem] + [any_] * 5,
        out_specs=[vmem] * 4 + [any_],
        scratch_shapes=[
            pltpu.VMEM((4 * rows, width), bf16),
            pltpu.VMEM((4 * rows, width), bf16),
            pltpu.VMEM((4 * rows, units), bf16),
            pltpu.VMEM((4 * rows, units), bf16),
            pltpu.VMEM((4 * rows, width), bf16),
            pltpu.VMEM((4 * rows, width), bf16),
            pltpu.VMEM((3, rows, width), bf16),
            pltpu.VMEM((2 * rows, width), bf16),
            pltpu.VMEM((rows, 512), f32),
            pltpu.VMEM((rows, 512), f32),
            pltpu.VMEM(gathered, bf16),
            pltpu.VMEM(w_up.shape, bf16),
            pltpu.VMEM(w_down.shape, bf16),
            dma((6,)),
            dma((1,)),
            dma((7,)),
            dma((7,)),
        ],
        compiler_params=pltpu.CompilerParams(
            collective_id=1, has_side_effects=True, vmem_limit_bytes=LIMIT
        ),
        cost_estimate=pl.CostEstimate(
            flops=75 * 10**9, bytes_accessed=30 * 10**6, transcendentals=2 * 10**6
        ),
        name="feed",
    )(hidden, gain, cot, cot_rows, w_up, w_down, far_up, far_down)


def retract_kernel(
    grad_hidden,
    y_send,
    w_out,
    q_in,
    k_in,
    v_in,
    gp_in,
    gn_in,
    gated_in,
    inv_in,
    p_in,
    r_in,
    cosine,
    sine,
    mask,
    q_scale,
    k_scale,
    decay,
    d_out,
    g_out,
    y_got,
    dx,
    q,
    k,
    v,
    gp,
    gn,
    gated,
    inv,
    weights,
    entering,
    wo,
    dall,
    do,
    do_low,
    tile,
    grown,
    dk,
    dv,
    state,
    state_in,
    state_to,
    g_wo,
    load,
    save,
    g_send,
    g_recv,
    c_send,
    c_recv,
    y_sems,
):
    f32, bf16 = jnp.float32, jnp.bfloat16
    depth, rows, width = dx.shape
    heads = mask.shape[0]
    hk, hv = q.shape[1], v.shape[1]
    s, z = lax.axis_index("seq"), lax.axis_index("mp")
    place = lax.rem(s, SEQ_DEVS)
    pair = z + 1 - 2 * lax.rem(z, 2)
    loads = [
        pltpu.make_async_copy(a, b, load.at[i])
        for i, (a, b) in enumerate(
            [
                (w_out, wo),
                (q_in, q),
                (k_in, k),
                (v_in, v),
                (gp_in, gp),
                (gn_in, gn),
                (gated_in, gated),
                (inv_in, inv),
                (p_in, weights),
                (r_in, entering),
            ]
        )
    ]
    for copy in loads:
        copy.start()

    def low(here, i):
        dx[z, here, :] = grad_hidden[here, :].astype(bf16)

    row_loop(rows, 32, low)
    greet(
        [
            (z > 0, s, z - 1),
            (z < depth - 1, s, z + 1),
            (place > 0, s - 1, z),
            (place < SEQ_DEVS - 1, s + 1, z),
        ]
    )

    @pl.when(place == SEQ_DEVS - 1)
    def _():
        state_in[...] = jnp.zeros_like(state_in)

    def turn_back(value, at, start):
        c, sn = cosine[at, :], sine[at, :]
        half = DK // 2
        a, b = value[:, :half], value[:, half:]
        dall[at, start : start + half] = (a * c + b * sn).astype(bf16)
        dall[at, start + half : start + DK] = (b * c - a * sn).astype(bf16)

    def use(j):
        at = block(rows, j)

        @pl.when(j == z)
        def _():
            for copy in loads:
                copy.wait()

        for h in range(heads):
            wide = slice(h * DV, (h + 1) * DV)
            tile[...] = product_rt(dx[j], wo[wide, :])

            def gate_back(here, i):
                there = pl.ds(pl.multiple_of(j * rows + i * 32, 32), 32)
                grad = tile[here, :]
                gate = gp[there, wide]
                unit = gn[there, wide]
                open_ = 1.0 / (1.0 + jnp.exp(-gate))
                slope = open_ * (1.0 + gate * (1.0 - open_))
                first = 2 * hk + hv + h * DV
                dall[there, first : first + DV] = (grad * unit * slope).astype(bf16)
                inverse = inv[h, there, :][:, :1]
                value = norm_rows_back(grad * gate * open_, unit, inverse)
                high = value.astype(bf16)
                do[there, wide] = high
                do_low[here, wide] = (value - high.astype(f32)).astype(bf16)

            row_loop(rows, 32, gate_back)
        for h in range(heads):
            cols = slice(h * DK, (h + 1) * DK)
            wide = slice(h * DV, (h + 1) * DV)
            qb, kb, vb, db = q[at, cols], k[at, cols], v[at, wide], do[at, wide]
            raw = product_rt(db, vb) + product_rt(do_low[:, wide], vb)
            ds = (raw * mask[h]).astype(bf16)
            dv[at, wide] = product_t(weights[h, j], db)
            dk[at, cols] = product_t(ds, qb)
            turn_back(dot(ds, kb) + q_scale[h] * product_rt(db, entering[h, j]), at, h * DK)
            qd = (qb.astype(f32) * q_scale[h]).astype(bf16)
            grown[h, j] = product_t(qd, db)

    line_gather(dx, g_send, g_recv, s, z, depth, use)
    swap = remote(y_send, y_got, y_sems.at[0], y_sems.at[1], s, pair)
    swap.start()
    def out_terms(m, _):
        cols = pl.ds(pl.multiple_of(m * 256, 256), 256)
        for n in range(0, width, 512):
            right = dx[:, :, n : n + 512].reshape(depth * rows, 512)
            g_wo[cols, n : n + 512] = product_t(gated[:, cols], right).astype(bf16)
        return 0

    def out_grad():
        lax.fori_loop(0, hv // 256, out_terms, 0)

    for h in range(heads):
        state[h] = grown[h, depth - 1]
        for b in reversed(range(depth - 1)):
            state[h] = decay[h, 0] * state[h] + grown[h, b]

    @pl.when(place <= 1)
    def _():
        out_grad()

    def chain(h, to):
        return remote(state_to.at[h], state_in.at[h], c_send.at[h], c_recv.at[h], to, z)

    for h in range(heads):

        @pl.when(place < SEQ_DEVS - 1)
        def _():
            chain(h, s + 1).wait_recv()

        @pl.when(place > 0)
        def _():
            state_to[h] = (decay[h, 1] * state_in[h].astype(f32) + state[h]).astype(bf16)
            chain(h, s - 1).start()

    for h in range(heads):
        cols = slice(h * DK, (h + 1) * DK)
        wide = slice(h * DV, (h + 1) * DV)
        state[h] = state_in[h].astype(f32)

        def cross(turn, _):
            b = depth - 1 - turn
            at = block(rows, b)
            leaving = state[h].astype(bf16)
            state[h] = grown[h, b] + decay[h, 0] * state[h]
            kb = k[at, cols]
            vd = (v[at, wide].astype(f32) * k_scale[h]).astype(bf16)
            turn_back(dk[at, cols] + product_rt(vd, leaving), at, hk + h * DK)
            dall[at, 2 * hk + h * DV : 2 * hk + (h + 1) * DV] = (
                dv[at, wide] + k_scale[h] * dot(kb, leaving)
            ).astype(bf16)
            return 0

        lax.fori_loop(0, depth, cross, 0)
    saves = [
        pltpu.make_async_copy(dall, d_out, save.at[0]),
        pltpu.make_async_copy(g_wo, g_out, save.at[1]),
    ]
    saves[0].start()

    @pl.when(place > 1)
    def _():
        out_grad()

    saves[1].start()
    line_gather_end(dx, g_send, g_recv, s, z, depth)

    @pl.when(place > 0)
    def _():
        for h in range(heads):
            chain(h, s - 1).wait_send()

    swap.wait()
    for copy in saves:
        copy.wait()


def retract(
    grad_hidden, y_send, w_out, q, k, v, gp, gn, gated, inv, p, r, cosine, sine, mask, q_scale, k_scale, decay
):
    f32, bf16 = jnp.float32, jnp.bfloat16
    depth = lax.axis_size("mp")
    rows, width = grad_hidden.shape
    span = depth * rows
    heads = mask.shape[0]
    hk, hv = q.shape[1], v.shape[1]
    any_ = pl.BlockSpec(memory_space=pl.ANY)
    vmem = pl.BlockSpec(memory_space=pltpu.VMEM)
    dma = pltpu.SemaphoreType.DMA
    return pl.pallas_call(
        retract_kernel,
        out_shape=[
            jax.ShapeDtypeStruct((span, 2 * hk + 2 * hv), bf16),
            jax.ShapeDtypeStruct((hv, width), bf16),
            jax.ShapeDtypeStruct((rows, width), bf16),
        ],
        in_specs=[vmem] + [any_] * 11 + [vmem] * 6,
        out_specs=[any_] * 3,
        scratch_shapes=[
            pltpu.VMEM((depth, rows, width), bf16),
            pltpu.VMEM((span, hk), bf16),
            pltpu.VMEM((span, hk), bf16),
            pltpu.VMEM((span, hv), bf16),
            pltpu.VMEM((span, hv), f32),
            pltpu.VMEM((span, hv), f32),
            pltpu.VMEM((span, hv), bf16),
            pltpu.VMEM((heads, span, 128), f32),
            pltpu.VMEM((heads, depth, rows, rows), bf16),
            pltpu.VMEM((heads, depth, DK, DV), bf16),
            pltpu.VMEM(w_out.shape, bf16),
            pltpu.VMEM((span, 2 * hk + 2 * hv), bf16),
            pltpu.VMEM((span, hv), bf16),
            pltpu.VMEM((rows, hv), bf16),
            pltpu.VMEM((rows, DV), f32),
            pltpu.VMEM((heads, depth, DK, DV), f32),
            pltpu.VMEM((span, hk), f32),
            pltpu.VMEM((span, hv), f32),
            pltpu.VMEM((heads, DK, DV), f32),
            pltpu.VMEM((heads, DK, DV), bf16),
            pltpu.VMEM((heads, DK, DV), bf16),
            pltpu.VMEM((hv, width), bf16),
            dma((10,)),
            dma((2,)),
            dma((2, depth)),
            dma((depth,)),
            dma((heads,)),
            dma((heads,)),
            dma((2,)),
        ],
        compiler_params=pltpu.CompilerParams(
            collective_id=2, has_side_effects=True, vmem_limit_bytes=LIMIT
        ),
        cost_estimate=pl.CostEstimate(
            flops=120 * 10**9, bytes_accessed=40 * 10**6, transcendentals=2 * 10**6
        ),
        name="retract",
    )(grad_hidden, y_send, w_out, q, k, v, gp, gn, gated, inv, p, r, cosine, sine, mask, q_scale, k_scale, decay)


def flip(index, bit):
    return index + bit - 2 * bit * lax.rem(index // bit, 2)


def pair_kernel(
    x, d, wo_parts, far, out, far_got, stage, got, wo_mine, wo_got, result, save, send, recv, w_sems, f_sems
):
    f32, bf16 = jnp.float32, jnp.bfloat16
    _, chips, rows, _ = stage.shape
    few = wo_mine.shape[1]
    third = result.shape[2]
    s, z = lax.axis_index("seq"), lax.axis_index("mp")
    core = lax.rem(s, 2)
    twin = flip(s, 1)
    across = flip(z, 2)
    edge = (z == 0) | (z == lax.axis_size("mp") - 1)
    greet([(z >= 0, twin, z), (z >= 0, s, across), (z >= 0, twin, across)])
    crossed = remote(far.at[0], far_got, f_sems.at[0], f_sems.at[1], twin, across)
    straight = remote(far.at[1], far_got, f_sems.at[2], f_sems.at[3], s, across)

    @pl.when(edge & (core == 1))
    def _():
        crossed.start()
        straight.start()

    wo_load = pltpu.make_async_copy(wo_parts.at[:, core], wo_mine, w_sems.at[0])
    wo_load.start()
    wo_send = remote(wo_parts.at[:, 1 - core], wo_got, w_sems.at[1], w_sems.at[2], twin, z)
    wo_send.start()
    span = max(256, 2 * rows)
    each = span // (2 * rows)

    def give(i):
        return remote(stage.at[1 - core, i], got.at[i], send.at[i], recv.at[i], twin, z)

    def keep(i):
        return pltpu.make_async_copy(result.at[i], out.at[i], save.at[i])

    def take(i):
        give(i).wait_recv()
        for t in range(d.shape[1] // third):

            def add(here, r):
                there = pl.ds(pl.multiple_of(t * rows + r * 32, 32), 32)
                cols = slice(t * third, (t + 1) * third)
                result[i, there, :] = (
                    stage[core, i, here, cols].astype(f32) + got[i, here, cols].astype(f32)
                ).astype(bf16)

            row_loop(rows, 32, add)

    def one(g, _):
        for c in range(span // 256):
            chunk = g * (span // 256) + c
            cols = pl.ds(pl.multiple_of(chunk * 256, 256), 256)
            for n in range(0, d.shape[1], 1024):
                value = product_t(x[:, cols], d[:, n : n + 1024]).astype(bf16)
                for part in range(max(1, 256 // rows)):
                    to = (c if each == 1 and rows >= 256 else part) % 2
                    i = g * each + (0 if rows >= 256 else part // 2)
                    stage[to, i, :, n : n + 1024] = value[part * rows : (part + 1) * rows]
        for e in range(each):
            give(g * each + e).start()

        @pl.when(g > 0)
        def _():
            for e in range(each):
                take((g - 1) * each + e)

        return 0

    groups = chips // each
    lax.fori_loop(0, groups, one, 0)
    wo_load.wait()
    wo_send.wait()
    base = rows * (d.shape[1] // third)

    def wo_add(i, _):
        for t in range(wo_mine.shape[2] // third):
            cols = slice(t * third, (t + 1) * third)
            result[i, base + t * few : base + (t + 1) * few, :] = (
                wo_mine[i, :, cols].astype(f32) + wo_got[i, :, cols].astype(f32)
            ).astype(bf16)
        return 0

    lax.fori_loop(0, chips, wo_add, 0)
    for e in range(each):
        take((groups - 1) * each + e)

    def begin(i, _):
        keep(i).start()
        return 0

    def end(i, _):
        keep(i).wait()
        give(i).wait_send()
        return 0

    lax.fori_loop(0, chips, begin, 0)
    lax.fori_loop(0, chips, end, 0)

    @pl.when(edge & (core == 1))
    def _():
        crossed.wait_send()
        straight.wait_send()

    @pl.when(jnp.logical_not(edge) & (core == 0))
    def _():
        crossed.wait_recv()

    @pl.when(jnp.logical_not(edge) & (core == 1))
    def _():
        straight.wait_recv()


def pair_sum(x, d, g_out, far):
    bf16 = jnp.bfloat16
    count = lax.axis_size("seq")
    chips = count // 2
    rows, few = x.shape[1] // count, g_out.shape[0] // count
    wide, third = d.shape[1], d.shape[1] // 3
    high = 3 * rows + few * g_out.shape[1] // third
    any_ = pl.BlockSpec(memory_space=pl.ANY)
    vmem = pl.BlockSpec(memory_space=pltpu.VMEM)
    dma = pltpu.SemaphoreType.DMA
    return pl.pallas_call(
        pair_kernel,
        out_shape=[
            jax.ShapeDtypeStruct((chips, high, third), bf16),
            jax.ShapeDtypeStruct(far.shape[1:], bf16),
        ],
        in_specs=[vmem, vmem, any_, any_],
        out_specs=[any_, any_],
        scratch_shapes=[
            pltpu.VMEM((2, chips, rows, wide), bf16),
            pltpu.VMEM((chips, rows, wide), bf16),
            pltpu.VMEM((chips, few, g_out.shape[1]), bf16),
            pltpu.VMEM((chips, few, g_out.shape[1]), bf16),
            pltpu.VMEM((chips, high, third), bf16),
            dma((chips,)),
            dma((chips,)),
            dma((chips,)),
            dma((3,)),
            dma((4,)),
        ],
        compiler_params=pltpu.CompilerParams(
            collective_id=3, has_side_effects=True, vmem_limit_bytes=LIMIT
        ),
        cost_estimate=pl.CostEstimate(
            flops=25 * 10**9, bytes_accessed=30 * 10**6, transcendentals=0
        ),
        name="pair_sum",
    )(x, d, g_out.reshape(chips, 2, few, g_out.shape[1]), far)


def finish_kernel(
    d_in,
    x_in,
    tok_in,
    gain,
    gain_part,
    grad_hidden_in,
    w_query,
    w_key,
    w_value,
    w_gate,
    far,
    far_got,
    grad_tok,
    gains,
    g_up,
    g_down,
    d,
    x,
    tok,
    grad_hidden,
    sbuf,
    rbuf,
    total,
    wq,
    wk,
    wv,
    wg,
    mine,
    other,
    gain_all,
    gain_line,
    load,
    s_send,
    s_recv,
    f_sems,
    h_send,
    h_recv,
    l_send,
    l_recv,
):
    f32, bf16 = jnp.float32, jnp.bfloat16
    depth, rows, width = x.shape
    s, z = lax.axis_index("seq"), lax.axis_index("mp")
    core = lax.rem(s, 2)
    twin, across = flip(s, 1), flip(z, 2)
    count = lax.axis_size("seq")
    loads = [
        pltpu.make_async_copy(a, b, load.at[i])
        for i, (a, b) in enumerate(
            [(d_in, d), (w_query, wq), (w_key, wk), (w_value, wv), (w_gate, wg), (x_in, x)]
        )
    ]
    late = [
        pltpu.make_async_copy(a, b, load.at[6 + i])
        for i, (a, b) in enumerate([(tok_in, tok), (grad_hidden_in, grad_hidden)])
    ]
    for copy in loads + late:
        copy.start()
    gains[...] = jnp.zeros_like(gains)
    gains[1:2, :] = gain_part[...]
    greet(
        [(z >= 0, twin, across)]
        + [(z != other, s, other) for other in range(depth)]
        + [(s != other, other, z) for other in range(count)]
    )
    near = remote(far.at[1], other, f_sems.at[0], f_sems.at[1], twin, z)
    crossed = remote(far.at[0], other, f_sems.at[0], f_sems.at[1], twin, across)
    straight = remote(far.at[1], mine, f_sems.at[2], f_sems.at[3], s, across)
    edge = (z == 0) | (z == depth - 1)
    inner = jnp.logical_not(edge)
    local = pltpu.make_async_copy(far.at[0], mine, f_sems.at[4])
    to_other = pltpu.make_async_copy(far_got, other, f_sems.at[5])
    to_mine = pltpu.make_async_copy(far_got, mine, f_sems.at[5])

    @pl.when(core == 0)
    def _():
        near.start()
        local.start()

    @pl.when(inner & (core == 0))
    def _():
        to_other.start()

    @pl.when(inner & (core == 1))
    def _():
        to_mine.start()
        crossed.start()
        straight.start()

    for copy in loads:
        copy.wait()
    step = 512
    starts, at_col = [], 0
    for w in (wq, wk, wv, wg):
        starts.append((w, at_col, at_col + w.shape[1]))
        at_col += w.shape[1]

    def term(j, n):
        at = block(rows, j)
        value = None
        for w, a, b in starts:
            one = product_rt(d[at, a:b], w[n : n + step, :])
            value = one if value is None else value + one
        gains[0:1, n : n + step] += jnp.sum(
            value * x[j, :, n : n + step].astype(f32), axis=0, keepdims=True
        )
        return value

    def partial(j):
        for n in range(0, width, step):
            sbuf[j, :, n : n + step] = term(j, n).astype(bf16)

    def plane(to):
        return remote(gain_all.at[s], gain_all.at[s], h_send.at[to], h_recv.at[s], to, z)

    def line(to):
        return remote(gain_line.at[z], gain_line.at[z], l_send.at[to], l_recv.at[z], s, to)

    def others(count, me, act):
        def one(i, _):
            @pl.when(i != me)
            def _():
                act(i)

            return 0

        lax.fori_loop(0, count, one, 0)

    def own():
        for n in range(0, width, step):
            total[:, n : n + step] = term(z, n)
        gains[0:1, :] = gains[0:1, :] / gain[...]
        gain_all[s] = gains[...]
        others(count, s, lambda to: plane(to).start())

    line_scatter(sbuf, rbuf, total, s_send, s_recv, s, z, depth, partial, own)

    def plane_came(i):
        remote(gain_all.at[i], gain_all.at[i], h_send.at[i], h_recv.at[i], twin, z).wait_recv()

    def line_came(i):
        remote(gain_line.at[i], gain_line.at[i], l_send.at[i], l_recv.at[i], s, across).wait_recv()

    others(count, s, plane_came)
    gains[...] = gain_all[0]
    for i in range(1, count):
        gains[...] += gain_all[i]
    gain_line[z] = gains[...]
    others(depth, z, lambda to: line(to).start())

    for copy in late:
        copy.wait()

    def last(here, i):
        unit, inverse = centred(tok[here, :].astype(f32))
        grad_tok[here, :] = (
            grad_hidden[here, :] + norm_rows_back(total[here, :] * gain[...], unit, inverse)
        ).astype(bf16)

    row_loop(rows, 32, last)
    others(depth, z, line_came)
    gains[...] = gain_line[0]
    for i in range(1, depth):
        gains[...] += gain_line[i]
    others(count, s, lambda to: plane(to).wait_send())
    others(depth, z, lambda to: line(to).wait_send())

    @pl.when(core == 0)
    def _():
        near.wait_send()
        local.wait()

    @pl.when(core == 1)
    def _():
        near.wait_recv()

    @pl.when(inner & (core == 0))
    def _():
        to_other.wait()

    @pl.when(edge & (core == 0))
    def _():
        crossed.wait_recv()

    @pl.when(inner & (core == 1))
    def _():
        to_mine.wait()
        crossed.wait_send()
        straight.wait_send()

    @pl.when(edge & (core == 1))
    def _():
        straight.wait_recv()

    high, few = g_up.shape[0], g_down.shape[0]
    third = g_up.shape[1]

    g_up[...] = mine[0:high, :].astype(f32) + other[0:high, :].astype(f32)
    for t in range(g_down.shape[1] // third):
        at = slice(high + t * few, high + (t + 1) * few)
        g_down[:, t * third : (t + 1) * third] = mine[at, :].astype(f32) + other[at, :].astype(f32)


def finish(d, x, tok, gain, gain_part, grad_hidden, w_query, w_key, w_value, w_gate, far, far_got):
    f32, bf16 = jnp.float32, jnp.bfloat16
    depth, rows, width = x.shape
    count = lax.axis_size("seq")
    units = far.shape[2]
    any_ = pl.BlockSpec(memory_space=pl.ANY)
    vmem = pl.BlockSpec(memory_space=pltpu.VMEM)
    dma = pltpu.SemaphoreType.DMA
    return pl.pallas_call(
        finish_kernel,
        out_shape=[
            jax.ShapeDtypeStruct((rows, width), bf16),
            jax.ShapeDtypeStruct((8, width), f32),
            jax.ShapeDtypeStruct((width // count, units), f32),
            jax.ShapeDtypeStruct((units // count, width), f32),
        ],
        in_specs=[any_] * 3 + [vmem] * 2 + [any_] * 7,
        out_specs=[vmem] * 4,
        scratch_shapes=[
            pltpu.VMEM(d.shape, bf16),
            pltpu.VMEM(x.shape, bf16),
            pltpu.VMEM((rows, width), bf16),
            pltpu.VMEM((rows, width), f32),
            pltpu.VMEM((depth, rows, width), bf16),
            pltpu.VMEM((depth + 1, rows, width), bf16),
            pltpu.VMEM((rows, width), f32),
            pltpu.VMEM(w_query.shape, bf16),
            pltpu.VMEM(w_key.shape, bf16),
            pltpu.VMEM(w_value.shape, bf16),
            pltpu.VMEM(w_gate.shape, bf16),
            pltpu.VMEM(far.shape[1:], bf16),
            pltpu.VMEM(far.shape[1:], bf16),
            pltpu.VMEM((count, 8, width), f32),
            pltpu.VMEM((depth, 8, width), f32),
            dma((8,)),
            dma((depth,)),
            dma((depth + 1,)),
            dma((6,)),
            dma((count,)),
            dma((count,)),
            dma((depth,)),
            dma((depth,)),
        ],
        compiler_params=pltpu.CompilerParams(
            collective_id=4, has_side_effects=True, vmem_limit_bytes=LIMIT
        ),
        cost_estimate=pl.CostEstimate(
            flops=110 * 10**9, bytes_accessed=30 * 10**6, transcendentals=0
        ),
        name="finish",
    )(d, x, tok, gain, gain_part, grad_hidden, w_query, w_key, w_value, w_gate, far, far_got)


def unpack_kernel(summed, tok, up, down, query, key, value, gate, out, tok_out, up_out, down_out):
    f32 = jnp.float32
    rows, wide = query.shape
    few, tall = out.shape[0], value.shape[1]
    query[...] = summed[0:rows, 0:wide].astype(f32)
    key[...] = summed[0:rows, wide : 2 * wide].astype(f32)
    value[...] = summed[rows : 2 * rows, :].astype(f32)
    gate[...] = summed[2 * rows : 3 * rows, :].astype(f32)
    for t in range(out.shape[1] // tall):
        at = slice(3 * rows + t * few, 3 * rows + (t + 1) * few)
        out[:, t * tall : (t + 1) * tall] = summed[at, :].astype(f32)
    tok_out[...] = tok[...]
    up_out[...] = up[...]
    down_out[...] = down[...]


def unpack(summed, tok, up, down, wide):
    f32 = jnp.float32
    count = lax.axis_size("seq")
    width, tall = tok.shape[1], summed.shape[1]
    rows, few = width // count, tall // count
    shapes = [(rows, wide)] * 2 + [(rows, tall)] * 2 + [(few, width)]
    return pl.pallas_call(
        unpack_kernel,
        out_shape=[jax.ShapeDtypeStruct(one, f32) for one in shapes]
        + [jax.ShapeDtypeStruct(a.shape, a.dtype) for a in (tok, up, down)],
        compiler_params=pltpu.CompilerParams(vmem_limit_bytes=LIMIT),
        name="unpack",
    )(summed, tok, up, down)


def shards(
    tokens, gain_mix, w_query, w_key, w_value, w_gate, w_out, gain_ffn, w_up, w_down, cotangent
):
    bf16 = jnp.bfloat16
    f32 = jnp.float32
    span_rows = lax.axis_size("mp") * tokens.shape[0]
    local_heads = w_query.shape[1] // DK
    place = lax.axis_index("seq") % SEQ_DEVS
    positions = place * span_rows + jnp.arange(span_rows, dtype=jnp.int32)
    cosine, sine = angles(positions)
    heads = (lax.axis_index("mp") * local_heads).astype(f32) + jnp.arange(local_heads, dtype=f32)
    logs = jnp.log1p(-jnp.exp2(-5.0 - heads))
    steps = jnp.arange(STRETCH, dtype=f32)
    gaps = steps[:, None] - steps[None, :]
    mask = jnp.where(gaps >= 0, jnp.exp(logs[:, None, None] * jnp.maximum(gaps, 0.0)), 0.0)
    q_scale = jnp.exp(logs[:, None] * (steps + 1.0))[:, :, None]
    k_scale = jnp.exp(logs[:, None] * (STRETCH - 1.0 - steps))[:, :, None]
    span_decay = jnp.exp(logs * span_rows)
    decay = jnp.broadcast_to(
        jnp.stack([jnp.exp(logs * STRETCH), span_decay], axis=1)[:, :, None, None],
        (local_heads, 2, 1, DV),
    )
    trig = (cosine[:, 0], sine[:, 0], mask, q_scale, k_scale, decay)
    (
        x_rows,
        q_all,
        k_all,
        v_all,
        gate,
        unit,
        gated,
        inverse,
        weights,
        entering,
        hidden,
        cot_rows,
        far_up,
        far_down,
    ) = attend(
        tokens, gain_mix[None, :], cotangent, w_query, w_key, w_value, w_gate, w_out, w_up, w_down, *trig
    )
    y_keep, y_send, grad_hidden, gain_ffn_part, grad_ffn = feed(
        hidden, gain_ffn[None, :], cotangent, cot_rows, w_up, w_down, far_up, far_down
    )
    far = lax.psum_scatter(
        grad_ffn, "seq", scatter_dimension=0, tiled=False, axis_index_groups=same_core()
    )
    grad_in, grad_out_w, y_got = retract(
        grad_hidden, y_send, w_out, q_all, k_all, v_all, gate, unit, gated, inverse, weights, entering, *trig
    )
    output = (y_keep + y_got.astype(f32)).astype(bf16)
    pairs, far_got = pair_sum(x_rows.reshape(span_rows, -1), grad_in, grad_out_w, far)
    summed = lax.psum_scatter(
        pairs, "seq", scatter_dimension=0, tiled=False, axis_index_groups=same_core()
    )
    grad_in, pairs = lax.optimization_barrier((grad_in, pairs))
    grad_tokens, gains, final_up, final_down = finish(
        grad_in, x_rows, tokens, gain_mix[None, :], gain_ffn_part, grad_hidden, w_query, w_key, w_value, w_gate, far, far_got
    )
    summed, gains = lax.optimization_barrier((summed, gains))
    gain_mix_sum, gain_ffn_sum = gains[0], gains[1]
    (
        final_query,
        final_key,
        final_value,
        final_gate,
        final_out,
        grad_tokens,
        final_up,
        final_down,
    ) = unpack(summed, grad_tokens, final_up, final_down, w_query.shape[1])
    return (
        output,
        grad_tokens,
        gain_mix_sum,
        final_query,
        final_key,
        final_value,
        final_gate,
        final_out,
        gain_ffn_sum,
        final_up,
        final_down,
    )


def solution(mesh):
    return jax.shard_map(
        shards,
        mesh=mesh,
        in_specs=(
            P(("seq", "mp"), None),
            P(),
            P(None, "mp"),
            P(None, "mp"),
            P(None, "mp"),
            P(None, "mp"),
            P("mp", None),
            P(),
            P(None, "mp"),
            P("mp", None),
            P(("seq", "mp"), None),
        ),
        out_specs=(
            P(("seq", "mp"), None),
            P(("seq", "mp"), None),
            P(),
            P("seq", "mp"),
            P("seq", "mp"),
            P("seq", "mp"),
            P("seq", "mp"),
            P(("mp", "seq"), None),
            P(),
            P("seq", "mp"),
            P(("mp", "seq"), None),
        ),
        check_vma=False,
    )
```

```python
import math

import jax
import jax.numpy as jnp
import numpy as np
from jax import lax
from jax.experimental import pallas as pl
from jax.experimental.pallas import tpu as pltpu
from jax.sharding import PartitionSpec as P

DK = 256
DV = 512
STRETCH = 256
SEQ_DEVS = 4


eps = 1e-05


def same_core():
    count = lax.axis_size("seq")
    return [list(range(core, count, 2)) for core in range(2)]


def decay_tables(span_rows, heads):
    half = DK // 2
    f32 = np.float32
    freq = np.exp(f32(-math.log(10000.0)) * np.arange(half, dtype=f32) / f32(half - 1)).astype(f32)
    phase = np.arange(SEQ_DEVS * span_rows, dtype=f32)[:, None] * freq[None, :]
    phase = phase.astype(np.float64)
    logs = np.log1p(-np.exp2(-5.0 - np.arange(heads)))
    steps = np.arange(STRETCH)
    gaps = steps[:, None] - steps[None, :]
    mask = np.where(gaps >= 0, np.exp(logs[:, None, None] * np.maximum(gaps, 0)), 0.0)
    q_scale = np.exp(logs[:, None] * (steps + 1))[:, :, None]
    k_scale = np.exp(logs[:, None] * (STRETCH - 1 - steps))[:, :, None]
    decay = np.exp(logs[:, None] * np.array([STRETCH, span_rows]))[:, :, None, None]
    decay = np.broadcast_to(decay, (heads, 2, 1, DV))
    return tuple(
        jnp.asarray(a.astype(f32))
        for a in (np.cos(phase), np.sin(phase), mask, q_scale, k_scale, decay)
    )


def product_t(left, right):
    return lax.dot_general(
        left, right, (((0,), (0,)), ((), ())), preferred_element_type=jnp.float32
    )


def product_rt(left, right):
    return lax.dot_general(
        left, right, (((1,), (1,)), ((), ())), preferred_element_type=jnp.float32
    )


MESH = pl.DeviceIdType.MESH
LIMIT = 62 * 1024 * 1024


def remote(src, dst, send, recv, s, z):
    return pltpu.make_async_remote_copy(
        src_ref=src,
        dst_ref=dst,
        send_sem=send,
        recv_sem=recv,
        device_id=(s, z),
        device_id_type=MESH,
    )


def greet(partners):
    barrier = pltpu.get_barrier_semaphore()
    count = 0
    for present, s, z in partners:

        @pl.when(present)
        def _():
            pl.semaphore_signal(barrier, inc=1, device_id=(s, z), device_id_type=MESH)

        count = count + jnp.where(present, 1, 0)
    pl.semaphore_wait(barrier, count)


def dot(left, right):
    return jnp.dot(left, right, preferred_element_type=jnp.float32)


def line_push(x, send, recv, s, z, slot, way):
    return remote(x.at[slot], x.at[slot], send.at[way, slot], recv.at[slot], s, z + 1 - 2 * way)


def line_gather(x, send, recv, s, z, depth, use, after=None):
    @pl.when(z < depth - 1)
    def _():
        line_push(x, send, recv, s, z, z, 0).start()

    @pl.when(z > 0)
    def _():
        line_push(x, send, recv, s, z, z, 1).start()

    def one(turn, _):
        away = (turn + 1) // 2
        left, right = z - away, z + away

        @pl.when((turn % 2 == 1) & (left >= 0))
        def _():
            remote(x.at[left], x.at[left], send.at[0, left], recv.at[left], s, z - 1).wait_recv()

            @pl.when(z < depth - 1)
            def _():
                line_push(x, send, recv, s, z, left, 0).start()

        @pl.when((turn % 2 == 1) & (right < depth))
        def _():
            remote(x.at[right], x.at[right], send.at[1, right], recv.at[right], s, z + 1).wait_recv()

            @pl.when(z > 0)
            def _():
                line_push(x, send, recv, s, z, right, 1).start()

        if after is not None:
            after(turn)
        slot = jnp.where(turn % 2 == 1, left, right)

        @pl.when((slot >= 0) & (slot < depth))
        def _():
            use(slot)

        return 0

    lax.fori_loop(0, 2 * depth - 1, one, 0)


def line_gather_end(x, send, recv, s, z, depth):
    def one(slot, _):
        @pl.when((slot <= z) & (z < depth - 1))
        def _():
            line_push(x, send, recv, s, z, slot, 0).wait_send()

        @pl.when((slot >= z) & (z > 0))
        def _():
            line_push(x, send, recv, s, z, slot, 1).wait_send()

        return 0

    lax.fori_loop(0, depth, one, 0)


def add_rows(into, other):
    step = 32

    def one(i, _):
        rows = pl.ds(pl.multiple_of(i * step, step), step)
        into[rows, :] = (
            into[rows, :].astype(jnp.float32) + other[rows, :].astype(jnp.float32)
        ).astype(into.dtype)
        return 0

    lax.fori_loop(0, into.shape[0] // step, one, 0)


def line_scatter(sbuf, rbuf, total, send, recv, s, z, depth, partial, own, hook=None):
    def right(j):
        return remote(sbuf.at[j], rbuf.at[j], send.at[j], recv.at[j], s, z + 1)

    def left(j):
        slot = jnp.where(j == z - 1, depth, j)
        return remote(sbuf.at[j], rbuf.at[slot], send.at[j], recv.at[slot], s, z - 1)

    def arrived(slot, sender):
        remote(sbuf.at[0], rbuf.at[slot], send.at[0], recv.at[slot], s, sender).wait_recv()

    def first(turn, _):
        up = depth - 1 + z - turn // 2
        down = turn // 2 - (depth - 1) + z
        j = jnp.where(turn % 2 == 0, up, down)
        valid = jnp.where(turn % 2 == 0, (up > z) & (up < depth), (down >= 0) & (down < z))

        @pl.when(valid)
        def _():
            partial(j)

            @pl.when((z == 0) & (j > z))
            def _():
                right(j).start()

            @pl.when((z == depth - 1) & (j < z))
            def _():
                left(j).start()

        return 0

    lax.fori_loop(0, 2 * (depth - 1), first, 0)
    own()

    def event(turn, _):
        up = depth - 1 + z - turn
        down = turn - (depth - 1) + z

        @pl.when((z > 0) & (up >= z) & (up < depth))
        def _():
            arrived(up, z - 1)

            @pl.when(up > z)
            def _():
                add_rows(sbuf.at[up], rbuf.at[up])
                right(up).start()

            @pl.when(up == z)
            def _():
                add_rows(total, rbuf.at[up])

        @pl.when((z < depth - 1) & (down >= 0) & (down <= z))
        def _():
            slot = jnp.where(down == z, depth, down)
            arrived(slot, z + 1)

            @pl.when(down < z)
            def _():
                add_rows(sbuf.at[down], rbuf.at[down])
                left(down).start()

            @pl.when(down == z)
            def _():
                add_rows(total, rbuf.at[depth])

        if hook is not None:
            hook(turn)
        return 0

    lax.fori_loop(0, depth, event, 0)

    def end(j, _):
        @pl.when(j > z)
        def _():
            right(j).wait_send()

        @pl.when(j < z)
        def _():
            left(j).wait_send()

        return 0

    lax.fori_loop(0, depth, end, 0)


def centred(rows):
    centre = rows - jnp.mean(rows, axis=-1, keepdims=True)
    inverse = lax.rsqrt(jnp.mean(centre * centre, axis=-1, keepdims=True) + eps)
    return centre * inverse, inverse


def block(rows, index):
    return pl.ds(pl.multiple_of(index * rows, rows), rows)


def attend_kernel(
    tok,
    gain,
    cot,
    w_query,
    w_key,
    w_value,
    w_gate,
    w_out,
    w_up,
    w_down,
    cosine_all,
    sine_all,
    mask_all,
    q_scale_all,
    k_scale_all,
    decay_all,
    x_out,
    q_out,
    k_out,
    v_out,
    gp_out,
    gn_out,
    gated_out,
    inv_out,
    p_out,
    r_out,
    hidden_out,
    cot_rows,
    far_up,
    far_down,
    cosine,
    sine,
    mask,
    q_scale,
    k_scale,
    decay,
    xg,
    q,
    k,
    v,
    gp,
    gn,
    gated,
    inv,
    weights,
    grown,
    entering,
    tile,
    state,
    state_in,
    state_to,
    rbuf,
    total,
    wq,
    wk,
    wv,
    wg,
    wo,
    load,
    save,
    g_send,
    g_recv,
    s_send,
    s_recv,
    c_send,
    c_recv,
    x_send,
    x_recv,
    f_send,
    f_recv,
    p_send,
    p_recv,
):
    f32, bf16 = jnp.float32, jnp.bfloat16
    depth = xg.shape[0]
    rows = xg.shape[1]
    heads = mask.shape[0]
    s, z = lax.axis_index("seq"), lax.axis_index("mp")
    place = lax.rem(s, SEQ_DEVS)
    pair = z + 1 - 2 * lax.rem(z, 2)
    twin = s + 1 - 2 * lax.rem(s, 2)
    def tables(place, z):
        at = block(cosine.shape[0], place)
        some = pl.ds(z * heads, heads)
        return [
            (cosine_all.at[at], cosine),
            (sine_all.at[at], sine),
            (mask_all.at[some], mask),
            (q_scale_all.at[some], q_scale),
            (k_scale_all.at[some], k_scale),
            (decay_all.at[some], decay),
        ]

    loads = [
        pltpu.make_async_copy(a, b, load.at[i])
        for i, (a, b) in enumerate(
            [(w_query, wq), (w_key, wk), (w_value, wv), (w_gate, wg), (w_out, wo)]
            + tables(place, z)
        )
    ]
    for copy in loads:
        copy.start()

    def norm(i, _):
        part = pl.ds(pl.multiple_of(i * 32, 32), 32)
        unit, _ = centred(tok[part, :].astype(f32))
        xg[z, part, :] = (unit * gain[...]).astype(bf16)
        return 0

    lax.fori_loop(0, rows // 32, norm, 0)
    count = lax.axis_size("seq")
    across = flip(z, 2)
    greet(
        [(z > 0, s, z - 1), (z < depth - 1, s, z + 1), (z >= 0, s, across)]
        + [(s != other, other, z) for other in range(count)]
    )
    tall, few = w_up.shape[0] // count, w_down.shape[0] // count
    mine = pltpu.make_async_copy(cot, cot_rows.at[0], x_send.at[3])
    near = remote(cot, cot_rows.at[2], x_send.at[1], x_recv.at[1], twin, z)
    swap = remote(cot, cot_rows.at[1], x_send.at[0], x_recv.at[0], s, pair)
    far = remote(cot_rows.at[1], cot_rows.at[3], x_send.at[2], x_recv.at[2], twin, z)

    def piece(source):
        return block(tall, source), block(few, source)

    up_at, down_at = piece(s)
    moves = [
        remote(w_up.at[up_at], far_up.at[up_at], f_send.at[0], f_recv.at[0], s, across),
        remote(w_down.at[down_at], far_down.at[down_at], f_send.at[1], f_recv.at[1], s, across),
    ]
    edge = (z == 0) | (z == depth - 1)

    def spread(source, chip):
        up_, down_ = piece(source)
        to = 2 * chip + 1
        return [
            remote(far_up.at[up_], far_up.at[up_], p_send.at[0, chip], p_recv.at[0, source], to, z),
            remote(
                far_down.at[down_], far_down.at[down_], p_send.at[1, chip], p_recv.at[1, source], to, z
            ),
        ]

    mine.start()
    near.start()

    @pl.when(place == 0)
    def _():
        state_in[...] = jnp.zeros_like(state_in)

    def after(turn):
        @pl.when(edge & (turn == 1))
        def _():
            swap.start()

        @pl.when(edge & (turn == 3))
        def _():
            for copy in moves:
                copy.start()

    def use(j):
        at = block(rows, j)

        @pl.when(j == z)
        def _():
            for copy in loads:
                copy.wait()

        rotated(j, wk, k)
        for h in range(heads):
            cols = slice(h * DK, (h + 1) * DK)
            wide = slice(h * DV, (h + 1) * DV)
            v[at, wide] = dot(xg[j], wv[:, wide]).astype(bf16)
            vd = (v[at, wide].astype(f32) * k_scale[h]).astype(bf16)
            grown[h, j] = product_t(k[at, cols], vd)

        @pl.when(j != last)
        def _():
            rest(j)

    last = jnp.where(z < depth // 2, depth - 1, 0)

    def rotated(j, w, out):
        at = block(rows, j)
        c, sn = cosine[at, :], sine[at, :]
        for h in range(heads):
            p = dot(xg[j], w[:, h * DK : (h + 1) * DK])
            a, b = p[:, : DK // 2], p[:, DK // 2 :]
            out[at, h * DK : h * DK + DK // 2] = (a * c - b * sn).astype(bf16)
            out[at, h * DK + DK // 2 : (h + 1) * DK] = (b * c + a * sn).astype(bf16)

    def rest(j):
        at = block(rows, j)
        rotated(j, wq, q)
        for h in range(heads):
            cols = slice(h * DK, (h + 1) * DK)
            wide = slice(h * DV, (h + 1) * DV)
            gp[at, wide] = dot(xg[j], wg[:, wide])
            weights[h, j] = (product_rt(q[at, cols], k[at, cols]) * mask[h]).astype(bf16)

    line_gather(xg, g_send, g_recv, s, z, depth, use, after)
    def chain(h, to):
        return remote(state_to.at[h], state_in.at[h], c_send.at[h], c_recv.at[h], to, z)

    for h in range(heads):
        state[h] = grown[h, 0]
        for b in range(1, depth):
            state[h] = decay[h, 0] * state[h] + grown[h, b]

        @pl.when(place == 0)
        def _():
            state_to[h] = state[h].astype(bf16)
            chain(h, s + 1).start()

    rest(last)

    @pl.when(place > 0)
    def _():
        for h in range(heads):
            chain(h, s - 1).wait_recv()

            @pl.when(place < SEQ_DEVS - 1)
            def _():
                state_to[h] = (decay[h, 1] * state_in[h].astype(f32) + state[h]).astype(bf16)
                chain(h, s + 1).start()

    saves = [
        pltpu.make_async_copy(a, b, save.at[i])
        for i, (a, b) in enumerate(
            [
                (xg, x_out),
                (q, q_out),
                (k, k_out),
                (v, v_out),
                (gp, gp_out),
                (weights, p_out),
                (entering, r_out),
                (gn, gn_out),
                (gated, gated_out),
                (inv, inv_out),
            ]
        )
    ]
    for copy in saves[:6]:
        copy.start()

    def hand_out():
        for copy in moves:
            copy.wait_recv()

        def to_chip(chip, _):
            @pl.when(2 * chip + 1 != s)
            def _():
                for copy in spread(s, chip):
                    copy.start()

            return 0

        lax.fori_loop(0, count // 2, to_chip, 0)

    for h in range(heads):
        cols = slice(h * DK, (h + 1) * DK)
        wide = slice(h * DV, (h + 1) * DV)
        state[h] = state_in[h].astype(f32)

        def cross(b, _):
            at = block(rows, b)
            entering[h, b] = state[h].astype(bf16)
            state[h] = decay[h, 0] * state[h] + grown[h, b]
            qd = (q[at, cols].astype(f32) * q_scale[h]).astype(bf16)
            tile[...] = dot(weights[h, b], v[at, wide]) + dot(qd, entering[h, b])

            def norm(i, _):
                here = block(32, i)
                there = pl.ds(pl.multiple_of(b * rows + i * 32, 32), 32)
                unit, inverse = centred(tile[here, :])
                gate = gp[there, wide]
                gn[there, wide] = unit
                gated[there, wide] = (unit * gate / (1.0 + jnp.exp(-gate))).astype(bf16)
                inv[h, there, :] = jnp.broadcast_to(inverse, (32, inv.shape[2]))
                return 0

            lax.fori_loop(0, rows // 32, norm, 0)
            return 0

        lax.fori_loop(0, depth, cross, 0)
    for copy in saves[6:]:
        copy.start()
    line_gather_end(xg, g_send, g_recv, s, z, depth)

    @pl.when(jnp.logical_not(edge))
    def _():
        hand_out()

    saves[0].wait()
    wide = 512

    def hook(turn):
        @pl.when((turn == 0) & jnp.logical_not(edge))
        def _():
            for copy in moves:
                copy.start()
            swap.start()

        @pl.when((turn == 0) & edge)
        def _():
            hand_out()

        @pl.when(turn == 2)
        def _():
            swap.wait_recv()
            far.start()

    def partial(j):
        for n in range(0, total.shape[1], wide):
            xg[j, :, n : n + wide] = dot(gated[block(rows, j), :], wo[:, n : n + wide]).astype(bf16)

    def own():
        for n in range(0, total.shape[1], wide):
            total[:, n : n + wide] = tok[:, n : n + wide].astype(f32) + dot(
                gated[block(rows, z), :], wo[:, n : n + wide]
            )

    line_scatter(xg, rbuf, total, s_send, s_recv, s, z, depth, partial, own, hook)
    done = pltpu.make_async_copy(total, hidden_out, save.at[0])
    done.start()

    @pl.when(place < SEQ_DEVS - 1)
    def _():
        for h in range(heads):
            chain(h, s + 1).wait_send()

    def sent(chip, _):
        @pl.when(2 * chip + 1 != s)
        def _():
            for copy in spread(s, chip):
                copy.wait_send()

        return 0

    lax.fori_loop(0, count // 2, sent, 0)

    def came(source, _):
        @pl.when((source != s) & (lax.rem(s, 2) == 1))
        def _():
            for copy in spread(source, 0):
                copy.wait_recv()

        return 0

    lax.fori_loop(0, count, came, 0)
    for copy in moves:
        copy.wait_send()
    swap.wait_send()
    near.wait()
    far.wait()
    mine.wait()
    for copy in saves[1:]:
        copy.wait()
    done.wait()


def attend(
    tok, gain, cot, w_query, w_key, w_value, w_gate, w_out, w_up, w_down, cosine, sine, mask, q_scale, k_scale, decay
):
    f32, bf16 = jnp.float32, jnp.bfloat16
    depth = lax.axis_size("mp")
    rows, width = tok.shape
    span = depth * rows
    heads = w_query.shape[1] // DK
    hk, hv = w_query.shape[1], w_value.shape[1]
    any_ = pl.BlockSpec(memory_space=pl.ANY)
    vmem = pl.BlockSpec(memory_space=pltpu.VMEM)
    shapes = [
        ((depth, rows, width), bf16),
        ((span, hk), bf16),
        ((span, hk), bf16),
        ((span, hv), bf16),
        ((span, hv), f32),
        ((span, hv), f32),
        ((span, hv), bf16),
        ((heads, span, 128), f32),
        ((heads, depth, rows, rows), bf16),
        ((heads, depth, DK, DV), bf16),
        ((rows, width), f32),
        ((4, rows, width), bf16),
        (w_up.shape, bf16),
        (w_down.shape, bf16),
    ]
    count = lax.axis_size("seq")
    dma = pltpu.SemaphoreType.DMA
    return pl.pallas_call(
        attend_kernel,
        out_shape=[jax.ShapeDtypeStruct(*one) for one in shapes],
        in_specs=[vmem, vmem, any_] + [any_] * 13,
        out_specs=[any_] * len(shapes),
        scratch_shapes=[
            pltpu.VMEM((span, DK // 2), f32),
            pltpu.VMEM((span, DK // 2), f32),
            pltpu.VMEM((heads, rows, rows), f32),
            pltpu.VMEM((heads, rows, 1), f32),
            pltpu.VMEM((heads, rows, 1), f32),
            pltpu.VMEM((heads, 2, 1, DV), f32),
            pltpu.VMEM((depth, rows, width), bf16),
            pltpu.VMEM((span, hk), bf16),
            pltpu.VMEM((span, hk), bf16),
            pltpu.VMEM((span, hv), bf16),
            pltpu.VMEM((span, hv), f32),
            pltpu.VMEM((span, hv), f32),
            pltpu.VMEM((span, hv), bf16),
            pltpu.VMEM((heads, span, 128), f32),
            pltpu.VMEM((heads, depth, rows, rows), bf16),
            pltpu.VMEM((heads, depth, DK, DV), f32),
            pltpu.VMEM((heads, depth, DK, DV), bf16),
            pltpu.VMEM((rows, DV), f32),
            pltpu.VMEM((heads, DK, DV), f32),
            pltpu.VMEM((heads, DK, DV), bf16),
            pltpu.VMEM((heads, DK, DV), bf16),
            pltpu.VMEM((depth + 1, rows, width), bf16),
            pltpu.VMEM((rows, width), f32),
            pltpu.VMEM(w_query.shape, bf16),
            pltpu.VMEM(w_key.shape, bf16),
            pltpu.VMEM(w_value.shape, bf16),
            pltpu.VMEM(w_gate.shape, bf16),
            pltpu.VMEM(w_out.shape, bf16),
            dma((11,)),
            dma((10,)),
            dma((2, depth)),
            dma((depth,)),
            dma((depth,)),
            dma((depth + 1,)),
            dma((heads,)),
            dma((heads,)),
            dma((4,)),
            dma((3,)),
            dma((2,)),
            dma((2,)),
            dma((2, count // 2)),
            dma((2, count)),
        ],
        compiler_params=pltpu.CompilerParams(
            collective_id=0, has_side_effects=True, vmem_limit_bytes=LIMIT
        ),
        cost_estimate=pl.CostEstimate(
            flops=190 * 10**9, bytes_accessed=60 * 10**6, transcendentals=2 * 10**6
        ),
        name="attend",
    )(tok, gain, cot, w_query, w_key, w_value, w_gate, w_out, w_up, w_down, cosine, sine, mask, q_scale, k_scale, decay)


def row_loop(rows, step, body):
    def one(i, _):
        body(pl.ds(pl.multiple_of(i * step, step), step), i)
        return 0

    lax.fori_loop(0, rows // step, one, 0)


def norm_rows_back(grad_hat, unit, inverse):
    first = jnp.mean(grad_hat, axis=-1, keepdims=True)
    second = jnp.mean(grad_hat * unit, axis=-1, keepdims=True)
    return inverse * (grad_hat - first - unit * second)


def feed_kernel(
    hidden,
    gain,
    cot,
    cot_rows,
    w_up,
    w_down,
    far_up,
    far_down,
    y_keep,
    y_send,
    grad_hidden,
    gain_part,
    g_all_out,
    x,
    dy,
    act,
    du,
    part_y,
    part_x,
    got_x,
    got_own,
    got_y,
    u_tile,
    d_tile,
    g_all,
    up,
    down,
    load,
    save,
    send,
    recv,
):
    f32, bf16 = jnp.float32, jnp.bfloat16
    rows, width = hidden.shape
    units = up.shape[1]
    half = rows // 2
    s, z = lax.axis_index("seq"), lax.axis_index("mp")
    pair = z + 1 - 2 * lax.rem(z, 2)
    twin = s + 1 - 2 * lax.rem(s, 2)
    own_loads = [
        pltpu.make_async_copy(w_up, up, load.at[0]),
        pltpu.make_async_copy(w_down, down, load.at[1]),
    ]
    far_loads = [
        pltpu.make_async_copy(far_up, up, load.at[0]),
        pltpu.make_async_copy(far_down, down, load.at[1]),
    ]

    @pl.when(lax.rem(s, 2) == 0)
    def _():
        for copy in own_loads:
            copy.start()

    @pl.when(lax.rem(s, 2) == 1)
    def _():
        for copy in far_loads:
            copy.start()

    rest = [
        pltpu.make_async_copy(cot_rows.at[a, pl.ds(at, n)], dy.at[pl.ds(to, n)], load.at[2 + i])
        for i, (a, at, n, to) in enumerate(
            [
                (0, 0, rows, 0),
                (2, 0, rows, rows),
                (1, 0, half, 2 * rows),
                (3, 0, half, 2 * rows + half),
                (1, half, half, 3 * rows),
                (3, half, half, 3 * rows + half),
            ]
        )
    ]
    loads = own_loads + rest
    for copy in rest:
        copy.start()

    def norm(here, i):
        unit, _ = centred(hidden[here, :])
        x[here, :] = (unit * gain[...]).astype(bf16)

    row_loop(rows, 32, norm)
    greet([(z >= 0, s, pair), (z >= 0, twin, z)])
    mine, theirs = pl.ds(0, rows), pl.ds(rows, rows)
    parts = [pl.ds(0, half), pl.ds(half, half)]
    pairs = [pl.ds(2 * rows, half), pl.ds(3 * rows, half)]
    twins = [pl.ds(2 * rows + half, half), pl.ds(3 * rows + half, half)]
    near = remote(x.at[mine], x.at[theirs], send.at[0], recv.at[0], twin, z)
    over, far, back_far, back_over, y_far = [], [], [], [], []
    for i in range(2):
        k = 1 + 5 * i
        over.append(remote(x.at[parts[i]], x.at[pairs[i]], send.at[k], recv.at[k], s, pair))
        far.append(remote(x.at[pairs[i]], x.at[twins[i]], send.at[k + 1], recv.at[k + 1], twin, z))
        back_far.append(
            remote(part_x.at[twins[i]], got_x.at[i], send.at[k + 2], recv.at[k + 2], twin, z)
        )
        back_over.append(
            remote(part_x.at[pairs[i]], got_x.at[2 + i], send.at[k + 3], recv.at[k + 3], s, pair)
        )
        y_far.append(
            remote(
                part_y.at[twins[i]], got_y.at[pl.ds(rows + i * half, half)], send.at[k + 4],
                recv.at[k + 4], twin, z,
            )
        )
    back_near = remote(part_x.at[theirs], got_own, send.at[11], recv.at[11], twin, z)
    y_near = remote(part_y.at[theirs], got_y.at[mine], send.at[12], recv.at[12], twin, z)
    over[0].start()
    near.start()
    over[1].start()
    for copy in loads:
        copy.wait()
    step = 512

    def y_terms(r):
        at = block(rows, r)
        for n in range(0, width, step):
            part_y[at, n : n + step] = dot(act[at, :], down[:, n : n + step]).astype(bf16)

    def return_pair(i):
        back_far[i].wait_recv()
        add_rows(part_x.at[pairs[i]], got_x.at[i])
        back_over[i].start()

    def one(r, _):
        at = block(rows, r)

        @pl.when(r == 1)
        def _():
            near.wait_recv()

        @pl.when(r == 2)
        def _():
            over[0].wait_recv()
            far[0].start()
            far[0].wait_recv()

        @pl.when(r == 3)
        def _():
            return_pair(0)
            lax.fori_loop(0, 2, lambda i, c: (y_terms(i), c)[1], 0)
            over[1].wait_recv()
            far[1].start()
            far[1].wait_recv()

        for n in range(0, units, step):
            cols = slice(n, n + step)
            u_tile[...] = dot(x[at, :], up[:, cols])
            d_tile[...] = product_rt(dy[at, :], down[cols, :])

            def gelu(here, i):
                there = pl.ds(pl.multiple_of(r * rows + i * 32, 32), 32)
                u = u_tile[here, :]
                normal = 0.5 * (1.0 + lax.erf(u * (2.0**-0.5)))
                slope = normal + u * (jnp.exp(-0.5 * u * u) * ((2.0 * math.pi) ** -0.5))
                act[there, cols] = (u * normal).astype(bf16)
                du[there, cols] = (d_tile[here, :] * slope).astype(bf16)

            row_loop(rows, 32, gelu)
        for n in range(0, width, step):
            part_x[at, n : n + step] = product_rt(du[at, :], up[n : n + step, :]).astype(bf16)

        @pl.when(r == 1)
        def _():
            back_near.start()

        @pl.when(r == 2)
        def _():
            back_far[0].start()

        @pl.when(r == 3)
        def _():
            back_far[1].start()

        return 0

    lax.fori_loop(0, 4, one, 0)
    return_pair(1)
    lax.fori_loop(2, 4, lambda i, c: (y_terms(i), c)[1], 0)
    y_near.start()
    for copy in y_far:
        copy.start()
    chips, _, high, _ = g_all.shape
    few = units // (2 * chips)
    tall = width // (2 * chips)

    def up_terms(m, _):
        cols = pl.ds(pl.multiple_of(m * 256, 256), 256)
        value = product_t(x[:, cols], du[...]).astype(bf16)
        for part in range(256 // tall):
            to = m * (256 // tall) + part
            g_all[to // 2, lax.rem(to, 2), 0:tall, :] = value[part * tall : (part + 1) * tall]
        return 0

    lax.fori_loop(0, width // 256, up_terms, 0)

    def down_terms(m, _):
        cols = pl.ds(pl.multiple_of(m * 256, 256), 256)
        for n in range(0, width, units):
            value = product_t(act[:, cols], dy[:, n : n + units]).astype(bf16)
            first = tall + n // units * few
            for part in range(256 // few):
                to = m * (256 // few) + part
                g_all[to // 2, lax.rem(to, 2), first : first + few, :] = value[
                    part * few : (part + 1) * few
                ]
        return 0

    lax.fori_loop(0, units // 256, down_terms, 0)
    saves = [pltpu.make_async_copy(g_all, g_all_out, save.at[0])]
    saves[0].start()
    y_near.wait_recv()
    for copy in y_far:
        copy.wait_recv()

    def y_sum(here, i):
        y_keep[here, :] = (
            hidden[here, :] + part_y[here, :].astype(f32) + got_y[here, :].astype(f32)
        )

    row_loop(rows, 32, y_sum)
    for i in range(2):

        def y_pair(here, j):
            there = pl.ds(pl.multiple_of((2 + i) * rows + j * 32, 32), 32)
            came = pl.ds(pl.multiple_of(rows + i * half + j * 32, 32), 32)
            to = pl.ds(pl.multiple_of(i * half + j * 32, 32), 32)
            y_send[to, :] = (part_y[there, :].astype(f32) + got_y[came, :].astype(f32)).astype(bf16)

        row_loop(half, 32, y_pair)
    back_near.wait_recv()
    gain_part[...] = jnp.zeros_like(gain_part)
    for i in range(2):
        back_over[i].wait_recv()

        def finish(here, j):
            at = pl.ds(pl.multiple_of(i * half + j * 32, 32), 32)
            unit, inverse = centred(hidden[at, :])
            grad = (part_x[at, :].astype(f32) + got_own[at, :].astype(f32)) + got_x[
                2 + i, here, :
            ].astype(f32)
            gain_part[...] += jnp.sum(grad * unit, axis=0, keepdims=True)
            grad_hidden[at, :] = cot[at, :].astype(f32) + norm_rows_back(
                grad * gain[...], unit, inverse
            )

        row_loop(half, 32, finish)
    for copy in [near, back_near, y_near] + over + far + back_far + back_over + y_far:
        copy.wait_send()
    for copy in saves:
        copy.wait()


def feed(hidden, gain, cot, cot_rows, w_up, w_down, far_up, far_down):
    f32, bf16 = jnp.float32, jnp.bfloat16
    rows, width = hidden.shape
    units = w_up.shape[1]
    count = lax.axis_size("seq")
    gathered = (count // 2, 2, width // count + width // count, units)
    any_ = pl.BlockSpec(memory_space=pl.ANY)
    vmem = pl.BlockSpec(memory_space=pltpu.VMEM)
    dma = pltpu.SemaphoreType.DMA
    return pl.pallas_call(
        feed_kernel,
        out_shape=[
            jax.ShapeDtypeStruct((rows, width), f32),
            jax.ShapeDtypeStruct((rows, width), bf16),
            jax.ShapeDtypeStruct((rows, width), f32),
            jax.ShapeDtypeStruct((1, width), f32),
            jax.ShapeDtypeStruct(gathered, bf16),
        ],
        in_specs=[vmem, vmem, vmem] + [any_] * 5,
        out_specs=[vmem] * 4 + [any_],
        scratch_shapes=[
            pltpu.VMEM((4 * rows, width), bf16),
            pltpu.VMEM((4 * rows, width), bf16),
            pltpu.VMEM((4 * rows, units), bf16),
            pltpu.VMEM((4 * rows, units), bf16),
            pltpu.VMEM((4 * rows, width), bf16),
            pltpu.VMEM((4 * rows, width), bf16),
            pltpu.VMEM((4, rows // 2, width), bf16),
            pltpu.VMEM((rows, width), bf16),
            pltpu.VMEM((2 * rows, width), bf16),
            pltpu.VMEM((rows, 512), f32),
            pltpu.VMEM((rows, 512), f32),
            pltpu.VMEM(gathered, bf16),
            pltpu.VMEM(w_up.shape, bf16),
            pltpu.VMEM(w_down.shape, bf16),
            dma((8,)),
            dma((1,)),
            dma((13,)),
            dma((13,)),
        ],
        compiler_params=pltpu.CompilerParams(
            collective_id=1, has_side_effects=True, vmem_limit_bytes=LIMIT
        ),
        cost_estimate=pl.CostEstimate(
            flops=75 * 10**9, bytes_accessed=30 * 10**6, transcendentals=2 * 10**6
        ),
        name="feed",
    )(hidden, gain, cot, cot_rows, w_up, w_down, far_up, far_down)


def retract_kernel(
    grad_hidden,
    y_send,
    w_out,
    q_in,
    k_in,
    v_in,
    gp_in,
    gn_in,
    gated_in,
    inv_in,
    p_in,
    r_in,
    cosine_all,
    sine_all,
    mask_all,
    q_scale_all,
    k_scale_all,
    decay_all,
    d_out,
    g_out,
    y_got,
    cosine,
    sine,
    mask,
    q_scale,
    k_scale,
    decay,
    dx,
    q,
    k,
    v,
    gp,
    gn,
    gated,
    inv,
    weights,
    entering,
    wo,
    dall,
    do,
    do_low,
    tile,
    grown,
    dk,
    dv,
    state,
    state_in,
    state_to,
    g_wo,
    load,
    save,
    save_rows,
    g_send,
    g_recv,
    c_send,
    c_recv,
    y_sems,
):
    f32, bf16 = jnp.float32, jnp.bfloat16
    depth, rows, width = dx.shape
    heads = mask.shape[0]
    hk, hv = q.shape[1], v.shape[1]
    s, z = lax.axis_index("seq"), lax.axis_index("mp")
    place = lax.rem(s, SEQ_DEVS)
    pair = z + 1 - 2 * lax.rem(z, 2)
    def tables(place, z):
        at = block(cosine.shape[0], place)
        some = pl.ds(z * heads, heads)
        return [
            (cosine_all.at[at], cosine),
            (sine_all.at[at], sine),
            (mask_all.at[some], mask),
            (q_scale_all.at[some], q_scale),
            (k_scale_all.at[some], k_scale),
            (decay_all.at[some], decay),
        ]

    loads = [
        pltpu.make_async_copy(a, b, load.at[i])
        for i, (a, b) in enumerate(
            [
                (w_out, wo),
                (q_in, q),
                (k_in, k),
                (v_in, v),
                (gp_in, gp),
                (gn_in, gn),
                (gated_in, gated),
                (inv_in, inv),
                (p_in, weights),
                (r_in, entering),
            ]
            + tables(place, z)
        )
    ]
    for copy in loads:
        copy.start()

    def low(here, i):
        dx[z, here, :] = grad_hidden[here, :].astype(bf16)

    row_loop(rows, 32, low)
    greet(
        [
            (z > 0, s, z - 1),
            (z < depth - 1, s, z + 1),
            (place > 0, s - 1, z),
            (place < SEQ_DEVS - 1, s + 1, z),
        ]
    )

    @pl.when(place == SEQ_DEVS - 1)
    def _():
        state_in[...] = jnp.zeros_like(state_in)

    def turn_back(value, at, start):
        c, sn = cosine[at, :], sine[at, :]
        half = DK // 2
        a, b = value[:, :half], value[:, half:]
        dall[at, start : start + half] = (a * c + b * sn).astype(bf16)
        dall[at, start + half : start + DK] = (b * c - a * sn).astype(bf16)

    def use(j):
        at = block(rows, j)

        @pl.when(j == z)
        def _():
            for copy in loads:
                copy.wait()

        for h in range(heads):
            wide = slice(h * DV, (h + 1) * DV)
            tile[...] = product_rt(dx[j], wo[wide, :])

            def gate_back(here, i):
                there = pl.ds(pl.multiple_of(j * rows + i * 32, 32), 32)
                grad = tile[here, :]
                gate = gp[there, wide]
                unit = gn[there, wide]
                open_ = 1.0 / (1.0 + jnp.exp(-gate))
                slope = open_ * (1.0 + gate * (1.0 - open_))
                first = 2 * hk + hv + h * DV
                dall[there, first : first + DV] = (grad * unit * slope).astype(bf16)
                inverse = inv[h, there, :][:, :1]
                value = norm_rows_back(grad * gate * open_, unit, inverse)
                high = value.astype(bf16)
                do[there, wide] = high
                do_low[here, wide] = (value - high.astype(f32)).astype(bf16)

            row_loop(rows, 32, gate_back)
        for h in range(heads):
            cols = slice(h * DK, (h + 1) * DK)
            wide = slice(h * DV, (h + 1) * DV)
            qd = (q[at, cols].astype(f32) * q_scale[h]).astype(bf16)
            grown[h, j] = product_t(qd, do[at, wide])

        @pl.when(j != last)
        def _():
            rest(j)

    last = jnp.where(z < depth // 2, depth - 1, 0)

    def rest(j):
        at = block(rows, j)
        for h in range(heads):
            cols = slice(h * DK, (h + 1) * DK)
            wide = slice(h * DV, (h + 1) * DV)
            qb, kb, vb, db = q[at, cols], k[at, cols], v[at, wide], do[at, wide]
            raw = product_rt(db, vb) + product_rt(do_low[:, wide], vb)
            ds = (raw * mask[h]).astype(bf16)
            dv[at, wide] = product_t(weights[h, j], db)
            dk[at, cols] = product_t(ds, qb)
            turn_back(dot(ds, kb) + q_scale[h] * product_rt(db, entering[h, j]), at, h * DK)

    def chain(h, to):
        return remote(state_to.at[h], state_in.at[h], c_send.at[h], c_recv.at[h], to, z)

    line_gather(dx, g_send, g_recv, s, z, depth, use)
    swap = remote(y_send, y_got, y_sems.at[0], y_sems.at[1], s, pair)
    swap.start()
    def out_terms(m, _):
        cols = pl.ds(pl.multiple_of(m * 256, 256), 256)
        for n in range(0, width, 512):
            right = dx[:, :, n : n + 512].reshape(depth * rows, 512)
            g_wo[cols, n : n + 512] = product_t(gated[:, cols], right).astype(bf16)
        return 0

    def out_grad():
        lax.fori_loop(0, hv // 256, out_terms, 0)

    for h in range(heads):
        state[h] = grown[h, depth - 1]
        for b in reversed(range(depth - 1)):
            state[h] = decay[h, 0] * state[h] + grown[h, b]

        @pl.when(place == SEQ_DEVS - 1)
        def _():
            state_to[h] = state[h].astype(bf16)
            chain(h, s - 1).start()

    rest(last)

    @pl.when(place == 0)
    def _():
        out_grad()

    for h in range(heads):

        @pl.when(place < SEQ_DEVS - 1)
        def _():
            chain(h, s + 1).wait_recv()

        @pl.when((place > 0) & (place < SEQ_DEVS - 1))
        def _():
            state_to[h] = (decay[h, 1] * state_in[h].astype(f32) + state[h]).astype(bf16)
            chain(h, s - 1).start()

    for h in range(heads):
        state[h] = state_in[h].astype(f32)

    def done(b):
        at = block(rows, b)
        return pltpu.make_async_copy(dall.at[at], d_out.at[at], save_rows.at[b])

    def cross(turn, _):
        b = depth - 1 - turn
        at = block(rows, b)
        for h in range(heads):
            cols = slice(h * DK, (h + 1) * DK)
            wide = slice(h * DV, (h + 1) * DV)
            leaving = state[h].astype(bf16)
            state[h] = grown[h, b] + decay[h, 0] * state[h]
            kb = k[at, cols]
            vd = (v[at, wide].astype(f32) * k_scale[h]).astype(bf16)
            turn_back(dk[at, cols] + product_rt(vd, leaving), at, hk + h * DK)
            dall[at, 2 * hk + h * DV : 2 * hk + (h + 1) * DV] = (
                dv[at, wide] + k_scale[h] * dot(kb, leaving)
            ).astype(bf16)
        done(b).start()
        return 0

    lax.fori_loop(0, depth, cross, 0)
    saves = [pltpu.make_async_copy(g_wo, g_out, save.at[0])]

    @pl.when(place > 0)
    def _():
        out_grad()

    saves[0].start()
    lax.fori_loop(0, depth, lambda b, c: (done(b).wait(), c)[1], 0)
    line_gather_end(dx, g_send, g_recv, s, z, depth)

    @pl.when(place > 0)
    def _():
        for h in range(heads):
            chain(h, s - 1).wait_send()

    swap.wait()
    for copy in saves:
        copy.wait()


def retract(
    grad_hidden, y_send, w_out, q, k, v, gp, gn, gated, inv, p, r, cosine, sine, mask, q_scale, k_scale, decay
):
    f32, bf16 = jnp.float32, jnp.bfloat16
    depth = lax.axis_size("mp")
    rows, width = grad_hidden.shape
    span = depth * rows
    heads = q.shape[1] // DK
    hk, hv = q.shape[1], v.shape[1]
    any_ = pl.BlockSpec(memory_space=pl.ANY)
    vmem = pl.BlockSpec(memory_space=pltpu.VMEM)
    dma = pltpu.SemaphoreType.DMA
    return pl.pallas_call(
        retract_kernel,
        out_shape=[
            jax.ShapeDtypeStruct((span, 2 * hk + 2 * hv), bf16),
            jax.ShapeDtypeStruct((hv, width), bf16),
            jax.ShapeDtypeStruct((rows, width), bf16),
        ],
        in_specs=[vmem] + [any_] * 17,
        out_specs=[any_] * 3,
        scratch_shapes=[
            pltpu.VMEM((span, DK // 2), f32),
            pltpu.VMEM((span, DK // 2), f32),
            pltpu.VMEM((heads, rows, rows), f32),
            pltpu.VMEM((heads, rows, 1), f32),
            pltpu.VMEM((heads, rows, 1), f32),
            pltpu.VMEM((heads, 2, 1, DV), f32),
            pltpu.VMEM((depth, rows, width), bf16),
            pltpu.VMEM((span, hk), bf16),
            pltpu.VMEM((span, hk), bf16),
            pltpu.VMEM((span, hv), bf16),
            pltpu.VMEM((span, hv), f32),
            pltpu.VMEM((span, hv), f32),
            pltpu.VMEM((span, hv), bf16),
            pltpu.VMEM((heads, span, 128), f32),
            pltpu.VMEM((heads, depth, rows, rows), bf16),
            pltpu.VMEM((heads, depth, DK, DV), bf16),
            pltpu.VMEM(w_out.shape, bf16),
            pltpu.VMEM((span, 2 * hk + 2 * hv), bf16),
            pltpu.VMEM((span, hv), bf16),
            pltpu.VMEM((rows, hv), bf16),
            pltpu.VMEM((rows, DV), f32),
            pltpu.VMEM((heads, depth, DK, DV), f32),
            pltpu.VMEM((span, hk), f32),
            pltpu.VMEM((span, hv), f32),
            pltpu.VMEM((heads, DK, DV), f32),
            pltpu.VMEM((heads, DK, DV), bf16),
            pltpu.VMEM((heads, DK, DV), bf16),
            pltpu.VMEM((hv, width), bf16),
            dma((16,)),
            dma((1,)),
            dma((depth,)),
            dma((2, depth)),
            dma((depth,)),
            dma((heads,)),
            dma((heads,)),
            dma((2,)),
        ],
        compiler_params=pltpu.CompilerParams(
            collective_id=2, has_side_effects=True, vmem_limit_bytes=LIMIT
        ),
        cost_estimate=pl.CostEstimate(
            flops=120 * 10**9, bytes_accessed=40 * 10**6, transcendentals=2 * 10**6
        ),
        name="retract",
    )(grad_hidden, y_send, w_out, q, k, v, gp, gn, gated, inv, p, r, cosine, sine, mask, q_scale, k_scale, decay)


def flip(index, bit):
    return index + bit - 2 * bit * lax.rem(index // bit, 2)


def pair_kernel(
    x, d, wo_parts, far, out, far_got, stage, got, wo_mine, wo_got, result, save, send, recv, w_sems, f_sems
):
    f32, bf16 = jnp.float32, jnp.bfloat16
    _, chips, rows, _ = stage.shape
    few = wo_mine.shape[1]
    third = result.shape[2]
    s, z = lax.axis_index("seq"), lax.axis_index("mp")
    core = lax.rem(s, 2)
    twin = flip(s, 1)
    across = flip(z, 2)
    edge = (z == 0) | (z == lax.axis_size("mp") - 1)
    greet([(z >= 0, twin, z), (z >= 0, s, across), (z >= 0, twin, across)])
    crossed = remote(far.at[0], far_got, f_sems.at[0], f_sems.at[1], twin, across)
    straight = remote(far.at[1], far_got, f_sems.at[2], f_sems.at[3], s, across)

    @pl.when(edge & (core == 1))
    def _():
        crossed.start()
        straight.start()

    wo_load = pltpu.make_async_copy(wo_parts.at[:, core], wo_mine, w_sems.at[0])
    wo_load.start()
    wo_send = remote(wo_parts.at[:, 1 - core], wo_got, w_sems.at[1], w_sems.at[2], twin, z)
    wo_send.start()
    span = max(256, 2 * rows)
    each = span // (2 * rows)

    def give(i):
        return remote(stage.at[1 - core, i], got.at[i], send.at[i], recv.at[i], twin, z)

    def keep(i):
        return pltpu.make_async_copy(result.at[i], out.at[i], save.at[i])

    def take(i):
        give(i).wait_recv()
        for t in range(d.shape[1] // third):

            def add(here, r):
                there = pl.ds(pl.multiple_of(t * rows + r * 32, 32), 32)
                cols = slice(t * third, (t + 1) * third)
                result[i, there, :] = (
                    stage[core, i, here, cols].astype(f32) + got[i, here, cols].astype(f32)
                ).astype(bf16)

            row_loop(rows, 32, add)

    def one(g, _):
        for c in range(span // 256):
            chunk = g * (span // 256) + c
            cols = pl.ds(pl.multiple_of(chunk * 256, 256), 256)
            for n in range(0, d.shape[1], 1024):
                value = product_t(x[:, cols], d[:, n : n + 1024]).astype(bf16)
                for part in range(max(1, 256 // rows)):
                    to = (c if each == 1 and rows >= 256 else part) % 2
                    i = g * each + (0 if rows >= 256 else part // 2)
                    stage[to, i, :, n : n + 1024] = value[part * rows : (part + 1) * rows]
        for e in range(each):
            give(g * each + e).start()

        @pl.when(g > 0)
        def _():
            for e in range(each):
                take((g - 1) * each + e)

        return 0

    groups = chips // each
    lax.fori_loop(0, groups, one, 0)
    wo_load.wait()
    wo_send.wait()
    base = rows * (d.shape[1] // third)

    def wo_add(i, _):
        for t in range(wo_mine.shape[2] // third):
            cols = slice(t * third, (t + 1) * third)
            result[i, base + t * few : base + (t + 1) * few, :] = (
                wo_mine[i, :, cols].astype(f32) + wo_got[i, :, cols].astype(f32)
            ).astype(bf16)
        return 0

    lax.fori_loop(0, chips, wo_add, 0)
    for e in range(each):
        take((groups - 1) * each + e)

    def begin(i, _):
        keep(i).start()
        return 0

    def end(i, _):
        keep(i).wait()
        give(i).wait_send()
        return 0

    lax.fori_loop(0, chips, begin, 0)
    lax.fori_loop(0, chips, end, 0)

    @pl.when(edge & (core == 1))
    def _():
        crossed.wait_send()
        straight.wait_send()

    @pl.when(jnp.logical_not(edge) & (core == 0))
    def _():
        crossed.wait_recv()

    @pl.when(jnp.logical_not(edge) & (core == 1))
    def _():
        straight.wait_recv()


def pair_sum(x, d, g_out, far):
    bf16 = jnp.bfloat16
    count = lax.axis_size("seq")
    chips = count // 2
    rows, few = x.shape[1] // count, g_out.shape[0] // count
    wide, third = d.shape[1], d.shape[1] // 3
    high = 3 * rows + few * g_out.shape[1] // third
    any_ = pl.BlockSpec(memory_space=pl.ANY)
    vmem = pl.BlockSpec(memory_space=pltpu.VMEM)
    dma = pltpu.SemaphoreType.DMA
    return pl.pallas_call(
        pair_kernel,
        out_shape=[
            jax.ShapeDtypeStruct((chips, high, third), bf16),
            jax.ShapeDtypeStruct(far.shape[1:], bf16),
        ],
        in_specs=[vmem, vmem, any_, any_],
        out_specs=[any_, any_],
        scratch_shapes=[
            pltpu.VMEM((2, chips, rows, wide), bf16),
            pltpu.VMEM((chips, rows, wide), bf16),
            pltpu.VMEM((chips, few, g_out.shape[1]), bf16),
            pltpu.VMEM((chips, few, g_out.shape[1]), bf16),
            pltpu.VMEM((chips, high, third), bf16),
            dma((chips,)),
            dma((chips,)),
            dma((chips,)),
            dma((3,)),
            dma((4,)),
        ],
        compiler_params=pltpu.CompilerParams(
            collective_id=3, has_side_effects=True, vmem_limit_bytes=LIMIT
        ),
        cost_estimate=pl.CostEstimate(
            flops=25 * 10**9, bytes_accessed=30 * 10**6, transcendentals=0
        ),
        name="pair_sum",
    )(x, d, g_out.reshape(chips, 2, few, g_out.shape[1]), far)


def finish_kernel(
    d_in,
    x_in,
    tok_in,
    gain,
    gain_part,
    grad_hidden_in,
    w_query,
    w_key,
    w_value,
    w_gate,
    far,
    far_got,
    grad_tok,
    gains,
    g_up,
    g_down,
    d,
    x,
    tok,
    grad_hidden,
    sbuf,
    rbuf,
    total,
    wq,
    wk,
    wv,
    wg,
    mine,
    other,
    gain_all,
    gain_line,
    load,
    d_load,
    x_load,
    s_send,
    s_recv,
    f_sems,
    h_send,
    h_recv,
    l_send,
    l_recv,
):
    f32, bf16 = jnp.float32, jnp.bfloat16
    depth, rows, width = x.shape
    s, z = lax.axis_index("seq"), lax.axis_index("mp")
    core = lax.rem(s, 2)
    twin, across = flip(s, 1), flip(z, 2)
    count = lax.axis_size("seq")
    loads = [
        pltpu.make_async_copy(a, b, load.at[i])
        for i, (a, b) in enumerate(
            [(w_query, wq), (w_key, wk), (w_value, wv), (w_gate, wg)]
        )
    ]

    def slot_loads(j):
        at = block(rows, j)
        return [
            pltpu.make_async_copy(d_in.at[at], d.at[at], d_load.at[j]),
            pltpu.make_async_copy(x_in.at[j], x.at[j], x_load.at[j]),
        ]

    late = [
        pltpu.make_async_copy(a, b, load.at[4 + i])
        for i, (a, b) in enumerate([(tok_in, tok), (grad_hidden_in, grad_hidden)])
    ]
    for copy in loads:
        copy.start()

    def pull(i, _):
        for copy in slot_loads(jnp.where(z < depth // 2, depth - 1 - i, i)):
            copy.start()
        return 0

    lax.fori_loop(0, depth, pull, 0)
    for copy in late:
        copy.start()
    gains[...] = jnp.zeros_like(gains)
    gains[1:2, :] = gain_part[...]
    greet(
        [(z >= 0, twin, across)]
        + [(z != other, s, other) for other in range(depth)]
        + [(s != other, other, z) for other in range(count)]
    )
    near = remote(far.at[1], other, f_sems.at[0], f_sems.at[1], twin, z)
    crossed = remote(far.at[0], other, f_sems.at[0], f_sems.at[1], twin, across)
    straight = remote(far.at[1], mine, f_sems.at[2], f_sems.at[3], s, across)
    edge = (z == 0) | (z == depth - 1)
    inner = jnp.logical_not(edge)
    local = pltpu.make_async_copy(far.at[0], mine, f_sems.at[4])
    to_other = pltpu.make_async_copy(far_got, other, f_sems.at[5])
    to_mine = pltpu.make_async_copy(far_got, mine, f_sems.at[5])

    @pl.when(core == 0)
    def _():
        near.start()
        local.start()

    @pl.when(inner & (core == 0))
    def _():
        to_other.start()

    @pl.when(inner & (core == 1))
    def _():
        to_mine.start()
        crossed.start()
        straight.start()

    for copy in loads:
        copy.wait()
    step = 512
    starts, at_col = [], 0
    for w in (wq, wk, wv, wg):
        starts.append((w, at_col, at_col + w.shape[1]))
        at_col += w.shape[1]

    def term(j, n):
        at = block(rows, j)
        value = None
        for w, a, b in starts:
            one = product_rt(d[at, a:b], w[n : n + step, :])
            value = one if value is None else value + one
        gains[0:1, n : n + step] += jnp.sum(
            value * x[j, :, n : n + step].astype(f32), axis=0, keepdims=True
        )
        return value

    def partial(j):
        for copy in slot_loads(j):
            copy.wait()
        for n in range(0, width, step):
            sbuf[j, :, n : n + step] = term(j, n).astype(bf16)

    def plane(to):
        return remote(gain_all.at[s], gain_all.at[s], h_send.at[to], h_recv.at[s], to, z)

    def line(to):
        return remote(gain_line.at[z], gain_line.at[z], l_send.at[to], l_recv.at[z], s, to)

    def others(count, me, act):
        def one(i, _):
            @pl.when(i != me)
            def _():
                act(i)

            return 0

        lax.fori_loop(0, count, one, 0)

    def own():
        for copy in slot_loads(z):
            copy.wait()
        for n in range(0, width, step):
            total[:, n : n + step] = term(z, n)
        gains[0:1, :] = gains[0:1, :] / gain[...]
        gain_all[s] = gains[...]
        others(count, s, lambda to: plane(to).start())

    line_scatter(sbuf, rbuf, total, s_send, s_recv, s, z, depth, partial, own)

    def plane_came(i):
        remote(gain_all.at[i], gain_all.at[i], h_send.at[i], h_recv.at[i], twin, z).wait_recv()

    def line_came(i):
        remote(gain_line.at[i], gain_line.at[i], l_send.at[i], l_recv.at[i], s, across).wait_recv()

    others(count, s, plane_came)
    gains[...] = gain_all[0]
    for i in range(1, count):
        gains[...] += gain_all[i]
    gain_line[z] = gains[...]
    others(depth, z, lambda to: line(to).start())

    for copy in late:
        copy.wait()

    def last(here, i):
        unit, inverse = centred(tok[here, :].astype(f32))
        grad_tok[here, :] = (
            grad_hidden[here, :] + norm_rows_back(total[here, :] * gain[...], unit, inverse)
        ).astype(bf16)

    row_loop(rows, 32, last)
    others(depth, z, line_came)
    gains[...] = gain_line[0]
    for i in range(1, depth):
        gains[...] += gain_line[i]
    others(count, s, lambda to: plane(to).wait_send())
    others(depth, z, lambda to: line(to).wait_send())

    @pl.when(core == 0)
    def _():
        near.wait_send()
        local.wait()

    @pl.when(core == 1)
    def _():
        near.wait_recv()

    @pl.when(inner & (core == 0))
    def _():
        to_other.wait()

    @pl.when(edge & (core == 0))
    def _():
        crossed.wait_recv()

    @pl.when(inner & (core == 1))
    def _():
        to_mine.wait()
        crossed.wait_send()
        straight.wait_send()

    @pl.when(edge & (core == 1))
    def _():
        straight.wait_recv()

    high, few = g_up.shape[0], g_down.shape[0]
    third = g_up.shape[1]

    g_up[...] = mine[0:high, :].astype(f32) + other[0:high, :].astype(f32)
    for t in range(g_down.shape[1] // third):
        at = slice(high + t * few, high + (t + 1) * few)
        g_down[:, t * third : (t + 1) * third] = mine[at, :].astype(f32) + other[at, :].astype(f32)


def finish(d, x, tok, gain, gain_part, grad_hidden, w_query, w_key, w_value, w_gate, far, far_got):
    f32, bf16 = jnp.float32, jnp.bfloat16
    depth, rows, width = x.shape
    count = lax.axis_size("seq")
    units = far.shape[2]
    any_ = pl.BlockSpec(memory_space=pl.ANY)
    vmem = pl.BlockSpec(memory_space=pltpu.VMEM)
    dma = pltpu.SemaphoreType.DMA
    return pl.pallas_call(
        finish_kernel,
        out_shape=[
            jax.ShapeDtypeStruct((rows, width), bf16),
            jax.ShapeDtypeStruct((8, width), f32),
            jax.ShapeDtypeStruct((width // count, units), f32),
            jax.ShapeDtypeStruct((units // count, width), f32),
        ],
        in_specs=[any_] * 3 + [vmem] * 2 + [any_] * 7,
        out_specs=[vmem] * 4,
        scratch_shapes=[
            pltpu.VMEM(d.shape, bf16),
            pltpu.VMEM(x.shape, bf16),
            pltpu.VMEM((rows, width), bf16),
            pltpu.VMEM((rows, width), f32),
            pltpu.VMEM((depth, rows, width), bf16),
            pltpu.VMEM((depth + 1, rows, width), bf16),
            pltpu.VMEM((rows, width), f32),
            pltpu.VMEM(w_query.shape, bf16),
            pltpu.VMEM(w_key.shape, bf16),
            pltpu.VMEM(w_value.shape, bf16),
            pltpu.VMEM(w_gate.shape, bf16),
            pltpu.VMEM(far.shape[1:], bf16),
            pltpu.VMEM(far.shape[1:], bf16),
            pltpu.VMEM((count, 8, width), f32),
            pltpu.VMEM((depth, 8, width), f32),
            dma((6,)),
            dma((depth,)),
            dma((depth,)),
            dma((depth,)),
            dma((depth + 1,)),
            dma((6,)),
            dma((count,)),
            dma((count,)),
            dma((depth,)),
            dma((depth,)),
        ],
        compiler_params=pltpu.CompilerParams(
            collective_id=4, has_side_effects=True, vmem_limit_bytes=LIMIT
        ),
        cost_estimate=pl.CostEstimate(
            flops=110 * 10**9, bytes_accessed=30 * 10**6, transcendentals=0
        ),
        name="finish",
    )(d, x, tok, gain, gain_part, grad_hidden, w_query, w_key, w_value, w_gate, far, far_got)


def unpack_kernel(summed, tok, up, down, query, key, value, gate, out, tok_out, up_out, down_out):
    f32 = jnp.float32
    rows, wide = query.shape
    few, tall = out.shape[0], value.shape[1]
    query[...] = summed[0:rows, 0:wide].astype(f32)
    key[...] = summed[0:rows, wide : 2 * wide].astype(f32)
    value[...] = summed[rows : 2 * rows, :].astype(f32)
    gate[...] = summed[2 * rows : 3 * rows, :].astype(f32)
    for t in range(out.shape[1] // tall):
        at = slice(3 * rows + t * few, 3 * rows + (t + 1) * few)
        out[:, t * tall : (t + 1) * tall] = summed[at, :].astype(f32)
    tok_out[...] = tok[...]
    up_out[...] = up[...]
    down_out[...] = down[...]


def unpack(summed, tok, up, down, wide):
    f32 = jnp.float32
    count = lax.axis_size("seq")
    width, tall = tok.shape[1], summed.shape[1]
    rows, few = width // count, tall // count
    shapes = [(rows, wide)] * 2 + [(rows, tall)] * 2 + [(few, width)]
    return pl.pallas_call(
        unpack_kernel,
        out_shape=[jax.ShapeDtypeStruct(one, f32) for one in shapes]
        + [jax.ShapeDtypeStruct(a.shape, a.dtype) for a in (tok, up, down)],
        compiler_params=pltpu.CompilerParams(vmem_limit_bytes=LIMIT),
        name="unpack",
    )(summed, tok, up, down)


def shards(
    tokens, gain_mix, w_query, w_key, w_value, w_gate, w_out, gain_ffn, w_up, w_down, cotangent
):
    bf16 = jnp.bfloat16
    f32 = jnp.float32
    span_rows = lax.axis_size("mp") * tokens.shape[0]
    local_heads = w_query.shape[1] // DK
    trig = decay_tables(span_rows, local_heads * lax.axis_size("mp"))
    (
        x_rows,
        q_all,
        k_all,
        v_all,
        gate,
        unit,
        gated,
        inverse,
        weights,
        entering,
        hidden,
        cot_rows,
        far_up,
        far_down,
    ) = attend(
        tokens, gain_mix[None, :], cotangent, w_query, w_key, w_value, w_gate, w_out, w_up, w_down, *trig
    )
    y_keep, y_send, grad_hidden, gain_ffn_part, grad_ffn = feed(
        hidden, gain_ffn[None, :], cotangent, cot_rows, w_up, w_down, far_up, far_down
    )
    far = lax.psum_scatter(
        grad_ffn, "seq", scatter_dimension=0, tiled=False, axis_index_groups=same_core()
    )
    grad_in, grad_out_w, y_got = retract(
        grad_hidden, y_send, w_out, q_all, k_all, v_all, gate, unit, gated, inverse, weights, entering, *trig
    )
    output = (y_keep + y_got.astype(f32)).astype(bf16)
    pairs, far_got = pair_sum(x_rows.reshape(span_rows, -1), grad_in, grad_out_w, far)
    summed = lax.psum_scatter(
        pairs, "seq", scatter_dimension=0, tiled=False, axis_index_groups=same_core()
    )
    grad_in, pairs = lax.optimization_barrier((grad_in, pairs))
    grad_tokens, gains, final_up, final_down = finish(
        grad_in, x_rows, tokens, gain_mix[None, :], gain_ffn_part, grad_hidden, w_query, w_key, w_value, w_gate, far, far_got
    )
    summed, gains = lax.optimization_barrier((summed, gains))
    gain_mix_sum, gain_ffn_sum = gains[0], gains[1]
    (
        final_query,
        final_key,
        final_value,
        final_gate,
        final_out,
        grad_tokens,
        final_up,
        final_down,
    ) = unpack(summed, grad_tokens, final_up, final_down, w_query.shape[1])
    return (
        output,
        grad_tokens,
        gain_mix_sum,
        final_query,
        final_key,
        final_value,
        final_gate,
        final_out,
        gain_ffn_sum,
        final_up,
        final_down,
    )


def solution(mesh):
    return jax.shard_map(
        shards,
        mesh=mesh,
        in_specs=(
            P(("seq", "mp"), None),
            P(),
            P(None, "mp"),
            P(None, "mp"),
            P(None, "mp"),
            P(None, "mp"),
            P("mp", None),
            P(),
            P(None, "mp"),
            P("mp", None),
            P(("seq", "mp"), None),
        ),
        out_specs=(
            P(("seq", "mp"), None),
            P(("seq", "mp"), None),
            P(),
            P("seq", "mp"),
            P("seq", "mp"),
            P("seq", "mp"),
            P("seq", "mp"),
            P(("mp", "seq"), None),
            P(),
            P("seq", "mp"),
            P(("mp", "seq"), None),
        ),
        check_vma=False,
    )
```

```python
import math

import jax
import jax.numpy as jnp
import numpy as np
from jax import lax
from jax.experimental import pallas as pl
from jax.experimental.pallas import tpu as pltpu
from jax.sharding import PartitionSpec as P

DK = 256
DV = 512
STRETCH = 256
SEQ_DEVS = 4


eps = 1e-05


def same_core():
    count = lax.axis_size("seq")
    return [list(range(core, count, 2)) for core in range(2)]


def decay_tables(span_rows, heads):
    half = DK // 2
    f32 = np.float32
    freq = np.exp(f32(-math.log(10000.0)) * np.arange(half, dtype=f32) / f32(half - 1)).astype(f32)
    phase = np.arange(SEQ_DEVS * span_rows, dtype=f32)[:, None] * freq[None, :]
    phase = phase.astype(np.float64)
    logs = np.log1p(-np.exp2(-5.0 - np.arange(heads)))
    steps = np.arange(STRETCH)
    gaps = steps[:, None] - steps[None, :]
    mask = np.where(gaps >= 0, np.exp(logs[:, None, None] * np.maximum(gaps, 0)), 0.0)
    q_scale = np.exp(logs[:, None] * (steps + 1))[:, :, None]
    k_scale = np.exp(logs[:, None] * (STRETCH - 1 - steps))[:, :, None]
    decay = np.exp(logs[:, None] * np.array([STRETCH, span_rows]))[:, :, None, None]
    decay = np.broadcast_to(decay, (heads, 2, 1, DV))
    return tuple(
        jnp.asarray(a.astype(f32))
        for a in (np.cos(phase), np.sin(phase), mask, q_scale, k_scale, decay)
    )


def product_t(left, right):
    return lax.dot_general(
        left, right, (((0,), (0,)), ((), ())), preferred_element_type=jnp.float32
    )


def product_rt(left, right):
    return lax.dot_general(
        left, right, (((1,), (1,)), ((), ())), preferred_element_type=jnp.float32
    )


MESH = pl.DeviceIdType.MESH
LIMIT = 62 * 1024 * 1024


def remote(src, dst, send, recv, s, z):
    return pltpu.make_async_remote_copy(
        src_ref=src,
        dst_ref=dst,
        send_sem=send,
        recv_sem=recv,
        device_id=(s, z),
        device_id_type=MESH,
    )


def greet(partners):
    barrier = pltpu.get_barrier_semaphore()
    count = 0
    for present, s, z in partners:

        @pl.when(present)
        def _():
            pl.semaphore_signal(barrier, inc=1, device_id=(s, z), device_id_type=MESH)

        count = count + jnp.where(present, 1, 0)
    pl.semaphore_wait(barrier, count)


def dot(left, right):
    return jnp.dot(left, right, preferred_element_type=jnp.float32)


HALVES = 2


def part_of(rows, part):
    return pl.ds(part * (rows // HALVES), rows // HALVES)


def line_copy(x, send, recv, s, to, slot, part, way):
    at = x.at[slot, part_of(x.shape[1], part)]
    return remote(at, at, send.at[way, slot, part], recv.at[slot, part], s, to)


def line_gather(x, send, recv, s, z, depth, use, ready, after=None):
    def right(slot, part):
        return line_copy(x, send, recv, s, z + 1, slot, part, 0)

    def left(slot, part):
        return line_copy(x, send, recv, s, z - 1, slot, part, 1)

    for part in range(HALVES):
        ready(part)

        @pl.when(z < depth - 1)
        def _():
            right(z, part).start()

        @pl.when(z > 0)
        def _():
            left(z, part).start()

    def one(turn, _):
        away = (turn + 1) // 2
        low, high = z - away, z + away
        for part in range(HALVES):

            @pl.when((turn % 2 == 1) & (low >= 0))
            def _():
                line_copy(x, send, recv, s, z - 1, low, part, 0).wait_recv()

                @pl.when(z < depth - 1)
                def _():
                    right(low, part).start()

            @pl.when((turn % 2 == 1) & (high < depth))
            def _():
                line_copy(x, send, recv, s, z + 1, high, part, 1).wait_recv()

                @pl.when(z > 0)
                def _():
                    left(high, part).start()

        if after is not None:
            after(turn)
        slot = jnp.where(turn % 2 == 1, low, high)

        @pl.when((slot >= 0) & (slot < depth))
        def _():
            use(slot)

        return 0

    lax.fori_loop(0, 2 * depth - 1, one, 0)


def line_gather_end(x, send, recv, s, z, depth):
    def one(slot, _):
        for part in range(HALVES):

            @pl.when((slot <= z) & (z < depth - 1))
            def _():
                line_copy(x, send, recv, s, z + 1, slot, part, 0).wait_send()

            @pl.when((slot >= z) & (z > 0))
            def _():
                line_copy(x, send, recv, s, z - 1, slot, part, 1).wait_send()

        return 0

    lax.fori_loop(0, depth, one, 0)


def add_rows(into, other):
    step = 32

    def one(i, _):
        rows = pl.ds(pl.multiple_of(i * step, step), step)
        into[rows, :] = (
            into[rows, :].astype(jnp.float32) + other[rows, :].astype(jnp.float32)
        ).astype(into.dtype)
        return 0

    lax.fori_loop(0, into.shape[0] // step, one, 0)


def line_scatter(sbuf, rbuf, total, send, recv, s, z, depth, partial, own, hook=None):
    rows = total.shape[0]

    def right(j, part):
        at = part_of(rows, part)
        return remote(
            sbuf.at[j, at], rbuf.at[j, at], send.at[j, part], recv.at[j, part], s, z + 1
        )

    def left(j, part):
        at = part_of(rows, part)
        slot = jnp.where(j == z - 1, depth, j)
        return remote(
            sbuf.at[j, at], rbuf.at[slot, at], send.at[j, part], recv.at[slot, part], s, z - 1
        )

    def arrived(slot, part, sender):
        at = part_of(rows, part)
        remote(
            sbuf.at[0, at], rbuf.at[slot, at], send.at[0, part], recv.at[slot, part], s, sender
        ).wait_recv()

    def first(turn, _):
        up = depth - 1 + z - turn // 2
        down = turn // 2 - (depth - 1) + z
        j = jnp.where(turn % 2 == 0, up, down)
        valid = jnp.where(turn % 2 == 0, (up > z) & (up < depth), (down >= 0) & (down < z))

        @pl.when(valid)
        def _():
            partial(j)

            @pl.when((z == 0) & (j > z))
            def _():
                for part in range(HALVES):
                    right(j, part).start()

            @pl.when((z == depth - 1) & (j < z))
            def _():
                for part in range(HALVES):
                    left(j, part).start()

        return 0

    lax.fori_loop(0, 2 * (depth - 1), first, 0)
    own()

    def event(turn, _):
        up = depth - 1 + z - turn
        down = turn - (depth - 1) + z
        slot = jnp.where(down == z, depth, down)
        for part in range(HALVES):
            at = part_of(rows, part)

            @pl.when((z > 0) & (up >= z) & (up < depth))
            def _():
                arrived(up, part, z - 1)

                @pl.when(up > z)
                def _():
                    add_rows(sbuf.at[up, at], rbuf.at[up, at])
                    right(up, part).start()

                @pl.when(up == z)
                def _():
                    add_rows(total.at[at], rbuf.at[up, at])

            @pl.when((z < depth - 1) & (down >= 0) & (down <= z))
            def _():
                arrived(slot, part, z + 1)

                @pl.when(down < z)
                def _():
                    add_rows(sbuf.at[down, at], rbuf.at[down, at])
                    left(down, part).start()

                @pl.when(down == z)
                def _():
                    add_rows(total.at[at], rbuf.at[depth, at])

        if hook is not None:
            hook(turn)
        return 0

    lax.fori_loop(0, depth, event, 0)

    def end(j, _):
        for part in range(HALVES):

            @pl.when(j > z)
            def _():
                right(j, part).wait_send()

            @pl.when(j < z)
            def _():
                left(j, part).wait_send()

        return 0

    lax.fori_loop(0, depth, end, 0)


def centred(rows):
    centre = rows - jnp.mean(rows, axis=-1, keepdims=True)
    inverse = lax.rsqrt(jnp.mean(centre * centre, axis=-1, keepdims=True) + eps)
    return centre * inverse, inverse


def block(rows, index):
    return pl.ds(pl.multiple_of(index * rows, rows), rows)


def attend_kernel(
    tok,
    gain,
    cot,
    w_query,
    w_key,
    w_value,
    w_gate,
    w_out,
    w_up,
    w_down,
    cosine_all,
    sine_all,
    mask_all,
    q_scale_all,
    k_scale_all,
    decay_all,
    x_out,
    q_out,
    k_out,
    v_out,
    gp_out,
    gn_out,
    gated_out,
    inv_out,
    p_out,
    r_out,
    hidden_out,
    cot_rows,
    far_up,
    far_down,
    cosine,
    sine,
    mask,
    q_scale,
    k_scale,
    decay,
    xg,
    q,
    k,
    v,
    gp,
    gn,
    gated,
    inv,
    weights,
    grown,
    entering,
    tile,
    state,
    state_in,
    state_to,
    rbuf,
    total,
    wq,
    wk,
    wv,
    wg,
    wo,
    load,
    save,
    g_send,
    g_recv,
    s_send,
    s_recv,
    c_send,
    c_recv,
    x_send,
    x_recv,
    f_send,
    f_recv,
    p_send,
    p_recv,
):
    f32, bf16 = jnp.float32, jnp.bfloat16
    depth = xg.shape[0]
    rows = xg.shape[1]
    heads = mask.shape[0]
    s, z = lax.axis_index("seq"), lax.axis_index("mp")
    place = lax.rem(s, SEQ_DEVS)
    pair = z + 1 - 2 * lax.rem(z, 2)
    twin = s + 1 - 2 * lax.rem(s, 2)
    def tables(place, z):
        at = block(cosine.shape[0], place)
        some = pl.ds(z * heads, heads)
        return [
            (cosine_all.at[at], cosine),
            (sine_all.at[at], sine),
            (mask_all.at[some], mask),
            (q_scale_all.at[some], q_scale),
            (k_scale_all.at[some], k_scale),
            (decay_all.at[some], decay),
        ]

    loads = [
        pltpu.make_async_copy(a, b, load.at[i])
        for i, (a, b) in enumerate(
            [(w_query, wq), (w_key, wk), (w_value, wv), (w_gate, wg), (w_out, wo)]
            + tables(place, z)
        )
    ]
    for copy in loads:
        copy.start()

    def norm(i, _):
        part = pl.ds(pl.multiple_of(i * 32, 32), 32)
        unit, _ = centred(tok[part, :].astype(f32))
        xg[z, part, :] = (unit * gain[...]).astype(bf16)
        return 0

    def ready(part):
        each = rows // 32 // HALVES
        lax.fori_loop(part * each, (part + 1) * each, norm, 0)

    count = lax.axis_size("seq")
    across = flip(z, 2)
    greet(
        [(z > 0, s, z - 1), (z < depth - 1, s, z + 1), (z >= 0, s, across)]
        + [(s != other, other, z) for other in range(count)]
    )
    tall, few = w_up.shape[0] // count, w_down.shape[0] // count
    mine = pltpu.make_async_copy(cot, cot_rows.at[0], x_send.at[3])
    near = remote(cot, cot_rows.at[2], x_send.at[1], x_recv.at[1], twin, z)
    swap = remote(cot, cot_rows.at[1], x_send.at[0], x_recv.at[0], s, pair)
    far = remote(cot_rows.at[1], cot_rows.at[3], x_send.at[2], x_recv.at[2], twin, z)

    def piece(source):
        return block(tall, source), block(few, source)

    up_at, down_at = piece(s)
    moves = [
        remote(w_up.at[up_at], far_up.at[up_at], f_send.at[0], f_recv.at[0], s, across),
        remote(w_down.at[down_at], far_down.at[down_at], f_send.at[1], f_recv.at[1], s, across),
    ]
    edge = (z == 0) | (z == depth - 1)

    def spread(source, chip):
        up_, down_ = piece(source)
        to = 2 * chip + 1
        return [
            remote(far_up.at[up_], far_up.at[up_], p_send.at[0, chip], p_recv.at[0, source], to, z),
            remote(
                far_down.at[down_], far_down.at[down_], p_send.at[1, chip], p_recv.at[1, source], to, z
            ),
        ]

    @pl.when(place == 0)
    def _():
        state_in[...] = jnp.zeros_like(state_in)

    def after(turn):
        @pl.when(turn == 0)
        def _():
            mine.start()
            near.start()

        @pl.when(edge & (turn == 1))
        def _():
            swap.start()

        @pl.when(edge & (turn == 3))
        def _():
            for copy in moves:
                copy.start()

    def use(j):
        at = block(rows, j)

        @pl.when(j == z)
        def _():
            for copy in loads:
                copy.wait()

        rotated(j, wk, k)
        for h in range(heads):
            cols = slice(h * DK, (h + 1) * DK)
            wide = slice(h * DV, (h + 1) * DV)
            v[at, wide] = dot(xg[j], wv[:, wide]).astype(bf16)
            vd = (v[at, wide].astype(f32) * k_scale[h]).astype(bf16)
            grown[h, j] = product_t(k[at, cols], vd)

        @pl.when(j != last)
        def _():
            rest(j)

    last = jnp.where(z < depth // 2, depth - 1, 0)

    def rotated(j, w, out):
        at = block(rows, j)
        c, sn = cosine[at, :], sine[at, :]
        for h in range(heads):
            p = dot(xg[j], w[:, h * DK : (h + 1) * DK])
            a, b = p[:, : DK // 2], p[:, DK // 2 :]
            out[at, h * DK : h * DK + DK // 2] = (a * c - b * sn).astype(bf16)
            out[at, h * DK + DK // 2 : (h + 1) * DK] = (b * c + a * sn).astype(bf16)

    def rest(j):
        at = block(rows, j)
        rotated(j, wq, q)
        for h in range(heads):
            cols = slice(h * DK, (h + 1) * DK)
            wide = slice(h * DV, (h + 1) * DV)
            gp[at, wide] = dot(xg[j], wg[:, wide])
            weights[h, j] = (product_rt(q[at, cols], k[at, cols]) * mask[h]).astype(bf16)

    line_gather(xg, g_send, g_recv, s, z, depth, use, ready, after)
    def chain(h, to):
        return remote(state_to.at[h], state_in.at[h], c_send.at[h], c_recv.at[h], to, z)

    for h in range(heads):
        state[h] = grown[h, 0]
        for b in range(1, depth):
            state[h] = decay[h, 0] * state[h] + grown[h, b]

        @pl.when(place == 0)
        def _():
            state_to[h] = state[h].astype(bf16)
            chain(h, s + 1).start()

    rest(last)

    @pl.when(place > 0)
    def _():
        for h in range(heads):
            chain(h, s - 1).wait_recv()

            @pl.when(place < SEQ_DEVS - 1)
            def _():
                state_to[h] = (decay[h, 1] * state_in[h].astype(f32) + state[h]).astype(bf16)
                chain(h, s + 1).start()

    saves = [
        pltpu.make_async_copy(a, b, save.at[i])
        for i, (a, b) in enumerate(
            [
                (xg, x_out),
                (q, q_out),
                (k, k_out),
                (v, v_out),
                (gp, gp_out),
                (weights, p_out),
                (entering, r_out),
                (gn, gn_out),
                (gated, gated_out),
                (inv, inv_out),
            ]
        )
    ]
    for copy in saves[:6]:
        copy.start()

    def hand_out():
        for copy in moves:
            copy.wait_recv()

        def to_chip(chip, _):
            @pl.when(2 * chip + 1 != s)
            def _():
                for copy in spread(s, chip):
                    copy.start()

            return 0

        lax.fori_loop(0, count // 2, to_chip, 0)

    for h in range(heads):
        state[h] = state_in[h].astype(f32)
        for b in range(depth):
            entering[h, b] = state[h].astype(bf16)
            if b < depth - 1:
                state[h] = decay[h, 0] * state[h] + grown[h, b]
    saves[6].start()

    def cross(b):
        at = block(rows, b)
        for h in range(heads):
            cols = slice(h * DK, (h + 1) * DK)
            wide = slice(h * DV, (h + 1) * DV)
            qd = (q[at, cols].astype(f32) * q_scale[h]).astype(bf16)
            tile[...] = dot(weights[h, b], v[at, wide]) + dot(qd, entering[h, b])

            def norm(here, i):
                there = pl.ds(pl.multiple_of(b * rows + i * 32, 32), 32)
                unit, inverse = centred(tile[here, :])
                gate = gp[there, wide]
                gn[there, wide] = unit
                gated[there, wide] = (unit * gate / (1.0 + jnp.exp(-gate))).astype(bf16)
                inv[h, there, :] = jnp.broadcast_to(inverse, (32, inv.shape[2]))

            row_loop(rows, 32, norm)

    line_gather_end(xg, g_send, g_recv, s, z, depth)

    @pl.when(jnp.logical_not(edge))
    def _():
        hand_out()

    saves[0].wait()
    wide = 512

    def hook(turn):
        @pl.when((turn == 0) & jnp.logical_not(edge))
        def _():
            for copy in moves:
                copy.start()
            swap.start()

        @pl.when((turn == 0) & edge)
        def _():
            hand_out()

        @pl.when(turn == 2)
        def _():
            swap.wait_recv()
            far.start()

    def partial(j):
        cross(j)
        for n in range(0, total.shape[1], wide):
            xg[j, :, n : n + wide] = dot(gated[block(rows, j), :], wo[:, n : n + wide]).astype(bf16)

    def own():
        cross(z)
        for copy in saves[7:]:
            copy.start()
        for n in range(0, total.shape[1], wide):
            total[:, n : n + wide] = tok[:, n : n + wide].astype(f32) + dot(
                gated[block(rows, z), :], wo[:, n : n + wide]
            )

    line_scatter(xg, rbuf, total, s_send, s_recv, s, z, depth, partial, own, hook)
    done = pltpu.make_async_copy(total, hidden_out, save.at[0])
    done.start()

    @pl.when(place < SEQ_DEVS - 1)
    def _():
        for h in range(heads):
            chain(h, s + 1).wait_send()

    def sent(chip, _):
        @pl.when(2 * chip + 1 != s)
        def _():
            for copy in spread(s, chip):
                copy.wait_send()

        return 0

    lax.fori_loop(0, count // 2, sent, 0)

    def came(source, _):
        @pl.when((source != s) & (lax.rem(s, 2) == 1))
        def _():
            for copy in spread(source, 0):
                copy.wait_recv()

        return 0

    lax.fori_loop(0, count, came, 0)
    for copy in moves:
        copy.wait_send()
    swap.wait_send()
    near.wait()
    far.wait()
    mine.wait()
    for copy in saves[1:]:
        copy.wait()
    done.wait()


def attend(
    tok, gain, cot, w_query, w_key, w_value, w_gate, w_out, w_up, w_down, cosine, sine, mask, q_scale, k_scale, decay
):
    f32, bf16 = jnp.float32, jnp.bfloat16
    depth = lax.axis_size("mp")
    rows, width = tok.shape
    span = depth * rows
    heads = w_query.shape[1] // DK
    hk, hv = w_query.shape[1], w_value.shape[1]
    any_ = pl.BlockSpec(memory_space=pl.ANY)
    vmem = pl.BlockSpec(memory_space=pltpu.VMEM)
    shapes = [
        ((depth, rows, width), bf16),
        ((span, hk), bf16),
        ((span, hk), bf16),
        ((span, hv), bf16),
        ((span, hv), f32),
        ((span, hv), f32),
        ((span, hv), bf16),
        ((heads, span, 128), f32),
        ((heads, depth, rows, rows), bf16),
        ((heads, depth, DK, DV), bf16),
        ((rows, width), f32),
        ((4, rows, width), bf16),
        (w_up.shape, bf16),
        (w_down.shape, bf16),
    ]
    count = lax.axis_size("seq")
    dma = pltpu.SemaphoreType.DMA
    return pl.pallas_call(
        attend_kernel,
        out_shape=[jax.ShapeDtypeStruct(*one) for one in shapes],
        in_specs=[vmem, vmem, any_] + [any_] * 13,
        out_specs=[any_] * len(shapes),
        scratch_shapes=[
            pltpu.VMEM((span, DK // 2), f32),
            pltpu.VMEM((span, DK // 2), f32),
            pltpu.VMEM((heads, rows, rows), f32),
            pltpu.VMEM((heads, rows, 1), f32),
            pltpu.VMEM((heads, rows, 1), f32),
            pltpu.VMEM((heads, 2, 1, DV), f32),
            pltpu.VMEM((depth, rows, width), bf16),
            pltpu.VMEM((span, hk), bf16),
            pltpu.VMEM((span, hk), bf16),
            pltpu.VMEM((span, hv), bf16),
            pltpu.VMEM((span, hv), f32),
            pltpu.VMEM((span, hv), f32),
            pltpu.VMEM((span, hv), bf16),
            pltpu.VMEM((heads, span, 128), f32),
            pltpu.VMEM((heads, depth, rows, rows), bf16),
            pltpu.VMEM((heads, depth, DK, DV), f32),
            pltpu.VMEM((heads, depth, DK, DV), bf16),
            pltpu.VMEM((rows, DV), f32),
            pltpu.VMEM((heads, DK, DV), f32),
            pltpu.VMEM((heads, DK, DV), bf16),
            pltpu.VMEM((heads, DK, DV), bf16),
            pltpu.VMEM((depth + 1, rows, width), bf16),
            pltpu.VMEM((rows, width), f32),
            pltpu.VMEM(w_query.shape, bf16),
            pltpu.VMEM(w_key.shape, bf16),
            pltpu.VMEM(w_value.shape, bf16),
            pltpu.VMEM(w_gate.shape, bf16),
            pltpu.VMEM(w_out.shape, bf16),
            dma((11,)),
            dma((10,)),
            dma((2, depth, HALVES)),
            dma((depth, HALVES)),
            dma((depth, HALVES)),
            dma((depth + 1, HALVES)),
            dma((heads,)),
            dma((heads,)),
            dma((4,)),
            dma((3,)),
            dma((2,)),
            dma((2,)),
            dma((2, count // 2)),
            dma((2, count)),
        ],
        compiler_params=pltpu.CompilerParams(
            collective_id=0, has_side_effects=True, vmem_limit_bytes=LIMIT
        ),
        cost_estimate=pl.CostEstimate(
            flops=190 * 10**9, bytes_accessed=60 * 10**6, transcendentals=2 * 10**6
        ),
        name="attend",
    )(tok, gain, cot, w_query, w_key, w_value, w_gate, w_out, w_up, w_down, cosine, sine, mask, q_scale, k_scale, decay)


def row_loop(rows, step, body):
    def one(i, _):
        body(pl.ds(pl.multiple_of(i * step, step), step), i)
        return 0

    lax.fori_loop(0, rows // step, one, 0)


def norm_rows_back(grad_hat, unit, inverse):
    first = jnp.mean(grad_hat, axis=-1, keepdims=True)
    second = jnp.mean(grad_hat * unit, axis=-1, keepdims=True)
    return inverse * (grad_hat - first - unit * second)


def feed_kernel(
    hidden,
    gain,
    cot,
    cot_rows,
    w_up,
    w_down,
    far_up,
    far_down,
    y_keep,
    y_send,
    grad_hidden,
    gain_part,
    g_all_out,
    x,
    dy,
    act,
    du,
    part_y,
    part_x,
    got_x,
    got_own,
    got_y,
    u_tile,
    d_tile,
    g_all,
    up,
    down,
    load,
    save,
    send,
    recv,
):
    f32, bf16 = jnp.float32, jnp.bfloat16
    rows, width = hidden.shape
    units = up.shape[1]
    half = rows // 2
    s, z = lax.axis_index("seq"), lax.axis_index("mp")
    pair = z + 1 - 2 * lax.rem(z, 2)
    twin = s + 1 - 2 * lax.rem(s, 2)
    own_loads = [
        pltpu.make_async_copy(w_up, up, load.at[0]),
        pltpu.make_async_copy(w_down, down, load.at[1]),
    ]
    far_loads = [
        pltpu.make_async_copy(far_up, up, load.at[0]),
        pltpu.make_async_copy(far_down, down, load.at[1]),
    ]

    @pl.when(lax.rem(s, 2) == 0)
    def _():
        for copy in own_loads:
            copy.start()

    @pl.when(lax.rem(s, 2) == 1)
    def _():
        for copy in far_loads:
            copy.start()

    rest = [
        pltpu.make_async_copy(cot_rows.at[a, pl.ds(at, n)], dy.at[pl.ds(to, n)], load.at[2 + i])
        for i, (a, at, n, to) in enumerate(
            [
                (0, 0, rows, 0),
                (2, 0, rows, rows),
                (1, 0, half, 2 * rows),
                (3, 0, half, 2 * rows + half),
                (1, half, half, 3 * rows),
                (3, half, half, 3 * rows + half),
            ]
        )
    ]
    loads = own_loads + rest
    for copy in rest:
        copy.start()

    def norm(here, i):
        unit, _ = centred(hidden[here, :])
        x[here, :] = (unit * gain[...]).astype(bf16)

    row_loop(rows, 32, norm)
    greet([(z >= 0, s, pair), (z >= 0, twin, z)])
    mine, theirs = pl.ds(0, rows), pl.ds(rows, rows)
    parts = [pl.ds(0, half), pl.ds(half, half)]
    pairs = [pl.ds(2 * rows, half), pl.ds(3 * rows, half)]
    twins = [pl.ds(2 * rows + half, half), pl.ds(3 * rows + half, half)]
    near = remote(x.at[mine], x.at[theirs], send.at[0], recv.at[0], twin, z)
    over, far, back_far, back_over, y_far = [], [], [], [], []
    for i in range(2):
        k = 1 + 5 * i
        over.append(remote(x.at[parts[i]], x.at[pairs[i]], send.at[k], recv.at[k], s, pair))
        far.append(remote(x.at[pairs[i]], x.at[twins[i]], send.at[k + 1], recv.at[k + 1], twin, z))
        back_far.append(
            remote(part_x.at[twins[i]], got_x.at[i], send.at[k + 2], recv.at[k + 2], twin, z)
        )
        back_over.append(
            remote(part_x.at[pairs[i]], got_x.at[2 + i], send.at[k + 3], recv.at[k + 3], s, pair)
        )
        y_far.append(
            remote(
                part_y.at[twins[i]], got_y.at[pl.ds(rows + i * half, half)], send.at[k + 4],
                recv.at[k + 4], twin, z,
            )
        )
    back_near = remote(part_x.at[theirs], got_own, send.at[11], recv.at[11], twin, z)
    y_near = remote(part_y.at[theirs], got_y.at[mine], send.at[12], recv.at[12], twin, z)
    over[0].start()
    near.start()
    over[1].start()
    for copy in loads:
        copy.wait()
    step = 512

    def y_terms(r):
        at = block(rows, r)
        for n in range(0, width, step):
            part_y[at, n : n + step] = dot(act[at, :], down[:, n : n + step]).astype(bf16)

    def return_pair(i):
        back_far[i].wait_recv()
        add_rows(part_x.at[pairs[i]], got_x.at[i])
        back_over[i].start()

    def one(r, _):
        at = block(rows, r)

        @pl.when(r == 1)
        def _():
            near.wait_recv()

        @pl.when(r == 2)
        def _():
            over[0].wait_recv()
            far[0].start()
            far[0].wait_recv()

        @pl.when(r == 3)
        def _():
            return_pair(0)
            lax.fori_loop(0, 2, lambda i, c: (y_terms(i), c)[1], 0)
            over[1].wait_recv()
            far[1].start()
            far[1].wait_recv()

        for n in range(0, units, step):
            cols = slice(n, n + step)
            u_tile[...] = dot(x[at, :], up[:, cols])
            d_tile[...] = product_rt(dy[at, :], down[cols, :])

            def gelu(here, i):
                there = pl.ds(pl.multiple_of(r * rows + i * 32, 32), 32)
                u = u_tile[here, :]
                normal = 0.5 * (1.0 + lax.erf(u * (2.0**-0.5)))
                slope = normal + u * (jnp.exp(-0.5 * u * u) * ((2.0 * math.pi) ** -0.5))
                act[there, cols] = (u * normal).astype(bf16)
                du[there, cols] = (d_tile[here, :] * slope).astype(bf16)

            row_loop(rows, 32, gelu)
        for n in range(0, width, step):
            part_x[at, n : n + step] = product_rt(du[at, :], up[n : n + step, :]).astype(bf16)

        @pl.when(r == 1)
        def _():
            back_near.start()

        @pl.when(r == 2)
        def _():
            back_far[0].start()

        @pl.when(r == 3)
        def _():
            back_far[1].start()

        return 0

    lax.fori_loop(0, 4, one, 0)
    return_pair(1)
    lax.fori_loop(2, 4, lambda i, c: (y_terms(i), c)[1], 0)
    y_near.start()
    for copy in y_far:
        copy.start()
    chips, _, high, _ = g_all.shape
    few = units // (2 * chips)
    tall = width // (2 * chips)

    def up_terms(m, _):
        cols = pl.ds(pl.multiple_of(m * 256, 256), 256)
        value = product_t(x[:, cols], du[...]).astype(bf16)
        for part in range(256 // tall):
            to = m * (256 // tall) + part
            g_all[to // 2, lax.rem(to, 2), 0:tall, :] = value[part * tall : (part + 1) * tall]
        return 0

    lax.fori_loop(0, width // 256, up_terms, 0)

    def down_terms(m, _):
        cols = pl.ds(pl.multiple_of(m * 256, 256), 256)
        for n in range(0, width, units):
            value = product_t(act[:, cols], dy[:, n : n + units]).astype(bf16)
            first = tall + n // units * few
            for part in range(256 // few):
                to = m * (256 // few) + part
                g_all[to // 2, lax.rem(to, 2), first : first + few, :] = value[
                    part * few : (part + 1) * few
                ]
        return 0

    lax.fori_loop(0, units // 256, down_terms, 0)
    saves = [pltpu.make_async_copy(g_all, g_all_out, save.at[0])]
    saves[0].start()
    y_near.wait_recv()
    for copy in y_far:
        copy.wait_recv()

    def y_sum(here, i):
        y_keep[here, :] = (
            hidden[here, :] + part_y[here, :].astype(f32) + got_y[here, :].astype(f32)
        )

    row_loop(rows, 32, y_sum)
    for i in range(2):

        def y_pair(here, j):
            there = pl.ds(pl.multiple_of((2 + i) * rows + j * 32, 32), 32)
            came = pl.ds(pl.multiple_of(rows + i * half + j * 32, 32), 32)
            to = pl.ds(pl.multiple_of(i * half + j * 32, 32), 32)
            y_send[to, :] = (part_y[there, :].astype(f32) + got_y[came, :].astype(f32)).astype(bf16)

        row_loop(half, 32, y_pair)
    back_near.wait_recv()
    gain_part[...] = jnp.zeros_like(gain_part)
    for i in range(2):
        back_over[i].wait_recv()

        def finish(here, j):
            at = pl.ds(pl.multiple_of(i * half + j * 32, 32), 32)
            unit, inverse = centred(hidden[at, :])
            grad = (part_x[at, :].astype(f32) + got_own[at, :].astype(f32)) + got_x[
                2 + i, here, :
            ].astype(f32)
            gain_part[...] += jnp.sum(grad * unit, axis=0, keepdims=True)
            grad_hidden[at, :] = cot[at, :].astype(f32) + norm_rows_back(
                grad * gain[...], unit, inverse
            )

        row_loop(half, 32, finish)
    for copy in [near, back_near, y_near] + over + far + back_far + back_over + y_far:
        copy.wait_send()
    for copy in saves:
        copy.wait()


def feed(hidden, gain, cot, cot_rows, w_up, w_down, far_up, far_down):
    f32, bf16 = jnp.float32, jnp.bfloat16
    rows, width = hidden.shape
    units = w_up.shape[1]
    count = lax.axis_size("seq")
    gathered = (count // 2, 2, width // count + width // count, units)
    any_ = pl.BlockSpec(memory_space=pl.ANY)
    vmem = pl.BlockSpec(memory_space=pltpu.VMEM)
    dma = pltpu.SemaphoreType.DMA
    return pl.pallas_call(
        feed_kernel,
        out_shape=[
            jax.ShapeDtypeStruct((rows, width), f32),
            jax.ShapeDtypeStruct((rows, width), bf16),
            jax.ShapeDtypeStruct((rows, width), f32),
            jax.ShapeDtypeStruct((1, width), f32),
            jax.ShapeDtypeStruct(gathered, bf16),
        ],
        in_specs=[vmem, vmem, vmem] + [any_] * 5,
        out_specs=[vmem] * 4 + [any_],
        scratch_shapes=[
            pltpu.VMEM((4 * rows, width), bf16),
            pltpu.VMEM((4 * rows, width), bf16),
            pltpu.VMEM((4 * rows, units), bf16),
            pltpu.VMEM((4 * rows, units), bf16),
            pltpu.VMEM((4 * rows, width), bf16),
            pltpu.VMEM((4 * rows, width), bf16),
            pltpu.VMEM((4, rows // 2, width), bf16),
            pltpu.VMEM((rows, width), bf16),
            pltpu.VMEM((2 * rows, width), bf16),
            pltpu.VMEM((rows, 512), f32),
            pltpu.VMEM((rows, 512), f32),
            pltpu.VMEM(gathered, bf16),
            pltpu.VMEM(w_up.shape, bf16),
            pltpu.VMEM(w_down.shape, bf16),
            dma((8,)),
            dma((1,)),
            dma((13,)),
            dma((13,)),
        ],
        compiler_params=pltpu.CompilerParams(
            collective_id=1, has_side_effects=True, vmem_limit_bytes=LIMIT
        ),
        cost_estimate=pl.CostEstimate(
            flops=75 * 10**9, bytes_accessed=30 * 10**6, transcendentals=2 * 10**6
        ),
        name="feed",
    )(hidden, gain, cot, cot_rows, w_up, w_down, far_up, far_down)


def retract_kernel(
    grad_hidden,
    y_send,
    w_out,
    q_in,
    k_in,
    v_in,
    gp_in,
    gn_in,
    gated_in,
    inv_in,
    p_in,
    r_in,
    cosine_all,
    sine_all,
    mask_all,
    q_scale_all,
    k_scale_all,
    decay_all,
    d_out,
    g_out,
    y_got,
    cosine,
    sine,
    mask,
    q_scale,
    k_scale,
    decay,
    dx,
    q,
    k,
    v,
    gp,
    gn,
    gated,
    inv,
    weights,
    entering,
    wo,
    dall,
    do,
    do_low,
    tile,
    grown,
    dk,
    dv,
    state,
    state_in,
    state_to,
    g_wo,
    load,
    save,
    save_rows,
    g_send,
    g_recv,
    c_send,
    c_recv,
    y_sems,
):
    f32, bf16 = jnp.float32, jnp.bfloat16
    depth, rows, width = dx.shape
    heads = mask.shape[0]
    hk, hv = q.shape[1], v.shape[1]
    s, z = lax.axis_index("seq"), lax.axis_index("mp")
    place = lax.rem(s, SEQ_DEVS)
    pair = z + 1 - 2 * lax.rem(z, 2)
    def tables(place, z):
        at = block(cosine.shape[0], place)
        some = pl.ds(z * heads, heads)
        return [
            (cosine_all.at[at], cosine),
            (sine_all.at[at], sine),
            (mask_all.at[some], mask),
            (q_scale_all.at[some], q_scale),
            (k_scale_all.at[some], k_scale),
            (decay_all.at[some], decay),
        ]

    loads = [
        pltpu.make_async_copy(a, b, load.at[i])
        for i, (a, b) in enumerate(
            [
                (w_out, wo),
                (q_in, q),
                (k_in, k),
                (v_in, v),
                (gp_in, gp),
                (gn_in, gn),
                (gated_in, gated),
                (inv_in, inv),
                (p_in, weights),
                (r_in, entering),
            ]
            + tables(place, z)
        )
    ]
    for copy in loads:
        copy.start()

    def low(here, i):
        dx[z, here, :] = grad_hidden[here, :].astype(bf16)

    def ready(part):
        row_loop(rows // HALVES, 32, lambda here, i: low(
            pl.ds(pl.multiple_of(part * (rows // HALVES) + i * 32, 32), 32), i))

    greet(
        [
            (z > 0, s, z - 1),
            (z < depth - 1, s, z + 1),
            (place > 0, s - 1, z),
            (place < SEQ_DEVS - 1, s + 1, z),
        ]
    )

    @pl.when(place == SEQ_DEVS - 1)
    def _():
        state_in[...] = jnp.zeros_like(state_in)

    def turn_back(value, at, start):
        c, sn = cosine[at, :], sine[at, :]
        half = DK // 2
        a, b = value[:, :half], value[:, half:]
        dall[at, start : start + half] = (a * c + b * sn).astype(bf16)
        dall[at, start + half : start + DK] = (b * c - a * sn).astype(bf16)

    def use(j):
        at = block(rows, j)

        @pl.when(j == z)
        def _():
            for copy in loads:
                copy.wait()

        for h in range(heads):
            wide = slice(h * DV, (h + 1) * DV)
            tile[...] = product_rt(dx[j], wo[wide, :])

            def gate_back(here, i):
                there = pl.ds(pl.multiple_of(j * rows + i * 32, 32), 32)
                grad = tile[here, :]
                gate = gp[there, wide]
                unit = gn[there, wide]
                open_ = 1.0 / (1.0 + jnp.exp(-gate))
                slope = open_ * (1.0 + gate * (1.0 - open_))
                first = 2 * hk + hv + h * DV
                dall[there, first : first + DV] = (grad * unit * slope).astype(bf16)
                inverse = inv[h, there, :][:, :1]
                value = norm_rows_back(grad * gate * open_, unit, inverse)
                high = value.astype(bf16)
                do[there, wide] = high
                do_low[here, wide] = (value - high.astype(f32)).astype(bf16)

            row_loop(rows, 32, gate_back)
        for h in range(heads):
            cols = slice(h * DK, (h + 1) * DK)
            wide = slice(h * DV, (h + 1) * DV)
            qd = (q[at, cols].astype(f32) * q_scale[h]).astype(bf16)
            grown[h, j] = product_t(qd, do[at, wide])

        @pl.when(j != last)
        def _():
            rest(j)

    last = jnp.where(z < depth // 2, depth - 1, 0)

    def rest(j):
        at = block(rows, j)
        for h in range(heads):
            cols = slice(h * DK, (h + 1) * DK)
            wide = slice(h * DV, (h + 1) * DV)
            qb, kb, vb, db = q[at, cols], k[at, cols], v[at, wide], do[at, wide]
            raw = product_rt(db, vb) + product_rt(do_low[:, wide], vb)
            ds = (raw * mask[h]).astype(bf16)
            dv[at, wide] = product_t(weights[h, j], db)
            dk[at, cols] = product_t(ds, qb)
            turn_back(dot(ds, kb) + q_scale[h] * product_rt(db, entering[h, j]), at, h * DK)

    def chain(h, to):
        return remote(state_to.at[h], state_in.at[h], c_send.at[h], c_recv.at[h], to, z)

    line_gather(dx, g_send, g_recv, s, z, depth, use, ready)
    swap = remote(y_send, y_got, y_sems.at[0], y_sems.at[1], s, pair)
    swap.start()
    def out_terms(m, _):
        cols = pl.ds(pl.multiple_of(m * 256, 256), 256)
        for n in range(0, width, 512):
            right = dx[:, :, n : n + 512].reshape(depth * rows, 512)
            g_wo[cols, n : n + 512] = product_t(gated[:, cols], right).astype(bf16)
        return 0

    def out_grad():
        lax.fori_loop(0, hv // 256, out_terms, 0)

    for h in range(heads):
        state[h] = grown[h, depth - 1]
        for b in reversed(range(depth - 1)):
            state[h] = decay[h, 0] * state[h] + grown[h, b]

        @pl.when(place == SEQ_DEVS - 1)
        def _():
            state_to[h] = state[h].astype(bf16)
            chain(h, s - 1).start()

    rest(last)

    @pl.when(place == 0)
    def _():
        out_grad()

    for h in range(heads):

        @pl.when(place < SEQ_DEVS - 1)
        def _():
            chain(h, s + 1).wait_recv()

        @pl.when((place > 0) & (place < SEQ_DEVS - 1))
        def _():
            state_to[h] = (decay[h, 1] * state_in[h].astype(f32) + state[h]).astype(bf16)
            chain(h, s - 1).start()

    for h in range(heads):
        state[h] = state_in[h].astype(f32)

    def done(b):
        at = block(rows, b)
        return pltpu.make_async_copy(dall.at[at], d_out.at[at], save_rows.at[b])

    def cross(turn, _):
        b = depth - 1 - turn
        at = block(rows, b)
        for h in range(heads):
            cols = slice(h * DK, (h + 1) * DK)
            wide = slice(h * DV, (h + 1) * DV)
            leaving = state[h].astype(bf16)
            state[h] = grown[h, b] + decay[h, 0] * state[h]
            kb = k[at, cols]
            vd = (v[at, wide].astype(f32) * k_scale[h]).astype(bf16)
            turn_back(dk[at, cols] + product_rt(vd, leaving), at, hk + h * DK)
            dall[at, 2 * hk + h * DV : 2 * hk + (h + 1) * DV] = (
                dv[at, wide] + k_scale[h] * dot(kb, leaving)
            ).astype(bf16)
        done(b).start()
        return 0

    lax.fori_loop(0, depth, cross, 0)
    saves = [pltpu.make_async_copy(g_wo, g_out, save.at[0])]

    @pl.when(place > 0)
    def _():
        out_grad()

    saves[0].start()
    lax.fori_loop(0, depth, lambda b, c: (done(b).wait(), c)[1], 0)
    line_gather_end(dx, g_send, g_recv, s, z, depth)

    @pl.when(place > 0)
    def _():
        for h in range(heads):
            chain(h, s - 1).wait_send()

    swap.wait()
    for copy in saves:
        copy.wait()


def retract(
    grad_hidden, y_send, w_out, q, k, v, gp, gn, gated, inv, p, r, cosine, sine, mask, q_scale, k_scale, decay
):
    f32, bf16 = jnp.float32, jnp.bfloat16
    depth = lax.axis_size("mp")
    rows, width = grad_hidden.shape
    span = depth * rows
    heads = q.shape[1] // DK
    hk, hv = q.shape[1], v.shape[1]
    any_ = pl.BlockSpec(memory_space=pl.ANY)
    vmem = pl.BlockSpec(memory_space=pltpu.VMEM)
    dma = pltpu.SemaphoreType.DMA
    return pl.pallas_call(
        retract_kernel,
        out_shape=[
            jax.ShapeDtypeStruct((span, 2 * hk + 2 * hv), bf16),
            jax.ShapeDtypeStruct((hv, width), bf16),
            jax.ShapeDtypeStruct((rows, width), bf16),
        ],
        in_specs=[vmem] + [any_] * 17,
        out_specs=[any_] * 3,
        scratch_shapes=[
            pltpu.VMEM((span, DK // 2), f32),
            pltpu.VMEM((span, DK // 2), f32),
            pltpu.VMEM((heads, rows, rows), f32),
            pltpu.VMEM((heads, rows, 1), f32),
            pltpu.VMEM((heads, rows, 1), f32),
            pltpu.VMEM((heads, 2, 1, DV), f32),
            pltpu.VMEM((depth, rows, width), bf16),
            pltpu.VMEM((span, hk), bf16),
            pltpu.VMEM((span, hk), bf16),
            pltpu.VMEM((span, hv), bf16),
            pltpu.VMEM((span, hv), f32),
            pltpu.VMEM((span, hv), f32),
            pltpu.VMEM((span, hv), bf16),
            pltpu.VMEM((heads, span, 128), f32),
            pltpu.VMEM((heads, depth, rows, rows), bf16),
            pltpu.VMEM((heads, depth, DK, DV), bf16),
            pltpu.VMEM(w_out.shape, bf16),
            pltpu.VMEM((span, 2 * hk + 2 * hv), bf16),
            pltpu.VMEM((span, hv), bf16),
            pltpu.VMEM((rows, hv), bf16),
            pltpu.VMEM((rows, DV), f32),
            pltpu.VMEM((heads, depth, DK, DV), f32),
            pltpu.VMEM((span, hk), f32),
            pltpu.VMEM((span, hv), f32),
            pltpu.VMEM((heads, DK, DV), f32),
            pltpu.VMEM((heads, DK, DV), bf16),
            pltpu.VMEM((heads, DK, DV), bf16),
            pltpu.VMEM((hv, width), bf16),
            dma((16,)),
            dma((1,)),
            dma((depth,)),
            dma((2, depth, HALVES)),
            dma((depth, HALVES)),
            dma((heads,)),
            dma((heads,)),
            dma((2,)),
        ],
        compiler_params=pltpu.CompilerParams(
            collective_id=2, has_side_effects=True, vmem_limit_bytes=LIMIT
        ),
        cost_estimate=pl.CostEstimate(
            flops=120 * 10**9, bytes_accessed=40 * 10**6, transcendentals=2 * 10**6
        ),
        name="retract",
    )(grad_hidden, y_send, w_out, q, k, v, gp, gn, gated, inv, p, r, cosine, sine, mask, q_scale, k_scale, decay)


def flip(index, bit):
    return index + bit - 2 * bit * lax.rem(index // bit, 2)


def pair_kernel(
    x, d, wo_parts, far, out, far_got, stage, got, wo_mine, wo_got, result, save, send, recv, w_sems, f_sems
):
    f32, bf16 = jnp.float32, jnp.bfloat16
    _, chips, rows, _ = stage.shape
    few = wo_mine.shape[1]
    third = result.shape[2]
    s, z = lax.axis_index("seq"), lax.axis_index("mp")
    core = lax.rem(s, 2)
    twin = flip(s, 1)
    across = flip(z, 2)
    edge = (z == 0) | (z == lax.axis_size("mp") - 1)
    greet([(z >= 0, twin, z), (z >= 0, s, across), (z >= 0, twin, across)])
    crossed = remote(far.at[0], far_got, f_sems.at[0], f_sems.at[1], twin, across)
    straight = remote(far.at[1], far_got, f_sems.at[2], f_sems.at[3], s, across)

    @pl.when(edge & (core == 1))
    def _():
        crossed.start()
        straight.start()

    wo_load = pltpu.make_async_copy(wo_parts.at[:, core], wo_mine, w_sems.at[0])
    wo_load.start()
    wo_send = remote(wo_parts.at[:, 1 - core], wo_got, w_sems.at[1], w_sems.at[2], twin, z)
    wo_send.start()
    span = max(256, 2 * rows)
    each = span // (2 * rows)

    def give(i):
        return remote(stage.at[1 - core, i], got.at[i], send.at[i], recv.at[i], twin, z)

    def keep(i):
        return pltpu.make_async_copy(result.at[i], out.at[i], save.at[i])

    def take(i):
        give(i).wait_recv()
        for t in range(d.shape[1] // third):

            def add(here, r):
                there = pl.ds(pl.multiple_of(t * rows + r * 32, 32), 32)
                cols = slice(t * third, (t + 1) * third)
                result[i, there, :] = (
                    stage[core, i, here, cols].astype(f32) + got[i, here, cols].astype(f32)
                ).astype(bf16)

            row_loop(rows, 32, add)

    def one(g, _):
        for c in range(span // 256):
            chunk = g * (span // 256) + c
            cols = pl.ds(pl.multiple_of(chunk * 256, 256), 256)
            for n in range(0, d.shape[1], 1024):
                value = product_t(x[:, cols], d[:, n : n + 1024]).astype(bf16)
                for part in range(max(1, 256 // rows)):
                    to = (c if each == 1 and rows >= 256 else part) % 2
                    i = g * each + (0 if rows >= 256 else part // 2)
                    stage[to, i, :, n : n + 1024] = value[part * rows : (part + 1) * rows]
        for e in range(each):
            give(g * each + e).start()

        @pl.when(g > 0)
        def _():
            for e in range(each):
                take((g - 1) * each + e)

        return 0

    groups = chips // each
    lax.fori_loop(0, groups, one, 0)
    wo_load.wait()
    wo_send.wait()
    base = rows * (d.shape[1] // third)

    def wo_add(i, _):
        for t in range(wo_mine.shape[2] // third):
            cols = slice(t * third, (t + 1) * third)
            result[i, base + t * few : base + (t + 1) * few, :] = (
                wo_mine[i, :, cols].astype(f32) + wo_got[i, :, cols].astype(f32)
            ).astype(bf16)
        return 0

    lax.fori_loop(0, chips, wo_add, 0)
    for e in range(each):
        take((groups - 1) * each + e)

    def begin(i, _):
        keep(i).start()
        return 0

    def end(i, _):
        keep(i).wait()
        give(i).wait_send()
        return 0

    lax.fori_loop(0, chips, begin, 0)
    lax.fori_loop(0, chips, end, 0)

    @pl.when(edge & (core == 1))
    def _():
        crossed.wait_send()
        straight.wait_send()

    @pl.when(jnp.logical_not(edge) & (core == 0))
    def _():
        crossed.wait_recv()

    @pl.when(jnp.logical_not(edge) & (core == 1))
    def _():
        straight.wait_recv()


def pair_sum(x, d, g_out, far):
    bf16 = jnp.bfloat16
    count = lax.axis_size("seq")
    chips = count // 2
    rows, few = x.shape[1] // count, g_out.shape[0] // count
    wide, third = d.shape[1], d.shape[1] // 3
    high = 3 * rows + few * g_out.shape[1] // third
    any_ = pl.BlockSpec(memory_space=pl.ANY)
    vmem = pl.BlockSpec(memory_space=pltpu.VMEM)
    dma = pltpu.SemaphoreType.DMA
    return pl.pallas_call(
        pair_kernel,
        out_shape=[
            jax.ShapeDtypeStruct((chips, high, third), bf16),
            jax.ShapeDtypeStruct(far.shape[1:], bf16),
        ],
        in_specs=[vmem, vmem, any_, any_],
        out_specs=[any_, any_],
        scratch_shapes=[
            pltpu.VMEM((2, chips, rows, wide), bf16),
            pltpu.VMEM((chips, rows, wide), bf16),
            pltpu.VMEM((chips, few, g_out.shape[1]), bf16),
            pltpu.VMEM((chips, few, g_out.shape[1]), bf16),
            pltpu.VMEM((chips, high, third), bf16),
            dma((chips,)),
            dma((chips,)),
            dma((chips,)),
            dma((3,)),
            dma((4,)),
        ],
        compiler_params=pltpu.CompilerParams(
            collective_id=3, has_side_effects=True, vmem_limit_bytes=LIMIT
        ),
        cost_estimate=pl.CostEstimate(
            flops=25 * 10**9, bytes_accessed=30 * 10**6, transcendentals=0
        ),
        name="pair_sum",
    )(x, d, g_out.reshape(chips, 2, few, g_out.shape[1]), far)


def finish_kernel(
    d_in,
    x_in,
    tok_in,
    gain,
    gain_part,
    grad_hidden_in,
    w_query,
    w_key,
    w_value,
    w_gate,
    far,
    far_got,
    grad_tok,
    gains,
    g_up,
    g_down,
    d,
    x,
    tok,
    grad_hidden,
    sbuf,
    rbuf,
    total,
    wq,
    wk,
    wv,
    wg,
    mine,
    other,
    gain_all,
    gain_line,
    load,
    d_load,
    x_load,
    s_send,
    s_recv,
    f_sems,
    h_send,
    h_recv,
    l_send,
    l_recv,
):
    f32, bf16 = jnp.float32, jnp.bfloat16
    depth, rows, width = x.shape
    s, z = lax.axis_index("seq"), lax.axis_index("mp")
    core = lax.rem(s, 2)
    twin, across = flip(s, 1), flip(z, 2)
    count = lax.axis_size("seq")
    loads = [
        pltpu.make_async_copy(a, b, load.at[i])
        for i, (a, b) in enumerate(
            [(w_query, wq), (w_key, wk), (w_value, wv), (w_gate, wg)]
        )
    ]

    def slot_loads(j):
        at = block(rows, j)
        return [
            pltpu.make_async_copy(d_in.at[at], d.at[at], d_load.at[j]),
            pltpu.make_async_copy(x_in.at[j], x.at[j], x_load.at[j]),
        ]

    late = [
        pltpu.make_async_copy(a, b, load.at[4 + i])
        for i, (a, b) in enumerate([(tok_in, tok), (grad_hidden_in, grad_hidden)])
    ]
    for copy in loads:
        copy.start()

    def pull(i, _):
        for copy in slot_loads(jnp.where(z < depth // 2, depth - 1 - i, i)):
            copy.start()
        return 0

    lax.fori_loop(0, depth, pull, 0)
    for copy in late:
        copy.start()
    gains[...] = jnp.zeros_like(gains)
    gains[1:2, :] = gain_part[...]
    greet(
        [(z >= 0, twin, across)]
        + [(z != other, s, other) for other in range(depth)]
        + [(s != other, other, z) for other in range(count)]
    )
    near = remote(far.at[1], other, f_sems.at[0], f_sems.at[1], twin, z)
    crossed = remote(far.at[0], other, f_sems.at[0], f_sems.at[1], twin, across)
    straight = remote(far.at[1], mine, f_sems.at[2], f_sems.at[3], s, across)
    edge = (z == 0) | (z == depth - 1)
    inner = jnp.logical_not(edge)
    local = pltpu.make_async_copy(far.at[0], mine, f_sems.at[4])
    to_other = pltpu.make_async_copy(far_got, other, f_sems.at[5])
    to_mine = pltpu.make_async_copy(far_got, mine, f_sems.at[5])

    @pl.when(core == 0)
    def _():
        near.start()
        local.start()

    @pl.when(inner & (core == 0))
    def _():
        to_other.start()

    @pl.when(inner & (core == 1))
    def _():
        to_mine.start()
        crossed.start()
        straight.start()

    for copy in loads:
        copy.wait()
    step = 512
    starts, at_col = [], 0
    for w in (wq, wk, wv, wg):
        starts.append((w, at_col, at_col + w.shape[1]))
        at_col += w.shape[1]

    def term(j, n):
        at = block(rows, j)
        value = None
        for w, a, b in starts:
            one = product_rt(d[at, a:b], w[n : n + step, :])
            value = one if value is None else value + one
        gains[0:1, n : n + step] += jnp.sum(
            value * x[j, :, n : n + step].astype(f32), axis=0, keepdims=True
        )
        return value

    def partial(j):
        for copy in slot_loads(j):
            copy.wait()
        for n in range(0, width, step):
            sbuf[j, :, n : n + step] = term(j, n).astype(bf16)

    def plane(to):
        return remote(gain_all.at[s], gain_all.at[s], h_send.at[to], h_recv.at[s], to, z)

    def line(to):
        return remote(gain_line.at[z], gain_line.at[z], l_send.at[to], l_recv.at[z], s, to)

    def others(count, me, act):
        def one(i, _):
            @pl.when(i != me)
            def _():
                act(i)

            return 0

        lax.fori_loop(0, count, one, 0)

    def own():
        for copy in slot_loads(z):
            copy.wait()
        for n in range(0, width, step):
            total[:, n : n + step] = term(z, n)
        gains[0:1, :] = gains[0:1, :] / gain[...]
        gain_all[s] = gains[...]
        others(count, s, lambda to: plane(to).start())

    line_scatter(sbuf, rbuf, total, s_send, s_recv, s, z, depth, partial, own)

    def plane_came(i):
        remote(gain_all.at[i], gain_all.at[i], h_send.at[i], h_recv.at[i], twin, z).wait_recv()

    def line_came(i):
        remote(gain_line.at[i], gain_line.at[i], l_send.at[i], l_recv.at[i], s, across).wait_recv()

    others(count, s, plane_came)
    gains[...] = gain_all[0]
    for i in range(1, count):
        gains[...] += gain_all[i]
    gain_line[z] = gains[...]
    others(depth, z, lambda to: line(to).start())

    for copy in late:
        copy.wait()

    def last(here, i):
        unit, inverse = centred(tok[here, :].astype(f32))
        grad_tok[here, :] = (
            grad_hidden[here, :] + norm_rows_back(total[here, :] * gain[...], unit, inverse)
        ).astype(bf16)

    row_loop(rows, 32, last)
    others(depth, z, line_came)
    gains[...] = gain_line[0]
    for i in range(1, depth):
        gains[...] += gain_line[i]
    others(count, s, lambda to: plane(to).wait_send())
    others(depth, z, lambda to: line(to).wait_send())

    @pl.when(core == 0)
    def _():
        near.wait_send()
        local.wait()

    @pl.when(core == 1)
    def _():
        near.wait_recv()

    @pl.when(inner & (core == 0))
    def _():
        to_other.wait()

    @pl.when(edge & (core == 0))
    def _():
        crossed.wait_recv()

    @pl.when(inner & (core == 1))
    def _():
        to_mine.wait()
        crossed.wait_send()
        straight.wait_send()

    @pl.when(edge & (core == 1))
    def _():
        straight.wait_recv()

    high, few = g_up.shape[0], g_down.shape[0]
    third = g_up.shape[1]

    g_up[...] = mine[0:high, :].astype(f32) + other[0:high, :].astype(f32)
    for t in range(g_down.shape[1] // third):
        at = slice(high + t * few, high + (t + 1) * few)
        g_down[:, t * third : (t + 1) * third] = mine[at, :].astype(f32) + other[at, :].astype(f32)


def finish(d, x, tok, gain, gain_part, grad_hidden, w_query, w_key, w_value, w_gate, far, far_got):
    f32, bf16 = jnp.float32, jnp.bfloat16
    depth, rows, width = x.shape
    count = lax.axis_size("seq")
    units = far.shape[2]
    any_ = pl.BlockSpec(memory_space=pl.ANY)
    vmem = pl.BlockSpec(memory_space=pltpu.VMEM)
    dma = pltpu.SemaphoreType.DMA
    return pl.pallas_call(
        finish_kernel,
        out_shape=[
            jax.ShapeDtypeStruct((rows, width), bf16),
            jax.ShapeDtypeStruct((8, width), f32),
            jax.ShapeDtypeStruct((width // count, units), f32),
            jax.ShapeDtypeStruct((units // count, width), f32),
        ],
        in_specs=[any_] * 3 + [vmem] * 2 + [any_] * 7,
        out_specs=[vmem] * 4,
        scratch_shapes=[
            pltpu.VMEM(d.shape, bf16),
            pltpu.VMEM(x.shape, bf16),
            pltpu.VMEM((rows, width), bf16),
            pltpu.VMEM((rows, width), f32),
            pltpu.VMEM((depth, rows, width), bf16),
            pltpu.VMEM((depth + 1, rows, width), bf16),
            pltpu.VMEM((rows, width), f32),
            pltpu.VMEM(w_query.shape, bf16),
            pltpu.VMEM(w_key.shape, bf16),
            pltpu.VMEM(w_value.shape, bf16),
            pltpu.VMEM(w_gate.shape, bf16),
            pltpu.VMEM(far.shape[1:], bf16),
            pltpu.VMEM(far.shape[1:], bf16),
            pltpu.VMEM((count, 8, width), f32),
            pltpu.VMEM((depth, 8, width), f32),
            dma((6,)),
            dma((depth,)),
            dma((depth,)),
            dma((depth, HALVES)),
            dma((depth + 1, HALVES)),
            dma((6,)),
            dma((count,)),
            dma((count,)),
            dma((depth,)),
            dma((depth,)),
        ],
        compiler_params=pltpu.CompilerParams(
            collective_id=4, has_side_effects=True, vmem_limit_bytes=LIMIT
        ),
        cost_estimate=pl.CostEstimate(
            flops=110 * 10**9, bytes_accessed=30 * 10**6, transcendentals=0
        ),
        name="finish",
    )(d, x, tok, gain, gain_part, grad_hidden, w_query, w_key, w_value, w_gate, far, far_got)


def unpack_kernel(summed, tok, up, down, query, key, value, gate, out, tok_out, up_out, down_out):
    f32 = jnp.float32
    rows, wide = query.shape
    few, tall = out.shape[0], value.shape[1]
    query[...] = summed[0:rows, 0:wide].astype(f32)
    key[...] = summed[0:rows, wide : 2 * wide].astype(f32)
    value[...] = summed[rows : 2 * rows, :].astype(f32)
    gate[...] = summed[2 * rows : 3 * rows, :].astype(f32)
    for t in range(out.shape[1] // tall):
        at = slice(3 * rows + t * few, 3 * rows + (t + 1) * few)
        out[:, t * tall : (t + 1) * tall] = summed[at, :].astype(f32)
    tok_out[...] = tok[...]
    up_out[...] = up[...]
    down_out[...] = down[...]


def unpack(summed, tok, up, down, wide):
    f32 = jnp.float32
    count = lax.axis_size("seq")
    width, tall = tok.shape[1], summed.shape[1]
    rows, few = width // count, tall // count
    shapes = [(rows, wide)] * 2 + [(rows, tall)] * 2 + [(few, width)]
    return pl.pallas_call(
        unpack_kernel,
        out_shape=[jax.ShapeDtypeStruct(one, f32) for one in shapes]
        + [jax.ShapeDtypeStruct(a.shape, a.dtype) for a in (tok, up, down)],
        compiler_params=pltpu.CompilerParams(vmem_limit_bytes=LIMIT),
        name="unpack",
    )(summed, tok, up, down)


def shards(
    tokens, gain_mix, w_query, w_key, w_value, w_gate, w_out, gain_ffn, w_up, w_down, cotangent
):
    bf16 = jnp.bfloat16
    f32 = jnp.float32
    span_rows = lax.axis_size("mp") * tokens.shape[0]
    local_heads = w_query.shape[1] // DK
    trig = decay_tables(span_rows, local_heads * lax.axis_size("mp"))
    (
        x_rows,
        q_all,
        k_all,
        v_all,
        gate,
        unit,
        gated,
        inverse,
        weights,
        entering,
        hidden,
        cot_rows,
        far_up,
        far_down,
    ) = attend(
        tokens, gain_mix[None, :], cotangent, w_query, w_key, w_value, w_gate, w_out, w_up, w_down, *trig
    )
    y_keep, y_send, grad_hidden, gain_ffn_part, grad_ffn = feed(
        hidden, gain_ffn[None, :], cotangent, cot_rows, w_up, w_down, far_up, far_down
    )
    far = lax.psum_scatter(
        grad_ffn, "seq", scatter_dimension=0, tiled=False, axis_index_groups=same_core()
    )
    grad_in, grad_out_w, y_got = retract(
        grad_hidden, y_send, w_out, q_all, k_all, v_all, gate, unit, gated, inverse, weights, entering, *trig
    )
    output = (y_keep + y_got.astype(f32)).astype(bf16)
    pairs, far_got = pair_sum(x_rows.reshape(span_rows, -1), grad_in, grad_out_w, far)
    summed = lax.psum_scatter(
        pairs, "seq", scatter_dimension=0, tiled=False, axis_index_groups=same_core()
    )
    grad_in, pairs = lax.optimization_barrier((grad_in, pairs))
    grad_tokens, gains, final_up, final_down = finish(
        grad_in, x_rows, tokens, gain_mix[None, :], gain_ffn_part, grad_hidden, w_query, w_key, w_value, w_gate, far, far_got
    )
    summed, gains = lax.optimization_barrier((summed, gains))
    gain_mix_sum, gain_ffn_sum = gains[0], gains[1]
    (
        final_query,
        final_key,
        final_value,
        final_gate,
        final_out,
        grad_tokens,
        final_up,
        final_down,
    ) = unpack(summed, grad_tokens, final_up, final_down, w_query.shape[1])
    return (
        output,
        grad_tokens,
        gain_mix_sum,
        final_query,
        final_key,
        final_value,
        final_gate,
        final_out,
        gain_ffn_sum,
        final_up,
        final_down,
    )


def solution(mesh):
    return jax.shard_map(
        shards,
        mesh=mesh,
        in_specs=(
            P(("seq", "mp"), None),
            P(),
            P(None, "mp"),
            P(None, "mp"),
            P(None, "mp"),
            P(None, "mp"),
            P("mp", None),
            P(),
            P(None, "mp"),
            P("mp", None),
            P(("seq", "mp"), None),
        ),
        out_specs=(
            P(("seq", "mp"), None),
            P(("seq", "mp"), None),
            P(),
            P("seq", "mp"),
            P("seq", "mp"),
            P("seq", "mp"),
            P("seq", "mp"),
            P(("mp", "seq"), None),
            P(),
            P("seq", "mp"),
            P(("mp", "seq"), None),
        ),
        check_vma=False,
    )
```

```python
import math

import jax
import jax.numpy as jnp
import numpy as np
from jax import lax
from jax.experimental import pallas as pl
from jax.experimental.pallas import tpu as pltpu
from jax.sharding import PartitionSpec as P

DK = 256
DV = 512
STRETCH = 256
SEQ_DEVS = 4


eps = 1e-05


def same_core():
    count = lax.axis_size("seq")
    return [list(range(core, count, 2)) for core in range(2)]


def decay_tables(span_rows, heads):
    half = DK // 2
    f32 = np.float32
    freq = np.exp(f32(-math.log(10000.0)) * np.arange(half, dtype=f32) / f32(half - 1)).astype(f32)
    phase = np.arange(SEQ_DEVS * span_rows, dtype=f32)[:, None] * freq[None, :]
    phase = phase.astype(np.float64)
    logs = np.log1p(-np.exp2(-5.0 - np.arange(heads)))
    steps = np.arange(STRETCH)
    gaps = steps[:, None] - steps[None, :]
    mask = np.where(gaps >= 0, np.exp(logs[:, None, None] * np.maximum(gaps, 0)), 0.0)
    q_scale = np.exp(logs[:, None] * (steps + 1))[:, :, None]
    k_scale = np.exp(logs[:, None] * (STRETCH - 1 - steps))[:, :, None]
    decay = np.exp(logs[:, None] * np.array([STRETCH, span_rows]))[:, :, None, None]
    decay = np.broadcast_to(decay, (heads, 2, 1, DV))
    return tuple(
        jnp.asarray(a.astype(f32))
        for a in (np.cos(phase), np.sin(phase), mask, q_scale, k_scale, decay)
    )


def product_t(left, right):
    return lax.dot_general(
        left, right, (((0,), (0,)), ((), ())), preferred_element_type=jnp.float32
    )


def product_rt(left, right):
    return lax.dot_general(
        left, right, (((1,), (1,)), ((), ())), preferred_element_type=jnp.float32
    )


MESH = pl.DeviceIdType.MESH
LIMIT = 62 * 1024 * 1024


def remote(src, dst, send, recv, s, z):
    return pltpu.make_async_remote_copy(
        src_ref=src,
        dst_ref=dst,
        send_sem=send,
        recv_sem=recv,
        device_id=(s, z),
        device_id_type=MESH,
    )


def greet(partners):
    barrier = pltpu.get_barrier_semaphore()
    count = 0
    for present, s, z in partners:

        @pl.when(present)
        def _():
            pl.semaphore_signal(barrier, inc=1, device_id=(s, z), device_id_type=MESH)

        count = count + jnp.where(present, 1, 0)
    pl.semaphore_wait(barrier, count)


def dot(left, right):
    return jnp.dot(left, right, preferred_element_type=jnp.float32)


HALVES = 2


def part_of(rows, part):
    return pl.ds(part * (rows // HALVES), rows // HALVES)


def line_copy(x, send, recv, s, to, slot, part, way):
    at = x.at[slot, part_of(x.shape[1], part)]
    return remote(at, at, send.at[way, slot, part], recv.at[slot, part], s, to)


def line_gather(x, send, recv, s, z, depth, use, ready, after=None):
    def right(slot, part):
        return line_copy(x, send, recv, s, z + 1, slot, part, 0)

    def left(slot, part):
        return line_copy(x, send, recv, s, z - 1, slot, part, 1)

    for part in range(HALVES):
        ready(part)

        @pl.when(z < depth - 1)
        def _():
            right(z, part).start()

        @pl.when(z > 0)
        def _():
            left(z, part).start()

    def one(turn, _):
        away = (turn + 1) // 2
        low, high = z - away, z + away
        for part in range(HALVES):

            @pl.when((turn % 2 == 1) & (low >= 0))
            def _():
                line_copy(x, send, recv, s, z - 1, low, part, 0).wait_recv()

                @pl.when(z < depth - 1)
                def _():
                    right(low, part).start()

            @pl.when((turn % 2 == 1) & (high < depth))
            def _():
                line_copy(x, send, recv, s, z + 1, high, part, 1).wait_recv()

                @pl.when(z > 0)
                def _():
                    left(high, part).start()

        if after is not None:
            after(turn)
        slot = jnp.where(turn % 2 == 1, low, high)

        @pl.when((slot >= 0) & (slot < depth))
        def _():
            use(slot)

        return 0

    lax.fori_loop(0, 2 * depth - 1, one, 0)


def line_gather_end(x, send, recv, s, z, depth):
    def one(slot, _):
        for part in range(HALVES):

            @pl.when((slot <= z) & (z < depth - 1))
            def _():
                line_copy(x, send, recv, s, z + 1, slot, part, 0).wait_send()

            @pl.when((slot >= z) & (z > 0))
            def _():
                line_copy(x, send, recv, s, z - 1, slot, part, 1).wait_send()

        return 0

    lax.fori_loop(0, depth, one, 0)


def add_rows(into, other):
    step = 32

    def one(i, _):
        rows = pl.ds(pl.multiple_of(i * step, step), step)
        into[rows, :] = (
            into[rows, :].astype(jnp.float32) + other[rows, :].astype(jnp.float32)
        ).astype(into.dtype)
        return 0

    lax.fori_loop(0, into.shape[0] // step, one, 0)


def line_scatter(sbuf, rbuf, total, send, recv, s, z, depth, partial, own, hook=None):
    rows = total.shape[0]

    def right(j, part):
        at = part_of(rows, part)
        return remote(
            sbuf.at[j, at], rbuf.at[j, at], send.at[j, part], recv.at[j, part], s, z + 1
        )

    def left(j, part):
        at = part_of(rows, part)
        slot = jnp.where(j == z - 1, depth, j)
        return remote(
            sbuf.at[j, at], rbuf.at[slot, at], send.at[j, part], recv.at[slot, part], s, z - 1
        )

    def arrived(slot, part, sender):
        at = part_of(rows, part)
        remote(
            sbuf.at[0, at], rbuf.at[slot, at], send.at[0, part], recv.at[slot, part], s, sender
        ).wait_recv()

    def first(turn, _):
        up = depth - 1 + z - turn // 2
        down = turn // 2 - (depth - 1) + z
        j = jnp.where(turn % 2 == 0, up, down)
        valid = jnp.where(turn % 2 == 0, (up > z) & (up < depth), (down >= 0) & (down < z))

        @pl.when(valid)
        def _():
            partial(j)

            @pl.when((z == 0) & (j > z))
            def _():
                for part in range(HALVES):
                    right(j, part).start()

            @pl.when((z == depth - 1) & (j < z))
            def _():
                for part in range(HALVES):
                    left(j, part).start()

        return 0

    lax.fori_loop(0, 2 * (depth - 1), first, 0)
    own()

    def event(turn, _):
        up = depth - 1 + z - turn
        down = turn - (depth - 1) + z
        slot = jnp.where(down == z, depth, down)
        for part in range(HALVES):
            at = part_of(rows, part)

            @pl.when((z > 0) & (up >= z) & (up < depth))
            def _():
                arrived(up, part, z - 1)

                @pl.when(up > z)
                def _():
                    add_rows(sbuf.at[up, at], rbuf.at[up, at])
                    right(up, part).start()

                @pl.when(up == z)
                def _():
                    add_rows(total.at[at], rbuf.at[up, at])

            @pl.when((z < depth - 1) & (down >= 0) & (down <= z))
            def _():
                arrived(slot, part, z + 1)

                @pl.when(down < z)
                def _():
                    add_rows(sbuf.at[down, at], rbuf.at[down, at])
                    left(down, part).start()

                @pl.when(down == z)
                def _():
                    add_rows(total.at[at], rbuf.at[depth, at])

        if hook is not None:
            hook(turn)
        return 0

    lax.fori_loop(0, depth, event, 0)

    def end(j, _):
        for part in range(HALVES):

            @pl.when(j > z)
            def _():
                right(j, part).wait_send()

            @pl.when(j < z)
            def _():
                left(j, part).wait_send()

        return 0

    lax.fori_loop(0, depth, end, 0)


def centred(rows):
    centre = rows - jnp.mean(rows, axis=-1, keepdims=True)
    inverse = lax.rsqrt(jnp.mean(centre * centre, axis=-1, keepdims=True) + eps)
    return centre * inverse, inverse


def block(rows, index):
    return pl.ds(pl.multiple_of(index * rows, rows), rows)


def attend_kernel(
    tok,
    gain,
    cot,
    w_query,
    w_key,
    w_value,
    w_gate,
    w_out,
    w_up,
    w_down,
    cosine_all,
    sine_all,
    mask_all,
    q_scale_all,
    k_scale_all,
    decay_all,
    x_out,
    q_out,
    k_out,
    v_out,
    gp_out,
    gn_out,
    gated_out,
    inv_out,
    p_out,
    r_out,
    hidden_out,
    cot_rows,
    far_up,
    far_down,
    cosine,
    sine,
    mask,
    q_scale,
    k_scale,
    decay,
    xg,
    q,
    k,
    v,
    gp,
    gn,
    gated,
    inv,
    weights,
    grown,
    entering,
    tile,
    state,
    state_in,
    state_to,
    rbuf,
    total,
    wq,
    wk,
    wv,
    wg,
    wo,
    load,
    save,
    g_send,
    g_recv,
    s_send,
    s_recv,
    c_send,
    c_recv,
    x_send,
    x_recv,
    f_send,
    f_recv,
    p_send,
    p_recv,
):
    f32, bf16 = jnp.float32, jnp.bfloat16
    depth = xg.shape[0]
    rows = xg.shape[1]
    heads = mask.shape[0]
    s, z = lax.axis_index("seq"), lax.axis_index("mp")
    place = lax.rem(s, SEQ_DEVS)
    pair = z + 1 - 2 * lax.rem(z, 2)
    twin = s + 1 - 2 * lax.rem(s, 2)
    def tables(place, z):
        at = block(cosine.shape[0], place)
        some = pl.ds(z * heads, heads)
        return [
            (cosine_all.at[at], cosine),
            (sine_all.at[at], sine),
            (mask_all.at[some], mask),
            (q_scale_all.at[some], q_scale),
            (k_scale_all.at[some], k_scale),
            (decay_all.at[some], decay),
        ]

    loads = [
        pltpu.make_async_copy(a, b, load.at[i])
        for i, (a, b) in enumerate(
            [(w_query, wq), (w_key, wk), (w_value, wv), (w_gate, wg), (w_out, wo)]
            + tables(place, z)
        )
    ]
    for copy in loads:
        copy.start()

    def norm(i, _):
        part = pl.ds(pl.multiple_of(i * 32, 32), 32)
        unit, _ = centred(tok[part, :].astype(f32))
        xg[z, part, :] = (unit * gain[...]).astype(bf16)
        return 0

    def ready(part):
        each = rows // 32 // HALVES
        lax.fori_loop(part * each, (part + 1) * each, norm, 0)

    count = lax.axis_size("seq")
    across = flip(z, 2)
    greet(
        [(z > 0, s, z - 1), (z < depth - 1, s, z + 1), (z >= 0, s, across)]
        + [(s != other, other, z) for other in range(count)]
    )
    tall, few = w_up.shape[0] // count, w_down.shape[0] // count
    mine = pltpu.make_async_copy(cot, cot_rows.at[0], x_send.at[3])
    near = remote(cot, cot_rows.at[2], x_send.at[1], x_recv.at[1], twin, z)
    swap = remote(cot, cot_rows.at[1], x_send.at[0], x_recv.at[0], s, pair)
    far = remote(cot_rows.at[1], cot_rows.at[3], x_send.at[2], x_recv.at[2], twin, z)

    def piece(source):
        return block(tall, source), block(few, source)

    up_at, down_at = piece(s)
    moves = [
        remote(w_up.at[up_at], far_up.at[up_at], f_send.at[0], f_recv.at[0], s, across),
        remote(w_down.at[down_at], far_down.at[down_at], f_send.at[1], f_recv.at[1], s, across),
    ]
    edge = (z == 0) | (z == depth - 1)

    def spread(source, chip):
        up_, down_ = piece(source)
        to = 2 * chip + 1
        return [
            remote(far_up.at[up_], far_up.at[up_], p_send.at[0, chip], p_recv.at[0, source], to, z),
            remote(
                far_down.at[down_], far_down.at[down_], p_send.at[1, chip], p_recv.at[1, source], to, z
            ),
        ]

    @pl.when(place == 0)
    def _():
        state_in[...] = jnp.zeros_like(state_in)

    def after(turn):
        @pl.when(turn == 0)
        def _():
            mine.start()
            near.start()

        @pl.when(edge & (turn == 1))
        def _():
            swap.start()

        @pl.when(edge & (turn == 3))
        def _():
            for copy in moves:
                copy.start()

    def use(j):
        at = block(rows, j)

        @pl.when(j == z)
        def _():
            for copy in loads:
                copy.wait()

        rotated(j, wk, k)
        for h in range(heads):
            cols = slice(h * DK, (h + 1) * DK)
            wide = slice(h * DV, (h + 1) * DV)
            v[at, wide] = dot(xg[j], wv[:, wide]).astype(bf16)
            vd = (v[at, wide].astype(f32) * k_scale[h]).astype(bf16)
            grown[h, j] = product_t(k[at, cols], vd)

        @pl.when(j != last)
        def _():
            rest(j)

    last = jnp.where(z < depth // 2, depth - 1, 0)

    def rotated(j, w, out):
        at = block(rows, j)
        c, sn = cosine[at, :], sine[at, :]
        for h in range(heads):
            p = dot(xg[j], w[:, h * DK : (h + 1) * DK])
            a, b = p[:, : DK // 2], p[:, DK // 2 :]
            out[at, h * DK : h * DK + DK // 2] = (a * c - b * sn).astype(bf16)
            out[at, h * DK + DK // 2 : (h + 1) * DK] = (b * c + a * sn).astype(bf16)

    def rest(j):
        at = block(rows, j)
        rotated(j, wq, q)
        for h in range(heads):
            cols = slice(h * DK, (h + 1) * DK)
            wide = slice(h * DV, (h + 1) * DV)
            gp[at, wide] = dot(xg[j], wg[:, wide])
            weights[h, j] = (product_rt(q[at, cols], k[at, cols]) * mask[h]).astype(bf16)

    line_gather(xg, g_send, g_recv, s, z, depth, use, ready, after)
    def chain(h, to):
        return remote(state_to.at[h], state_in.at[h], c_send.at[h], c_recv.at[h], to, z)

    for h in range(heads):
        state[h] = grown[h, 0]
        for b in range(1, depth):
            state[h] = decay[h, 0] * state[h] + grown[h, b]

        @pl.when(place == 0)
        def _():
            state_to[h] = state[h].astype(bf16)
            chain(h, s + 1).start()

    rest(last)

    @pl.when(place > 0)
    def _():
        for h in range(heads):
            chain(h, s - 1).wait_recv()

            @pl.when(place < SEQ_DEVS - 1)
            def _():
                state_to[h] = (decay[h, 1] * state_in[h].astype(f32) + state[h]).astype(bf16)
                chain(h, s + 1).start()

    saves = [
        pltpu.make_async_copy(a, b, save.at[i])
        for i, (a, b) in enumerate(
            [
                (xg, x_out),
                (q, q_out),
                (k, k_out),
                (v, v_out),
                (gp, gp_out),
                (weights, p_out),
                (entering, r_out),
                (gn, gn_out),
                (gated, gated_out),
                (inv, inv_out),
            ]
        )
    ]
    for copy in saves[:6]:
        copy.start()

    def hand_out():
        for copy in moves:
            copy.wait_recv()

        def to_chip(chip, _):
            @pl.when(2 * chip + 1 != s)
            def _():
                for copy in spread(s, chip):
                    copy.start()

            return 0

        lax.fori_loop(0, count // 2, to_chip, 0)

    for h in range(heads):
        state[h] = state_in[h].astype(f32)
        for b in range(depth):
            entering[h, b] = state[h].astype(bf16)
            if b < depth - 1:
                state[h] = decay[h, 0] * state[h] + grown[h, b]
    saves[6].start()

    def cross(b):
        at = block(rows, b)
        for h in range(heads):
            cols = slice(h * DK, (h + 1) * DK)
            wide = slice(h * DV, (h + 1) * DV)
            qd = (q[at, cols].astype(f32) * q_scale[h]).astype(bf16)
            tile[...] = dot(weights[h, b], v[at, wide]) + dot(qd, entering[h, b])

            def norm(here, i):
                there = pl.ds(pl.multiple_of(b * rows + i * 32, 32), 32)
                unit, inverse = centred(tile[here, :])
                gate = gp[there, wide]
                gn[there, wide] = unit
                gated[there, wide] = (unit * gate / (1.0 + jnp.exp(-gate))).astype(bf16)
                inv[h, there, :] = jnp.broadcast_to(inverse, (32, inv.shape[2]))

            row_loop(rows, 32, norm)

    line_gather_end(xg, g_send, g_recv, s, z, depth)

    @pl.when(jnp.logical_not(edge))
    def _():
        hand_out()

    saves[0].wait()
    wide = 512

    def hook(turn):
        @pl.when((turn == 0) & jnp.logical_not(edge))
        def _():
            for copy in moves:
                copy.start()
            swap.start()

        @pl.when((turn == 0) & edge)
        def _():
            hand_out()

        @pl.when(turn == 2)
        def _():
            swap.wait_recv()
            far.start()

    def partial(j):
        cross(j)
        for n in range(0, total.shape[1], wide):
            xg[j, :, n : n + wide] = dot(gated[block(rows, j), :], wo[:, n : n + wide]).astype(bf16)

    def own():
        cross(z)
        for copy in saves[7:]:
            copy.start()
        for n in range(0, total.shape[1], wide):
            total[:, n : n + wide] = tok[:, n : n + wide].astype(f32) + dot(
                gated[block(rows, z), :], wo[:, n : n + wide]
            )

    line_scatter(xg, rbuf, total, s_send, s_recv, s, z, depth, partial, own, hook)
    done = pltpu.make_async_copy(total, hidden_out, save.at[0])
    done.start()

    @pl.when(place < SEQ_DEVS - 1)
    def _():
        for h in range(heads):
            chain(h, s + 1).wait_send()

    def sent(chip, _):
        @pl.when(2 * chip + 1 != s)
        def _():
            for copy in spread(s, chip):
                copy.wait_send()

        return 0

    lax.fori_loop(0, count // 2, sent, 0)

    def came(source, _):
        @pl.when((source != s) & (lax.rem(s, 2) == 1))
        def _():
            for copy in spread(source, 0):
                copy.wait_recv()

        return 0

    lax.fori_loop(0, count, came, 0)
    for copy in moves:
        copy.wait_send()
    swap.wait_send()
    near.wait()
    far.wait()
    mine.wait()
    for copy in saves[1:]:
        copy.wait()
    done.wait()


def attend(
    tok, gain, cot, w_query, w_key, w_value, w_gate, w_out, w_up, w_down, cosine, sine, mask, q_scale, k_scale, decay
):
    f32, bf16 = jnp.float32, jnp.bfloat16
    depth = lax.axis_size("mp")
    rows, width = tok.shape
    span = depth * rows
    heads = w_query.shape[1] // DK
    hk, hv = w_query.shape[1], w_value.shape[1]
    any_ = pl.BlockSpec(memory_space=pl.ANY)
    vmem = pl.BlockSpec(memory_space=pltpu.VMEM)
    shapes = [
        ((depth, rows, width), bf16),
        ((span, hk), bf16),
        ((span, hk), bf16),
        ((span, hv), bf16),
        ((span, hv), f32),
        ((span, hv), f32),
        ((span, hv), bf16),
        ((heads, span, 128), f32),
        ((heads, depth, rows, rows), bf16),
        ((heads, depth, DK, DV), bf16),
        ((rows, width), f32),
        ((4, rows, width), bf16),
        (w_up.shape, bf16),
        (w_down.shape, bf16),
    ]
    count = lax.axis_size("seq")
    dma = pltpu.SemaphoreType.DMA
    return pl.pallas_call(
        attend_kernel,
        out_shape=[jax.ShapeDtypeStruct(*one) for one in shapes],
        in_specs=[vmem, vmem, any_] + [any_] * 13,
        out_specs=[any_] * len(shapes),
        scratch_shapes=[
            pltpu.VMEM((span, DK // 2), f32),
            pltpu.VMEM((span, DK // 2), f32),
            pltpu.VMEM((heads, rows, rows), f32),
            pltpu.VMEM((heads, rows, 1), f32),
            pltpu.VMEM((heads, rows, 1), f32),
            pltpu.VMEM((heads, 2, 1, DV), f32),
            pltpu.VMEM((depth, rows, width), bf16),
            pltpu.VMEM((span, hk), bf16),
            pltpu.VMEM((span, hk), bf16),
            pltpu.VMEM((span, hv), bf16),
            pltpu.VMEM((span, hv), f32),
            pltpu.VMEM((span, hv), f32),
            pltpu.VMEM((span, hv), bf16),
            pltpu.VMEM((heads, span, 128), f32),
            pltpu.VMEM((heads, depth, rows, rows), bf16),
            pltpu.VMEM((heads, depth, DK, DV), f32),
            pltpu.VMEM((heads, depth, DK, DV), bf16),
            pltpu.VMEM((rows, DV), f32),
            pltpu.VMEM((heads, DK, DV), f32),
            pltpu.VMEM((heads, DK, DV), bf16),
            pltpu.VMEM((heads, DK, DV), bf16),
            pltpu.VMEM((depth + 1, rows, width), bf16),
            pltpu.VMEM((rows, width), f32),
            pltpu.VMEM(w_query.shape, bf16),
            pltpu.VMEM(w_key.shape, bf16),
            pltpu.VMEM(w_value.shape, bf16),
            pltpu.VMEM(w_gate.shape, bf16),
            pltpu.VMEM(w_out.shape, bf16),
            dma((11,)),
            dma((10,)),
            dma((2, depth, HALVES)),
            dma((depth, HALVES)),
            dma((depth, HALVES)),
            dma((depth + 1, HALVES)),
            dma((heads,)),
            dma((heads,)),
            dma((4,)),
            dma((3,)),
            dma((2,)),
            dma((2,)),
            dma((2, count // 2)),
            dma((2, count)),
        ],
        compiler_params=pltpu.CompilerParams(
            collective_id=0, has_side_effects=True, vmem_limit_bytes=LIMIT
        ),
        cost_estimate=pl.CostEstimate(
            flops=190 * 10**9, bytes_accessed=60 * 10**6, transcendentals=2 * 10**6
        ),
        name="attend",
    )(tok, gain, cot, w_query, w_key, w_value, w_gate, w_out, w_up, w_down, cosine, sine, mask, q_scale, k_scale, decay)


def row_loop(rows, step, body):
    def one(i, _):
        body(pl.ds(pl.multiple_of(i * step, step), step), i)
        return 0

    lax.fori_loop(0, rows // step, one, 0)


def norm_rows_back(grad_hat, unit, inverse):
    first = jnp.mean(grad_hat, axis=-1, keepdims=True)
    second = jnp.mean(grad_hat * unit, axis=-1, keepdims=True)
    return inverse * (grad_hat - first - unit * second)


def feed_kernel(
    hidden,
    gain,
    cot,
    cot_rows,
    w_up,
    w_down,
    far_up,
    far_down,
    y_keep,
    y_send,
    grad_hidden,
    gain_part,
    g_all_out,
    x,
    dy,
    act,
    du,
    part_y,
    part_x,
    got_x,
    got_own,
    got_y,
    u_tile,
    d_tile,
    g_all,
    up,
    down,
    load,
    save,
    send,
    recv,
):
    f32, bf16 = jnp.float32, jnp.bfloat16
    rows, width = hidden.shape
    units = up.shape[1]
    half = rows // 2
    s, z = lax.axis_index("seq"), lax.axis_index("mp")
    pair = z + 1 - 2 * lax.rem(z, 2)
    twin = s + 1 - 2 * lax.rem(s, 2)
    own_loads = [
        pltpu.make_async_copy(w_up, up, load.at[0]),
        pltpu.make_async_copy(w_down, down, load.at[1]),
    ]
    far_loads = [
        pltpu.make_async_copy(far_up, up, load.at[0]),
        pltpu.make_async_copy(far_down, down, load.at[1]),
    ]

    @pl.when(lax.rem(s, 2) == 0)
    def _():
        for copy in own_loads:
            copy.start()

    @pl.when(lax.rem(s, 2) == 1)
    def _():
        for copy in far_loads:
            copy.start()

    rest = [
        pltpu.make_async_copy(cot_rows.at[a, pl.ds(at, n)], dy.at[pl.ds(to, n)], load.at[2 + i])
        for i, (a, at, n, to) in enumerate(
            [
                (0, 0, rows, 0),
                (2, 0, rows, rows),
                (1, 0, half, 2 * rows),
                (3, 0, half, 2 * rows + half),
                (1, half, half, 3 * rows),
                (3, half, half, 3 * rows + half),
            ]
        )
    ]
    loads = own_loads + rest
    for copy in rest:
        copy.start()

    def norm(here, i):
        unit, _ = centred(hidden[here, :])
        x[here, :] = (unit * gain[...]).astype(bf16)

    row_loop(rows, 32, norm)
    greet([(z >= 0, s, pair), (z >= 0, twin, z)])
    mine, theirs = pl.ds(0, rows), pl.ds(rows, rows)
    parts = [pl.ds(0, half), pl.ds(half, half)]
    pairs = [pl.ds(2 * rows, half), pl.ds(3 * rows, half)]
    twins = [pl.ds(2 * rows + half, half), pl.ds(3 * rows + half, half)]
    near = remote(x.at[mine], x.at[theirs], send.at[0], recv.at[0], twin, z)
    over, far, back_far, back_over, y_far = [], [], [], [], []
    for i in range(2):
        k = 1 + 5 * i
        over.append(remote(x.at[parts[i]], x.at[pairs[i]], send.at[k], recv.at[k], s, pair))
        far.append(remote(x.at[pairs[i]], x.at[twins[i]], send.at[k + 1], recv.at[k + 1], twin, z))
        back_far.append(
            remote(part_x.at[twins[i]], got_x.at[i], send.at[k + 2], recv.at[k + 2], twin, z)
        )
        back_over.append(
            remote(part_x.at[pairs[i]], got_x.at[2 + i], send.at[k + 3], recv.at[k + 3], s, pair)
        )
        y_far.append(
            remote(
                part_y.at[twins[i]], got_y.at[pl.ds(rows + i * half, half)], send.at[k + 4],
                recv.at[k + 4], twin, z,
            )
        )
    back_near = remote(part_x.at[theirs], got_own, send.at[11], recv.at[11], twin, z)
    y_near = remote(part_y.at[theirs], got_y.at[mine], send.at[12], recv.at[12], twin, z)
    over[0].start()
    near.start()
    over[1].start()
    for copy in loads:
        copy.wait()
    step = 512

    def y_terms(r):
        at = block(rows, r)
        for n in range(0, width, step):
            part_y[at, n : n + step] = dot(act[at, :], down[:, n : n + step]).astype(bf16)

    def return_pair(i):
        back_far[i].wait_recv()
        add_rows(part_x.at[pairs[i]], got_x.at[i])
        back_over[i].start()

    def one(r, _):
        at = block(rows, r)

        @pl.when(r == 1)
        def _():
            near.wait_recv()

        @pl.when(r == 2)
        def _():
            over[0].wait_recv()
            far[0].start()
            far[0].wait_recv()

        @pl.when(r == 3)
        def _():
            return_pair(0)
            lax.fori_loop(0, 2, lambda i, c: (y_terms(i), c)[1], 0)
            over[1].wait_recv()
            far[1].start()
            far[1].wait_recv()

        for n in range(0, units, step):
            cols = slice(n, n + step)
            u_tile[...] = dot(x[at, :], up[:, cols])
            d_tile[...] = product_rt(dy[at, :], down[cols, :])

            def gelu(here, i):
                there = pl.ds(pl.multiple_of(r * rows + i * 32, 32), 32)
                u = u_tile[here, :]
                normal = 0.5 * (1.0 + lax.erf(u * (2.0**-0.5)))
                slope = normal + u * (jnp.exp(-0.5 * u * u) * ((2.0 * math.pi) ** -0.5))
                act[there, cols] = (u * normal).astype(bf16)
                du[there, cols] = (d_tile[here, :] * slope).astype(bf16)

            row_loop(rows, 32, gelu)
        for n in range(0, width, step):
            part_x[at, n : n + step] = product_rt(du[at, :], up[n : n + step, :]).astype(bf16)

        @pl.when(r == 1)
        def _():
            back_near.start()

        @pl.when(r == 2)
        def _():
            back_far[0].start()

        @pl.when(r == 3)
        def _():
            back_far[1].start()

        return 0

    lax.fori_loop(0, 4, one, 0)
    return_pair(1)
    lax.fori_loop(2, 4, lambda i, c: (y_terms(i), c)[1], 0)
    y_near.start()
    for copy in y_far:
        copy.start()
    chips, _, high, _ = g_all.shape
    few = units // (2 * chips)
    tall = width // (2 * chips)

    def up_terms(m, _):
        cols = pl.ds(pl.multiple_of(m * 256, 256), 256)
        value = product_t(x[:, cols], du[...]).astype(bf16)
        for part in range(256 // tall):
            to = m * (256 // tall) + part
            g_all[to // 2, lax.rem(to, 2), 0:tall, :] = value[part * tall : (part + 1) * tall]
        return 0

    lax.fori_loop(0, width // 256, up_terms, 0)

    def down_terms(m, _):
        cols = pl.ds(pl.multiple_of(m * 256, 256), 256)
        for n in range(0, width, units):
            value = product_t(act[:, cols], dy[:, n : n + units]).astype(bf16)
            first = tall + n // units * few
            for part in range(256 // few):
                to = m * (256 // few) + part
                g_all[to // 2, lax.rem(to, 2), first : first + few, :] = value[
                    part * few : (part + 1) * few
                ]
        return 0

    lax.fori_loop(0, units // 256, down_terms, 0)
    saves = [pltpu.make_async_copy(g_all, g_all_out, save.at[0])]
    saves[0].start()
    y_near.wait_recv()
    for copy in y_far:
        copy.wait_recv()

    def y_sum(here, i):
        y_keep[here, :] = (
            hidden[here, :] + part_y[here, :].astype(f32) + got_y[here, :].astype(f32)
        )

    row_loop(rows, 32, y_sum)
    for i in range(2):

        def y_pair(here, j):
            there = pl.ds(pl.multiple_of((2 + i) * rows + j * 32, 32), 32)
            came = pl.ds(pl.multiple_of(rows + i * half + j * 32, 32), 32)
            to = pl.ds(pl.multiple_of(i * half + j * 32, 32), 32)
            y_send[to, :] = (part_y[there, :].astype(f32) + got_y[came, :].astype(f32)).astype(bf16)

        row_loop(half, 32, y_pair)
    back_near.wait_recv()
    gain_part[...] = jnp.zeros_like(gain_part)
    for i in range(2):
        back_over[i].wait_recv()

        def finish(here, j):
            at = pl.ds(pl.multiple_of(i * half + j * 32, 32), 32)
            unit, inverse = centred(hidden[at, :])
            grad = (part_x[at, :].astype(f32) + got_own[at, :].astype(f32)) + got_x[
                2 + i, here, :
            ].astype(f32)
            gain_part[...] += jnp.sum(grad * unit, axis=0, keepdims=True)
            grad_hidden[at, :] = cot[at, :].astype(f32) + norm_rows_back(
                grad * gain[...], unit, inverse
            )

        row_loop(half, 32, finish)
    for copy in [near, back_near, y_near] + over + far + back_far + back_over + y_far:
        copy.wait_send()
    for copy in saves:
        copy.wait()


def feed(hidden, gain, cot, cot_rows, w_up, w_down, far_up, far_down):
    f32, bf16 = jnp.float32, jnp.bfloat16
    rows, width = hidden.shape
    units = w_up.shape[1]
    count = lax.axis_size("seq")
    gathered = (count // 2, 2, width // count + width // count, units)
    any_ = pl.BlockSpec(memory_space=pl.ANY)
    vmem = pl.BlockSpec(memory_space=pltpu.VMEM)
    dma = pltpu.SemaphoreType.DMA
    return pl.pallas_call(
        feed_kernel,
        out_shape=[
            jax.ShapeDtypeStruct((rows, width), f32),
            jax.ShapeDtypeStruct((rows, width), bf16),
            jax.ShapeDtypeStruct((rows, width), f32),
            jax.ShapeDtypeStruct((1, width), f32),
            jax.ShapeDtypeStruct(gathered, bf16),
        ],
        in_specs=[vmem, vmem, vmem] + [any_] * 5,
        out_specs=[vmem] * 4 + [any_],
        scratch_shapes=[
            pltpu.VMEM((4 * rows, width), bf16),
            pltpu.VMEM((4 * rows, width), bf16),
            pltpu.VMEM((4 * rows, units), bf16),
            pltpu.VMEM((4 * rows, units), bf16),
            pltpu.VMEM((4 * rows, width), bf16),
            pltpu.VMEM((4 * rows, width), bf16),
            pltpu.VMEM((4, rows // 2, width), bf16),
            pltpu.VMEM((rows, width), bf16),
            pltpu.VMEM((2 * rows, width), bf16),
            pltpu.VMEM((rows, 512), f32),
            pltpu.VMEM((rows, 512), f32),
            pltpu.VMEM(gathered, bf16),
            pltpu.VMEM(w_up.shape, bf16),
            pltpu.VMEM(w_down.shape, bf16),
            dma((8,)),
            dma((1,)),
            dma((13,)),
            dma((13,)),
        ],
        compiler_params=pltpu.CompilerParams(
            collective_id=1, has_side_effects=True, vmem_limit_bytes=LIMIT
        ),
        cost_estimate=pl.CostEstimate(
            flops=75 * 10**9, bytes_accessed=30 * 10**6, transcendentals=2 * 10**6
        ),
        name="feed",
    )(hidden, gain, cot, cot_rows, w_up, w_down, far_up, far_down)


def retract_kernel(
    grad_hidden,
    y_send,
    w_out,
    q_in,
    k_in,
    v_in,
    gp_in,
    gn_in,
    gated_in,
    inv_in,
    p_in,
    r_in,
    cosine_all,
    sine_all,
    mask_all,
    q_scale_all,
    k_scale_all,
    decay_all,
    d_out,
    g_out,
    y_got,
    cosine,
    sine,
    mask,
    q_scale,
    k_scale,
    decay,
    dx,
    q,
    k,
    v,
    gp,
    gn,
    gated,
    inv,
    weights,
    entering,
    wo,
    dall,
    do,
    do_low,
    tile,
    grown,
    dk,
    dv,
    state,
    state_in,
    state_to,
    g_wo,
    load,
    save,
    save_rows,
    g_send,
    g_recv,
    c_send,
    c_recv,
    y_sems,
):
    f32, bf16 = jnp.float32, jnp.bfloat16
    depth, rows, width = dx.shape
    heads = mask.shape[0]
    hk, hv = q.shape[1], v.shape[1]
    s, z = lax.axis_index("seq"), lax.axis_index("mp")
    place = lax.rem(s, SEQ_DEVS)
    pair = z + 1 - 2 * lax.rem(z, 2)
    def tables(place, z):
        at = block(cosine.shape[0], place)
        some = pl.ds(z * heads, heads)
        return [
            (cosine_all.at[at], cosine),
            (sine_all.at[at], sine),
            (mask_all.at[some], mask),
            (q_scale_all.at[some], q_scale),
            (k_scale_all.at[some], k_scale),
            (decay_all.at[some], decay),
        ]

    loads = [
        pltpu.make_async_copy(a, b, load.at[i])
        for i, (a, b) in enumerate(
            [
                (w_out, wo),
                (q_in, q),
                (k_in, k),
                (v_in, v),
                (gp_in, gp),
                (gn_in, gn),
                (gated_in, gated),
                (inv_in, inv),
                (p_in, weights),
                (r_in, entering),
            ]
            + tables(place, z)
        )
    ]
    for copy in loads:
        copy.start()

    def low(here, i):
        dx[z, here, :] = grad_hidden[here, :].astype(bf16)

    def ready(part):
        row_loop(rows // HALVES, 32, lambda here, i: low(
            pl.ds(pl.multiple_of(part * (rows // HALVES) + i * 32, 32), 32), i))

    greet(
        [
            (z > 0, s, z - 1),
            (z < depth - 1, s, z + 1),
            (place > 0, s - 1, z),
            (place < SEQ_DEVS - 1, s + 1, z),
        ]
    )

    @pl.when(place == SEQ_DEVS - 1)
    def _():
        state_in[...] = jnp.zeros_like(state_in)

    def turn_back(value, at, start):
        c, sn = cosine[at, :], sine[at, :]
        half = DK // 2
        a, b = value[:, :half], value[:, half:]
        dall[at, start : start + half] = (a * c + b * sn).astype(bf16)
        dall[at, start + half : start + DK] = (b * c - a * sn).astype(bf16)

    def use(j):
        at = block(rows, j)

        @pl.when(j == z)
        def _():
            for copy in loads:
                copy.wait()

        for h in range(heads):
            wide = slice(h * DV, (h + 1) * DV)
            tile[...] = product_rt(dx[j], wo[wide, :])

            def gate_back(here, i):
                there = pl.ds(pl.multiple_of(j * rows + i * 32, 32), 32)
                grad = tile[here, :]
                gate = gp[there, wide]
                unit = gn[there, wide]
                open_ = 1.0 / (1.0 + jnp.exp(-gate))
                slope = open_ * (1.0 + gate * (1.0 - open_))
                first = 2 * hk + hv + h * DV
                dall[there, first : first + DV] = (grad * unit * slope).astype(bf16)
                inverse = inv[h, there, :][:, :1]
                value = norm_rows_back(grad * gate * open_, unit, inverse)
                high = value.astype(bf16)
                do[there, wide] = high
                do_low[here, wide] = (value - high.astype(f32)).astype(bf16)

            row_loop(rows, 32, gate_back)
        for h in range(heads):
            cols = slice(h * DK, (h + 1) * DK)
            wide = slice(h * DV, (h + 1) * DV)
            qd = (q[at, cols].astype(f32) * q_scale[h]).astype(bf16)
            grown[h, j] = product_t(qd, do[at, wide])

        @pl.when(j != last)
        def _():
            rest(j)

    last = jnp.where(z < depth // 2, depth - 1, 0)

    def rest(j):
        at = block(rows, j)
        for h in range(heads):
            cols = slice(h * DK, (h + 1) * DK)
            wide = slice(h * DV, (h + 1) * DV)
            qb, kb, vb, db = q[at, cols], k[at, cols], v[at, wide], do[at, wide]
            raw = product_rt(db, vb) + product_rt(do_low[:, wide], vb)
            ds = (raw * mask[h]).astype(bf16)
            dv[at, wide] = product_t(weights[h, j], db)
            dk[at, cols] = product_t(ds, qb)
            turn_back(dot(ds, kb) + q_scale[h] * product_rt(db, entering[h, j]), at, h * DK)

    def chain(h, to):
        return remote(state_to.at[h], state_in.at[h], c_send.at[h], c_recv.at[h], to, z)

    line_gather(dx, g_send, g_recv, s, z, depth, use, ready)
    swap = remote(y_send, y_got, y_sems.at[0], y_sems.at[1], s, pair)
    swap.start()
    def out_terms(m, _):
        cols = pl.ds(pl.multiple_of(m * 256, 256), 256)
        for n in range(0, width, 512):
            right = dx[:, :, n : n + 512].reshape(depth * rows, 512)
            g_wo[cols, n : n + 512] = product_t(gated[:, cols], right).astype(bf16)
        return 0

    def out_grad():
        lax.fori_loop(0, hv // 256, out_terms, 0)

    for h in range(heads):
        state[h] = grown[h, depth - 1]
        for b in reversed(range(depth - 1)):
            state[h] = decay[h, 0] * state[h] + grown[h, b]

        @pl.when(place == SEQ_DEVS - 1)
        def _():
            state_to[h] = state[h].astype(bf16)
            chain(h, s - 1).start()

    rest(last)

    @pl.when(place == 0)
    def _():
        out_grad()

    for h in range(heads):

        @pl.when(place < SEQ_DEVS - 1)
        def _():
            chain(h, s + 1).wait_recv()

        @pl.when((place > 0) & (place < SEQ_DEVS - 1))
        def _():
            state_to[h] = (decay[h, 1] * state_in[h].astype(f32) + state[h]).astype(bf16)
            chain(h, s - 1).start()

    for h in range(heads):
        state[h] = state_in[h].astype(f32)

    def done(b):
        at = block(rows, b)
        return pltpu.make_async_copy(dall.at[at], d_out.at[at], save_rows.at[b])

    def cross(turn, _):
        b = depth - 1 - turn
        at = block(rows, b)
        for h in range(heads):
            cols = slice(h * DK, (h + 1) * DK)
            wide = slice(h * DV, (h + 1) * DV)
            leaving = state[h].astype(bf16)
            state[h] = grown[h, b] + decay[h, 0] * state[h]
            kb = k[at, cols]
            vd = (v[at, wide].astype(f32) * k_scale[h]).astype(bf16)
            turn_back(dk[at, cols] + product_rt(vd, leaving), at, hk + h * DK)
            dall[at, 2 * hk + h * DV : 2 * hk + (h + 1) * DV] = (
                dv[at, wide] + k_scale[h] * dot(kb, leaving)
            ).astype(bf16)
        done(b).start()
        return 0

    lax.fori_loop(0, depth, cross, 0)
    saves = [pltpu.make_async_copy(g_wo, g_out, save.at[0])]

    @pl.when(place > 0)
    def _():
        out_grad()

    saves[0].start()
    lax.fori_loop(0, depth, lambda b, c: (done(b).wait(), c)[1], 0)
    line_gather_end(dx, g_send, g_recv, s, z, depth)

    @pl.when(place > 0)
    def _():
        for h in range(heads):
            chain(h, s - 1).wait_send()

    swap.wait()
    for copy in saves:
        copy.wait()


def retract(
    grad_hidden, y_send, w_out, q, k, v, gp, gn, gated, inv, p, r, cosine, sine, mask, q_scale, k_scale, decay
):
    f32, bf16 = jnp.float32, jnp.bfloat16
    depth = lax.axis_size("mp")
    rows, width = grad_hidden.shape
    span = depth * rows
    heads = q.shape[1] // DK
    hk, hv = q.shape[1], v.shape[1]
    any_ = pl.BlockSpec(memory_space=pl.ANY)
    vmem = pl.BlockSpec(memory_space=pltpu.VMEM)
    dma = pltpu.SemaphoreType.DMA
    return pl.pallas_call(
        retract_kernel,
        out_shape=[
            jax.ShapeDtypeStruct((span, 2 * hk + 2 * hv), bf16),
            jax.ShapeDtypeStruct((hv, width), bf16),
            jax.ShapeDtypeStruct((rows, width), bf16),
        ],
        in_specs=[vmem] + [any_] * 17,
        out_specs=[any_] * 3,
        scratch_shapes=[
            pltpu.VMEM((span, DK // 2), f32),
            pltpu.VMEM((span, DK // 2), f32),
            pltpu.VMEM((heads, rows, rows), f32),
            pltpu.VMEM((heads, rows, 1), f32),
            pltpu.VMEM((heads, rows, 1), f32),
            pltpu.VMEM((heads, 2, 1, DV), f32),
            pltpu.VMEM((depth, rows, width), bf16),
            pltpu.VMEM((span, hk), bf16),
            pltpu.VMEM((span, hk), bf16),
            pltpu.VMEM((span, hv), bf16),
            pltpu.VMEM((span, hv), f32),
            pltpu.VMEM((span, hv), f32),
            pltpu.VMEM((span, hv), bf16),
            pltpu.VMEM((heads, span, 128), f32),
            pltpu.VMEM((heads, depth, rows, rows), bf16),
            pltpu.VMEM((heads, depth, DK, DV), bf16),
            pltpu.VMEM(w_out.shape, bf16),
            pltpu.VMEM((span, 2 * hk + 2 * hv), bf16),
            pltpu.VMEM((span, hv), bf16),
            pltpu.VMEM((rows, hv), bf16),
            pltpu.VMEM((rows, DV), f32),
            pltpu.VMEM((heads, depth, DK, DV), f32),
            pltpu.VMEM((span, hk), f32),
            pltpu.VMEM((span, hv), f32),
            pltpu.VMEM((heads, DK, DV), f32),
            pltpu.VMEM((heads, DK, DV), bf16),
            pltpu.VMEM((heads, DK, DV), bf16),
            pltpu.VMEM((hv, width), bf16),
            dma((16,)),
            dma((1,)),
            dma((depth,)),
            dma((2, depth, HALVES)),
            dma((depth, HALVES)),
            dma((heads,)),
            dma((heads,)),
            dma((2,)),
        ],
        compiler_params=pltpu.CompilerParams(
            collective_id=2, has_side_effects=True, vmem_limit_bytes=LIMIT
        ),
        cost_estimate=pl.CostEstimate(
            flops=120 * 10**9, bytes_accessed=40 * 10**6, transcendentals=2 * 10**6
        ),
        name="retract",
    )(grad_hidden, y_send, w_out, q, k, v, gp, gn, gated, inv, p, r, cosine, sine, mask, q_scale, k_scale, decay)


def flip(index, bit):
    return index + bit - 2 * bit * lax.rem(index // bit, 2)


def pair_kernel(
    x_in, d_in, wo_parts, far, out, far_got, x, d, stage, got, wo_mine, wo_got, result, load, save, send, recv, w_sems, f_sems
):
    f32, bf16 = jnp.float32, jnp.bfloat16
    _, chips, rows, _ = stage.shape
    few = wo_mine.shape[1]
    third = result.shape[2]
    s, z = lax.axis_index("seq"), lax.axis_index("mp")
    core = lax.rem(s, 2)
    twin = flip(s, 1)
    across = flip(z, 2)
    edge = (z == 0) | (z == lax.axis_size("mp") - 1)
    loads = [
        pltpu.make_async_copy(d_in, d, load.at[0]),
        pltpu.make_async_copy(x_in, x, load.at[1]),
    ]
    for copy in loads:
        copy.start()
    greet([(z >= 0, twin, z), (z >= 0, s, across), (z >= 0, twin, across)])
    crossed = remote(far.at[0], far_got, f_sems.at[0], f_sems.at[1], twin, across)
    straight = remote(far.at[1], far_got, f_sems.at[2], f_sems.at[3], s, across)

    @pl.when(edge & (core == 1))
    def _():
        crossed.start()
        straight.start()

    wo_load = pltpu.make_async_copy(wo_parts.at[:, core], wo_mine, w_sems.at[0])
    wo_load.start()
    wo_send = remote(wo_parts.at[:, 1 - core], wo_got, w_sems.at[1], w_sems.at[2], twin, z)
    wo_send.start()
    span = max(256, 2 * rows)
    each = span // (2 * rows)

    def give(i):
        return remote(stage.at[1 - core, i], got.at[i], send.at[i], recv.at[i], twin, z)

    def keep(i):
        return pltpu.make_async_copy(result.at[i], out.at[i], save.at[i])

    base = rows * (d.shape[1] // third)

    def take(i):
        give(i).wait_recv()
        for t in range(d.shape[1] // third):

            def add(here, r):
                there = pl.ds(pl.multiple_of(t * rows + r * 32, 32), 32)
                cols = slice(t * third, (t + 1) * third)
                result[i, there, :] = (
                    stage[core, i, here, cols].astype(f32) + got[i, here, cols].astype(f32)
                ).astype(bf16)

            row_loop(rows, 32, add)
        for t in range(wo_mine.shape[2] // third):
            cols = slice(t * third, (t + 1) * third)
            result[i, base + t * few : base + (t + 1) * few, :] = (
                wo_mine[i, :, cols].astype(f32) + wo_got[i, :, cols].astype(f32)
            ).astype(bf16)
        keep(i).start()

    for copy in loads:
        copy.wait()

    def one(g, _):
        for c in range(span // 256):
            chunk = g * (span // 256) + c
            cols = pl.ds(pl.multiple_of(chunk * 256, 256), 256)
            for n in range(0, d.shape[1], 1024):
                value = product_t(x[:, cols], d[:, n : n + 1024]).astype(bf16)
                for part in range(max(1, 256 // rows)):
                    to = (c if each == 1 and rows >= 256 else part) % 2
                    i = g * each + (0 if rows >= 256 else part // 2)
                    stage[to, i, :, n : n + 1024] = value[part * rows : (part + 1) * rows]
        for e in range(each):
            give(g * each + e).start()

        @pl.when(g == 1)
        def _():
            wo_load.wait()
            wo_send.wait()

        @pl.when(g > 0)
        def _():
            for e in range(each):
                take((g - 1) * each + e)

        return 0

    groups = chips // each
    lax.fori_loop(0, groups, one, 0)
    for e in range(each):
        take((groups - 1) * each + e)

    def end(i, _):
        keep(i).wait()
        give(i).wait_send()
        return 0

    lax.fori_loop(0, chips, end, 0)

    @pl.when(edge & (core == 1))
    def _():
        crossed.wait_send()
        straight.wait_send()

    @pl.when(jnp.logical_not(edge) & (core == 0))
    def _():
        crossed.wait_recv()

    @pl.when(jnp.logical_not(edge) & (core == 1))
    def _():
        straight.wait_recv()


def pair_sum(x, d, g_out, far):
    bf16 = jnp.bfloat16
    count = lax.axis_size("seq")
    chips = count // 2
    rows, few = x.shape[1] // count, g_out.shape[0] // count
    wide, third = d.shape[1], d.shape[1] // 3
    high = 3 * rows + few * g_out.shape[1] // third
    any_ = pl.BlockSpec(memory_space=pl.ANY)
    dma = pltpu.SemaphoreType.DMA
    return pl.pallas_call(
        pair_kernel,
        out_shape=[
            jax.ShapeDtypeStruct((chips, high, third), bf16),
            jax.ShapeDtypeStruct(far.shape[1:], bf16),
        ],
        in_specs=[any_] * 4,
        out_specs=[any_, any_],
        scratch_shapes=[
            pltpu.VMEM(x.shape, bf16),
            pltpu.VMEM(d.shape, bf16),
            pltpu.VMEM((2, chips, rows, wide), bf16),
            pltpu.VMEM((chips, rows, wide), bf16),
            pltpu.VMEM((chips, few, g_out.shape[1]), bf16),
            pltpu.VMEM((chips, few, g_out.shape[1]), bf16),
            pltpu.VMEM((chips, high, third), bf16),
            dma((2,)),
            dma((chips,)),
            dma((chips,)),
            dma((chips,)),
            dma((3,)),
            dma((4,)),
        ],
        compiler_params=pltpu.CompilerParams(
            collective_id=3, has_side_effects=True, vmem_limit_bytes=LIMIT
        ),
        cost_estimate=pl.CostEstimate(
            flops=25 * 10**9, bytes_accessed=30 * 10**6, transcendentals=0
        ),
        name="pair_sum",
    )(x, d, g_out.reshape(chips, 2, few, g_out.shape[1]), far)


def finish_kernel(
    d_in,
    x_in,
    tok_in,
    gain,
    gain_part,
    grad_hidden_in,
    w_query,
    w_key,
    w_value,
    w_gate,
    far,
    far_got,
    grad_tok,
    gains,
    g_up,
    g_down,
    d,
    x,
    tok,
    grad_hidden,
    sbuf,
    rbuf,
    total,
    wq,
    wk,
    wv,
    wg,
    mine,
    other,
    gain_all,
    gain_line,
    load,
    d_load,
    x_load,
    s_send,
    s_recv,
    f_sems,
    h_send,
    h_recv,
    l_send,
    l_recv,
):
    f32, bf16 = jnp.float32, jnp.bfloat16
    depth, rows, width = x.shape
    s, z = lax.axis_index("seq"), lax.axis_index("mp")
    core = lax.rem(s, 2)
    twin, across = flip(s, 1), flip(z, 2)
    count = lax.axis_size("seq")
    loads = [
        pltpu.make_async_copy(a, b, load.at[i])
        for i, (a, b) in enumerate(
            [(w_query, wq), (w_key, wk), (w_value, wv), (w_gate, wg)]
        )
    ]

    def slot_loads(j):
        at = block(rows, j)
        return [
            pltpu.make_async_copy(d_in.at[at], d.at[at], d_load.at[j]),
            pltpu.make_async_copy(x_in.at[j], x.at[j], x_load.at[j]),
        ]

    late = [
        pltpu.make_async_copy(a, b, load.at[4 + i])
        for i, (a, b) in enumerate([(tok_in, tok), (grad_hidden_in, grad_hidden)])
    ]
    for copy in loads:
        copy.start()

    def pull(i, _):
        for copy in slot_loads(jnp.where(z < depth // 2, depth - 1 - i, i)):
            copy.start()
        return 0

    lax.fori_loop(0, depth, pull, 0)
    for copy in late:
        copy.start()
    gains[...] = jnp.zeros_like(gains)
    gains[1:2, :] = gain_part[...]
    greet(
        [(z >= 0, twin, across)]
        + [(z != other, s, other) for other in range(depth)]
        + [(s != other, other, z) for other in range(count)]
    )
    near = remote(far.at[1], other, f_sems.at[0], f_sems.at[1], twin, z)
    crossed = remote(far.at[0], other, f_sems.at[0], f_sems.at[1], twin, across)
    straight = remote(far.at[1], mine, f_sems.at[2], f_sems.at[3], s, across)
    edge = (z == 0) | (z == depth - 1)
    inner = jnp.logical_not(edge)
    local = pltpu.make_async_copy(far.at[0], mine, f_sems.at[4])
    to_other = pltpu.make_async_copy(far_got, other, f_sems.at[5])
    to_mine = pltpu.make_async_copy(far_got, mine, f_sems.at[5])

    @pl.when(core == 0)
    def _():
        near.start()
        local.start()

    @pl.when(inner & (core == 0))
    def _():
        to_other.start()

    @pl.when(inner & (core == 1))
    def _():
        to_mine.start()
        crossed.start()
        straight.start()

    for copy in loads:
        copy.wait()
    step = 512
    starts, at_col = [], 0
    for w in (wq, wk, wv, wg):
        starts.append((w, at_col, at_col + w.shape[1]))
        at_col += w.shape[1]

    def term(j, n):
        at = block(rows, j)
        value = None
        for w, a, b in starts:
            one = product_rt(d[at, a:b], w[n : n + step, :])
            value = one if value is None else value + one
        gains[0:1, n : n + step] += jnp.sum(
            value * x[j, :, n : n + step].astype(f32), axis=0, keepdims=True
        )
        return value

    def partial(j):
        for copy in slot_loads(j):
            copy.wait()
        for n in range(0, width, step):
            sbuf[j, :, n : n + step] = term(j, n).astype(bf16)

    def plane(to):
        return remote(gain_all.at[s], gain_all.at[s], h_send.at[to], h_recv.at[s], to, z)

    def line(to):
        return remote(gain_line.at[z], gain_line.at[z], l_send.at[to], l_recv.at[z], s, to)

    def others(count, me, act):
        def one(i, _):
            @pl.when(i != me)
            def _():
                act(i)

            return 0

        lax.fori_loop(0, count, one, 0)

    def own():
        for copy in slot_loads(z):
            copy.wait()
        for n in range(0, width, step):
            total[:, n : n + step] = term(z, n)
        gains[0:1, :] = gains[0:1, :] / gain[...]
        gain_all[s] = gains[...]
        others(count, s, lambda to: plane(to).start())

    line_scatter(sbuf, rbuf, total, s_send, s_recv, s, z, depth, partial, own)

    def plane_came(i):
        remote(gain_all.at[i], gain_all.at[i], h_send.at[i], h_recv.at[i], twin, z).wait_recv()

    def line_came(i):
        remote(gain_line.at[i], gain_line.at[i], l_send.at[i], l_recv.at[i], s, across).wait_recv()

    others(count, s, plane_came)
    gains[...] = gain_all[0]
    for i in range(1, count):
        gains[...] += gain_all[i]
    gain_line[z] = gains[...]
    others(depth, z, lambda to: line(to).start())

    for copy in late:
        copy.wait()

    def last(here, i):
        unit, inverse = centred(tok[here, :].astype(f32))
        grad_tok[here, :] = (
            grad_hidden[here, :] + norm_rows_back(total[here, :] * gain[...], unit, inverse)
        ).astype(bf16)

    row_loop(rows, 32, last)
    others(depth, z, line_came)
    gains[...] = gain_line[0]
    for i in range(1, depth):
        gains[...] += gain_line[i]
    others(count, s, lambda to: plane(to).wait_send())
    others(depth, z, lambda to: line(to).wait_send())

    @pl.when(core == 0)
    def _():
        near.wait_send()
        local.wait()

    @pl.when(core == 1)
    def _():
        near.wait_recv()

    @pl.when(inner & (core == 0))
    def _():
        to_other.wait()

    @pl.when(edge & (core == 0))
    def _():
        crossed.wait_recv()

    @pl.when(inner & (core == 1))
    def _():
        to_mine.wait()
        crossed.wait_send()
        straight.wait_send()

    @pl.when(edge & (core == 1))
    def _():
        straight.wait_recv()

    high, few = g_up.shape[0], g_down.shape[0]
    third = g_up.shape[1]

    g_up[...] = mine[0:high, :].astype(f32) + other[0:high, :].astype(f32)
    for t in range(g_down.shape[1] // third):
        at = slice(high + t * few, high + (t + 1) * few)
        g_down[:, t * third : (t + 1) * third] = mine[at, :].astype(f32) + other[at, :].astype(f32)


def finish(d, x, tok, gain, gain_part, grad_hidden, w_query, w_key, w_value, w_gate, far, far_got):
    f32, bf16 = jnp.float32, jnp.bfloat16
    depth, rows, width = x.shape
    count = lax.axis_size("seq")
    units = far.shape[2]
    any_ = pl.BlockSpec(memory_space=pl.ANY)
    vmem = pl.BlockSpec(memory_space=pltpu.VMEM)
    dma = pltpu.SemaphoreType.DMA
    return pl.pallas_call(
        finish_kernel,
        out_shape=[
            jax.ShapeDtypeStruct((rows, width), bf16),
            jax.ShapeDtypeStruct((8, width), f32),
            jax.ShapeDtypeStruct((width // count, units), f32),
            jax.ShapeDtypeStruct((units // count, width), f32),
        ],
        in_specs=[any_] * 3 + [vmem] * 2 + [any_] * 7,
        out_specs=[vmem] * 4,
        scratch_shapes=[
            pltpu.VMEM(d.shape, bf16),
            pltpu.VMEM(x.shape, bf16),
            pltpu.VMEM((rows, width), bf16),
            pltpu.VMEM((rows, width), f32),
            pltpu.VMEM((depth, rows, width), bf16),
            pltpu.VMEM((depth + 1, rows, width), bf16),
            pltpu.VMEM((rows, width), f32),
            pltpu.VMEM(w_query.shape, bf16),
            pltpu.VMEM(w_key.shape, bf16),
            pltpu.VMEM(w_value.shape, bf16),
            pltpu.VMEM(w_gate.shape, bf16),
            pltpu.VMEM(far.shape[1:], bf16),
            pltpu.VMEM(far.shape[1:], bf16),
            pltpu.VMEM((count, 8, width), f32),
            pltpu.VMEM((depth, 8, width), f32),
            dma((6,)),
            dma((depth,)),
            dma((depth,)),
            dma((depth, HALVES)),
            dma((depth + 1, HALVES)),
            dma((6,)),
            dma((count,)),
            dma((count,)),
            dma((depth,)),
            dma((depth,)),
        ],
        compiler_params=pltpu.CompilerParams(
            collective_id=4, has_side_effects=True, vmem_limit_bytes=LIMIT
        ),
        cost_estimate=pl.CostEstimate(
            flops=110 * 10**9, bytes_accessed=30 * 10**6, transcendentals=0
        ),
        name="finish",
    )(d, x, tok, gain, gain_part, grad_hidden, w_query, w_key, w_value, w_gate, far, far_got)


def unpack_kernel(summed, tok, up, down, query, key, value, gate, out, tok_out, up_out, down_out):
    f32 = jnp.float32
    rows, wide = query.shape
    few, tall = out.shape[0], value.shape[1]
    query[...] = summed[0:rows, 0:wide].astype(f32)
    key[...] = summed[0:rows, wide : 2 * wide].astype(f32)
    value[...] = summed[rows : 2 * rows, :].astype(f32)
    gate[...] = summed[2 * rows : 3 * rows, :].astype(f32)
    for t in range(out.shape[1] // tall):
        at = slice(3 * rows + t * few, 3 * rows + (t + 1) * few)
        out[:, t * tall : (t + 1) * tall] = summed[at, :].astype(f32)
    tok_out[...] = tok[...]
    up_out[...] = up[...]
    down_out[...] = down[...]


def unpack(summed, tok, up, down, wide):
    f32 = jnp.float32
    count = lax.axis_size("seq")
    width, tall = tok.shape[1], summed.shape[1]
    rows, few = width // count, tall // count
    shapes = [(rows, wide)] * 2 + [(rows, tall)] * 2 + [(few, width)]
    return pl.pallas_call(
        unpack_kernel,
        out_shape=[jax.ShapeDtypeStruct(one, f32) for one in shapes]
        + [jax.ShapeDtypeStruct(a.shape, a.dtype) for a in (tok, up, down)],
        compiler_params=pltpu.CompilerParams(vmem_limit_bytes=LIMIT),
        name="unpack",
    )(summed, tok, up, down)


def shards(
    tokens, gain_mix, w_query, w_key, w_value, w_gate, w_out, gain_ffn, w_up, w_down, cotangent
):
    bf16 = jnp.bfloat16
    f32 = jnp.float32
    span_rows = lax.axis_size("mp") * tokens.shape[0]
    local_heads = w_query.shape[1] // DK
    trig = decay_tables(span_rows, local_heads * lax.axis_size("mp"))
    (
        x_rows,
        q_all,
        k_all,
        v_all,
        gate,
        unit,
        gated,
        inverse,
        weights,
        entering,
        hidden,
        cot_rows,
        far_up,
        far_down,
    ) = attend(
        tokens, gain_mix[None, :], cotangent, w_query, w_key, w_value, w_gate, w_out, w_up, w_down, *trig
    )
    y_keep, y_send, grad_hidden, gain_ffn_part, grad_ffn = feed(
        hidden, gain_ffn[None, :], cotangent, cot_rows, w_up, w_down, far_up, far_down
    )
    far = lax.psum_scatter(
        grad_ffn, "seq", scatter_dimension=0, tiled=False, axis_index_groups=same_core()
    )
    grad_in, grad_out_w, y_got = retract(
        grad_hidden, y_send, w_out, q_all, k_all, v_all, gate, unit, gated, inverse, weights, entering, *trig
    )
    output = (y_keep + y_got.astype(f32)).astype(bf16)
    pairs, far_got = pair_sum(x_rows.reshape(span_rows, -1), grad_in, grad_out_w, far)
    summed = lax.psum_scatter(
        pairs, "seq", scatter_dimension=0, tiled=False, axis_index_groups=same_core()
    )
    grad_in, pairs = lax.optimization_barrier((grad_in, pairs))
    grad_tokens, gains, final_up, final_down = finish(
        grad_in, x_rows, tokens, gain_mix[None, :], gain_ffn_part, grad_hidden, w_query, w_key, w_value, w_gate, far, far_got
    )
    summed, gains = lax.optimization_barrier((summed, gains))
    gain_mix_sum, gain_ffn_sum = gains[0], gains[1]
    (
        final_query,
        final_key,
        final_value,
        final_gate,
        final_out,
        grad_tokens,
        final_up,
        final_down,
    ) = unpack(summed, grad_tokens, final_up, final_down, w_query.shape[1])
    return (
        output,
        grad_tokens,
        gain_mix_sum,
        final_query,
        final_key,
        final_value,
        final_gate,
        final_out,
        gain_ffn_sum,
        final_up,
        final_down,
    )


def solution(mesh):
    return jax.shard_map(
        shards,
        mesh=mesh,
        in_specs=(
            P(("seq", "mp"), None),
            P(),
            P(None, "mp"),
            P(None, "mp"),
            P(None, "mp"),
            P(None, "mp"),
            P("mp", None),
            P(),
            P(None, "mp"),
            P("mp", None),
            P(("seq", "mp"), None),
        ),
        out_specs=(
            P(("seq", "mp"), None),
            P(("seq", "mp"), None),
            P(),
            P("seq", "mp"),
            P("seq", "mp"),
            P("seq", "mp"),
            P("seq", "mp"),
            P(("mp", "seq"), None),
            P(),
            P("seq", "mp"),
            P(("mp", "seq"), None),
        ),
        check_vma=False,
    )
```

```python
import math

import jax
import jax.numpy as jnp
import numpy as np
from jax import lax
from jax.experimental import pallas as pl
from jax.experimental.pallas import tpu as pltpu
from jax.sharding import PartitionSpec as P

DK = 256
DV = 512
STRETCH = 256
SEQ_DEVS = 4


eps = 1e-05


def same_core():
    count = lax.axis_size("seq")
    return [list(range(core, count, 2)) for core in range(2)]


def decay_tables(span_rows, heads):
    half = DK // 2
    f32 = np.float32
    freq = np.exp(f32(-math.log(10000.0)) * np.arange(half, dtype=f32) / f32(half - 1)).astype(f32)
    phase = np.arange(SEQ_DEVS * span_rows, dtype=f32)[:, None] * freq[None, :]
    phase = phase.astype(np.float64)
    logs = np.log1p(-np.exp2(-5.0 - np.arange(heads)))
    steps = np.arange(STRETCH)
    gaps = steps[:, None] - steps[None, :]
    mask = np.where(gaps >= 0, np.exp(logs[:, None, None] * np.maximum(gaps, 0)), 0.0)
    q_scale = np.exp(logs[:, None] * (steps + 1))[:, :, None]
    k_scale = np.exp(logs[:, None] * (STRETCH - 1 - steps))[:, :, None]
    decay = np.exp(logs[:, None] * np.array([STRETCH, span_rows]))[:, :, None, None]
    decay = np.broadcast_to(decay, (heads, 2, 1, DV))
    return tuple(
        jnp.asarray(a.astype(f32))
        for a in (np.cos(phase), np.sin(phase), mask, q_scale, k_scale, decay)
    )


def product_t(left, right):
    return lax.dot_general(
        left, right, (((0,), (0,)), ((), ())), preferred_element_type=jnp.float32
    )


def product_rt(left, right):
    return lax.dot_general(
        left, right, (((1,), (1,)), ((), ())), preferred_element_type=jnp.float32
    )


MESH = pl.DeviceIdType.MESH
LIMIT = 62 * 1024 * 1024


def remote(src, dst, send, recv, s, z):
    return pltpu.make_async_remote_copy(
        src_ref=src,
        dst_ref=dst,
        send_sem=send,
        recv_sem=recv,
        device_id=(s, z),
        device_id_type=MESH,
    )


def greet(partners):
    barrier = pltpu.get_barrier_semaphore()
    count = 0
    for present, s, z in partners:

        @pl.when(present)
        def _():
            pl.semaphore_signal(barrier, inc=1, device_id=(s, z), device_id_type=MESH)

        count = count + jnp.where(present, 1, 0)
    pl.semaphore_wait(barrier, count)


def dot(left, right):
    return jnp.dot(left, right, preferred_element_type=jnp.float32)


HALVES = 2


def part_of(rows, part):
    return pl.ds(part * (rows // HALVES), rows // HALVES)


def line_copy(x, send, recv, s, to, slot, part, way):
    at = x.at[slot, part_of(x.shape[1], part)]
    return remote(at, at, send.at[way, slot, part], recv.at[slot, part], s, to)


def line_gather(x, send, recv, s, z, depth, use, ready, after=None):
    def right(slot, part):
        return line_copy(x, send, recv, s, z + 1, slot, part, 0)

    def left(slot, part):
        return line_copy(x, send, recv, s, z - 1, slot, part, 1)

    for part in range(HALVES):
        ready(part)

        @pl.when(z < depth - 1)
        def _():
            right(z, part).start()

        @pl.when(z > 0)
        def _():
            left(z, part).start()

    def one(turn, _):
        away = (turn + 1) // 2
        low, high = z - away, z + away
        for part in range(HALVES):

            @pl.when((turn % 2 == 1) & (low >= 0))
            def _():
                line_copy(x, send, recv, s, z - 1, low, part, 0).wait_recv()

                @pl.when(z < depth - 1)
                def _():
                    right(low, part).start()

            @pl.when((turn % 2 == 1) & (high < depth))
            def _():
                line_copy(x, send, recv, s, z + 1, high, part, 1).wait_recv()

                @pl.when(z > 0)
                def _():
                    left(high, part).start()

        if after is not None:
            after(turn)
        slot = jnp.where(turn % 2 == 1, low, high)

        @pl.when((slot >= 0) & (slot < depth))
        def _():
            use(slot)

        return 0

    lax.fori_loop(0, 2 * depth - 1, one, 0)


def line_gather_end(x, send, recv, s, z, depth):
    def one(slot, _):
        for part in range(HALVES):

            @pl.when((slot <= z) & (z < depth - 1))
            def _():
                line_copy(x, send, recv, s, z + 1, slot, part, 0).wait_send()

            @pl.when((slot >= z) & (z > 0))
            def _():
                line_copy(x, send, recv, s, z - 1, slot, part, 1).wait_send()

        return 0

    lax.fori_loop(0, depth, one, 0)


def add_rows(into, other):
    step = 32

    def one(i, _):
        rows = pl.ds(pl.multiple_of(i * step, step), step)
        into[rows, :] = (
            into[rows, :].astype(jnp.float32) + other[rows, :].astype(jnp.float32)
        ).astype(into.dtype)
        return 0

    lax.fori_loop(0, into.shape[0] // step, one, 0)


def line_scatter(sbuf, rbuf, total, send, recv, s, z, depth, partial, own, hook=None):
    rows = total.shape[0]

    def right(j, part):
        at = part_of(rows, part)
        return remote(
            sbuf.at[j, at], rbuf.at[j, at], send.at[j, part], recv.at[j, part], s, z + 1
        )

    def left(j, part):
        at = part_of(rows, part)
        slot = jnp.where(j == z - 1, depth, j)
        return remote(
            sbuf.at[j, at], rbuf.at[slot, at], send.at[j, part], recv.at[slot, part], s, z - 1
        )

    def arrived(slot, part, sender):
        at = part_of(rows, part)
        remote(
            sbuf.at[0, at], rbuf.at[slot, at], send.at[0, part], recv.at[slot, part], s, sender
        ).wait_recv()

    def first(turn, _):
        up = depth - 1 + z - turn // 2
        down = turn // 2 - (depth - 1) + z
        j = jnp.where(turn % 2 == 0, up, down)
        valid = jnp.where(turn % 2 == 0, (up > z) & (up < depth), (down >= 0) & (down < z))

        @pl.when(valid)
        def _():
            partial(j)

            @pl.when((z == 0) & (j > z))
            def _():
                for part in range(HALVES):
                    right(j, part).start()

            @pl.when((z == depth - 1) & (j < z))
            def _():
                for part in range(HALVES):
                    left(j, part).start()

        return 0

    lax.fori_loop(0, 2 * (depth - 1), first, 0)
    own()

    def event(turn, _):
        up = depth - 1 + z - turn
        down = turn - (depth - 1) + z
        slot = jnp.where(down == z, depth, down)
        for part in range(HALVES):
            at = part_of(rows, part)

            @pl.when((z > 0) & (up >= z) & (up < depth))
            def _():
                arrived(up, part, z - 1)

                @pl.when(up > z)
                def _():
                    add_rows(sbuf.at[up, at], rbuf.at[up, at])
                    right(up, part).start()

                @pl.when(up == z)
                def _():
                    add_rows(total.at[at], rbuf.at[up, at])

            @pl.when((z < depth - 1) & (down >= 0) & (down <= z))
            def _():
                arrived(slot, part, z + 1)

                @pl.when(down < z)
                def _():
                    add_rows(sbuf.at[down, at], rbuf.at[down, at])
                    left(down, part).start()

                @pl.when(down == z)
                def _():
                    add_rows(total.at[at], rbuf.at[depth, at])

        if hook is not None:
            hook(turn)
        return 0

    lax.fori_loop(0, depth, event, 0)

    def end(j, _):
        for part in range(HALVES):

            @pl.when(j > z)
            def _():
                right(j, part).wait_send()

            @pl.when(j < z)
            def _():
                left(j, part).wait_send()

        return 0

    lax.fori_loop(0, depth, end, 0)


def centred(rows):
    centre = rows - jnp.mean(rows, axis=-1, keepdims=True)
    inverse = lax.rsqrt(jnp.mean(centre * centre, axis=-1, keepdims=True) + eps)
    return centre * inverse, inverse


def block(rows, index):
    return pl.ds(pl.multiple_of(index * rows, rows), rows)


def attend_kernel(
    tok,
    gain,
    cot,
    w_query,
    w_key,
    w_value,
    w_gate,
    w_out,
    w_up,
    w_down,
    cosine_all,
    sine_all,
    mask_all,
    q_scale_all,
    k_scale_all,
    decay_all,
    x_out,
    q_out,
    k_out,
    v_out,
    gp_out,
    gn_out,
    gated_out,
    inv_out,
    p_out,
    r_out,
    hidden_out,
    cot_rows,
    far_up,
    far_down,
    cosine,
    sine,
    mask,
    q_scale,
    k_scale,
    decay,
    xg,
    q,
    k,
    v,
    gp,
    gn,
    gated,
    inv,
    weights,
    grown,
    entering,
    tile,
    state,
    state_in,
    state_to,
    rbuf,
    total,
    wq,
    wk,
    wv,
    wg,
    wo,
    load,
    save,
    g_send,
    g_recv,
    s_send,
    s_recv,
    c_send,
    c_recv,
    x_send,
    x_recv,
    f_send,
    f_recv,
    p_send,
    p_recv,
):
    f32, bf16 = jnp.float32, jnp.bfloat16
    depth = xg.shape[0]
    rows = xg.shape[1]
    heads = mask.shape[0]
    s, z = lax.axis_index("seq"), lax.axis_index("mp")
    place = lax.rem(s, SEQ_DEVS)
    pair = z + 1 - 2 * lax.rem(z, 2)
    twin = s + 1 - 2 * lax.rem(s, 2)
    def tables(place, z):
        at = block(cosine.shape[0], place)
        some = pl.ds(z * heads, heads)
        return [
            (cosine_all.at[at], cosine),
            (sine_all.at[at], sine),
            (mask_all.at[some], mask),
            (q_scale_all.at[some], q_scale),
            (k_scale_all.at[some], k_scale),
            (decay_all.at[some], decay),
        ]

    loads = [
        pltpu.make_async_copy(a, b, load.at[i])
        for i, (a, b) in enumerate(
            [(w_query, wq), (w_key, wk), (w_value, wv), (w_gate, wg), (w_out, wo)]
            + tables(place, z)
        )
    ]
    for copy in loads:
        copy.start()

    def norm(i, _):
        part = pl.ds(pl.multiple_of(i * 32, 32), 32)
        unit, _ = centred(tok[part, :].astype(f32))
        xg[z, part, :] = (unit * gain[...]).astype(bf16)
        return 0

    def ready(part):
        each = rows // 32 // HALVES
        lax.fori_loop(part * each, (part + 1) * each, norm, 0)

    count = lax.axis_size("seq")
    across = flip(z, 2)
    greet(
        [(z > 0, s, z - 1), (z < depth - 1, s, z + 1), (z >= 0, s, across)]
        + [(s != other, other, z) for other in range(count)]
    )
    tall, few = w_up.shape[0] // count, w_down.shape[0] // count
    mine = pltpu.make_async_copy(cot, cot_rows.at[0], x_send.at[3])
    near = remote(cot, cot_rows.at[2], x_send.at[1], x_recv.at[1], twin, z)
    swap = remote(cot, cot_rows.at[1], x_send.at[0], x_recv.at[0], s, pair)
    far = remote(cot_rows.at[1], cot_rows.at[3], x_send.at[2], x_recv.at[2], twin, z)

    def piece(source):
        return block(tall, source), block(few, source)

    up_at, down_at = piece(s)
    moves = [
        remote(w_up.at[up_at], far_up.at[up_at], f_send.at[0], f_recv.at[0], s, across),
        remote(w_down.at[down_at], far_down.at[down_at], f_send.at[1], f_recv.at[1], s, across),
    ]
    edge = (z == 0) | (z == depth - 1)

    def spread(source, chip):
        up_, down_ = piece(source)
        to = 2 * chip + 1
        return [
            remote(far_up.at[up_], far_up.at[up_], p_send.at[0, chip], p_recv.at[0, source], to, z),
            remote(
                far_down.at[down_], far_down.at[down_], p_send.at[1, chip], p_recv.at[1, source], to, z
            ),
        ]

    @pl.when(place == 0)
    def _():
        state_in[...] = jnp.zeros_like(state_in)

    def after(turn):
        @pl.when(turn == 0)
        def _():
            mine.start()
            near.start()

        @pl.when(edge & (turn == 1))
        def _():
            swap.start()

        @pl.when(edge & (turn == 3))
        def _():
            for copy in moves:
                copy.start()

    def use(j):
        at = block(rows, j)

        @pl.when(j == z)
        def _():
            for copy in loads:
                copy.wait()

        rotated(j, wk, k)
        for h in range(heads):
            cols = slice(h * DK, (h + 1) * DK)
            wide = slice(h * DV, (h + 1) * DV)
            v[at, wide] = dot(xg[j], wv[:, wide]).astype(bf16)
            vd = (v[at, wide].astype(f32) * k_scale[h]).astype(bf16)
            grown[h, j] = product_t(k[at, cols], vd)

        @pl.when(j != last)
        def _():
            rest(j)

    last = jnp.where(z < depth // 2, depth - 1, 0)

    def rotated(j, w, out):
        at = block(rows, j)
        c, sn = cosine[at, :], sine[at, :]
        for h in range(heads):
            p = dot(xg[j], w[:, h * DK : (h + 1) * DK])
            a, b = p[:, : DK // 2], p[:, DK // 2 :]
            out[at, h * DK : h * DK + DK // 2] = (a * c - b * sn).astype(bf16)
            out[at, h * DK + DK // 2 : (h + 1) * DK] = (b * c + a * sn).astype(bf16)

    def rest(j):
        at = block(rows, j)
        rotated(j, wq, q)
        for h in range(heads):
            cols = slice(h * DK, (h + 1) * DK)
            wide = slice(h * DV, (h + 1) * DV)
            gp[at, wide] = dot(xg[j], wg[:, wide])
            weights[h, j] = (product_rt(q[at, cols], k[at, cols]) * mask[h]).astype(bf16)

    line_gather(xg, g_send, g_recv, s, z, depth, use, ready, after)
    def chain(h, to):
        return remote(state_to.at[h], state_in.at[h], c_send.at[h], c_recv.at[h], to, z)

    for h in range(heads):
        state[h] = grown[h, 0]
        for b in range(1, depth):
            state[h] = decay[h, 0] * state[h] + grown[h, b]

        @pl.when(place == 0)
        def _():
            state_to[h] = state[h].astype(bf16)
            chain(h, s + 1).start()

    rest(last)

    @pl.when(place > 0)
    def _():
        for h in range(heads):
            chain(h, s - 1).wait_recv()

            @pl.when(place < SEQ_DEVS - 1)
            def _():
                state_to[h] = (decay[h, 1] * state_in[h].astype(f32) + state[h]).astype(bf16)
                chain(h, s + 1).start()

    saves = [
        pltpu.make_async_copy(a, b, save.at[i])
        for i, (a, b) in enumerate(
            [
                (xg, x_out),
                (q, q_out),
                (k, k_out),
                (v, v_out),
                (gp, gp_out),
                (weights, p_out),
                (entering, r_out),
                (gn, gn_out),
                (gated, gated_out),
                (inv, inv_out),
            ]
        )
    ]
    for copy in saves[:6]:
        copy.start()

    def hand_out():
        for copy in moves:
            copy.wait_recv()

        def to_chip(chip, _):
            @pl.when(2 * chip + 1 != s)
            def _():
                for copy in spread(s, chip):
                    copy.start()

            return 0

        lax.fori_loop(0, count // 2, to_chip, 0)

    for h in range(heads):
        state[h] = state_in[h].astype(f32)
        for b in range(depth):
            entering[h, b] = state[h].astype(bf16)
            if b < depth - 1:
                state[h] = decay[h, 0] * state[h] + grown[h, b]
    saves[6].start()

    def cross(b):
        at = block(rows, b)
        for h in range(heads):
            cols = slice(h * DK, (h + 1) * DK)
            wide = slice(h * DV, (h + 1) * DV)
            qd = (q[at, cols].astype(f32) * q_scale[h]).astype(bf16)
            tile[...] = dot(weights[h, b], v[at, wide]) + dot(qd, entering[h, b])

            def norm(here, i):
                there = pl.ds(pl.multiple_of(b * rows + i * 32, 32), 32)
                unit, inverse = centred(tile[here, :])
                gate = gp[there, wide]
                gn[there, wide] = unit
                gated[there, wide] = (unit * gate / (1.0 + jnp.exp(-gate))).astype(bf16)
                inv[h, there, :] = jnp.broadcast_to(inverse, (32, inv.shape[2]))

            row_loop(rows, 32, norm)

    line_gather_end(xg, g_send, g_recv, s, z, depth)

    @pl.when(jnp.logical_not(edge))
    def _():
        hand_out()

    saves[0].wait()
    wide = 512

    def hook(turn):
        @pl.when((turn == 0) & jnp.logical_not(edge))
        def _():
            for copy in moves:
                copy.start()
            swap.start()

        @pl.when((turn == 0) & edge)
        def _():
            hand_out()

        @pl.when(turn == 2)
        def _():
            swap.wait_recv()
            far.start()

    def partial(j):
        cross(j)
        for n in range(0, total.shape[1], wide):
            xg[j, :, n : n + wide] = dot(gated[block(rows, j), :], wo[:, n : n + wide]).astype(bf16)

    def own():
        cross(z)
        for copy in saves[7:]:
            copy.start()
        for n in range(0, total.shape[1], wide):
            total[:, n : n + wide] = tok[:, n : n + wide].astype(f32) + dot(
                gated[block(rows, z), :], wo[:, n : n + wide]
            )

    line_scatter(xg, rbuf, total, s_send, s_recv, s, z, depth, partial, own, hook)
    done = pltpu.make_async_copy(total, hidden_out, save.at[0])
    done.start()

    @pl.when(place < SEQ_DEVS - 1)
    def _():
        for h in range(heads):
            chain(h, s + 1).wait_send()

    def sent(chip, _):
        @pl.when(2 * chip + 1 != s)
        def _():
            for copy in spread(s, chip):
                copy.wait_send()

        return 0

    lax.fori_loop(0, count // 2, sent, 0)

    def came(source, _):
        @pl.when((source != s) & (lax.rem(s, 2) == 1))
        def _():
            for copy in spread(source, 0):
                copy.wait_recv()

        return 0

    lax.fori_loop(0, count, came, 0)
    for copy in moves:
        copy.wait_send()
    swap.wait_send()
    near.wait()
    far.wait()
    mine.wait()
    for copy in saves[1:]:
        copy.wait()
    done.wait()


def attend(
    tok, gain, cot, w_query, w_key, w_value, w_gate, w_out, w_up, w_down, cosine, sine, mask, q_scale, k_scale, decay
):
    f32, bf16 = jnp.float32, jnp.bfloat16
    depth = lax.axis_size("mp")
    rows, width = tok.shape
    span = depth * rows
    heads = w_query.shape[1] // DK
    hk, hv = w_query.shape[1], w_value.shape[1]
    any_ = pl.BlockSpec(memory_space=pl.ANY)
    vmem = pl.BlockSpec(memory_space=pltpu.VMEM)
    shapes = [
        ((depth, rows, width), bf16),
        ((span, hk), bf16),
        ((span, hk), bf16),
        ((span, hv), bf16),
        ((span, hv), f32),
        ((span, hv), f32),
        ((span, hv), bf16),
        ((heads, span, 128), f32),
        ((heads, depth, rows, rows), bf16),
        ((heads, depth, DK, DV), bf16),
        ((rows, width), f32),
        ((4, rows, width), bf16),
        (w_up.shape, bf16),
        (w_down.shape, bf16),
    ]
    count = lax.axis_size("seq")
    dma = pltpu.SemaphoreType.DMA
    return pl.pallas_call(
        attend_kernel,
        out_shape=[jax.ShapeDtypeStruct(*one) for one in shapes],
        in_specs=[vmem, vmem, any_] + [any_] * 13,
        out_specs=[any_] * len(shapes),
        scratch_shapes=[
            pltpu.VMEM((span, DK // 2), f32),
            pltpu.VMEM((span, DK // 2), f32),
            pltpu.VMEM((heads, rows, rows), f32),
            pltpu.VMEM((heads, rows, 1), f32),
            pltpu.VMEM((heads, rows, 1), f32),
            pltpu.VMEM((heads, 2, 1, DV), f32),
            pltpu.VMEM((depth, rows, width), bf16),
            pltpu.VMEM((span, hk), bf16),
            pltpu.VMEM((span, hk), bf16),
            pltpu.VMEM((span, hv), bf16),
            pltpu.VMEM((span, hv), f32),
            pltpu.VMEM((span, hv), f32),
            pltpu.VMEM((span, hv), bf16),
            pltpu.VMEM((heads, span, 128), f32),
            pltpu.VMEM((heads, depth, rows, rows), bf16),
            pltpu.VMEM((heads, depth, DK, DV), f32),
            pltpu.VMEM((heads, depth, DK, DV), bf16),
            pltpu.VMEM((rows, DV), f32),
            pltpu.VMEM((heads, DK, DV), f32),
            pltpu.VMEM((heads, DK, DV), bf16),
            pltpu.VMEM((heads, DK, DV), bf16),
            pltpu.VMEM((depth + 1, rows, width), bf16),
            pltpu.VMEM((rows, width), f32),
            pltpu.VMEM(w_query.shape, bf16),
            pltpu.VMEM(w_key.shape, bf16),
            pltpu.VMEM(w_value.shape, bf16),
            pltpu.VMEM(w_gate.shape, bf16),
            pltpu.VMEM(w_out.shape, bf16),
            dma((11,)),
            dma((10,)),
            dma((2, depth, HALVES)),
            dma((depth, HALVES)),
            dma((depth, HALVES)),
            dma((depth + 1, HALVES)),
            dma((heads,)),
            dma((heads,)),
            dma((4,)),
            dma((3,)),
            dma((2,)),
            dma((2,)),
            dma((2, count // 2)),
            dma((2, count)),
        ],
        compiler_params=pltpu.CompilerParams(
            collective_id=0, has_side_effects=True, vmem_limit_bytes=LIMIT
        ),
        cost_estimate=pl.CostEstimate(
            flops=190 * 10**9, bytes_accessed=60 * 10**6, transcendentals=2 * 10**6
        ),
        name="attend",
    )(tok, gain, cot, w_query, w_key, w_value, w_gate, w_out, w_up, w_down, cosine, sine, mask, q_scale, k_scale, decay)


def row_loop(rows, step, body):
    def one(i, _):
        body(pl.ds(pl.multiple_of(i * step, step), step), i)
        return 0

    lax.fori_loop(0, rows // step, one, 0)


def norm_rows_back(grad_hat, unit, inverse):
    first = jnp.mean(grad_hat, axis=-1, keepdims=True)
    second = jnp.mean(grad_hat * unit, axis=-1, keepdims=True)
    return inverse * (grad_hat - first - unit * second)


def feed_kernel(
    hidden,
    gain,
    cot,
    cot_rows,
    w_up,
    w_down,
    far_up,
    far_down,
    y_keep,
    y_send,
    grad_hidden,
    gain_part,
    g_all_out,
    x,
    dy,
    act,
    du,
    part_y,
    part_x,
    got_x,
    got_own,
    got_y,
    u_tile,
    d_tile,
    g_all,
    up,
    down,
    load,
    save,
    send,
    recv,
):
    f32, bf16 = jnp.float32, jnp.bfloat16
    rows, width = hidden.shape
    units = up.shape[1]
    half = rows // 2
    s, z = lax.axis_index("seq"), lax.axis_index("mp")
    pair = z + 1 - 2 * lax.rem(z, 2)
    twin = s + 1 - 2 * lax.rem(s, 2)
    own_loads = [
        pltpu.make_async_copy(w_up, up, load.at[0]),
        pltpu.make_async_copy(w_down, down, load.at[1]),
    ]
    far_loads = [
        pltpu.make_async_copy(far_up, up, load.at[0]),
        pltpu.make_async_copy(far_down, down, load.at[1]),
    ]

    @pl.when(lax.rem(s, 2) == 0)
    def _():
        for copy in own_loads:
            copy.start()

    @pl.when(lax.rem(s, 2) == 1)
    def _():
        for copy in far_loads:
            copy.start()

    rest = [
        pltpu.make_async_copy(cot_rows.at[a, pl.ds(at, n)], dy.at[pl.ds(to, n)], load.at[2 + i])
        for i, (a, at, n, to) in enumerate(
            [
                (0, 0, rows, 0),
                (2, 0, rows, rows),
                (1, 0, half, 2 * rows),
                (3, 0, half, 2 * rows + half),
                (1, half, half, 3 * rows),
                (3, half, half, 3 * rows + half),
            ]
        )
    ]
    loads = own_loads + rest
    for copy in rest:
        copy.start()

    def norm(here, i):
        unit, _ = centred(hidden[here, :])
        x[here, :] = (unit * gain[...]).astype(bf16)

    row_loop(rows, 32, norm)
    greet([(z >= 0, s, pair), (z >= 0, twin, z)])
    mine, theirs = pl.ds(0, rows), pl.ds(rows, rows)
    parts = [pl.ds(0, half), pl.ds(half, half)]
    pairs = [pl.ds(2 * rows, half), pl.ds(3 * rows, half)]
    twins = [pl.ds(2 * rows + half, half), pl.ds(3 * rows + half, half)]
    near = remote(x.at[mine], x.at[theirs], send.at[0], recv.at[0], twin, z)
    over, far, back_far, back_over, y_far = [], [], [], [], []
    for i in range(2):
        k = 1 + 5 * i
        over.append(remote(x.at[parts[i]], x.at[pairs[i]], send.at[k], recv.at[k], s, pair))
        far.append(remote(x.at[pairs[i]], x.at[twins[i]], send.at[k + 1], recv.at[k + 1], twin, z))
        back_far.append(
            remote(part_x.at[twins[i]], got_x.at[i], send.at[k + 2], recv.at[k + 2], twin, z)
        )
        back_over.append(
            remote(part_x.at[pairs[i]], got_x.at[2 + i], send.at[k + 3], recv.at[k + 3], s, pair)
        )
        y_far.append(
            remote(
                part_y.at[twins[i]], got_y.at[pl.ds(rows + i * half, half)], send.at[k + 4],
                recv.at[k + 4], twin, z,
            )
        )
    back_near = remote(part_x.at[theirs], got_own, send.at[11], recv.at[11], twin, z)
    y_near = remote(part_y.at[theirs], got_y.at[mine], send.at[12], recv.at[12], twin, z)
    over[0].start()
    near.start()
    over[1].start()
    for copy in loads:
        copy.wait()
    step = 512

    def y_terms(r):
        at = block(rows, r)
        for n in range(0, width, step):
            part_y[at, n : n + step] = dot(act[at, :], down[:, n : n + step]).astype(bf16)

    def return_pair(i):
        back_far[i].wait_recv()
        add_rows(part_x.at[pairs[i]], got_x.at[i])
        back_over[i].start()

    def one(r, _):
        at = block(rows, r)

        @pl.when(r == 1)
        def _():
            near.wait_recv()

        @pl.when(r == 2)
        def _():
            over[0].wait_recv()
            far[0].start()
            far[0].wait_recv()

        @pl.when(r == 3)
        def _():
            return_pair(0)
            lax.fori_loop(0, 2, lambda i, c: (y_terms(i), c)[1], 0)
            over[1].wait_recv()
            far[1].start()
            far[1].wait_recv()

        for n in range(0, units, step):
            cols = slice(n, n + step)
            u_tile[...] = dot(x[at, :], up[:, cols])
            d_tile[...] = product_rt(dy[at, :], down[cols, :])

            def gelu(here, i):
                there = pl.ds(pl.multiple_of(r * rows + i * 32, 32), 32)
                u = u_tile[here, :]
                normal = 0.5 * (1.0 + lax.erf(u * (2.0**-0.5)))
                slope = normal + u * (jnp.exp(-0.5 * u * u) * ((2.0 * math.pi) ** -0.5))
                act[there, cols] = (u * normal).astype(bf16)
                du[there, cols] = (d_tile[here, :] * slope).astype(bf16)

            row_loop(rows, 32, gelu)
        for n in range(0, width, step):
            part_x[at, n : n + step] = product_rt(du[at, :], up[n : n + step, :]).astype(bf16)

        @pl.when(r == 1)
        def _():
            back_near.start()

        @pl.when(r == 2)
        def _():
            back_far[0].start()

        @pl.when(r == 3)
        def _():
            back_far[1].start()

        return 0

    lax.fori_loop(0, 4, one, 0)
    return_pair(1)
    lax.fori_loop(2, 4, lambda i, c: (y_terms(i), c)[1], 0)
    y_near.start()
    for copy in y_far:
        copy.start()
    chips, _, high, _ = g_all.shape
    few = units // (2 * chips)
    tall = width // (2 * chips)

    def up_terms(m, _):
        cols = pl.ds(pl.multiple_of(m * 256, 256), 256)
        value = product_t(x[:, cols], du[...]).astype(bf16)
        for part in range(256 // tall):
            to = m * (256 // tall) + part
            g_all[to // 2, lax.rem(to, 2), 0:tall, :] = value[part * tall : (part + 1) * tall]
        return 0

    lax.fori_loop(0, width // 256, up_terms, 0)

    def down_terms(m, _):
        cols = pl.ds(pl.multiple_of(m * 256, 256), 256)
        for n in range(0, width, units):
            value = product_t(act[:, cols], dy[:, n : n + units]).astype(bf16)
            first = tall + n // units * few
            for part in range(256 // few):
                to = m * (256 // few) + part
                g_all[to // 2, lax.rem(to, 2), first : first + few, :] = value[
                    part * few : (part + 1) * few
                ]
        return 0

    lax.fori_loop(0, units // 256, down_terms, 0)
    saves = [pltpu.make_async_copy(g_all, g_all_out, save.at[0])]
    saves[0].start()
    y_near.wait_recv()
    for copy in y_far:
        copy.wait_recv()

    def y_sum(here, i):
        y_keep[here, :] = (
            hidden[here, :] + part_y[here, :].astype(f32) + got_y[here, :].astype(f32)
        )

    row_loop(rows, 32, y_sum)
    for i in range(2):

        def y_pair(here, j):
            there = pl.ds(pl.multiple_of((2 + i) * rows + j * 32, 32), 32)
            came = pl.ds(pl.multiple_of(rows + i * half + j * 32, 32), 32)
            to = pl.ds(pl.multiple_of(i * half + j * 32, 32), 32)
            y_send[to, :] = (part_y[there, :].astype(f32) + got_y[came, :].astype(f32)).astype(bf16)

        row_loop(half, 32, y_pair)
    back_near.wait_recv()
    gain_part[...] = jnp.zeros_like(gain_part)
    for i in range(2):
        back_over[i].wait_recv()

        def finish(here, j):
            at = pl.ds(pl.multiple_of(i * half + j * 32, 32), 32)
            unit, inverse = centred(hidden[at, :])
            grad = (part_x[at, :].astype(f32) + got_own[at, :].astype(f32)) + got_x[
                2 + i, here, :
            ].astype(f32)
            gain_part[...] += jnp.sum(grad * unit, axis=0, keepdims=True)
            grad_hidden[at, :] = cot[at, :].astype(f32) + norm_rows_back(
                grad * gain[...], unit, inverse
            )

        row_loop(half, 32, finish)
    for copy in [near, back_near, y_near] + over + far + back_far + back_over + y_far:
        copy.wait_send()
    for copy in saves:
        copy.wait()


def feed(hidden, gain, cot, cot_rows, w_up, w_down, far_up, far_down):
    f32, bf16 = jnp.float32, jnp.bfloat16
    rows, width = hidden.shape
    units = w_up.shape[1]
    count = lax.axis_size("seq")
    gathered = (count // 2, 2, width // count + width // count, units)
    any_ = pl.BlockSpec(memory_space=pl.ANY)
    vmem = pl.BlockSpec(memory_space=pltpu.VMEM)
    dma = pltpu.SemaphoreType.DMA
    return pl.pallas_call(
        feed_kernel,
        out_shape=[
            jax.ShapeDtypeStruct((rows, width), f32),
            jax.ShapeDtypeStruct((rows, width), bf16),
            jax.ShapeDtypeStruct((rows, width), f32),
            jax.ShapeDtypeStruct((1, width), f32),
            jax.ShapeDtypeStruct(gathered, bf16),
        ],
        in_specs=[vmem, vmem, vmem] + [any_] * 5,
        out_specs=[vmem] * 4 + [any_],
        scratch_shapes=[
            pltpu.VMEM((4 * rows, width), bf16),
            pltpu.VMEM((4 * rows, width), bf16),
            pltpu.VMEM((4 * rows, units), bf16),
            pltpu.VMEM((4 * rows, units), bf16),
            pltpu.VMEM((4 * rows, width), bf16),
            pltpu.VMEM((4 * rows, width), bf16),
            pltpu.VMEM((4, rows // 2, width), bf16),
            pltpu.VMEM((rows, width), bf16),
            pltpu.VMEM((2 * rows, width), bf16),
            pltpu.VMEM((rows, 512), f32),
            pltpu.VMEM((rows, 512), f32),
            pltpu.VMEM(gathered, bf16),
            pltpu.VMEM(w_up.shape, bf16),
            pltpu.VMEM(w_down.shape, bf16),
            dma((8,)),
            dma((1,)),
            dma((13,)),
            dma((13,)),
        ],
        compiler_params=pltpu.CompilerParams(
            collective_id=1, has_side_effects=True, vmem_limit_bytes=LIMIT
        ),
        cost_estimate=pl.CostEstimate(
            flops=75 * 10**9, bytes_accessed=30 * 10**6, transcendentals=2 * 10**6
        ),
        name="feed",
    )(hidden, gain, cot, cot_rows, w_up, w_down, far_up, far_down)


def retract_kernel(
    grad_hidden,
    y_send,
    w_out,
    q_in,
    k_in,
    v_in,
    gp_in,
    gn_in,
    gated_in,
    inv_in,
    p_in,
    r_in,
    cosine_all,
    sine_all,
    mask_all,
    q_scale_all,
    k_scale_all,
    decay_all,
    d_out,
    g_out,
    y_got,
    cosine,
    sine,
    mask,
    q_scale,
    k_scale,
    decay,
    dx,
    q,
    k,
    v,
    gp,
    gn,
    gated,
    inv,
    weights,
    entering,
    wo,
    dall,
    do,
    do_low,
    tile,
    grown,
    dk,
    dv,
    state,
    state_in,
    state_to,
    g_wo,
    load,
    save,
    save_rows,
    g_send,
    g_recv,
    c_send,
    c_recv,
    y_sems,
):
    f32, bf16 = jnp.float32, jnp.bfloat16
    depth, rows, width = dx.shape
    heads = mask.shape[0]
    hk, hv = q.shape[1], v.shape[1]
    s, z = lax.axis_index("seq"), lax.axis_index("mp")
    place = lax.rem(s, SEQ_DEVS)
    pair = z + 1 - 2 * lax.rem(z, 2)
    def tables(place, z):
        at = block(cosine.shape[0], place)
        some = pl.ds(z * heads, heads)
        return [
            (cosine_all.at[at], cosine),
            (sine_all.at[at], sine),
            (mask_all.at[some], mask),
            (q_scale_all.at[some], q_scale),
            (k_scale_all.at[some], k_scale),
            (decay_all.at[some], decay),
        ]

    loads = [
        pltpu.make_async_copy(a, b, load.at[i])
        for i, (a, b) in enumerate(
            [
                (w_out, wo),
                (q_in, q),
                (k_in, k),
                (v_in, v),
                (gp_in, gp),
                (gn_in, gn),
                (gated_in, gated),
                (inv_in, inv),
                (p_in, weights),
                (r_in, entering),
            ]
            + tables(place, z)
        )
    ]
    for copy in loads:
        copy.start()

    def low(here, i):
        dx[z, here, :] = grad_hidden[here, :].astype(bf16)

    def ready(part):
        row_loop(rows // HALVES, 32, lambda here, i: low(
            pl.ds(pl.multiple_of(part * (rows // HALVES) + i * 32, 32), 32), i))

    greet(
        [
            (z > 0, s, z - 1),
            (z < depth - 1, s, z + 1),
            (place > 0, s - 1, z),
            (place < SEQ_DEVS - 1, s + 1, z),
        ]
    )

    @pl.when(place == SEQ_DEVS - 1)
    def _():
        state_in[...] = jnp.zeros_like(state_in)

    def turn_back(value, at, start):
        c, sn = cosine[at, :], sine[at, :]
        half = DK // 2
        a, b = value[:, :half], value[:, half:]
        dall[at, start : start + half] = (a * c + b * sn).astype(bf16)
        dall[at, start + half : start + DK] = (b * c - a * sn).astype(bf16)

    def use(j):
        at = block(rows, j)

        @pl.when(j == z)
        def _():
            for copy in loads:
                copy.wait()

        for h in range(heads):
            wide = slice(h * DV, (h + 1) * DV)
            tile[...] = product_rt(dx[j], wo[wide, :])

            def gate_back(here, i):
                there = pl.ds(pl.multiple_of(j * rows + i * 32, 32), 32)
                grad = tile[here, :]
                gate = gp[there, wide]
                unit = gn[there, wide]
                open_ = 1.0 / (1.0 + jnp.exp(-gate))
                slope = open_ * (1.0 + gate * (1.0 - open_))
                first = 2 * hk + hv + h * DV
                dall[there, first : first + DV] = (grad * unit * slope).astype(bf16)
                inverse = inv[h, there, :][:, :1]
                value = norm_rows_back(grad * gate * open_, unit, inverse)
                high = value.astype(bf16)
                do[there, wide] = high
                do_low[here, wide] = (value - high.astype(f32)).astype(bf16)

            row_loop(rows, 32, gate_back)
        for h in range(heads):
            cols = slice(h * DK, (h + 1) * DK)
            wide = slice(h * DV, (h + 1) * DV)
            qd = (q[at, cols].astype(f32) * q_scale[h]).astype(bf16)
            grown[h, j] = product_t(qd, do[at, wide])

        @pl.when(j != last)
        def _():
            rest(j)

    last = jnp.where(z < depth // 2, depth - 1, 0)

    def rest(j):
        at = block(rows, j)
        for h in range(heads):
            cols = slice(h * DK, (h + 1) * DK)
            wide = slice(h * DV, (h + 1) * DV)
            qb, kb, vb, db = q[at, cols], k[at, cols], v[at, wide], do[at, wide]
            raw = product_rt(db, vb) + product_rt(do_low[:, wide], vb)
            ds = (raw * mask[h]).astype(bf16)
            dv[at, wide] = product_t(weights[h, j], db)
            dk[at, cols] = product_t(ds, qb)
            turn_back(dot(ds, kb) + q_scale[h] * product_rt(db, entering[h, j]), at, h * DK)

    def chain(h, to):
        return remote(state_to.at[h], state_in.at[h], c_send.at[h], c_recv.at[h], to, z)

    line_gather(dx, g_send, g_recv, s, z, depth, use, ready)
    swap = remote(y_send, y_got, y_sems.at[0], y_sems.at[1], s, pair)
    swap.start()
    def out_terms(m, _):
        cols = pl.ds(pl.multiple_of(m * 256, 256), 256)
        for n in range(0, width, 512):
            right = dx[:, :, n : n + 512].reshape(depth * rows, 512)
            g_wo[cols, n : n + 512] = product_t(gated[:, cols], right).astype(bf16)
        return 0

    def out_grad():
        lax.fori_loop(0, hv // 256, out_terms, 0)

    for h in range(heads):
        state[h] = grown[h, depth - 1]
        for b in reversed(range(depth - 1)):
            state[h] = decay[h, 0] * state[h] + grown[h, b]

        @pl.when(place == SEQ_DEVS - 1)
        def _():
            state_to[h] = state[h].astype(bf16)
            chain(h, s - 1).start()

    rest(last)

    @pl.when(place == 0)
    def _():
        out_grad()

    for h in range(heads):

        @pl.when(place < SEQ_DEVS - 1)
        def _():
            chain(h, s + 1).wait_recv()

        @pl.when((place > 0) & (place < SEQ_DEVS - 1))
        def _():
            state_to[h] = (decay[h, 1] * state_in[h].astype(f32) + state[h]).astype(bf16)
            chain(h, s - 1).start()

    for h in range(heads):
        state[h] = state_in[h].astype(f32)

    def done(b):
        at = block(rows, b)
        return pltpu.make_async_copy(dall.at[at], d_out.at[at], save_rows.at[b])

    def cross(turn, _):
        b = depth - 1 - turn
        at = block(rows, b)
        for h in range(heads):
            cols = slice(h * DK, (h + 1) * DK)
            wide = slice(h * DV, (h + 1) * DV)
            leaving = state[h].astype(bf16)
            state[h] = grown[h, b] + decay[h, 0] * state[h]
            kb = k[at, cols]
            vd = (v[at, wide].astype(f32) * k_scale[h]).astype(bf16)
            turn_back(dk[at, cols] + product_rt(vd, leaving), at, hk + h * DK)
            dall[at, 2 * hk + h * DV : 2 * hk + (h + 1) * DV] = (
                dv[at, wide] + k_scale[h] * dot(kb, leaving)
            ).astype(bf16)
        done(b).start()
        return 0

    lax.fori_loop(0, depth, cross, 0)
    saves = [pltpu.make_async_copy(g_wo, g_out, save.at[0])]

    @pl.when(place > 0)
    def _():
        out_grad()

    saves[0].start()
    lax.fori_loop(0, depth, lambda b, c: (done(b).wait(), c)[1], 0)
    line_gather_end(dx, g_send, g_recv, s, z, depth)

    @pl.when(place > 0)
    def _():
        for h in range(heads):
            chain(h, s - 1).wait_send()

    swap.wait()
    for copy in saves:
        copy.wait()


def retract(
    grad_hidden, y_send, w_out, q, k, v, gp, gn, gated, inv, p, r, cosine, sine, mask, q_scale, k_scale, decay
):
    f32, bf16 = jnp.float32, jnp.bfloat16
    depth = lax.axis_size("mp")
    rows, width = grad_hidden.shape
    span = depth * rows
    heads = q.shape[1] // DK
    hk, hv = q.shape[1], v.shape[1]
    any_ = pl.BlockSpec(memory_space=pl.ANY)
    vmem = pl.BlockSpec(memory_space=pltpu.VMEM)
    dma = pltpu.SemaphoreType.DMA
    return pl.pallas_call(
        retract_kernel,
        out_shape=[
            jax.ShapeDtypeStruct((span, 2 * hk + 2 * hv), bf16),
            jax.ShapeDtypeStruct((hv, width), bf16),
            jax.ShapeDtypeStruct((rows, width), bf16),
        ],
        in_specs=[vmem] + [any_] * 17,
        out_specs=[any_] * 3,
        scratch_shapes=[
            pltpu.VMEM((span, DK // 2), f32),
            pltpu.VMEM((span, DK // 2), f32),
            pltpu.VMEM((heads, rows, rows), f32),
            pltpu.VMEM((heads, rows, 1), f32),
            pltpu.VMEM((heads, rows, 1), f32),
            pltpu.VMEM((heads, 2, 1, DV), f32),
            pltpu.VMEM((depth, rows, width), bf16),
            pltpu.VMEM((span, hk), bf16),
            pltpu.VMEM((span, hk), bf16),
            pltpu.VMEM((span, hv), bf16),
            pltpu.VMEM((span, hv), f32),
            pltpu.VMEM((span, hv), f32),
            pltpu.VMEM((span, hv), bf16),
            pltpu.VMEM((heads, span, 128), f32),
            pltpu.VMEM((heads, depth, rows, rows), bf16),
            pltpu.VMEM((heads, depth, DK, DV), bf16),
            pltpu.VMEM(w_out.shape, bf16),
            pltpu.VMEM((span, 2 * hk + 2 * hv), bf16),
            pltpu.VMEM((span, hv), bf16),
            pltpu.VMEM((rows, hv), bf16),
            pltpu.VMEM((rows, DV), f32),
            pltpu.VMEM((heads, depth, DK, DV), f32),
            pltpu.VMEM((span, hk), f32),
            pltpu.VMEM((span, hv), f32),
            pltpu.VMEM((heads, DK, DV), f32),
            pltpu.VMEM((heads, DK, DV), bf16),
            pltpu.VMEM((heads, DK, DV), bf16),
            pltpu.VMEM((hv, width), bf16),
            dma((16,)),
            dma((1,)),
            dma((depth,)),
            dma((2, depth, HALVES)),
            dma((depth, HALVES)),
            dma((heads,)),
            dma((heads,)),
            dma((2,)),
        ],
        compiler_params=pltpu.CompilerParams(
            collective_id=2, has_side_effects=True, vmem_limit_bytes=LIMIT
        ),
        cost_estimate=pl.CostEstimate(
            flops=120 * 10**9, bytes_accessed=40 * 10**6, transcendentals=2 * 10**6
        ),
        name="retract",
    )(grad_hidden, y_send, w_out, q, k, v, gp, gn, gated, inv, p, r, cosine, sine, mask, q_scale, k_scale, decay)


def flip(index, bit):
    return index + bit - 2 * bit * lax.rem(index // bit, 2)


def pair_kernel(
    x_in, d_in, wo_parts, far, out, far_got, x, d, stage, got, wo_mine, wo_got, result, load, save, send, recv, w_sems, f_sems
):
    f32, bf16 = jnp.float32, jnp.bfloat16
    _, chips, rows, _ = stage.shape
    few = wo_mine.shape[1]
    third = result.shape[2]
    s, z = lax.axis_index("seq"), lax.axis_index("mp")
    core = lax.rem(s, 2)
    twin = flip(s, 1)
    across = flip(z, 2)
    edge = (z == 0) | (z == lax.axis_size("mp") - 1)
    loads = [
        pltpu.make_async_copy(d_in, d, load.at[0]),
        pltpu.make_async_copy(x_in, x, load.at[1]),
    ]
    for copy in loads:
        copy.start()
    greet([(z >= 0, twin, z), (z >= 0, s, across), (z >= 0, twin, across)])
    crossed = remote(far.at[0], far_got, f_sems.at[0], f_sems.at[1], twin, across)
    straight = remote(far.at[1], far_got, f_sems.at[2], f_sems.at[3], s, across)

    @pl.when(edge & (core == 1))
    def _():
        crossed.start()
        straight.start()

    wo_load = pltpu.make_async_copy(wo_parts.at[:, core], wo_mine, w_sems.at[0])
    wo_load.start()
    wo_send = remote(wo_parts.at[:, 1 - core], wo_got, w_sems.at[1], w_sems.at[2], twin, z)
    wo_send.start()
    span = max(256, 2 * rows)
    each = span // (2 * rows)

    def give(i):
        return remote(stage.at[1 - core, i], got.at[i], send.at[i], recv.at[i], twin, z)

    def keep(i):
        return pltpu.make_async_copy(result.at[i], out.at[i], save.at[i])

    base = rows * (d.shape[1] // third)

    def take(i):
        give(i).wait_recv()
        for t in range(d.shape[1] // third):

            def add(here, r):
                there = pl.ds(pl.multiple_of(t * rows + r * 32, 32), 32)
                cols = slice(t * third, (t + 1) * third)
                result[i, there, :] = (
                    stage[core, i, here, cols].astype(f32) + got[i, here, cols].astype(f32)
                ).astype(bf16)

            row_loop(rows, 32, add)
        for t in range(wo_mine.shape[2] // third):
            cols = slice(t * third, (t + 1) * third)
            result[i, base + t * few : base + (t + 1) * few, :] = (
                wo_mine[i, :, cols].astype(f32) + wo_got[i, :, cols].astype(f32)
            ).astype(bf16)
        keep(i).start()

    for copy in loads:
        copy.wait()

    def one(g, _):
        for c in range(span // 256):
            chunk = g * (span // 256) + c
            cols = pl.ds(pl.multiple_of(chunk * 256, 256), 256)
            for n in range(0, d.shape[1], 1024):
                value = product_t(x[:, cols], d[:, n : n + 1024]).astype(bf16)
                for part in range(max(1, 256 // rows)):
                    to = (c if each == 1 and rows >= 256 else part) % 2
                    i = g * each + (0 if rows >= 256 else part // 2)
                    stage[to, i, :, n : n + 1024] = value[part * rows : (part + 1) * rows]
        for e in range(each):
            give(g * each + e).start()

        @pl.when(g == 1)
        def _():
            wo_load.wait()
            wo_send.wait()

        @pl.when(g > 0)
        def _():
            for e in range(each):
                take((g - 1) * each + e)

        return 0

    groups = chips // each
    lax.fori_loop(0, groups, one, 0)
    for e in range(each):
        take((groups - 1) * each + e)

    def end(i, _):
        keep(i).wait()
        give(i).wait_send()
        return 0

    lax.fori_loop(0, chips, end, 0)

    @pl.when(edge & (core == 1))
    def _():
        crossed.wait_send()
        straight.wait_send()

    @pl.when(jnp.logical_not(edge) & (core == 0))
    def _():
        crossed.wait_recv()

    @pl.when(jnp.logical_not(edge) & (core == 1))
    def _():
        straight.wait_recv()


def pair_sum(x, d, g_out, far):
    bf16 = jnp.bfloat16
    count = lax.axis_size("seq")
    chips = count // 2
    rows, few = x.shape[1] // count, g_out.shape[0] // count
    wide, third = d.shape[1], d.shape[1] // 3
    high = 3 * rows + few * g_out.shape[1] // third
    any_ = pl.BlockSpec(memory_space=pl.ANY)
    dma = pltpu.SemaphoreType.DMA
    return pl.pallas_call(
        pair_kernel,
        out_shape=[
            jax.ShapeDtypeStruct((chips, high, third), bf16),
            jax.ShapeDtypeStruct(far.shape[1:], bf16),
        ],
        in_specs=[any_] * 4,
        out_specs=[any_, any_],
        scratch_shapes=[
            pltpu.VMEM(x.shape, bf16),
            pltpu.VMEM(d.shape, bf16),
            pltpu.VMEM((2, chips, rows, wide), bf16),
            pltpu.VMEM((chips, rows, wide), bf16),
            pltpu.VMEM((chips, few, g_out.shape[1]), bf16),
            pltpu.VMEM((chips, few, g_out.shape[1]), bf16),
            pltpu.VMEM((chips, high, third), bf16),
            dma((2,)),
            dma((chips,)),
            dma((chips,)),
            dma((chips,)),
            dma((3,)),
            dma((4,)),
        ],
        compiler_params=pltpu.CompilerParams(
            collective_id=3, has_side_effects=True, vmem_limit_bytes=LIMIT
        ),
        cost_estimate=pl.CostEstimate(
            flops=25 * 10**9, bytes_accessed=30 * 10**6, transcendentals=0
        ),
        name="pair_sum",
    )(x, d, g_out.reshape(chips, 2, few, g_out.shape[1]), far)


def finish_kernel(
    d_in,
    x_in,
    tok_in,
    gain,
    gain_part,
    grad_hidden_in,
    w_query,
    w_key,
    w_value,
    w_gate,
    far,
    far_got,
    grad_tok,
    gains,
    g_up,
    g_down,
    d,
    x,
    tok,
    grad_hidden,
    sbuf,
    rbuf,
    total,
    wq,
    wk,
    wv,
    wg,
    mine,
    other,
    gain_all,
    gain_line,
    load,
    d_load,
    x_load,
    s_send,
    s_recv,
    f_sems,
    h_send,
    h_recv,
    l_send,
    l_recv,
):
    f32, bf16 = jnp.float32, jnp.bfloat16
    depth, rows, width = x.shape
    s, z = lax.axis_index("seq"), lax.axis_index("mp")
    core = lax.rem(s, 2)
    twin, across = flip(s, 1), flip(z, 2)
    count = lax.axis_size("seq")
    loads = [
        pltpu.make_async_copy(a, b, load.at[i])
        for i, (a, b) in enumerate(
            [(w_query, wq), (w_key, wk), (w_value, wv), (w_gate, wg)]
        )
    ]

    def slot_loads(j):
        at = block(rows, j)
        return [
            pltpu.make_async_copy(d_in.at[at], d.at[at], d_load.at[j]),
            pltpu.make_async_copy(x_in.at[j], x.at[j], x_load.at[j]),
        ]

    late = [
        pltpu.make_async_copy(a, b, load.at[4 + i])
        for i, (a, b) in enumerate([(tok_in, tok), (grad_hidden_in, grad_hidden)])
    ]
    for copy in loads:
        copy.start()

    def pull(i, _):
        for copy in slot_loads(jnp.where(z < depth // 2, depth - 1 - i, i)):
            copy.start()
        return 0

    lax.fori_loop(0, depth, pull, 0)
    for copy in late:
        copy.start()
    gains[...] = jnp.zeros_like(gains)
    gains[1:2, :] = gain_part[...]
    greet(
        [(z >= 0, twin, across)]
        + [(z != other, s, other) for other in range(depth)]
        + [(s != other, other, z) for other in range(count)]
    )
    near = remote(far.at[1], other, f_sems.at[0], f_sems.at[1], twin, z)
    crossed = remote(far.at[0], other, f_sems.at[0], f_sems.at[1], twin, across)
    straight = remote(far.at[1], mine, f_sems.at[2], f_sems.at[3], s, across)
    edge = (z == 0) | (z == depth - 1)
    inner = jnp.logical_not(edge)
    local = pltpu.make_async_copy(far.at[0], mine, f_sems.at[4])
    to_other = pltpu.make_async_copy(far_got, other, f_sems.at[5])
    to_mine = pltpu.make_async_copy(far_got, mine, f_sems.at[5])

    @pl.when(core == 0)
    def _():
        near.start()
        local.start()

    @pl.when(inner & (core == 0))
    def _():
        to_other.start()

    @pl.when(inner & (core == 1))
    def _():
        to_mine.start()
        crossed.start()
        straight.start()

    for copy in loads:
        copy.wait()
    step = 512
    starts, at_col = [], 0
    for w in (wq, wk, wv, wg):
        starts.append((w, at_col, at_col + w.shape[1]))
        at_col += w.shape[1]

    def term(j, n):
        at = block(rows, j)
        value = None
        for w, a, b in starts:
            one = product_rt(d[at, a:b], w[n : n + step, :])
            value = one if value is None else value + one
        gains[0:1, n : n + step] += jnp.sum(
            value * x[j, :, n : n + step].astype(f32), axis=0, keepdims=True
        )
        return value

    def partial(j):
        for copy in slot_loads(j):
            copy.wait()
        for n in range(0, width, step):
            sbuf[j, :, n : n + step] = term(j, n).astype(bf16)

    def plane(to):
        return remote(gain_all.at[s], gain_all.at[s], h_send.at[to], h_recv.at[s], to, z)

    def line(to):
        return remote(gain_line.at[z], gain_line.at[z], l_send.at[to], l_recv.at[z], s, to)

    def others(count, me, act):
        def one(i, _):
            @pl.when(i != me)
            def _():
                act(i)

            return 0

        lax.fori_loop(0, count, one, 0)

    def own():
        for copy in slot_loads(z):
            copy.wait()
        for n in range(0, width, step):
            total[:, n : n + step] = term(z, n)
        gains[0:1, :] = gains[0:1, :] / gain[...]
        gain_all[s] = gains[...]
        others(count, s, lambda to: plane(to).start())

    line_scatter(sbuf, rbuf, total, s_send, s_recv, s, z, depth, partial, own)

    def plane_came(i):
        remote(gain_all.at[i], gain_all.at[i], h_send.at[i], h_recv.at[i], twin, z).wait_recv()

    def line_came(i):
        remote(gain_line.at[i], gain_line.at[i], l_send.at[i], l_recv.at[i], s, across).wait_recv()

    others(count, s, plane_came)
    gains[...] = gain_all[0]
    for i in range(1, count):
        gains[...] += gain_all[i]
    gain_line[z] = gains[...]
    others(depth, z, lambda to: line(to).start())

    for copy in late:
        copy.wait()

    def last(here, i):
        unit, inverse = centred(tok[here, :].astype(f32))
        grad_tok[here, :] = (
            grad_hidden[here, :] + norm_rows_back(total[here, :] * gain[...], unit, inverse)
        ).astype(bf16)

    row_loop(rows, 32, last)
    others(depth, z, line_came)
    gains[...] = gain_line[0]
    for i in range(1, depth):
        gains[...] += gain_line[i]
    others(count, s, lambda to: plane(to).wait_send())
    others(depth, z, lambda to: line(to).wait_send())

    @pl.when(core == 0)
    def _():
        near.wait_send()
        local.wait()

    @pl.when(core == 1)
    def _():
        near.wait_recv()

    @pl.when(inner & (core == 0))
    def _():
        to_other.wait()

    @pl.when(edge & (core == 0))
    def _():
        crossed.wait_recv()

    @pl.when(inner & (core == 1))
    def _():
        to_mine.wait()
        crossed.wait_send()
        straight.wait_send()

    @pl.when(edge & (core == 1))
    def _():
        straight.wait_recv()

    high, few = g_up.shape[0], g_down.shape[0]
    third = g_up.shape[1]

    g_up[...] = mine[0:high, :].astype(f32) + other[0:high, :].astype(f32)
    for t in range(g_down.shape[1] // third):
        at = slice(high + t * few, high + (t + 1) * few)
        g_down[:, t * third : (t + 1) * third] = mine[at, :].astype(f32) + other[at, :].astype(f32)


def finish(d, x, tok, gain, gain_part, grad_hidden, w_query, w_key, w_value, w_gate, far, far_got):
    f32, bf16 = jnp.float32, jnp.bfloat16
    depth, rows, width = x.shape
    count = lax.axis_size("seq")
    units = far.shape[2]
    any_ = pl.BlockSpec(memory_space=pl.ANY)
    vmem = pl.BlockSpec(memory_space=pltpu.VMEM)
    dma = pltpu.SemaphoreType.DMA
    return pl.pallas_call(
        finish_kernel,
        out_shape=[
            jax.ShapeDtypeStruct((rows, width), bf16),
            jax.ShapeDtypeStruct((8, width), f32),
            jax.ShapeDtypeStruct((width // count, units), f32),
            jax.ShapeDtypeStruct((units // count, width), f32),
        ],
        in_specs=[any_] * 3 + [vmem] * 2 + [any_] * 7,
        out_specs=[vmem] * 4,
        scratch_shapes=[
            pltpu.VMEM(d.shape, bf16),
            pltpu.VMEM(x.shape, bf16),
            pltpu.VMEM((rows, width), bf16),
            pltpu.VMEM((rows, width), f32),
            pltpu.VMEM((depth, rows, width), bf16),
            pltpu.VMEM((depth + 1, rows, width), bf16),
            pltpu.VMEM((rows, width), f32),
            pltpu.VMEM(w_query.shape, bf16),
            pltpu.VMEM(w_key.shape, bf16),
            pltpu.VMEM(w_value.shape, bf16),
            pltpu.VMEM(w_gate.shape, bf16),
            pltpu.VMEM(far.shape[1:], bf16),
            pltpu.VMEM(far.shape[1:], bf16),
            pltpu.VMEM((count, 8, width), f32),
            pltpu.VMEM((depth, 8, width), f32),
            dma((6,)),
            dma((depth,)),
            dma((depth,)),
            dma((depth, HALVES)),
            dma((depth + 1, HALVES)),
            dma((6,)),
            dma((count,)),
            dma((count,)),
            dma((depth,)),
            dma((depth,)),
        ],
        compiler_params=pltpu.CompilerParams(
            collective_id=4, has_side_effects=True, vmem_limit_bytes=LIMIT
        ),
        cost_estimate=pl.CostEstimate(
            flops=110 * 10**9, bytes_accessed=30 * 10**6, transcendentals=0
        ),
        name="finish",
    )(d, x, tok, gain, gain_part, grad_hidden, w_query, w_key, w_value, w_gate, far, far_got)


def unpack_kernel(
    summed, tok, up, down, y_keep, y_got, query, key, value, gate, out, tok_out, up_out, down_out, output
):
    f32 = jnp.float32
    rows, wide = query.shape
    few, tall = out.shape[0], value.shape[1]
    query[...] = summed[0:rows, 0:wide].astype(f32)
    key[...] = summed[0:rows, wide : 2 * wide].astype(f32)
    value[...] = summed[rows : 2 * rows, :].astype(f32)
    gate[...] = summed[2 * rows : 3 * rows, :].astype(f32)
    for t in range(out.shape[1] // tall):
        at = slice(3 * rows + t * few, 3 * rows + (t + 1) * few)
        out[:, t * tall : (t + 1) * tall] = summed[at, :].astype(f32)
    tok_out[...] = tok[...]
    up_out[...] = up[...]
    down_out[...] = down[...]
    output[...] = (y_keep[...] + y_got[...].astype(f32)).astype(output.dtype)


def unpack(summed, tok, up, down, y_keep, y_got, wide):
    f32 = jnp.float32
    count = lax.axis_size("seq")
    width, tall = tok.shape[1], summed.shape[1]
    rows, few = width // count, tall // count
    shapes = [(rows, wide)] * 2 + [(rows, tall)] * 2 + [(few, width)]
    return pl.pallas_call(
        unpack_kernel,
        out_shape=[jax.ShapeDtypeStruct(one, f32) for one in shapes]
        + [jax.ShapeDtypeStruct(a.shape, a.dtype) for a in (tok, up, down, y_got)],
        compiler_params=pltpu.CompilerParams(vmem_limit_bytes=LIMIT),
        name="unpack",
    )(summed, tok, up, down, y_keep, y_got)


def shards(
    tokens, gain_mix, w_query, w_key, w_value, w_gate, w_out, gain_ffn, w_up, w_down, cotangent
):
    bf16 = jnp.bfloat16
    f32 = jnp.float32
    span_rows = lax.axis_size("mp") * tokens.shape[0]
    local_heads = w_query.shape[1] // DK
    trig = decay_tables(span_rows, local_heads * lax.axis_size("mp"))
    (
        x_rows,
        q_all,
        k_all,
        v_all,
        gate,
        unit,
        gated,
        inverse,
        weights,
        entering,
        hidden,
        cot_rows,
        far_up,
        far_down,
    ) = attend(
        tokens, gain_mix[None, :], cotangent, w_query, w_key, w_value, w_gate, w_out, w_up, w_down, *trig
    )
    y_keep, y_send, grad_hidden, gain_ffn_part, grad_ffn = feed(
        hidden, gain_ffn[None, :], cotangent, cot_rows, w_up, w_down, far_up, far_down
    )
    far = lax.psum_scatter(
        grad_ffn, "seq", scatter_dimension=0, tiled=False, axis_index_groups=same_core()
    )
    grad_in, grad_out_w, y_got = retract(
        grad_hidden, y_send, w_out, q_all, k_all, v_all, gate, unit, gated, inverse, weights, entering, *trig
    )
    pairs, far_got = pair_sum(x_rows.reshape(span_rows, -1), grad_in, grad_out_w, far)
    summed = lax.psum_scatter(
        pairs, "seq", scatter_dimension=0, tiled=False, axis_index_groups=same_core()
    )
    grad_in, pairs = lax.optimization_barrier((grad_in, pairs))
    grad_tokens, gains, final_up, final_down = finish(
        grad_in, x_rows, tokens, gain_mix[None, :], gain_ffn_part, grad_hidden, w_query, w_key, w_value, w_gate, far, far_got
    )
    summed, gains = lax.optimization_barrier((summed, gains))
    gain_mix_sum, gain_ffn_sum = gains[0], gains[1]
    (
        final_query,
        final_key,
        final_value,
        final_gate,
        final_out,
        grad_tokens,
        final_up,
        final_down,
        output,
    ) = unpack(summed, grad_tokens, final_up, final_down, y_keep, y_got, w_query.shape[1])
    return (
        output,
        grad_tokens,
        gain_mix_sum,
        final_query,
        final_key,
        final_value,
        final_gate,
        final_out,
        gain_ffn_sum,
        final_up,
        final_down,
    )


def solution(mesh):
    return jax.shard_map(
        shards,
        mesh=mesh,
        in_specs=(
            P(("seq", "mp"), None),
            P(),
            P(None, "mp"),
            P(None, "mp"),
            P(None, "mp"),
            P(None, "mp"),
            P("mp", None),
            P(),
            P(None, "mp"),
            P("mp", None),
            P(("seq", "mp"), None),
        ),
        out_specs=(
            P(("seq", "mp"), None),
            P(("seq", "mp"), None),
            P(),
            P("seq", "mp"),
            P("seq", "mp"),
            P("seq", "mp"),
            P("seq", "mp"),
            P(("mp", "seq"), None),
            P(),
            P("seq", "mp"),
            P(("mp", "seq"), None),
        ),
        check_vma=False,
    )
```
